32 devices in a mesh: gx: 4 (over y, core), gy: 2 (over x), gz: 4 (over z).
Axes of the slice: x: 2, y: 2, z: 4, core: 2. Of those that a mesh axis runs over, the one named last changes fastest.
Arguments:
- rhs: float32 [4, 2, 3, 162, 1024], P('gx', 'gy', None, None, 'gz'), may hold values from -6 to 6
- angles: float32 [4, 2, 3, 1024], P('gx', 'gy', None, 'gz'), may hold values from -3.140625 to 3.140625
- self_mob: float32 [486, 486], replicated, may hold values from -0.25 to 0.25
- near_mat: float32 [486, 486], replicated, may hold values from -0.25 to 0.25
- near_weight: float32 [4, 2, 8, 1024], P('gx', 'gy', None, 'gz'), may hold values from -2 to 2
- neighbours: int32 [4, 2, 8, 1024], P('gx', 'gy', None, 'gz'), may hold values from 0 to 2111, as said below
- cells: int32 [4, 2, 1024], P('gx', 'gy', 'gz'), may hold values from 0 to 191
- blob_weight: float32 [162], replicated, may hold values from -0.5 to 0.5
- skel_perm: int32 [2, 384], replicated, may hold values from 0 to 383, each once within a row
- interp: float32 [2, 192, 192], replicated, may hold values from -0.4375 to 0.4375
- sibling_ops: float32 [2, 192, 192], replicated, may hold values from -0.375 to 0.375
- root_op: float32 [192, 192], replicated, may hold values from -0.0625 to 0.0625
Outputs:
- solution: float32 [4, 2, 3, 162, 1024], P('gx', 'gy', None, None, 'gz')
- lsq_residual: float32 [], replicated
The draws below stay inside these ranges and needn't reach their ends.
Inputs may be any that keep to these rules, and one draw needn't show every extreme that they name: `neighbours`: each id is s * 256 + j with slot s in 0..8 and j < 256; j < 64 whenever s != 4, and some id in every draw reaches j = 63 in slot 8.
All inputs are finite; a program needn't handle non-finite values.
Results may differ from the reference program's by a relative error of at most 0.0003.
Values sent between devices are 32-bit elements; how exact they have to be, the bound alone decides.
No kernel may reach another device: no remote copies, remote signals or barrier semaphores. Data moves between devices by JAX's collectives and lax.ppermute only.
A program may use at most 128 MiB of HBM per device.

```python
import jax
import jax.numpy as jnp
from jax import lax

BLOBS = 162
SKEL = 192
NEIGH = 8
LEVELS = 2
B_DEV = 256
DOF = 486
RIM = 64
COLS = 1024
N_GX = 4
N_GY = 2
N_GZ = 4


def draw_neighbours(key, part):
    key_slot, key_own, key_rim = jax.random.split(key, 3)
    shape = (N_GX, N_GY, NEIGH, COLS)
    box_slot = jax.random.randint(key_slot, shape, 0, 9)
    own_body = jax.random.randint(key_own, shape, 0, B_DEV)
    rim_body = jax.random.randint(key_rim, shape, 0, RIM)
    ids = jnp.where(box_slot == 4, box_slot * B_DEV + own_body, box_slot * B_DEV + rim_body)
    ids = ids.at[0, 0, 0, 0].set(0)
    ids = ids.at[0, 0, 1, 0].set(8 * B_DEV + RIM - 1)
    return ids.astype(jnp.int32)


def set_ends(entries, stream_key, least, top_value):
    extent = entries.shape
    index_at = [jax.random.randint(jax.random.fold_in(stream_key, axis), (), 0, extent[axis]) for axis in range(len(extent))]
    entries = entries.at[tuple(index_at)].set(least)
    longest = extent.index(max(extent))
    index_at[longest] = (index_at[longest] + 1) % extent[longest]
    return entries.at[tuple(index_at)].set(top_value)


def steps_of(own_key, extent, cuts, smallest, high):
    factor_of = 1.0
    for position, shards_of in cuts:
        heights = jax.random.uniform(jax.random.fold_in(jax.random.fold_in(own_key, 6), position), (shards_of,), jnp.float32, smallest / len(cuts), high / len(cuts))
        factor_of = factor_of * jnp.repeat(jnp.exp(heights), extent[position] // shards_of).reshape((-1,) + (1,) * (len(extent) - 1 - position))
    return factor_of


def bell_draw(own_key, extent, width, most, pieces=(), kind=jnp.bfloat16):
    drawn = width * jax.random.normal(own_key, extent, jnp.float32)
    if pieces:
        drawn = drawn * steps_of(own_key, extent, pieces, -0.22, 0.18)
    return jnp.clip(drawn, -most, most).astype(kind)


def setup_inputs(seed: int = 0) -> dict:
    seeds = jax.random.split(jax.random.key(seed), 13)
    return {
        "rhs": bell_draw(seeds[0], (N_GX, N_GY, 3, BLOBS, COLS), 1.0, 6.0, ((0, 4), (1, 2), (4, 4)), jnp.float32),
        "angles": jnp.clip(jax.random.uniform(seeds[1], (N_GX, N_GY, 3, COLS), jnp.float32, -3.140625, 3.140625), -3.140625, 3.140625),
        "self_mob": bell_draw(seeds[2], (DOF, DOF), DOF ** -0.5, 0.25, (), jnp.float32),
        "near_mat": bell_draw(seeds[3], (DOF, DOF), DOF ** -0.5, 0.25, (), jnp.float32),
        "near_weight": bell_draw(seeds[4], (N_GX, N_GY, NEIGH, COLS), 0.35, 2.0, ((0, 4), (1, 2), (3, 4)), jnp.float32),
        "neighbours": draw_neighbours(jax.random.fold_in(seeds[12], 71), 0),
        "cells": set_ends(jax.random.randint(seeds[6], (N_GX, N_GY, COLS), 0, SKEL), jax.random.fold_in(seeds[6], 1), 0, SKEL - 1).astype(jnp.int32),
        "blob_weight": bell_draw(seeds[7], (BLOBS,), BLOBS ** -0.5, 0.5, (), jnp.float32),
        "skel_perm": jax.vmap(lambda own: jax.random.permutation(own, 2 * SKEL))(jax.random.split(seeds[8], LEVELS)).reshape((LEVELS, 2 * SKEL)).astype(jnp.int32),
        "interp": bell_draw(seeds[9], (LEVELS, SKEL, SKEL), SKEL ** -0.5, 0.4375, (), jnp.float32),
        "sibling_ops": bell_draw(seeds[10], (LEVELS, SKEL, SKEL), 0.06, 0.375, (), jnp.float32),
        "root_op": bell_draw(seeds[11], (SKEL, SKEL), 0.01, 0.0625, (), jnp.float32),
    }


highest = lax.Precision.HIGHEST
epsilon = 1e-06

def frame(angles):
    cos_yaw = jnp.cos(angles[0])
    sin_yaw = jnp.sin(angles[0])
    cos_pitch = jnp.cos(angles[1])
    sin_pitch = jnp.sin(angles[1])
    cos_roll = jnp.cos(angles[2])
    sin_roll = jnp.sin(angles[2])
    return ((cos_yaw * cos_pitch, cos_yaw * sin_pitch * sin_roll - sin_yaw * cos_roll, cos_yaw * sin_pitch * cos_roll + sin_yaw * sin_roll), (sin_yaw * cos_pitch, sin_yaw * sin_pitch * sin_roll + cos_yaw * cos_roll, sin_yaw * sin_pitch * cos_roll - cos_yaw * sin_roll), (-sin_pitch, cos_pitch * sin_roll, cos_pitch * cos_roll))

def rotate(source, rotation, inverse):
    components = []
    for target_axis in range(3):
        summed = jnp.zeros_like(source[0])
        for source_axis in range(3):
            factor = rotation[source_axis][target_axis] if inverse else rotation[target_axis][source_axis]
            summed = summed + factor[None, :] * source[source_axis]
        components.append(summed)
    return jnp.stack(components)

def least_squares(beta, diag_first, below_first, above_second, diag_second, below_second):
    first_norm = jnp.sqrt(diag_first * diag_first + below_first * below_first)
    first_cos = diag_first / first_norm
    first_sin = below_first / first_norm
    top_right = first_cos * above_second + first_sin * diag_second
    lower_right = first_cos * diag_second - first_sin * above_second
    second_norm = jnp.sqrt(lower_right * lower_right + below_second * below_second)
    second_cos = lower_right / second_norm
    second_sin = below_second / second_norm
    carried = -first_sin * beta
    coef_two = second_cos * carried / second_norm
    coef_one = (first_cos * beta - top_right * coef_two) / first_norm
    return (coef_one, coef_two, jnp.abs(second_sin * carried))

def reference(rhs, angles, self_mob, near_mat, near_weight, neighbours, cells, blob_weight, skel_perm, interp, sibling_ops, root_op):
    vector = jnp.transpose(rhs, (2, 3, 0, 1, 4)).reshape(3, BLOBS, -1)
    rotation = frame(jnp.transpose(angles, (2, 0, 1, 3)).reshape(3, -1))
    coef = jnp.transpose(near_weight, (2, 0, 1, 3)).reshape(NEIGH, -1)
    box_x = jnp.arange(N_GX, dtype=jnp.int32)[:, None, None, None]
    box_y = jnp.arange(N_GY, dtype=jnp.int32)[None, :, None, None]
    column = jnp.arange(COLS, dtype=jnp.int32)[None, None, None, :]
    box_slot = neighbours // B_DEV
    body_slot = neighbours % B_DEV
    target_x = (box_x + box_slot // 3 - 1) % N_GX
    target_y = (box_y + box_slot % 3 - 1) % N_GY
    target = (target_x * N_GY + target_y) * COLS + column // B_DEV * B_DEV + body_slot
    global_ids = jnp.transpose(target, (2, 0, 1, 3)).reshape(NEIGH, -1).astype(jnp.int32)
    leaf_cells = cells.reshape(N_GX, N_GY, N_GZ, B_DEV)
    occupancy = (leaf_cells[..., None] == jnp.arange(SKEL, dtype=jnp.int32)).astype(jnp.float32)
    layers = jnp.arange(N_GZ, dtype=jnp.int32)

    def operate(source):
        turned = rotate(source, rotation, False).reshape(DOF, -1)
        mixture = jnp.dot(self_mob, turned, precision=highest).reshape(3, BLOBS, -1)
        own_part = source + rotate(mixture, rotation, True)
        flat = source.reshape(DOF, -1)
        gathered = jnp.zeros_like(flat)
        for link_index in range(NEIGH):
            gathered = gathered + coef[link_index][None, :] * jnp.take(flat, global_ids[link_index], axis=1)
        near_part = jnp.dot(near_mat, gathered, precision=highest).reshape(3, BLOBS, -1)
        moments = jnp.einsum('cqn,q->cn', source, blob_weight, precision=highest)
        moments = moments.reshape(3, N_GX, N_GY, N_GZ, B_DEV)
        charges = jnp.einsum('cxyzb,xyzbj->xyzcj', moments, occupancy, precision=highest)
        partners = []
        high_flags = []
        for tree_level in range(LEVELS):
            partner = charges[:, :, layers ^ 1 << tree_level]
            high_side = (layers >> tree_level & 1 == 1)[None, None, :, None, None]
            low_child = jnp.where(high_side, partner, charges)
            higher = jnp.where(high_side, charges, partner)
            joined = jnp.concatenate([low_child, higher], axis=-1)
            picked = joined[..., skel_perm[tree_level]]
            charges = picked[..., :SKEL] + jnp.einsum('xyzcj,jk->xyzck', picked[..., SKEL:], interp[tree_level], precision=highest)
            partners.append(partner)
            high_flags.append(high_side)
        root_total = lax.optimization_barrier(jnp.sum(charges, axis=(0, 1), keepdims=True))
        potential = jnp.einsum('xyzcj,jk->xyzck', root_total - charges, root_op, precision=highest)
        for tree_level in reversed(range(LEVELS)):
            extra = jnp.einsum('xyzcj,kj->xyzck', potential, interp[tree_level], precision=highest)
            spread = jnp.concatenate([potential, extra], axis=-1)
            placed = jnp.zeros_like(spread).at[..., skel_perm[tree_level]].set(spread)
            child_part = jnp.where(high_flags[tree_level], placed[..., SKEL:], placed[..., :SKEL])
            potential = child_part + jnp.einsum('xyzcj,jk->xyzck', partners[tree_level], sibling_ops[tree_level], precision=highest)
        body_values = jnp.einsum('xyzcj,xyzbj->cxyzb', potential, occupancy, precision=highest).reshape(3, -1)
        far_part = blob_weight[None, :, None] * body_values[:, None, :]
        return own_part + near_part + far_part
    beta = jnp.sqrt(jnp.sum(vector * vector) + epsilon)
    basis_one = vector / beta
    image_one = operate(basis_one)
    diag_first = jnp.sum(image_one * basis_one)
    residue_one = image_one - diag_first * basis_one
    below_first = jnp.sqrt(jnp.sum(residue_one * residue_one) + epsilon)
    basis_two = residue_one / below_first
    image_two = operate(basis_two)
    above_second = jnp.sum(image_two * basis_one)
    diag_second = jnp.sum(image_two * basis_two)
    residue_two = image_two - above_second * basis_one - diag_second * basis_two
    below_second = jnp.sqrt(jnp.sum(residue_two * residue_two) + epsilon)
    coef_one, coef_two, lsq_residual = least_squares(beta, diag_first, below_first, above_second, diag_second, below_second)
    result = coef_one * basis_one + coef_two * basis_two
    solution = jnp.transpose(result.reshape(3, BLOBS, N_GX, N_GY, COLS), (2, 3, 0, 1, 4))
    return (solution, lsq_residual)
```

```python
import functools

import jax
import jax.numpy as jnp
from jax import lax
from jax.experimental import pallas as pl
from jax.experimental.pallas import tpu as pltpu
from jax.sharding import PartitionSpec as P

epsilon = 1e-06
f32 = jnp.float32
bf16 = jnp.bfloat16
RIM = 64
LANES = 128


def round_up(value, unit):
    return -(-value // unit) * unit


def split(x):
    hi = x.astype(bf16)
    lo = (x - hi.astype(f32)).astype(bf16)
    return hi, lo


def mm(a, b):
    return lax.dot_general(a, b, (((1,), (0,)), ((), ())), preferred_element_type=f32)


def mt(a, b):
    return lax.dot_general(a, b, (((1,), (1,)), ((), ())), preferred_element_type=f32)


def product(dot, a, b):
    return dot(a[0], b[0]) + (dot(a[0], b[1]) + dot(a[1], b[0]))


def total(x):
    return jnp.sum(jnp.sum(x, axis=0, keepdims=True), axis=1, keepdims=True)


class Sizes:
    def __init__(self, mesh_shape, rhs, skel_perm):
        self.nx, self.ny, self.nz = (mesh_shape[a] for a in ("gx", "gy", "gz"))
        self.devices = self.nx * self.ny * self.nz
        self.blobs, self.bodies = rhs.shape[-2:]
        self.step = round_up(self.blobs, 8)
        self.rows = round_up(3 * self.step, 16)
        self.half = self.rows // 2
        self.levels = skel_perm.shape[0]
        self.skel = skel_perm.shape[1] // 2
        self.own_slots = []
        self.sources = []
        self.slot_base = []
        for slot in range(9):
            offset = ((slot // 3 - 1) % self.nx, (slot % 3 - 1) % self.ny)
            if offset == (0, 0):
                self.slot_base.append(0)
                continue
            if offset not in self.sources:
                self.sources.append(offset)
            self.slot_base.append(self.bodies + RIM * self.sources.index(offset))
        self.ghosts = round_up(max(1, len(self.sources)) * RIM, LANES)


def pieces(x, s):
    return [x[c * s.step : c * s.step + s.step] for c in range(3)]


def turn(parts, rot, inverse):
    out = []
    for target in range(3):
        acc = None
        for source in range(3):
            row = 3 * source + target if inverse else 3 * target + source
            term = rot[row : row + 1] * parts[source]
            acc = term if acc is None else acc + term
        out.append(acc)
    return out


def stacked(parts, s):
    rest = s.rows - 3 * s.step
    if rest:
        parts = list(parts) + [jnp.zeros((rest, s.bodies), f32)]
    return jnp.concatenate(parts, axis=0)


def occupancy(cells, s):
    row = lax.broadcasted_iota(jnp.int32, (s.skel, s.bodies), 0)
    return jnp.where(cells == row, 1.0, 0.0).astype(bf16)


def pack_charges(parts, weight_col, occ, s):
    moments = [jnp.sum(part * weight_col, axis=0, keepdims=True) for part in parts]
    moments = jnp.concatenate(moments + [jnp.zeros((5, s.bodies), f32)], axis=0)
    high, rest = split(moments)
    mid, low = split(moments - high.astype(f32))
    stack = jnp.concatenate([high.astype(f32), mid.astype(f32), low.astype(f32)], axis=0).astype(bf16)
    sums = mt(stack, occ)
    charges = sums[0:8] + (sums[8:16] + sums[16:24])
    tail = jnp.concatenate([charges[:, LANES:], jnp.zeros((8, 2 * LANES - s.skel), f32)], axis=1)
    row = lax.broadcasted_iota(jnp.int32, (8, LANES), 0)
    return jnp.where(row < 4, charges[:, :LANES], pltpu.roll(tail, 4, 0))


def pack_rim(x, s):
    lane = lax.broadcasted_iota(jnp.int32, (s.half, LANES), 1)
    top, bottom = x[: s.half, :LANES], x[s.half :, :LANES]
    return jnp.where(lane < RIM, top, pltpu.roll(bottom, RIM, 1))


def unpack_rims(rims, s):
    lane = lax.broadcasted_iota(jnp.int32, (s.half, LANES), 1)
    tops, bottoms = [], []
    for i in range(0, s.ghosts // RIM, 2):
        a = rims[i]
        b = rims[i + 1] if i + 1 < len(rims) else jnp.zeros_like(a)
        tops.append(jnp.where(lane < RIM, a, pltpu.roll(b, RIM, 1)))
        bottoms.append(jnp.where(lane < RIM, pltpu.roll(a, RIM, 1), b))
    return jnp.concatenate(
        [jnp.concatenate(tops, axis=1), jnp.concatenate(bottoms, axis=1)], axis=0
    )


def start_kernel(s, rhs, cells, weight, q_out, rim_out, col_out, f_out):
    f_out[...] = jnp.zeros_like(f_out)
    for c in range(3):
        f_out[c * s.step : c * s.step + s.blobs, :] = rhs[0, 0, c]
    f = f_out[...]
    wide = jnp.concatenate([weight[...], jnp.zeros((1, 2 * LANES - s.blobs), f32)], axis=1)
    col = jnp.broadcast_to(wide, (LANES, 2 * LANES)).T[: s.step]
    col_out[...] = col
    rim_out[...] = pack_rim(f, s)
    occ = occupancy(cells[0], s)
    q_out[...] = pack_charges(pieces(f, s), col[:, :1], occ, s)


def frame_rows(angles):
    cos, sin = jnp.cos(angles), jnp.sin(angles)
    cy, cp, cr = cos[0:1], cos[1:2], cos[2:3]
    sy, sp, sr = sin[0:1], sin[1:2], sin[2:3]
    return [
        cy * cp,
        cy * sp * sr - sy * cr,
        cy * sp * cr + sy * sr,
        sy * cp,
        sy * sp * sr + cy * cr,
        sy * sp * cr - cy * sr,
        -sp,
        cp * sr,
        cp * cr,
    ]


def local_part(f, s, rot, mob, own):
    parts = pieces(f, s)
    turned = stacked(turn(parts, rot, False), s)
    mixed = product(mm, mob, split(turned))
    back = turn(pieces(mixed, s), rot, True)
    return f + stacked(back, s), product(mm, split(f), own)


def expand(block, level, ups):
    if level == 0:
        return [block]
    up = ups[level - 1]
    n = up.shape[0] // 2
    both = product(mm, split(up), split(block))
    return expand(both[:n], level - 1, ups) + expand(both[n:], level - 1, ups)


def setup_kernel(
    s, ids, f_in, angles, self_mob, near_mat, near_weight, neighbours, perm, interp, sibling, root,
    loc_out, gat_out, rot_out, sh_out, sl_out, nh_out, nl_out, oh_out, ol_out, gh_out, gl_out,
    th_out, tl_out, padded, ups_ref,
):
    f = f_in[...]
    rot = jnp.concatenate(frame_rows(angles[0, 0]) + [jnp.zeros((7, s.bodies), f32)], axis=0)
    rot_out[...] = rot

    padded[...] = jnp.zeros_like(padded)
    for matrix, hi_out, lo_out in ((self_mob, sh_out, sl_out), (near_mat, nh_out, nl_out)):
        for c in range(3):
            for d in range(3):
                padded[c * s.step : c * s.step + s.blobs, d * s.step : d * s.step + s.blobs] = matrix[
                    c * s.blobs : (c + 1) * s.blobs, d * s.blobs : (d + 1) * s.blobs
                ]
        hi, lo = split(padded[...])
        hi_out[...] = hi
        lo_out[...] = lo

    links = neighbours[0, 0]
    slot = links // s.bodies
    base = jnp.zeros_like(links)
    for index, start in enumerate(s.slot_base):
        base = jnp.where(slot == index, start, base)
    column = base + links % s.bodies
    coef = near_weight[0, 0]
    for first, count, hi_out, lo_out in (
        (0, s.bodies, oh_out, ol_out),
        (s.bodies, s.ghosts, gh_out, gl_out),
    ):
        for r in range(0, count, 64):
            row = lax.broadcasted_iota(jnp.int32, (64, s.bodies), 0) + (first + r)
            acc = jnp.zeros((64, s.bodies), f32)
            for k in range(coef.shape[0]):
                acc = acc + jnp.where(column[k : k + 1] == row, coef[k : k + 1], 0.0)
            hi, lo = split(acc)
            hi_out[r : r + 64, :] = hi
            lo_out[r : r + 64, :] = lo

    loc, gat = local_part(f, s, rot, (sh_out[...], sl_out[...]), (oh_out[...], ol_out[...]))
    loc_out[...] = loc
    gat_out[...] = gat

    n = s.skel
    z = ids[1]
    ups = []
    eye_row = lax.broadcasted_iota(jnp.int32, (n, n), 0)
    eye_col = lax.broadcasted_iota(jnp.int32, (n, n), 1)
    eye = jnp.where(eye_row == eye_col, 1.0, 0.0)
    for level in range(s.levels):
        spot = lax.broadcasted_iota(jnp.int32, (2 * n, 2 * n), 0)
        onehot = jnp.where(perm[level : level + 1, :] == spot, 1.0, 0.0).astype(bf16)
        hi, lo = split(jnp.concatenate([eye, interp[level]], axis=0))
        up = mm(onehot, hi) + mm(onehot, lo)
        ups.append(up)
        ups_ref[level] = up

    def down(block, level):
        bit = (z >> level) & 1
        half = ups_ref[level, pl.ds(pl.multiple_of(bit * n, 8), n), :]
        return product(mt, split(block), split(half))

    spread = root[...]
    beside = []
    for level in reversed(range(s.levels)):
        spread = down(spread, level)
        beside = [down(block, level) for block in beside]
        beside.append(sibling[level])
    far_leaves = expand(spread, s.levels, ups)
    near_leaves = [jnp.zeros((n, n), f32) for _ in range(s.nz)]
    for level, block in zip(reversed(range(s.levels)), beside):
        sub = expand(block, level, ups)
        for leaf in range(s.nz):
            hit = (leaf >> level) == ((z >> level) ^ 1)
            near_leaves[leaf] = jnp.where(hit, near_leaves[leaf] + sub[leaf % (1 << level)], near_leaves[leaf])
    pad = jnp.zeros((2 * LANES - n, n), f32)
    for leaf in range(s.nz):
        for group, block in ((0, near_leaves[leaf] - far_leaves[leaf]), (s.nz, far_leaves[leaf])):
            hi, lo = split(jnp.concatenate([block, pad], axis=0))
            at = (group + leaf) * 2 * LANES
            th_out[at : at + 2 * LANES, :] = hi
            tl_out[at : at + 2 * LANES, :] = lo


def image(s, ids, loc, gat, rims, near, ghost, charges, far_op, cells, col):
    column = ids[0]
    chunks = []
    for leaf in range(s.nz):
        chunks.append(charges[column * s.nz + leaf])
    for leaf in range(s.nz):
        acc = charges[leaf]
        for c in range(1, s.nx * s.ny):
            acc = acc + charges[c * s.nz + leaf]
        chunks.append(acc)
    left = jnp.concatenate([x for tile in chunks for x in (tile, pltpu.roll(tile, 4, 0))], axis=1)
    potential = product(mm, split(left), far_op)
    occ = occupancy(cells[0], s)
    p_hi, p_lo = split(potential)
    p_mid, p_low = split(potential - p_hi.astype(f32))
    stack = jnp.concatenate([p_hi.astype(f32), p_mid.astype(f32), p_low.astype(f32)], axis=0).astype(bf16)
    values = mm(stack, occ)
    values = values[0:8] + (values[8:16] + values[16:24])
    far = stacked([col * values[c : c + 1] for c in range(3)], s)
    gathered = gat + product(mm, split(unpack_rims(rims, s)), ghost)
    return (loc + far) + product(mm, near, split(gathered))


def first_kernel(s, n_rims, ids, loc, gat, nh, nl, gh, gl, charges, th, tl, cells, col, *rest):
    rims, (u_out, q_out, rim_out) = rest[:n_rims], rest[n_rims:]
    weight_col = col[:, :1]
    u = image(
        s, ids, loc[...], gat[...], [r[...] for r in rims], (nh[...], nl[...]), (gh[...], gl[...]),
        charges, (th[...], tl[...]), cells, weight_col,
    )
    u_out[...] = u
    rim_out[...] = pack_rim(u, s)
    q_out[...] = pack_charges(pieces(u, s), weight_col, occupancy(cells[0], s), s)


def safe_inverse(x):
    return jnp.where(x > 0.0, 1.0 / jnp.where(x > 0.0, x, 1.0), 0.0)


def middle_kernel(s, u_in, f_in, rot, sh, sl, oh, ol, loc_out, gat_out, ortho_out, stat_out):
    u, f = u_in[...], f_in[...]
    loc, gat = local_part(u, s, rot[...], (sh[...], sl[...]), (oh[...], ol[...]))
    loc_out[...] = loc
    gat_out[...] = gat
    ff = total(f * f)
    fu = total(f * u) * safe_inverse(ff)
    ortho = u - fu * f
    ortho_out[...] = ortho
    oo = total(ortho * ortho)
    stat_out[...] = jnp.broadcast_to(
        jnp.concatenate([ff, fu, oo, jnp.zeros((5, 1), f32)], axis=0), (8, LANES)
    )


def second_kernel(
    s, n_rims, ids, loc, gat, nh, nl, gh, gl, charges, th, tl, cells, col, f_in, ortho_in, stat, *rest
):
    rims, (stat_out,) = rest[:n_rims], rest[n_rims:]
    t = image(
        s, ids, loc[...], gat[...], [r[...] for r in rims], (nh[...], nl[...]), (gh[...], gl[...]),
        charges, (th[...], tl[...]), cells, col[:, :1],
    )
    f, ortho = f_in[...], ortho_in[...]
    ff, fu, oo = (stat[i : i + 1, :1] for i in range(3))
    ft = total(f * t) * safe_inverse(ff)
    ot = total(ortho * t) * safe_inverse(oo)
    rest_t = t - ft * f - ot * ortho
    tt = total(rest_t * rest_t)
    rf, ro = jnp.sqrt(ff), jnp.sqrt(oo)
    stat_out[...] = jnp.broadcast_to(
        jnp.concatenate(
            [rf, rf * fu, ro, rf * ft, ro * ot, jnp.sqrt(tt), jnp.zeros((2, 1), f32)], axis=0
        ),
        (8, LANES),
    )


def finish_kernel(s, stats, rhs, u_in, x_out, lsq_out):
    groups = []
    for g in range(0, s.devices, LANES):
        acc = jnp.zeros((8, LANES), f32)
        lane = lax.broadcasted_iota(jnp.int32, (8, LANES), 1)
        for d in range(g, min(s.devices, g + LANES)):
            acc = acc + jnp.where(lane == d - g, stats[d], 0.0)
        groups.append(acc)
    rows = jnp.concatenate(groups, axis=1) if len(groups) > 1 else groups[0]
    f1, u1, u2, t1, t2, t3 = (rows[i : i + 1] for i in range(6))

    def along(x):
        return jnp.sum(x, axis=1, keepdims=True)

    beta = jnp.sqrt(along(f1 * f1) + epsilon)
    v = f1 / beta
    w1, w2 = u1 / beta, u2 / beta
    h11 = along(w1 * v)
    r1 = w1 - h11 * v
    h21 = jnp.sqrt(along(r1 * r1 + w2 * w2) + epsilon)
    b1, b2 = r1 / h21, w2 / h21
    z1, z2, z3 = ((t1 / beta - h11 * w1) / h21, (t2 / beta - h11 * w2) / h21, t3 / beta / h21)
    h12 = along(z1 * v)
    h22 = along(z1 * b1 + z2 * b2)
    d1, d2 = z1 - h12 * v - h22 * b1, z2 - h22 * b2
    h32 = jnp.sqrt(along(d1 * d1 + d2 * d2 + z3 * z3) + epsilon)
    first_norm = jnp.sqrt(h11 * h11 + h21 * h21)
    c1, s1 = h11 / first_norm, h21 / first_norm
    t12, t22 = c1 * h12 + s1 * h22, c1 * h22 - s1 * h12
    second_norm = jnp.sqrt(t22 * t22 + h32 * h32)
    c2, s2 = t22 / second_norm, h32 / second_norm
    g2 = -s1 * beta
    y2 = c2 * g2 / second_norm
    y1 = (c1 * beta - t12 * y2) / first_norm
    lsq_out[...] = jnp.abs(s2 * g2)
    on_u = y2 / h21 / beta
    on_f = y1 / beta - on_u * h11
    for c in range(3):
        x_out[0, 0, c] = on_f * rhs[0, 0, c] + on_u * u_in[c * s.step : c * s.step + s.blobs, :]


def call(kernel, outs, args, scalars=0, scratch=(), flops=0):
    vmem = pl.BlockSpec(memory_space=pltpu.VMEM)
    smem = pl.BlockSpec(memory_space=pltpu.SMEM)
    return pl.pallas_call(
        kernel,
        out_shape=[jax.ShapeDtypeStruct(shape, kind) for shape, kind in outs],
        in_specs=[smem] * scalars + [vmem] * (len(args) - scalars),
        out_specs=[vmem] * len(outs),
        scratch_shapes=list(scratch),
        compiler_params=pltpu.CompilerParams(vmem_limit_bytes=32 * 2**20),
        cost_estimate=pl.CostEstimate(flops=flops, bytes_accessed=2**20, transcendentals=0),
    )(*args)


def body(
    mesh_shape, rhs, angles, self_mob, near_mat, near_weight, neighbours, cells, blob_weight,
    skel_perm, interp, sibling_ops, root_op,
):
    s = Sizes(mesh_shape, rhs, skel_perm)
    full = (s.rows, s.bodies)
    square = (s.rows, s.rows)
    tile = (8, LANES)
    rim = (s.half, LANES)
    far_shape = (2 * s.nz * 2 * LANES, s.skel)
    column = lax.axis_index("gx") * s.ny + lax.axis_index("gy")
    ids = jnp.stack([column, lax.axis_index("gz")]).astype(jnp.int32)

    def fetch_rims(packed):
        out = []
        for dx, dy in s.sources:
            pairs = []
            for x in range(s.nx):
                for y in range(s.ny):
                    pairs.append((((x + dx) % s.nx) * s.ny + (y + dy) % s.ny, x * s.ny + y))
            out.append(lax.ppermute(packed, ("gx", "gy"), pairs))
        return out

    def everywhere(x):
        return lax.all_gather(x, ("gx", "gy", "gz"), axis=0, tiled=False)

    charges, packed, col, f = call(
        functools.partial(start_kernel, s),
        [(tile, f32), (rim, f32), ((s.step, LANES), f32), (full, f32)],
        [rhs, cells, blob_weight.reshape(1, -1)],
        flops=10**7,
    )
    rims = fetch_rims(packed)
    charges = everywhere(charges)
    loc, gat, rot, sh, sl, nh, nl, oh, ol, gh, gl, th, tl = call(
        functools.partial(setup_kernel, s),
        [(full, f32), (full, f32), ((16, s.bodies), f32)]
        + [(square, bf16)] * 4
        + [((s.bodies, s.bodies), bf16)] * 2
        + [((s.ghosts, s.bodies), bf16)] * 2
        + [(far_shape, bf16)] * 2,
        [ids, f, angles, self_mob, near_mat, near_weight, neighbours, skel_perm, interp, sibling_ops, root_op],
        scalars=1,
        scratch=[pltpu.VMEM(square, f32), pltpu.VMEM((s.levels, 2 * s.skel, s.skel), f32)],
        flops=10**9,
    )
    u, charges, packed = call(
        functools.partial(first_kernel, s, len(rims)),
        [(full, f32), (tile, f32), (rim, f32)],
        [ids, loc, gat, nh, nl, gh, gl, charges, th, tl, cells, col, *rims],
        scalars=1,
        flops=10**9,
    )
    rims = fetch_rims(packed)
    charges = everywhere(charges)
    loc, gat, ortho, stat = call(
        functools.partial(middle_kernel, s),
        [(full, f32), (full, f32), (full, f32), (tile, f32)],
        [u, f, rot, sh, sl, oh, ol],
        flops=10**9,
    )
    (stat,) = call(
        functools.partial(second_kernel, s, len(rims)),
        [(tile, f32)],
        [ids, loc, gat, nh, nl, gh, gl, charges, th, tl, cells, col, f, ortho, stat, *rims],
        scalars=1,
        flops=10**9,
    )
    stats = everywhere(stat)
    result, lsq = call(
        functools.partial(finish_kernel, s),
        [(rhs.shape, f32), ((1, 1), f32)],
        [stats, rhs, u],
        flops=10**7,
    )
    return result, lsq.reshape(())


def solution(mesh):
    in_specs = (
        P("gx", "gy", None, None, "gz"),
        P("gx", "gy", None, "gz"),
        P(),
        P(),
        P("gx", "gy", None, "gz"),
        P("gx", "gy", None, "gz"),
        P("gx", "gy", "gz"),
        P(),
        P(),
        P(),
        P(),
        P(),
    )
    out_specs = (P("gx", "gy", None, None, "gz"), P())
    inner = functools.partial(body, dict(mesh.shape))
    return jax.shard_map(inner, mesh=mesh, in_specs=in_specs, out_specs=out_specs, check_vma=False)
```

```python
import functools

import jax
import jax.numpy as jnp
from jax import lax
from jax.experimental import pallas as pl
from jax.experimental.pallas import tpu as pltpu
from jax.sharding import PartitionSpec as P

epsilon = 1e-06
f32 = jnp.float32
bf16 = jnp.bfloat16
RIM = 64
LANES = 128


def round_up(value, unit):
    return -(-value // unit) * unit


def split(x):
    hi = x.astype(bf16)
    lo = (x - hi.astype(f32)).astype(bf16)
    return hi, lo


def mm(a, b):
    return lax.dot_general(a, b, (((1,), (0,)), ((), ())), preferred_element_type=f32)


def mt(a, b):
    return lax.dot_general(a, b, (((1,), (1,)), ((), ())), preferred_element_type=f32)


def product(dot, a, b):
    return dot(a[0], b[0]) + (dot(a[0], b[1]) + dot(a[1], b[0]))


def total(x):
    return jnp.sum(jnp.sum(x, axis=0, keepdims=True), axis=1, keepdims=True)


class Sizes:
    def __init__(self, mesh_shape, rhs, skel_perm):
        self.nx, self.ny, self.nz = (mesh_shape[a] for a in ("gx", "gy", "gz"))
        self.devices = self.nx * self.ny * self.nz
        self.blobs, self.bodies = rhs.shape[-2:]
        self.step = round_up(self.blobs, 8)
        self.rows = round_up(3 * self.step, 16)
        self.half = self.rows // 2
        self.levels = skel_perm.shape[0]
        self.skel = skel_perm.shape[1] // 2
        self.own_slots = []
        self.sources = []
        self.slot_base = []
        for slot in range(9):
            offset = ((slot // 3 - 1) % self.nx, (slot % 3 - 1) % self.ny)
            if offset == (0, 0):
                self.slot_base.append(0)
                continue
            if offset not in self.sources:
                self.sources.append(offset)
            self.slot_base.append(self.bodies + RIM * self.sources.index(offset))
        self.ghosts = round_up(max(1, len(self.sources)) * RIM, LANES)


def pieces(x, s):
    return [x[c * s.step : c * s.step + s.step] for c in range(3)]


def turn(parts, rot, inverse):
    out = []
    for target in range(3):
        acc = None
        for source in range(3):
            row = 3 * source + target if inverse else 3 * target + source
            term = rot[row : row + 1] * parts[source]
            acc = term if acc is None else acc + term
        out.append(acc)
    return out


def stacked(parts, s):
    rest = s.rows - 3 * s.step
    if rest:
        parts = list(parts) + [jnp.zeros((rest, s.bodies), f32)]
    return jnp.concatenate(parts, axis=0)


def occupancy(cells, s):
    row = lax.broadcasted_iota(jnp.int32, (s.skel, s.bodies), 0)
    return jnp.where(cells == row, 1.0, 0.0).astype(bf16)


def pack_charges(parts, weight_col, occ, s):
    moments = [jnp.sum(part * weight_col, axis=0, keepdims=True) for part in parts]
    moments = jnp.concatenate(moments + [jnp.zeros((5, s.bodies), f32)], axis=0)
    high, rest = split(moments)
    mid, low = split(moments - high.astype(f32))
    stack = jnp.concatenate([high.astype(f32), mid.astype(f32), low.astype(f32)], axis=0).astype(bf16)
    sums = mt(stack, occ)
    charges = sums[0:8] + (sums[8:16] + sums[16:24])
    tail = jnp.concatenate([charges[:, LANES:], jnp.zeros((8, 2 * LANES - s.skel), f32)], axis=1)
    row = lax.broadcasted_iota(jnp.int32, (8, LANES), 0)
    return jnp.where(row < 4, charges[:, :LANES], pltpu.roll(tail, 4, 0))


def pack_rim(x, s):
    lane = lax.broadcasted_iota(jnp.int32, (s.half, LANES), 1)
    top, bottom = x[: s.half, :LANES], x[s.half :, :LANES]
    return jnp.where(lane < RIM, top, pltpu.roll(bottom, RIM, 1))


def unpack_rims(rims, s):
    lane = lax.broadcasted_iota(jnp.int32, (s.half, LANES), 1)
    tops, bottoms = [], []
    for i in range(0, s.ghosts // RIM, 2):
        a = rims[i]
        b = rims[i + 1] if i + 1 < len(rims) else jnp.zeros_like(a)
        tops.append(jnp.where(lane < RIM, a, pltpu.roll(b, RIM, 1)))
        bottoms.append(jnp.where(lane < RIM, pltpu.roll(a, RIM, 1), b))
    return jnp.concatenate(
        [jnp.concatenate(tops, axis=1), jnp.concatenate(bottoms, axis=1)], axis=0
    )


def start_kernel(s, rhs, cells, weight, q_out, rim_out, col_out, f_out):
    f_out[...] = jnp.zeros_like(f_out)
    for c in range(3):
        f_out[c * s.step : c * s.step + s.blobs, :] = rhs[0, 0, c]
    f = f_out[...]
    wide = jnp.concatenate([weight[...], jnp.zeros((1, 2 * LANES - s.blobs), f32)], axis=1)
    col = jnp.broadcast_to(wide, (LANES, 2 * LANES)).T[: s.step]
    col_out[...] = col
    rim_out[...] = pack_rim(f, s)
    occ = occupancy(cells[0], s)
    q_out[...] = pack_charges(pieces(f, s), col[:, :1], occ, s)


def frame_rows(angles):
    cos, sin = jnp.cos(angles), jnp.sin(angles)
    cy, cp, cr = cos[0:1], cos[1:2], cos[2:3]
    sy, sp, sr = sin[0:1], sin[1:2], sin[2:3]
    return [
        cy * cp,
        cy * sp * sr - sy * cr,
        cy * sp * cr + sy * sr,
        sy * cp,
        sy * sp * sr + cy * cr,
        sy * sp * cr - cy * sr,
        -sp,
        cp * sr,
        cp * cr,
    ]


def local_part(f, s, rot, mob, own):
    parts = pieces(f, s)
    turned = stacked(turn(parts, rot, False), s)
    mixed = product(mm, mob, split(turned))
    back = turn(pieces(mixed, s), rot, True)
    return f + stacked(back, s), product(mm, split(f), own)


def expand(block, level, ups):
    if level == 0:
        return [block]
    up = ups[level - 1]
    n = up.shape[0] // 2
    both = product(mm, split(up), split(block))
    return expand(both[:n], level - 1, ups) + expand(both[n:], level - 1, ups)


def setup_kernel(
    s, ids, f_in, angles, self_mob, near_mat, near_weight, neighbours, perm, interp, sibling, root,
    loc_out, gat_out, rot_out, sh_out, sl_out, nh_out, nl_out, oh_out, ol_out, gh_out, gl_out,
    th_out, tl_out, padded, ups_ref,
):
    f = f_in[...]
    rot = jnp.concatenate(frame_rows(angles[0, 0]) + [jnp.zeros((7, s.bodies), f32)], axis=0)
    rot_out[...] = rot

    padded[...] = jnp.zeros_like(padded)
    for matrix, hi_out, lo_out in ((self_mob, sh_out, sl_out), (near_mat, nh_out, nl_out)):
        for c in range(3):
            for d in range(3):
                padded[c * s.step : c * s.step + s.blobs, d * s.step : d * s.step + s.blobs] = matrix[
                    c * s.blobs : (c + 1) * s.blobs, d * s.blobs : (d + 1) * s.blobs
                ]
        hi, lo = split(padded[...])
        hi_out[...] = hi
        lo_out[...] = lo

    links = neighbours[0, 0]
    slot = links // s.bodies
    base = jnp.zeros_like(links)
    for index, start in enumerate(s.slot_base):
        base = jnp.where(slot == index, start, base)
    column = base + links % s.bodies
    coef = near_weight[0, 0]
    for first, count, hi_out, lo_out in (
        (0, s.bodies, oh_out, ol_out),
        (s.bodies, s.ghosts, gh_out, gl_out),
    ):
        for r in range(0, count, 64):
            row = lax.broadcasted_iota(jnp.int32, (64, s.bodies), 0) + (first + r)
            acc = jnp.zeros((64, s.bodies), f32)
            for k in range(coef.shape[0]):
                acc = acc + jnp.where(column[k : k + 1] == row, coef[k : k + 1], 0.0)
            hi, lo = split(acc)
            hi_out[r : r + 64, :] = hi
            lo_out[r : r + 64, :] = lo

    loc, gat = local_part(f, s, rot, (sh_out[...], sl_out[...]), (oh_out[...], ol_out[...]))
    loc_out[...] = loc
    gat_out[...] = gat

    n = s.skel
    z = ids[1]
    ups = []
    eye_row = lax.broadcasted_iota(jnp.int32, (n, n), 0)
    eye_col = lax.broadcasted_iota(jnp.int32, (n, n), 1)
    eye = jnp.where(eye_row == eye_col, 1.0, 0.0)
    for level in range(s.levels):
        spot = lax.broadcasted_iota(jnp.int32, (2 * n, 2 * n), 0)
        onehot = jnp.where(perm[level : level + 1, :] == spot, 1.0, 0.0).astype(bf16)
        hi, lo = split(jnp.concatenate([eye, interp[level]], axis=0))
        up = mm(onehot, hi) + mm(onehot, lo)
        ups.append(up)
        ups_ref[level] = up

    def down(block, level):
        bit = (z >> level) & 1
        half = ups_ref[level, pl.ds(pl.multiple_of(bit * n, 8), n), :]
        return product(mt, split(block), split(half))

    spread = root[...]
    beside = []
    for level in reversed(range(s.levels)):
        spread = down(spread, level)
        beside = [down(block, level) for block in beside]
        beside.append(sibling[level])
    far_leaves = expand(spread, s.levels, ups)
    near_leaves = [jnp.zeros((n, n), f32) for _ in range(s.nz)]
    for level, block in zip(reversed(range(s.levels)), beside):
        sub = expand(block, level, ups)
        for leaf in range(s.nz):
            hit = (leaf >> level) == ((z >> level) ^ 1)
            near_leaves[leaf] = jnp.where(hit, near_leaves[leaf] + sub[leaf % (1 << level)], near_leaves[leaf])
    pad = jnp.zeros((2 * LANES - n, n), f32)
    for leaf in range(s.nz):
        for group, block in ((0, near_leaves[leaf] - far_leaves[leaf]), (s.nz, far_leaves[leaf])):
            hi, lo = split(jnp.concatenate([block, pad], axis=0))
            at = (group + leaf) * 2 * LANES
            th_out[at : at + 2 * LANES, :] = hi
            tl_out[at : at + 2 * LANES, :] = lo


def image(s, ids, loc, gat, rims, near, ghost, charges, far_op, cells, col):
    column = ids[0]
    chunks = []
    for leaf in range(s.nz):
        chunks.append(charges[column * s.nz + leaf])
    for leaf in range(s.nz):
        acc = charges[leaf]
        for c in range(1, s.nx * s.ny):
            acc = acc + charges[c * s.nz + leaf]
        chunks.append(acc)
    left = jnp.concatenate([x for tile in chunks for x in (tile, pltpu.roll(tile, 4, 0))], axis=1)
    potential = product(mm, split(left), far_op)
    occ = occupancy(cells[0], s)
    p_hi, p_lo = split(potential)
    p_mid, p_low = split(potential - p_hi.astype(f32))
    stack = jnp.concatenate([p_hi.astype(f32), p_mid.astype(f32), p_low.astype(f32)], axis=0).astype(bf16)
    values = mm(stack, occ)
    values = values[0:8] + (values[8:16] + values[16:24])
    far = stacked([col * values[c : c + 1] for c in range(3)], s)
    gathered = gat + product(mm, split(unpack_rims(rims, s)), ghost)
    return (loc + far) + product(mm, near, split(gathered))


def first_kernel(s, n_rims, ids, loc, gat, nh, nl, gh, gl, charges, th, tl, cells, col, *rest):
    rims, (u_out, q_out, rim_out) = rest[:n_rims], rest[n_rims:]
    weight_col = col[:, :1]
    u = image(
        s, ids, loc[...], gat[...], [r[...] for r in rims], (nh[...], nl[...]), (gh[...], gl[...]),
        charges, (th[...], tl[...]), cells, weight_col,
    )
    u_out[...] = u
    rim_out[...] = pack_rim(u, s)
    q_out[...] = pack_charges(pieces(u, s), weight_col, occupancy(cells[0], s), s)


def safe_inverse(x):
    return jnp.where(x > 0.0, 1.0 / jnp.where(x > 0.0, x, 1.0), 0.0)


def middle_kernel(s, u_in, f_in, rot, sh, sl, oh, ol, loc_out, gat_out, ortho_out, stat_out):
    u, f = u_in[...], f_in[...]
    loc, gat = local_part(u, s, rot[...], (sh[...], sl[...]), (oh[...], ol[...]))
    loc_out[...] = loc
    gat_out[...] = gat
    ff = total(f * f)
    fu = total(f * u) * safe_inverse(ff)
    ortho = u - fu * f
    ortho_out[...] = ortho
    oo = total(ortho * ortho)
    stat_out[...] = jnp.broadcast_to(
        jnp.concatenate([ff, fu, oo, jnp.zeros((5, 1), f32)], axis=0), (8, LANES)
    )


def second_kernel(
    s, n_rims, ids, loc, gat, nh, nl, gh, gl, charges, th, tl, cells, col, f_in, ortho_in, stat, *rest
):
    rims, (stat_out,) = rest[:n_rims], rest[n_rims:]
    t = image(
        s, ids, loc[...], gat[...], [r[...] for r in rims], (nh[...], nl[...]), (gh[...], gl[...]),
        charges, (th[...], tl[...]), cells, col[:, :1],
    )
    f, ortho = f_in[...], ortho_in[...]
    ff, fu, oo = (stat[i : i + 1, :1] for i in range(3))
    ft = total(f * t) * safe_inverse(ff)
    ot = total(ortho * t) * safe_inverse(oo)
    rest_t = t - ft * f - ot * ortho
    tt = total(rest_t * rest_t)
    rf, ro = jnp.sqrt(ff), jnp.sqrt(oo)
    stat_out[...] = jnp.broadcast_to(
        jnp.concatenate(
            [rf, rf * fu, ro, rf * ft, ro * ot, jnp.sqrt(tt), jnp.zeros((2, 1), f32)], axis=0
        ),
        (8, LANES),
    )


def finish_kernel(s, stats, rhs, u_in, x_out, lsq_out):
    groups = []
    for g in range(0, s.devices, LANES):
        acc = jnp.zeros((8, LANES), f32)
        lane = lax.broadcasted_iota(jnp.int32, (8, LANES), 1)
        for d in range(g, min(s.devices, g + LANES)):
            acc = acc + jnp.where(lane == d - g, stats[d], 0.0)
        groups.append(acc)
    rows = jnp.concatenate(groups, axis=1) if len(groups) > 1 else groups[0]
    f1, u1, u2, t1, t2, t3 = (rows[i : i + 1] for i in range(6))

    def along(x):
        return jnp.sum(x, axis=1, keepdims=True)

    beta = jnp.sqrt(along(f1 * f1) + epsilon)
    v = f1 / beta
    w1, w2 = u1 / beta, u2 / beta
    h11 = along(w1 * v)
    r1 = w1 - h11 * v
    h21 = jnp.sqrt(along(r1 * r1 + w2 * w2) + epsilon)
    b1, b2 = r1 / h21, w2 / h21
    z1, z2, z3 = ((t1 / beta - h11 * w1) / h21, (t2 / beta - h11 * w2) / h21, t3 / beta / h21)
    h12 = along(z1 * v)
    h22 = along(z1 * b1 + z2 * b2)
    d1, d2 = z1 - h12 * v - h22 * b1, z2 - h22 * b2
    h32 = jnp.sqrt(along(d1 * d1 + d2 * d2 + z3 * z3) + epsilon)
    first_norm = jnp.sqrt(h11 * h11 + h21 * h21)
    c1, s1 = h11 / first_norm, h21 / first_norm
    t12, t22 = c1 * h12 + s1 * h22, c1 * h22 - s1 * h12
    second_norm = jnp.sqrt(t22 * t22 + h32 * h32)
    c2, s2 = t22 / second_norm, h32 / second_norm
    g2 = -s1 * beta
    y2 = c2 * g2 / second_norm
    y1 = (c1 * beta - t12 * y2) / first_norm
    lsq_out[...] = jnp.abs(s2 * g2)
    on_u = y2 / h21 / beta
    on_f = y1 / beta - on_u * h11
    for c in range(3):
        x_out[0, 0, c] = on_f * rhs[0, 0, c] + on_u * u_in[c * s.step : c * s.step + s.blobs, :]


def call(kernel, outs, args, scalars=0, scratch=(), flops=0):
    vmem = pl.BlockSpec(memory_space=pltpu.VMEM)
    smem = pl.BlockSpec(memory_space=pltpu.SMEM)
    return pl.pallas_call(
        kernel,
        out_shape=[jax.ShapeDtypeStruct(shape, kind) for shape, kind in outs],
        in_specs=[smem] * scalars + [vmem] * (len(args) - scalars),
        out_specs=[vmem] * len(outs),
        scratch_shapes=list(scratch),
        compiler_params=pltpu.CompilerParams(vmem_limit_bytes=32 * 2**20),
        cost_estimate=pl.CostEstimate(flops=flops, bytes_accessed=2**20, transcendentals=0),
    )(*args)


def body(
    mesh_shape, rhs, angles, self_mob, near_mat, near_weight, neighbours, cells, blob_weight,
    skel_perm, interp, sibling_ops, root_op,
):
    s = Sizes(mesh_shape, rhs, skel_perm)
    full = (s.rows, s.bodies)
    square = (s.rows, s.rows)
    tile = (8, LANES)
    rim = (s.half, LANES)
    far_shape = (2 * s.nz * 2 * LANES, s.skel)
    column = lax.axis_index("gx") * s.ny + lax.axis_index("gy")
    ids = jnp.stack([column, lax.axis_index("gz")]).astype(jnp.int32)

    def fetch_rims(packed):
        out = []
        for dx, dy in s.sources:
            pairs = []
            for x in range(s.nx):
                for y in range(s.ny):
                    pairs.append((((x + dx) % s.nx) * s.ny + (y + dy) % s.ny, x * s.ny + y))
            out.append(lax.ppermute(packed, ("gx", "gy"), pairs))
        return out

    def everywhere(x):
        copies = jnp.broadcast_to(x[None], (s.devices,) + x.shape)
        return lax.all_to_all(copies, ("gx", "gy", "gz"), 0, 0)

    charges, packed, col, f = call(
        functools.partial(start_kernel, s),
        [(tile, f32), (rim, f32), ((s.step, LANES), f32), (full, f32)],
        [rhs, cells, blob_weight.reshape(1, -1)],
        flops=10**7,
    )
    rims = fetch_rims(packed)
    charges = everywhere(charges)
    loc, gat, rot, sh, sl, nh, nl, oh, ol, gh, gl, th, tl = call(
        functools.partial(setup_kernel, s),
        [(full, f32), (full, f32), ((16, s.bodies), f32)]
        + [(square, bf16)] * 4
        + [((s.bodies, s.bodies), bf16)] * 2
        + [((s.ghosts, s.bodies), bf16)] * 2
        + [(far_shape, bf16)] * 2,
        [ids, f, angles, self_mob, near_mat, near_weight, neighbours, skel_perm, interp, sibling_ops, root_op],
        scalars=1,
        scratch=[pltpu.VMEM(square, f32), pltpu.VMEM((s.levels, 2 * s.skel, s.skel), f32)],
        flops=10**9,
    )
    u, charges, packed = call(
        functools.partial(first_kernel, s, len(rims)),
        [(full, f32), (tile, f32), (rim, f32)],
        [ids, loc, gat, nh, nl, gh, gl, charges, th, tl, cells, col, *rims],
        scalars=1,
        flops=10**9,
    )
    rims = fetch_rims(packed)
    charges = everywhere(charges)
    loc, gat, ortho, stat = call(
        functools.partial(middle_kernel, s),
        [(full, f32), (full, f32), (full, f32), (tile, f32)],
        [u, f, rot, sh, sl, oh, ol],
        flops=10**9,
    )
    (stat,) = call(
        functools.partial(second_kernel, s, len(rims)),
        [(tile, f32)],
        [ids, loc, gat, nh, nl, gh, gl, charges, th, tl, cells, col, f, ortho, stat, *rims],
        scalars=1,
        flops=10**9,
    )
    stats = everywhere(stat)
    result, lsq = call(
        functools.partial(finish_kernel, s),
        [(rhs.shape, f32), ((1, 1), f32)],
        [stats, rhs, u],
        flops=10**7,
    )
    return result, lsq.reshape(())


def solution(mesh):
    in_specs = (
        P("gx", "gy", None, None, "gz"),
        P("gx", "gy", None, "gz"),
        P(),
        P(),
        P("gx", "gy", None, "gz"),
        P("gx", "gy", None, "gz"),
        P("gx", "gy", "gz"),
        P(),
        P(),
        P(),
        P(),
        P(),
    )
    out_specs = (P("gx", "gy", None, None, "gz"), P())
    inner = functools.partial(body, dict(mesh.shape))
    return jax.shard_map(inner, mesh=mesh, in_specs=in_specs, out_specs=out_specs, check_vma=False)
```

```python
import functools

import jax
import jax.numpy as jnp
from jax import lax
from jax.experimental import pallas as pl
from jax.experimental.pallas import tpu as pltpu
from jax.sharding import PartitionSpec as P

epsilon = 1e-06
f32 = jnp.float32
bf16 = jnp.bfloat16
RIM = 64
LANES = 128


def round_up(value, unit):
    return -(-value // unit) * unit


def split(x):
    hi = x.astype(bf16)
    lo = (x - hi.astype(f32)).astype(bf16)
    return hi, lo


def mm(a, b):
    return lax.dot_general(a, b, (((1,), (0,)), ((), ())), preferred_element_type=f32)


def mt(a, b):
    return lax.dot_general(a, b, (((1,), (1,)), ((), ())), preferred_element_type=f32)


def product(dot, a, b):
    return dot(a[0], b[0]) + (dot(a[0], b[1]) + dot(a[1], b[0]))


def total(x):
    return jnp.sum(jnp.sum(x, axis=0, keepdims=True), axis=1, keepdims=True)


class Sizes:
    def __init__(self, mesh_shape, rhs, skel_perm):
        self.nx, self.ny, self.nz = (mesh_shape[a] for a in ("gx", "gy", "gz"))
        self.devices = self.nx * self.ny * self.nz
        self.blobs, self.bodies = rhs.shape[-2:]
        self.step = round_up(self.blobs, 8)
        self.rows = round_up(3 * self.step, 16)
        self.half = self.rows // 2
        self.levels = skel_perm.shape[0]
        self.skel = skel_perm.shape[1] // 2
        shifts = sorted({(dy % self.ny) for dy in (-1, 1)} - {0})
        self.shifts = shifts
        self.sources = [("same", dy) for dy in shifts]
        for kind in ("other", "partner"):
            self.sources += [(kind, dy) for dy in [0] + shifts]
        self.ghosts = round_up(len(self.sources) * RIM, LANES)
        self.far_tiles = self.nz + -(-self.nz // 2)

    def slot_start(self, slot, parity):
        dx, dy = slot // 3 - 1, (slot % 3 - 1) % self.ny
        kind = "same" if dx == 0 else "partner" if dx == 1 - 2 * parity else "other"
        if (kind, dy) == ("same", 0):
            return 0
        return self.bodies + RIM * self.sources.index((kind, dy))

    def beside(self, kind, x):
        if kind == "same":
            return x
        if kind == "partner":
            return x ^ 1
        return (x + 2 * (x % 2) - 1) % self.nx


def pieces(x, s):
    return [x[c * s.step : c * s.step + s.step] for c in range(3)]


def turn(parts, rot, inverse):
    out = []
    for target in range(3):
        acc = None
        for source in range(3):
            row = 3 * source + target if inverse else 3 * target + source
            term = rot[row : row + 1] * parts[source]
            acc = term if acc is None else acc + term
        out.append(acc)
    return out


def stacked(parts, s):
    rest = s.rows - 3 * s.step
    if rest:
        parts = list(parts) + [jnp.zeros((rest, s.bodies), f32)]
    return jnp.concatenate(parts, axis=0)


def occupancy(cells, s):
    row = lax.broadcasted_iota(jnp.int32, (s.skel, s.bodies), 0)
    return jnp.where(cells == row, 1.0, 0.0).astype(bf16)


def pack_charges(parts, weight_col, occ, s):
    moments = [jnp.sum(part * weight_col, axis=0, keepdims=True) for part in parts]
    moments = jnp.concatenate(moments + [jnp.zeros((5, s.bodies), f32)], axis=0)
    high, rest = split(moments)
    mid, low = split(moments - high.astype(f32))
    stack = jnp.concatenate([high.astype(f32), mid.astype(f32), low.astype(f32)], axis=0).astype(bf16)
    sums = mt(stack, occ)
    charges = sums[0:8] + (sums[8:16] + sums[16:24])
    tail = jnp.concatenate([charges[:, LANES:], jnp.zeros((8, 2 * LANES - s.skel), f32)], axis=1)
    row = lax.broadcasted_iota(jnp.int32, (8, LANES), 0)
    return jnp.where(row < 4, charges[:, :LANES], pltpu.roll(tail, 4, 0))


def pack_rim(x, s):
    lane = lax.broadcasted_iota(jnp.int32, (s.half, LANES), 1)
    top, bottom = x[: s.half, :LANES], x[s.half :, :LANES]
    return jnp.where(lane < RIM, top, pltpu.roll(bottom, RIM, 1))


def unpack_rims(rims, s):
    lane = lax.broadcasted_iota(jnp.int32, (s.half, LANES), 1)
    tops, bottoms = [], []
    for i in range(0, s.ghosts // RIM, 2):
        a = rims[i]
        b = rims[i + 1] if i + 1 < len(rims) else jnp.zeros_like(a)
        tops.append(jnp.where(lane < RIM, a, pltpu.roll(b, RIM, 1)))
        bottoms.append(jnp.where(lane < RIM, pltpu.roll(a, RIM, 1), b))
    return jnp.concatenate(
        [jnp.concatenate(tops, axis=1), jnp.concatenate(bottoms, axis=1)], axis=0
    )


def start_kernel(s, rhs, cells, weight, q_out, rim_out, col_out, f_out):
    f_out[...] = jnp.zeros_like(f_out)
    for c in range(3):
        f_out[c * s.step : c * s.step + s.blobs, :] = rhs[0, 0, c]
    f = f_out[...]
    wide = jnp.concatenate([weight[...], jnp.zeros((1, 2 * LANES - s.blobs), f32)], axis=1)
    col = jnp.broadcast_to(wide, (LANES, 2 * LANES)).T[: s.step]
    col_out[...] = col
    rim_out[...] = pack_rim(f, s)
    occ = occupancy(cells[0], s)
    charges = pack_charges(pieces(f, s), col[:, :1], occ, s)
    q_out[...] = jnp.broadcast_to(charges[None], q_out.shape)


def frame_rows(angles):
    cos, sin = jnp.cos(angles), jnp.sin(angles)
    cy, cp, cr = cos[0:1], cos[1:2], cos[2:3]
    sy, sp, sr = sin[0:1], sin[1:2], sin[2:3]
    return [
        cy * cp,
        cy * sp * sr - sy * cr,
        cy * sp * cr + sy * sr,
        sy * cp,
        sy * sp * sr + cy * cr,
        sy * sp * cr - cy * sr,
        -sp,
        cp * sr,
        cp * cr,
    ]


def local_part(f, s, rot, mob, own):
    parts = pieces(f, s)
    turned = stacked(turn(parts, rot, False), s)
    mixed = product(mm, mob, split(turned))
    back = turn(pieces(mixed, s), rot, True)
    return f + stacked(back, s), product(mm, split(f), own)


def expand(block, level, ups):
    if level == 0:
        return [block]
    up = ups[level - 1]
    n = up.shape[0] // 2
    block = split(block)
    low, high = (product(mt, block, split(half)) for half in (up[:n], up[n:]))
    return expand(low, level - 1, ups) + expand(high, level - 1, ups)


def setup_kernel(
    s, ids, f_in, angles, self_mob, near_mat, near_weight, neighbours, perm, interp, sibling, root,
    loc_out, gat_out, rot_out, sh_out, sl_out, nh_out, nl_out, oh_out, ol_out, gh_out, gl_out,
    far_out, padded, ups_ref,
):
    f = f_in[...]
    rot = jnp.concatenate(frame_rows(angles[0, 0]) + [jnp.zeros((7, s.bodies), f32)], axis=0)
    rot_out[...] = rot

    padded[...] = jnp.zeros_like(padded)
    for matrix, hi_out, lo_out in ((self_mob, sh_out, sl_out), (near_mat, nh_out, nl_out)):
        for c in range(3):
            for d in range(3):
                padded[c * s.step : c * s.step + s.blobs, d * s.step : d * s.step + s.blobs] = matrix[
                    c * s.blobs : (c + 1) * s.blobs, d * s.blobs : (d + 1) * s.blobs
                ]
        hi, lo = split(padded[...])
        hi_out[...] = hi
        lo_out[...] = lo

    links = neighbours[0, 0]
    slot = links // s.bodies
    base = jnp.zeros_like(links)
    odd = (ids[0] // s.ny) % 2
    for index in range(9):
        start = jnp.where(odd == 1, s.slot_start(index, 1), s.slot_start(index, 0))
        base = jnp.where(slot == index, start, base)
    column = base + links % s.bodies
    coef = near_weight[0, 0]
    for first, count, hi_out, lo_out in (
        (0, s.bodies, oh_out, ol_out),
        (s.bodies, s.ghosts, gh_out, gl_out),
    ):
        for r in range(0, count, 64):
            row = lax.broadcasted_iota(jnp.int32, (64, s.bodies), 0) + (first + r)
            acc = jnp.zeros((64, s.bodies), f32)
            for k in range(coef.shape[0]):
                acc = acc + jnp.where(column[k : k + 1] == row, coef[k : k + 1], 0.0)
            hi, lo = split(acc)
            hi_out[r : r + 64, :] = hi
            lo_out[r : r + 64, :] = lo

    loc, gat = local_part(f, s, rot, (sh_out[...], sl_out[...]), (oh_out[...], ol_out[...]))
    loc_out[...] = loc
    gat_out[...] = gat

    n = s.skel
    z = ids[1]
    ups = []
    eye_row = lax.broadcasted_iota(jnp.int32, (n, n), 0)
    eye_col = lax.broadcasted_iota(jnp.int32, (n, n), 1)
    eye = jnp.where(eye_row == eye_col, 1.0, 0.0)
    for level in range(s.levels):
        spot = lax.broadcasted_iota(jnp.int32, (2 * n, 2 * n), 0)
        onehot = jnp.where(perm[level : level + 1, :] == spot, 1.0, 0.0).astype(bf16)
        hi, lo = split(jnp.concatenate([eye, interp[level]], axis=0))
        up = mm(onehot, hi) + mm(onehot, lo)
        ups.append(up)
        ups_ref[level] = up

    def down(block, level, dot):
        bit = (z >> level) & 1
        half = ups_ref[level, pl.ds(pl.multiple_of(bit * n, 8), n), :]
        return product(dot, split(half), split(block))

    spread = root[...]
    beside = []
    for level in reversed(range(s.levels)):
        last = level == s.levels - 1
        spread = down(spread, level, mt if last else mm)
        beside = [down(block, level, mt if fresh else mm) for block, fresh in beside]
        beside = [(block, False) for block in beside] + [(sibling[level], True)]
    far_leaves = expand(spread, s.levels, ups)
    near_leaves = [jnp.zeros((n, n), f32) for _ in range(s.nz)]
    for level, (block, fresh) in zip(reversed(range(s.levels)), beside):
        sub = expand(block.T if fresh else block, level, ups)
        for leaf in range(s.nz):
            hit = (leaf >> level) == ((z >> level) ^ 1)
            near_leaves[leaf] = jnp.where(hit, near_leaves[leaf] + sub[leaf % (1 << level)], near_leaves[leaf])
    tail = n - LANES
    far_out[...] = jnp.zeros_like(far_out)
    own = [a - b for a, b in zip(near_leaves, far_leaves)]
    for group, blocks in enumerate((own, far_leaves)):
        for leaf, block in enumerate(blocks):
            at = (group * s.far_tiles + leaf) * LANES
            far_out[:, at : at + LANES] = block[:, :LANES]
            at = (group * s.far_tiles + s.nz + leaf // 2) * LANES + leaf % 2 * RIM
            far_out[:, at : at + tail] = block[:, LANES:]


def merge_kernel(s, ids, tiles, out):
    acc = tiles[0]
    for c in range(1, s.nx * s.ny):
        acc = acc + tiles[c]
    own = tiles[ids[0]]
    for leaf in range(s.nz):
        out[leaf, 0] = own
        out[leaf, 1] = acc


def far_potential(s, charges, far_op):
    rows = []
    for group in range(2):
        tiles = [charges[leaf, group] for leaf in range(s.nz)]
        rows += tiles
        for leaf in range(0, s.nz, 2):
            pair = tiles[leaf]
            if leaf + 1 < s.nz:
                lane = lax.broadcasted_iota(jnp.int32, (8, LANES), 1)
                pair = jnp.where(lane < RIM, pair, pltpu.roll(tiles[leaf + 1], RIM, 1))
            rows.append(pltpu.roll(pair, 4, 0))
    columns = [[], [], []]
    for r in range(0, s.skel, 64):
        acc = [None] * 3
        for index, row in enumerate(rows):
            block = far_op[r : r + 64, index * LANES : (index + 1) * LANES]
            for c in range(3):
                term = block * row[c : c + 1]
                acc[c] = term if acc[c] is None else acc[c] + term
        for c in range(3):
            columns[c].append(jnp.sum(acc[c], axis=1, keepdims=True))
    return columns


def far_values(s, charges, far_op, cells):
    columns = far_potential(s, charges, far_op)
    out = []
    for c in range(3):
        acc = jnp.zeros((1, s.bodies), f32)
        for index, r in enumerate(range(0, s.skel, 64)):
            row = lax.broadcasted_iota(jnp.int32, (64, s.bodies), 0) + r
            acc = acc + jnp.sum(jnp.where(cells == row, columns[c][index], 0.0), axis=0, keepdims=True)
        out.append(acc)
    return out


def image(s, loc, gat, rims, near, ghost, charges, far_op, cells, col):
    values = far_values(s, charges, far_op, cells[0])
    far = stacked([col * value for value in values], s)
    gathered = gat + product(mm, split(unpack_rims(rims, s)), ghost)
    return (loc + far) + product(mm, near, split(gathered))


def first_kernel(s, n_rims, loc, gat, nh, nl, gh, gl, charges, far_op, cells, col, *rest):
    rims, (u_out, q_out, rim_out) = rest[:n_rims], rest[n_rims:]
    weight_col = col[:, :1]
    u = image(
        s, loc[...], gat[...], [r[...] for r in rims], (nh[...], nl[...]), (gh[...], gl[...]),
        charges, far_op, cells, weight_col,
    )
    u_out[...] = u
    rim_out[...] = pack_rim(u, s)
    charges = pack_charges(pieces(u, s), weight_col, occupancy(cells[0], s), s)
    q_out[...] = jnp.broadcast_to(charges[None], q_out.shape)


def safe_inverse(x):
    return jnp.where(x > 0.0, 1.0 / jnp.where(x > 0.0, x, 1.0), 0.0)


def middle_kernel(s, u_in, f_in, rot, sh, sl, oh, ol, loc_out, gat_out, ortho_out, stat_out):
    u, f = u_in[...], f_in[...]
    loc, gat = local_part(u, s, rot[...], (sh[...], sl[...]), (oh[...], ol[...]))
    loc_out[...] = loc
    gat_out[...] = gat
    ff = total(f * f)
    fu = total(f * u) * safe_inverse(ff)
    ortho = u - fu * f
    ortho_out[...] = ortho
    oo = total(ortho * ortho)
    stat_out[...] = jnp.broadcast_to(
        jnp.concatenate([ff, fu, oo, jnp.zeros((5, 1), f32)], axis=0), (8, LANES)
    )


def second_kernel(
    s, n_rims, loc, gat, nh, nl, gh, gl, charges, far_op, cells, col, f_in, ortho_in, stat, *rest
):
    rims, (stat_out,) = rest[:n_rims], rest[n_rims:]
    t = image(
        s, loc[...], gat[...], [r[...] for r in rims], (nh[...], nl[...]), (gh[...], gl[...]),
        charges, far_op, cells, col[:, :1],
    )
    f, ortho = f_in[...], ortho_in[...]
    ff, fu, oo = (stat[i : i + 1, :1] for i in range(3))
    ft = total(f * t) * safe_inverse(ff)
    ot = total(ortho * t) * safe_inverse(oo)
    rest_t = t - ft * f - ot * ortho
    tt = total(rest_t * rest_t)
    rf, ro = jnp.sqrt(ff), jnp.sqrt(oo)
    stats = jnp.concatenate(
        [rf, rf * fu, ro, rf * ft, ro * ot, jnp.sqrt(tt), jnp.zeros((2, 1), f32)], axis=0
    )
    stat_out[...] = jnp.broadcast_to(jnp.broadcast_to(stats, (8, LANES))[None], stat_out.shape)


def spread_kernel(s, ids, tiles, out):
    count = s.nx * s.ny
    lane = lax.broadcasted_iota(jnp.int32, (8, LANES), 1)
    groups = s.devices // min(s.devices, LANES)
    per = count // groups
    for g in range(groups):
        acc = jnp.zeros((8, LANES), f32)
        for d in range(per):
            acc = acc + jnp.where(lane == d * s.nz + ids[1], tiles[g * per + d], 0.0)
        for leaf in range(s.nz):
            out[leaf, g] = acc


def finish_kernel(s, stats, rhs, u_in, x_out, lsq_out):
    groups = []
    for g in range(stats.shape[1]):
        acc = stats[0, g]
        for leaf in range(1, s.nz):
            acc = acc + stats[leaf, g]
        groups.append(acc)
    rows = jnp.concatenate(groups, axis=1) if len(groups) > 1 else groups[0]
    f1, u1, u2, t1, t2, t3 = (rows[i : i + 1] for i in range(6))

    def along(x):
        return jnp.sum(x, axis=1, keepdims=True)

    beta = jnp.sqrt(along(f1 * f1) + epsilon)
    v = f1 / beta
    w1, w2 = u1 / beta, u2 / beta
    h11 = along(w1 * v)
    r1 = w1 - h11 * v
    h21 = jnp.sqrt(along(r1 * r1 + w2 * w2) + epsilon)
    b1, b2 = r1 / h21, w2 / h21
    z1, z2, z3 = ((t1 / beta - h11 * w1) / h21, (t2 / beta - h11 * w2) / h21, t3 / beta / h21)
    h12 = along(z1 * v)
    h22 = along(z1 * b1 + z2 * b2)
    d1, d2 = z1 - h12 * v - h22 * b1, z2 - h22 * b2
    h32 = jnp.sqrt(along(d1 * d1 + d2 * d2 + z3 * z3) + epsilon)
    first_norm = jnp.sqrt(h11 * h11 + h21 * h21)
    c1, s1 = h11 / first_norm, h21 / first_norm
    t12, t22 = c1 * h12 + s1 * h22, c1 * h22 - s1 * h12
    second_norm = jnp.sqrt(t22 * t22 + h32 * h32)
    c2, s2 = t22 / second_norm, h32 / second_norm
    g2 = -s1 * beta
    y2 = c2 * g2 / second_norm
    y1 = (c1 * beta - t12 * y2) / first_norm
    lsq_out[...] = jnp.abs(s2 * g2)
    on_u = y2 / h21 / beta
    on_f = y1 / beta - on_u * h11
    for c in range(3):
        x_out[0, 0, c] = on_f * rhs[0, 0, c] + on_u * u_in[c * s.step : c * s.step + s.blobs, :]


def call(kernel, outs, args, scalars=0, scratch=(), flops=0):
    vmem = pl.BlockSpec(memory_space=pltpu.VMEM)
    smem = pl.BlockSpec(memory_space=pltpu.SMEM)
    return pl.pallas_call(
        kernel,
        out_shape=[jax.ShapeDtypeStruct(shape, kind) for shape, kind in outs],
        in_specs=[smem] * scalars + [vmem] * (len(args) - scalars),
        out_specs=[vmem] * len(outs),
        scratch_shapes=list(scratch),
        compiler_params=pltpu.CompilerParams(vmem_limit_bytes=32 * 2**20),
        cost_estimate=pl.CostEstimate(flops=flops, bytes_accessed=2**20, transcendentals=0),
    )(*args)


def body(
    mesh_shape, rhs, angles, self_mob, near_mat, near_weight, neighbours, cells, blob_weight,
    skel_perm, interp, sibling_ops, root_op,
):
    s = Sizes(mesh_shape, rhs, skel_perm)
    full = (s.rows, s.bodies)
    square = (s.rows, s.rows)
    tile = (8, LANES)
    rim = (s.half, LANES)
    far_shape = (s.skel, 2 * s.far_tiles * LANES)
    column = lax.axis_index("gx") * s.ny + lax.axis_index("gy")
    ids = jnp.stack([column, lax.axis_index("gz")]).astype(jnp.int32)

    def fetch(x, kind, dy):
        pairs = []
        for gx in range(s.nx):
            for gy in range(s.ny):
                pairs.append((s.beside(kind, gx) * s.ny + (gy + dy) % s.ny, gx * s.ny + gy))
        return lax.ppermute(x, ("gx", "gy"), pairs)

    def fetch_rims(packed):
        rims = {}
        for dy in s.shifts:
            rims["same", dy] = fetch(packed, "same", dy)
        for dy in s.shifts:
            rims["other", dy] = fetch(packed, "other", dy)
        rims["other", 0] = fetch(packed, "other", 0)
        rims["partner", 0] = fetch(packed, "partner", 0)
        for dy in s.shifts:
            rims["partner", dy] = fetch(rims["same", dy], "partner", 0)
        return [rims[key] for key in s.sources]

    def over_plane(x):
        return lax.all_to_all(x, ("gx", "gy"), 0, 0)

    def over_layers(x):
        return lax.all_to_all(x, "gz", 0, 0)

    planes = (s.nx * s.ny,) + tile

    def share_charges(tiles):
        (merged,) = call(
            functools.partial(merge_kernel, s), [((s.nz, 2) + tile, f32)], [ids, over_plane(tiles)], scalars=1
        )
        return over_layers(merged)

    charges, packed, col, f = call(
        functools.partial(start_kernel, s),
        [(planes, f32), (rim, f32), ((s.step, LANES), f32), (full, f32)],
        [rhs, cells, blob_weight.reshape(1, -1)],
        flops=10**7,
    )
    rims = fetch_rims(packed)
    charges = share_charges(charges)
    f, charges = lax.optimization_barrier((f, charges))
    loc, gat, rot, sh, sl, nh, nl, oh, ol, gh, gl, far_op = call(
        functools.partial(setup_kernel, s),
        [(full, f32), (full, f32), ((16, s.bodies), f32)]
        + [(square, bf16)] * 4
        + [((s.bodies, s.bodies), bf16)] * 2
        + [((s.ghosts, s.bodies), bf16)] * 2
        + [(far_shape, f32)],
        [ids, f, angles, self_mob, near_mat, near_weight, neighbours, skel_perm, interp, sibling_ops, root_op],
        scalars=1,
        scratch=[pltpu.VMEM(square, f32), pltpu.VMEM((s.levels, 2 * s.skel, s.skel), f32)],
        flops=10**9,
    )
    u, charges, packed = call(
        functools.partial(first_kernel, s, len(rims)),
        [(full, f32), (planes, f32), (rim, f32)],
        [loc, gat, nh, nl, gh, gl, charges, far_op, cells, col, *rims],
        flops=10**9,
    )
    rims = fetch_rims(packed)
    charges = share_charges(charges)
    u, charges = lax.optimization_barrier((u, charges))
    loc, gat, ortho, stat = call(
        functools.partial(middle_kernel, s),
        [(full, f32), (full, f32), (full, f32), (tile, f32)],
        [u, f, rot, sh, sl, oh, ol],
        flops=10**9,
    )
    (stat,) = call(
        functools.partial(second_kernel, s, len(rims)),
        [(planes, f32)],
        [loc, gat, nh, nl, gh, gl, charges, far_op, cells, col, f, ortho, stat, *rims],
        flops=10**9,
    )
    groups = s.devices // min(s.devices, LANES)
    (stats,) = call(
        functools.partial(spread_kernel, s), [((s.nz, groups) + tile, f32)], [ids, over_plane(stat)], scalars=1
    )
    result, lsq = call(
        functools.partial(finish_kernel, s),
        [(rhs.shape, f32), ((1, 1), f32)],
        [over_layers(stats), rhs, u],
        flops=10**7,
    )
    return result, lsq.reshape(())


def solution(mesh):
    in_specs = (
        P("gx", "gy", None, None, "gz"),
        P("gx", "gy", None, "gz"),
        P(),
        P(),
        P("gx", "gy", None, "gz"),
        P("gx", "gy", None, "gz"),
        P("gx", "gy", "gz"),
        P(),
        P(),
        P(),
        P(),
        P(),
    )
    out_specs = (P("gx", "gy", None, None, "gz"), P())
    inner = functools.partial(body, dict(mesh.shape))
    return jax.shard_map(inner, mesh=mesh, in_specs=in_specs, out_specs=out_specs, check_vma=False)
```

```python
import functools

import jax
import jax.numpy as jnp
from jax import lax
from jax.experimental import pallas as pl
from jax.experimental.pallas import tpu as pltpu
from jax.sharding import PartitionSpec as P

epsilon = 1e-06
f32 = jnp.float32
bf16 = jnp.bfloat16
RIM = 64
LANES = 128


def round_up(value, unit):
    return -(-value // unit) * unit


def split(x):
    hi = x.astype(bf16)
    lo = (x - hi.astype(f32)).astype(bf16)
    return hi, lo


def mm(a, b):
    return lax.dot_general(a, b, (((1,), (0,)), ((), ())), preferred_element_type=f32)


def mt(a, b):
    return lax.dot_general(a, b, (((1,), (1,)), ((), ())), preferred_element_type=f32)


def product(dot, a, b):
    return dot(a[0], b[0]) + (dot(a[0], b[1]) + dot(a[1], b[0]))


def total(x):
    return jnp.sum(jnp.sum(x, axis=0, keepdims=True), axis=1, keepdims=True)


class Sizes:
    def __init__(self, mesh_shape, rhs, skel_perm):
        self.nx, self.ny, self.nz = (mesh_shape[a] for a in ("gx", "gy", "gz"))
        self.devices = self.nx * self.ny * self.nz
        self.blobs, self.bodies = rhs.shape[-2:]
        self.step = round_up(self.blobs, 8)
        self.rows = round_up(3 * self.step, 16)
        self.half = self.rows // 2
        self.message = self.half + 8
        self.direct = (self.nx, self.ny) == (4, 2)
        self.groups = -(-self.devices // LANES)
        self.levels = skel_perm.shape[0]
        self.skel = skel_perm.shape[1] // 2
        shifts = sorted({(dy % self.ny) for dy in (-1, 1)} - {0})
        self.shifts = shifts
        self.sources = [("same", dy) for dy in shifts]
        for kind in ("other", "partner"):
            self.sources += [(kind, dy) for dy in [0] + shifts]
        self.ghosts = round_up(len(self.sources) * RIM, LANES)
        self.far_tiles = self.nz + -(-self.nz // 2)

    def slot_start(self, slot, parity):
        dx, dy = slot // 3 - 1, (slot % 3 - 1) % self.ny
        kind = "same" if dx == 0 else "partner" if dx == 1 - 2 * parity else "other"
        if (kind, dy) == ("same", 0):
            return 0
        return self.bodies + RIM * self.sources.index((kind, dy))

    def beside(self, kind, x):
        if kind == "same":
            return x
        if kind == "partner":
            return x ^ 1
        return (x + 2 * (x % 2) - 1) % self.nx


def pieces(x, s):
    return [x[c * s.step : c * s.step + s.step] for c in range(3)]


def turn(parts, rot, inverse):
    out = []
    for target in range(3):
        acc = None
        for source in range(3):
            row = 3 * source + target if inverse else 3 * target + source
            term = rot[row : row + 1] * parts[source]
            acc = term if acc is None else acc + term
        out.append(acc)
    return out


def stacked(parts, s):
    rest = s.rows - 3 * s.step
    if rest:
        parts = list(parts) + [jnp.zeros((rest, s.bodies), f32)]
    return jnp.concatenate(parts, axis=0)


def occupancy(cells, s):
    row = lax.broadcasted_iota(jnp.int32, (s.skel, s.bodies), 0)
    return jnp.where(cells == row, 1.0, 0.0).astype(bf16)


def pack_charges(parts, weight_col, occ, s):
    moments = [jnp.sum(part * weight_col, axis=0, keepdims=True) for part in parts]
    moments = jnp.concatenate(moments + [jnp.zeros((5, s.bodies), f32)], axis=0)
    high, rest = split(moments)
    mid, low = split(moments - high.astype(f32))
    stack = jnp.concatenate([high.astype(f32), mid.astype(f32), low.astype(f32)], axis=0).astype(bf16)
    sums = mt(stack, occ)
    charges = sums[0:8] + (sums[8:16] + sums[16:24])
    tail = jnp.concatenate([charges[:, LANES:], jnp.zeros((8, 2 * LANES - s.skel), f32)], axis=1)
    row = lax.broadcasted_iota(jnp.int32, (8, LANES), 0)
    return jnp.where(row < 4, charges[:, :LANES], pltpu.roll(tail, 4, 0))


def pack_rim(x, s):
    lane = lax.broadcasted_iota(jnp.int32, (s.half, LANES), 1)
    top, bottom = x[: s.half, :LANES], x[s.half :, :LANES]
    return jnp.where(lane < RIM, top, pltpu.roll(bottom, RIM, 1))


def unpack_rims(rims, s):
    lane = lax.broadcasted_iota(jnp.int32, (s.half, LANES), 1)
    tops, bottoms = [], []
    for i in range(0, s.ghosts // RIM, 2):
        a = rims[i]
        b = rims[i + 1] if i + 1 < len(rims) else jnp.zeros_like(a)
        tops.append(jnp.where(lane < RIM, a, pltpu.roll(b, RIM, 1)))
        bottoms.append(jnp.where(lane < RIM, pltpu.roll(a, RIM, 1), b))
    return jnp.concatenate(
        [jnp.concatenate(tops, axis=1), jnp.concatenate(bottoms, axis=1)], axis=0
    )


def pack_message(x, weight_col, cells, s):
    charges = pack_charges(pieces(x, s), weight_col, occupancy(cells, s), s)
    return jnp.concatenate([pack_rim(x, s), charges], axis=0)


def start_kernel(s, rhs, cells, weight, message_out, col_out, f_out):
    f_out[...] = jnp.zeros_like(f_out)
    for c in range(3):
        f_out[c * s.step : c * s.step + s.blobs, :] = rhs[0, 0, c]
    f = f_out[...]
    wide = jnp.concatenate([weight[...], jnp.zeros((1, 2 * LANES - s.blobs), f32)], axis=1)
    col = jnp.broadcast_to(wide, (LANES, 2 * LANES)).T[: s.step]
    col_out[...] = col
    message_out[...] = pack_message(f, col[:, :1], cells[0], s)


def frame_rows(angles):
    cos, sin = jnp.cos(angles), jnp.sin(angles)
    cy, cp, cr = cos[0:1], cos[1:2], cos[2:3]
    sy, sp, sr = sin[0:1], sin[1:2], sin[2:3]
    return [
        cy * cp,
        cy * sp * sr - sy * cr,
        cy * sp * cr + sy * sr,
        sy * cp,
        sy * sp * sr + cy * cr,
        sy * sp * cr - cy * sr,
        -sp,
        cp * sr,
        cp * cr,
    ]


def local_part(f, s, rot, mob, own):
    parts = pieces(f, s)
    turned = stacked(turn(parts, rot, False), s)
    mixed = product(mm, mob, split(turned))
    back = turn(pieces(mixed, s), rot, True)
    return f + stacked(back, s), product(mm, split(f), own)


def expand(block, level, halves):
    if level == 0:
        return [block]
    block = split(block)
    near, far = (product(mt, block, split(half)) for half in halves[level - 1])
    return expand(near, level - 1, halves) + expand(far, level - 1, halves)


def setup_kernel(
    s, ids, f_in, angles, self_mob, near_mat, near_weight, neighbours, perm, interp, sibling, root,
    loc_out, gat_out, rot_out, sh_out, sl_out, nh_out, nl_out, oh_out, ol_out, gh_out, gl_out,
    far_out, padded, ups_ref,
):
    f = f_in[...]
    rot = jnp.concatenate(frame_rows(angles[0, 0]) + [jnp.zeros((7, s.bodies), f32)], axis=0)
    rot_out[...] = rot

    padded[...] = jnp.zeros_like(padded)
    for matrix, hi_out, lo_out in ((self_mob, sh_out, sl_out), (near_mat, nh_out, nl_out)):
        for c in range(3):
            for d in range(3):
                padded[c * s.step : c * s.step + s.blobs, d * s.step : d * s.step + s.blobs] = matrix[
                    c * s.blobs : (c + 1) * s.blobs, d * s.blobs : (d + 1) * s.blobs
                ]
        hi, lo = split(padded[...])
        hi_out[...] = hi
        lo_out[...] = lo

    links = neighbours[0, 0]
    slot = links // s.bodies
    base = jnp.zeros_like(links)
    odd = (ids[0] // s.ny) % 2
    for index in range(9):
        start = jnp.where(odd == 1, s.slot_start(index, 1), s.slot_start(index, 0))
        base = jnp.where(slot == index, start, base)
    column = base + links % s.bodies
    coef = near_weight[0, 0]
    for first, count, hi_out, lo_out in (
        (0, s.bodies, oh_out, ol_out),
        (s.bodies, s.ghosts, gh_out, gl_out),
    ):
        for r in range(0, count, 64):
            row = lax.broadcasted_iota(jnp.int32, (64, s.bodies), 0) + (first + r)
            acc = jnp.zeros((64, s.bodies), f32)
            for k in range(coef.shape[0]):
                acc = acc + jnp.where(column[k : k + 1] == row, coef[k : k + 1], 0.0)
            hi, lo = split(acc)
            hi_out[r : r + 64, :] = hi
            lo_out[r : r + 64, :] = lo

    loc, gat = local_part(f, s, rot, (sh_out[...], sl_out[...]), (oh_out[...], ol_out[...]))
    loc_out[...] = loc
    gat_out[...] = gat

    n = s.skel
    z = ids[1]
    halves = []
    eye_row = lax.broadcasted_iota(jnp.int32, (n, n), 0)
    eye_col = lax.broadcasted_iota(jnp.int32, (n, n), 1)
    eye = jnp.where(eye_row == eye_col, 1.0, 0.0)
    for level in range(s.levels):
        spot = lax.broadcasted_iota(jnp.int32, (2 * n, 2 * n), 0)
        onehot = jnp.where(perm[level : level + 1, :] == spot, 1.0, 0.0).astype(bf16)
        hi, lo = split(jnp.concatenate([eye, interp[level]], axis=0))
        ups_ref[level] = mm(onehot, hi) + mm(onehot, lo)
        bit = (z >> level) & 1
        halves.append(
            [ups_ref[level, pl.ds(pl.multiple_of(side * n, 8), n), :] for side in (bit, 1 - bit)]
        )

    def down(block, level, dot):
        return product(dot, split(halves[level][0]), split(block))

    spread = root[...]
    beside = []
    for level in reversed(range(s.levels)):
        spread = down(spread, level, mt if level == s.levels - 1 else mm)
        beside = [(down(block, level, mt if fresh else mm), False) for block, fresh in beside]
        beside.append((sibling[level], True))
    far_leaves = expand(spread, s.levels, halves)
    near_leaves = [jnp.zeros((n, n), f32)]
    for level, (block, fresh) in enumerate(reversed(beside)):
        near_leaves += expand(block.T if fresh else block, level, halves)
    tail = n - LANES
    far_out[...] = jnp.zeros_like(far_out)
    own = [a - b for a, b in zip(near_leaves, far_leaves)]
    for group, blocks in enumerate((own, far_leaves)):
        for leaf, block in enumerate(blocks):
            at = (group * s.far_tiles + leaf) * LANES
            far_out[:, at : at + LANES] = block[:, :LANES]
            at = (group * s.far_tiles + s.nz + leaf // 2) * LANES + leaf % 2 * RIM
            far_out[:, at : at + tail] = block[:, LANES:]


def half_kernel(s, *refs):
    *messages, out = refs
    acc = messages[0][s.half :, :]
    for message in messages[1:]:
        acc = acc + message[s.half :, :]
    out[...] = acc


def layer_kernel(s, message, *refs):
    *sums, out = refs
    acc = sums[0][...]
    for part in sums[1:]:
        acc = acc + part[...]
    out[0] = message[s.half :, :]
    out[1] = acc


def far_potential(s, charges, far_op):
    rows = []
    for group in range(2):
        tiles = [layer[group] for layer in charges]
        rows += tiles
        for leaf in range(0, s.nz, 2):
            pair = tiles[leaf]
            if leaf + 1 < s.nz:
                lane = lax.broadcasted_iota(jnp.int32, (8, LANES), 1)
                pair = jnp.where(lane < RIM, pair, pltpu.roll(tiles[leaf + 1], RIM, 1))
            rows.append(pltpu.roll(pair, 4, 0))
    columns = [[], [], []]
    for r in range(0, s.skel, 64):
        acc = [None] * 3
        for index, row in enumerate(rows):
            block = far_op[r : r + 64, index * LANES : (index + 1) * LANES]
            for c in range(3):
                term = block * row[c : c + 1]
                acc[c] = term if acc[c] is None else acc[c] + term
        for c in range(3):
            columns[c].append(jnp.sum(acc[c], axis=1, keepdims=True))
    return columns


def far_values(s, charges, far_op, cells):
    columns = far_potential(s, charges, far_op)
    out = []
    for c in range(3):
        acc = jnp.zeros((1, s.bodies), f32)
        for index, r in enumerate(range(0, s.skel, 64)):
            row = lax.broadcasted_iota(jnp.int32, (64, s.bodies), 0) + r
            acc = acc + jnp.sum(jnp.where(cells == row, columns[c][index], 0.0), axis=0, keepdims=True)
        out.append(acc)
    return out


def near_kernel(s, loc, gat, nh, nl, gh, gl, *refs):
    *messages, out = refs
    rims = [message[: s.half, :] for message in messages]
    gathered = gat[...] + product(mm, split(unpack_rims(rims, s)), (gh[...], gl[...]))
    out[...] = loc[...] + product(mm, (nh[...], nl[...]), split(gathered))


def with_far(s, part, layers, far_op, cells, col):
    values = far_values(s, layers, far_op, cells[0])
    return part[...] + stacked([col * value for value in values], s)


def first_kernel(s, part, far_op, cells, col, *refs):
    *layers, u_out, message_out = refs
    weight_col = col[:, :1]
    u = with_far(s, part, layers, far_op, cells, weight_col)
    u_out[...] = u
    message_out[...] = pack_message(u, weight_col, cells[0], s)


def safe_inverse(x):
    return jnp.where(x > 0.0, 1.0 / jnp.where(x > 0.0, x, 1.0), 0.0)


def middle_kernel(s, u_in, f_in, rot, sh, sl, oh, ol, loc_out, gat_out, ortho_out, stat_out):
    u, f = u_in[...], f_in[...]
    loc, gat = local_part(u, s, rot[...], (sh[...], sl[...]), (oh[...], ol[...]))
    loc_out[...] = loc
    gat_out[...] = gat
    ff = total(f * f)
    fu = total(f * u) * safe_inverse(ff)
    ortho = u - fu * f
    ortho_out[...] = ortho
    oo = total(ortho * ortho)
    stat_out[...] = jnp.broadcast_to(
        jnp.concatenate([ff, fu, oo, jnp.zeros((5, 1), f32)], axis=0), (8, LANES)
    )


def second_kernel(s, ids, part, far_op, cells, col, f_in, ortho_in, stat, *refs):
    *layers, stat_out = refs
    t = with_far(s, part, layers, far_op, cells, col[:, :1])
    f, ortho = f_in[...], ortho_in[...]
    ff, fu, oo = (stat[i : i + 1, :1] for i in range(3))
    ft = total(f * t) * safe_inverse(ff)
    ot = total(ortho * t) * safe_inverse(oo)
    rest_t = t - ft * f - ot * ortho
    tt = total(rest_t * rest_t)
    rf, ro = jnp.sqrt(ff), jnp.sqrt(oo)
    stats = jnp.concatenate(
        [rf, rf * fu, ro, rf * ft, ro * ot, jnp.sqrt(tt), jnp.zeros((2, 1), f32)], axis=0
    )
    device = ids[0] * s.nz + ids[1]
    for g in range(s.groups):
        lane = lax.broadcasted_iota(jnp.int32, (8, LANES), 1) + g * LANES
        stat_out[g] = jnp.where(lane == device, stats, 0.0)


def finish_kernel(s, rhs, u_in, *refs):
    *stats, x_out, lsq_out = refs
    groups = []
    for g in range(s.groups):
        acc = stats[0][g]
        for part in stats[1:]:
            acc = acc + part[g]
        groups.append(acc)
    rows = jnp.concatenate(groups, axis=1) if len(groups) > 1 else groups[0]
    f1, u1, u2, t1, t2, t3 = (rows[i : i + 1] for i in range(6))

    def along(x):
        return jnp.sum(x, axis=1, keepdims=True)

    beta = jnp.sqrt(along(f1 * f1) + epsilon)
    v = f1 / beta
    w1, w2 = u1 / beta, u2 / beta
    h11 = along(w1 * v)
    r1 = w1 - h11 * v
    h21 = jnp.sqrt(along(r1 * r1 + w2 * w2) + epsilon)
    b1, b2 = r1 / h21, w2 / h21
    z1, z2, z3 = ((t1 / beta - h11 * w1) / h21, (t2 / beta - h11 * w2) / h21, t3 / beta / h21)
    h12 = along(z1 * v)
    h22 = along(z1 * b1 + z2 * b2)
    d1, d2 = z1 - h12 * v - h22 * b1, z2 - h22 * b2
    h32 = jnp.sqrt(along(d1 * d1 + d2 * d2 + z3 * z3) + epsilon)
    first_norm = jnp.sqrt(h11 * h11 + h21 * h21)
    c1, s1 = h11 / first_norm, h21 / first_norm
    t12, t22 = c1 * h12 + s1 * h22, c1 * h22 - s1 * h12
    second_norm = jnp.sqrt(t22 * t22 + h32 * h32)
    c2, s2 = t22 / second_norm, h32 / second_norm
    g2 = -s1 * beta
    y2 = c2 * g2 / second_norm
    y1 = (c1 * beta - t12 * y2) / first_norm
    lsq_out[...] = jnp.abs(s2 * g2)
    on_u = y2 / h21 / beta
    on_f = y1 / beta - on_u * h11
    for c in range(3):
        x_out[0, 0, c] = on_f * rhs[0, 0, c] + on_u * u_in[c * s.step : c * s.step + s.blobs, :]


def call(kernel, outs, args, scalars=0, scratch=(), flops=0):
    vmem = pl.BlockSpec(memory_space=pltpu.VMEM)
    smem = pl.BlockSpec(memory_space=pltpu.SMEM)
    return pl.pallas_call(
        kernel,
        out_shape=[jax.ShapeDtypeStruct(shape, kind) for shape, kind in outs],
        in_specs=[smem] * scalars + [vmem] * (len(args) - scalars),
        out_specs=[vmem] * len(outs),
        scratch_shapes=list(scratch),
        compiler_params=pltpu.CompilerParams(vmem_limit_bytes=16 * 2**20),
        cost_estimate=pl.CostEstimate(flops=flops, bytes_accessed=2**20, transcendentals=0),
    )(*args)


def body(
    mesh_shape, rhs, angles, self_mob, near_mat, near_weight, neighbours, cells, blob_weight,
    skel_perm, interp, sibling_ops, root_op,
):
    s = Sizes(mesh_shape, rhs, skel_perm)
    full = (s.rows, s.bodies)
    square = (s.rows, s.rows)
    tile = (8, LANES)
    far_shape = (s.skel, 2 * s.far_tiles * LANES)
    column = lax.axis_index("gx") * s.ny + lax.axis_index("gy")
    ids = jnp.stack([column, lax.axis_index("gz")]).astype(jnp.int32)

    def fetch(x, kind, dy):
        pairs = []
        for gx in range(s.nx):
            for gy in range(s.ny):
                pairs.append((s.beside(kind, gx) * s.ny + (gy + dy) % s.ny, gx * s.ny + gy))
        return lax.ppermute(x, ("gx", "gy"), pairs)

    def fetch_layers(x):
        return [x] + [
            lax.ppermute(x, "gz", [(z ^ k, z) for z in range(s.nz)]) for k in range(1, s.nz)
        ]

    def fetch_messages(message):
        got = {}
        for dy in s.shifts:
            got["same", dy] = fetch(message, "same", dy)
        for dy in s.shifts:
            got["other", dy] = fetch(message, "other", dy)
        got["other", 0] = fetch(message, "other", 0)
        got["partner", 0] = fetch(message, "partner", 0)
        for dy in s.shifts:
            got["partner", dy] = fetch(got["same", dy], "partner", 0)
        return got

    def share_charges(message, got):
        if s.direct:
            quarter = [message] + [got[key] for key in s.sources if key[0] != "partner"]
            (half,) = call(functools.partial(half_kernel, s), [(tile, f32)], quarter)
            sums = [half, fetch(half, "partner", 0)]
        else:
            sums = [lax.psum(message[s.half :], ("gx", "gy"))]
        (pair,) = call(functools.partial(layer_kernel, s), [((2,) + tile, f32)], [message] + sums)
        return fetch_layers(pair)

    def near_part(loc, gat, got):
        return call(
            functools.partial(near_kernel, s),
            [(full, f32)],
            [loc, gat, nh, nl, gh, gl] + [got[key] for key in s.sources],
            flops=10**9,
        )[0]

    message, col, f = call(
        functools.partial(start_kernel, s),
        [((s.message, LANES), f32), ((s.step, LANES), f32), (full, f32)],
        [rhs, cells, blob_weight.reshape(1, -1)],
        flops=10**7,
    )
    got = fetch_messages(message)
    loc, gat, rot, sh, sl, nh, nl, oh, ol, gh, gl, far_op = call(
        functools.partial(setup_kernel, s),
        [(full, f32), (full, f32), ((16, s.bodies), f32)]
        + [(square, bf16)] * 4
        + [((s.bodies, s.bodies), bf16)] * 2
        + [((s.ghosts, s.bodies), bf16)] * 2
        + [(far_shape, f32)],
        [ids, f, angles, self_mob, near_mat, near_weight, neighbours, skel_perm, interp, sibling_ops, root_op],
        scalars=1,
        scratch=[pltpu.VMEM(square, f32), pltpu.VMEM((s.levels, 2 * s.skel, s.skel), f32)],
        flops=5 * 10**9,
    )
    part = near_part(loc, gat, got)
    layers = share_charges(message, got)
    u, message = call(
        functools.partial(first_kernel, s),
        [(full, f32), ((s.message, LANES), f32)],
        [part, far_op, cells, col, *layers],
        flops=10**8,
    )
    got = fetch_messages(message)
    loc, gat, ortho, stat = call(
        functools.partial(middle_kernel, s),
        [(full, f32), (full, f32), (full, f32), (tile, f32)],
        [u, f, rot, sh, sl, oh, ol],
        flops=10**9,
    )
    part = near_part(loc, gat, got)
    layers = share_charges(message, got)
    (stats,) = call(
        functools.partial(second_kernel, s),
        [((s.groups,) + tile, f32)],
        [ids, part, far_op, cells, col, f, ortho, stat, *layers],
        scalars=1,
        flops=10**8,
    )
    if s.direct:
        stats = stats + fetch(stats, "partner", 0)
        stats = stats + fetch(stats, "same", 1) + fetch(stats, "other", 0) + fetch(stats, "other", 1)
    else:
        stats = lax.psum(stats, ("gx", "gy"))
    result, lsq = call(
        functools.partial(finish_kernel, s),
        [(rhs.shape, f32), ((1, 1), f32)],
        [rhs, u, *fetch_layers(stats)],
        flops=10**7,
    )
    return result, lsq.reshape(())


def solution(mesh):
    in_specs = (
        P("gx", "gy", None, None, "gz"),
        P("gx", "gy", None, "gz"),
        P(),
        P(),
        P("gx", "gy", None, "gz"),
        P("gx", "gy", None, "gz"),
        P("gx", "gy", "gz"),
        P(),
        P(),
        P(),
        P(),
        P(),
    )
    out_specs = (P("gx", "gy", None, None, "gz"), P())
    inner = functools.partial(body, dict(mesh.shape))
    return jax.shard_map(inner, mesh=mesh, in_specs=in_specs, out_specs=out_specs, check_vma=False)
```

```python
import functools

import jax
import jax.numpy as jnp
from jax import lax
from jax.experimental import pallas as pl
from jax.experimental.pallas import tpu as pltpu
from jax.sharding import PartitionSpec as P

epsilon = 1e-06
f32 = jnp.float32
bf16 = jnp.bfloat16
RIM = 64
LANES = 128


def round_up(value, unit):
    return -(-value // unit) * unit


def split(x):
    hi = x.astype(bf16)
    lo = (x - hi.astype(f32)).astype(bf16)
    return hi, lo


def mm(a, b):
    return lax.dot_general(a, b, (((1,), (0,)), ((), ())), preferred_element_type=f32)


def mt(a, b):
    return lax.dot_general(a, b, (((1,), (1,)), ((), ())), preferred_element_type=f32)


def product(dot, a, b):
    return dot(a[0], b[0]) + (dot(a[0], b[1]) + dot(a[1], b[0]))


def total(x):
    return jnp.sum(jnp.sum(x, axis=0, keepdims=True), axis=1, keepdims=True)


class Sizes:
    def __init__(self, mesh_shape, rhs, skel_perm):
        self.nx, self.ny, self.nz = (mesh_shape[a] for a in ("gx", "gy", "gz"))
        self.devices = self.nx * self.ny * self.nz
        self.blobs, self.bodies = rhs.shape[-2:]
        self.step = round_up(self.blobs, 8)
        self.rows = round_up(3 * self.step, 16)
        self.half = self.rows // 2
        self.message = self.half + 8
        self.direct = (self.nx, self.ny) == (4, 2)
        self.groups = -(-self.devices // LANES)
        self.levels = skel_perm.shape[0]
        self.skel = skel_perm.shape[1] // 2
        shifts = sorted({(dy % self.ny) for dy in (-1, 1)} - {0})
        self.shifts = shifts
        self.sources = [("same", dy) for dy in shifts]
        for kind in ("other", "partner"):
            self.sources += [(kind, dy) for dy in [0] + shifts]
        self.ghosts = round_up(len(self.sources) * RIM, LANES)
        self.far_tiles = self.nz + -(-self.nz // 2)

    def slot_start(self, slot, parity):
        dx, dy = slot // 3 - 1, (slot % 3 - 1) % self.ny
        kind = "same" if dx == 0 else "partner" if dx == 1 - 2 * parity else "other"
        if (kind, dy) == ("same", 0):
            return 0
        return self.bodies + RIM * self.sources.index((kind, dy))

    def beside(self, kind, x):
        if kind == "same":
            return x
        if kind == "partner":
            return x ^ 1
        return (x + 2 * (x % 2) - 1) % self.nx


def pieces(x, s):
    return [x[c * s.step : c * s.step + s.step] for c in range(3)]


def turn(parts, rot, inverse):
    out = []
    for target in range(3):
        acc = None
        for source in range(3):
            row = 3 * source + target if inverse else 3 * target + source
            term = rot[row : row + 1] * parts[source]
            acc = term if acc is None else acc + term
        out.append(acc)
    return out


def stacked(parts, s):
    rest = s.rows - 3 * s.step
    if rest:
        parts = list(parts) + [jnp.zeros((rest, s.bodies), f32)]
    return jnp.concatenate(parts, axis=0)


def occupancy(cells, s):
    row = lax.broadcasted_iota(jnp.int32, (s.skel, s.bodies), 0)
    return jnp.where(cells == row, 1.0, 0.0).astype(bf16)


def pack_charges(parts, weight_col, occ, s):
    moments = [jnp.sum(part * weight_col, axis=0, keepdims=True) for part in parts]
    moments = jnp.concatenate(moments + [jnp.zeros((5, s.bodies), f32)], axis=0)
    high, rest = split(moments)
    mid, low = split(moments - high.astype(f32))
    stack = jnp.concatenate([high.astype(f32), mid.astype(f32), low.astype(f32)], axis=0).astype(bf16)
    sums = mt(stack, occ)
    charges = sums[0:8] + (sums[8:16] + sums[16:24])
    tail = jnp.concatenate([charges[:, LANES:], jnp.zeros((8, 2 * LANES - s.skel), f32)], axis=1)
    row = lax.broadcasted_iota(jnp.int32, (8, LANES), 0)
    return jnp.where(row < 4, charges[:, :LANES], pltpu.roll(tail, 4, 0))


def pack_rim(x, s):
    lane = lax.broadcasted_iota(jnp.int32, (s.half, LANES), 1)
    top, bottom = x[: s.half, :LANES], x[s.half :, :LANES]
    return jnp.where(lane < RIM, top, pltpu.roll(bottom, RIM, 1))


def unpack_rims(rims, s):
    lane = lax.broadcasted_iota(jnp.int32, (s.half, LANES), 1)
    tops, bottoms = [], []
    for i in range(0, s.ghosts // RIM, 2):
        a = rims[i]
        b = rims[i + 1] if i + 1 < len(rims) else jnp.zeros_like(a)
        tops.append(jnp.where(lane < RIM, a, pltpu.roll(b, RIM, 1)))
        bottoms.append(jnp.where(lane < RIM, pltpu.roll(a, RIM, 1), b))
    return jnp.concatenate(
        [jnp.concatenate(tops, axis=1), jnp.concatenate(bottoms, axis=1)], axis=0
    )


def pack_message(x, weight_col, cells, s):
    charges = pack_charges(pieces(x, s), weight_col, occupancy(cells, s), s)
    return jnp.concatenate([pack_rim(x, s), charges], axis=0)


def begin(sources, targets, sems):
    moves = [pltpu.make_async_copy(a, b, sems.at[i]) for i, (a, b) in enumerate(zip(sources, targets))]
    for move in moves:
        move.start()
    return moves


def start_kernel(s, rhs, cells, weight, message_out, col_out, cells_out, f_out, raw, wide, sems):
    moves = begin((weight, cells, rhs), (wide, cells_out, raw), sems)
    f_out[...] = jnp.zeros_like(f_out)
    moves[0].wait()
    row = jnp.concatenate([wide[...], jnp.zeros((1, 2 * LANES - s.blobs), f32)], axis=1)
    col = jnp.broadcast_to(row, (LANES, 2 * LANES)).T[: s.step]
    col_out[...] = col
    for move in moves[1:]:
        move.wait()
    for c in range(3):
        f_out[c * s.step : c * s.step + s.blobs, :] = raw[c * s.blobs : (c + 1) * s.blobs, 0, :]
    message_out[...] = pack_message(f_out[...], col[:, :1], cells_out[0], s)


def frame_rows(angles):
    cos, sin = jnp.cos(angles), jnp.sin(angles)
    cy, cp, cr = cos[0:1], cos[1:2], cos[2:3]
    sy, sp, sr = sin[0:1], sin[1:2], sin[2:3]
    return [
        cy * cp,
        cy * sp * sr - sy * cr,
        cy * sp * cr + sy * sr,
        sy * cp,
        sy * sp * sr + cy * cr,
        sy * sp * cr - cy * sr,
        -sp,
        cp * sr,
        cp * cr,
    ]


def local_part(f, s, rot, mob, own):
    parts = pieces(f, s)
    turned = stacked(turn(parts, rot, False), s)
    mixed = product(mm, mob, split(turned))
    back = turn(pieces(mixed, s), rot, True)
    return f + stacked(back, s), product(mm, split(f), own)


def expand(block, level, halves):
    if level == 0:
        return [block]
    block = split(block)
    near, far = (product(mt, block, split(half)) for half in halves[level - 1])
    return expand(near, level - 1, halves) + expand(far, level - 1, halves)


def setup_kernel(
    s, ids, f_in, *refs
):
    count = 9
    sources, refs = refs[:count], refs[count:]
    copies, refs = refs[-1 - count :], refs[: -1 - count]
    copies, sems = copies[:-1], copies[-1]
    setup(s, ids, f_in, begin(sources, copies, sems), *copies, *refs)


def setup(
    s, ids, f_in, moves, angles, near_weight, neighbours, self_mob, near_mat, perm, interp, sibling, root,
    loc_out, gat_out, rot_out, sh_out, sl_out, nh_out, nl_out, oh_out, ol_out, gh_out, gl_out,
    far_out, padded, ups_ref,
):
    f = f_in[...]
    for move in moves[:3]:
        move.wait()
    rot = jnp.concatenate(frame_rows(angles[:, 0, :]) + [jnp.zeros((7, s.bodies), f32)], axis=0)
    rot_out[...] = rot

    links = neighbours[0, 0]
    slot = links // s.bodies
    base = jnp.zeros_like(links)
    odd = (ids[0] // s.ny) % 2
    for index in range(9):
        start = jnp.where(odd == 1, s.slot_start(index, 1), s.slot_start(index, 0))
        base = jnp.where(slot == index, start, base)
    column = base + links % s.bodies
    coef = near_weight[0, 0]
    for first, count, hi_out, lo_out in (
        (0, s.bodies, oh_out, ol_out),
        (s.bodies, s.ghosts, gh_out, gl_out),
    ):
        for r in range(0, count, 64):
            row = lax.broadcasted_iota(jnp.int32, (64, s.bodies), 0) + (first + r)
            acc = jnp.zeros((64, s.bodies), f32)
            for k in range(coef.shape[0]):
                acc = acc + jnp.where(column[k : k + 1] == row, coef[k : k + 1], 0.0)
            hi, lo = split(acc)
            hi_out[r : r + 64, :] = hi
            lo_out[r : r + 64, :] = lo

    for move in moves[3:]:
        move.wait()
    padded[...] = jnp.zeros_like(padded)
    for matrix, hi_out, lo_out in ((self_mob, sh_out, sl_out), (near_mat, nh_out, nl_out)):
        for c in range(3):
            for d in range(3):
                padded[c * s.step : c * s.step + s.blobs, d * s.step : d * s.step + s.blobs] = matrix[
                    c * s.blobs : (c + 1) * s.blobs, d * s.blobs : (d + 1) * s.blobs
                ]
        hi, lo = split(padded[...])
        hi_out[...] = hi
        lo_out[...] = lo

    loc, gat = local_part(f, s, rot, (sh_out[...], sl_out[...]), (oh_out[...], ol_out[...]))
    loc_out[...] = loc
    gat_out[...] = gat

    n = s.skel
    z = ids[1]
    halves = []
    eye_row = lax.broadcasted_iota(jnp.int32, (n, n), 0)
    eye_col = lax.broadcasted_iota(jnp.int32, (n, n), 1)
    eye = jnp.where(eye_row == eye_col, 1.0, 0.0)
    for level in range(s.levels):
        spot = lax.broadcasted_iota(jnp.int32, (2 * n, 2 * n), 0)
        onehot = jnp.where(perm[level : level + 1, :] == spot, 1.0, 0.0).astype(bf16)
        hi, lo = split(jnp.concatenate([eye, interp[level]], axis=0))
        ups_ref[level] = mm(onehot, hi) + mm(onehot, lo)
        bit = (z >> level) & 1
        halves.append(
            [ups_ref[level, pl.ds(pl.multiple_of(side * n, 8), n), :] for side in (bit, 1 - bit)]
        )

    def down(block, level, dot):
        return product(dot, split(halves[level][0]), split(block))

    spread = root[...]
    beside = []
    for level in reversed(range(s.levels)):
        spread = down(spread, level, mt if level == s.levels - 1 else mm)
        beside = [(down(block, level, mt if fresh else mm), False) for block, fresh in beside]
        beside.append((sibling[level], True))
    far_leaves = expand(spread, s.levels, halves)
    near_leaves = [jnp.zeros((n, n), f32)]
    for level, (block, fresh) in enumerate(reversed(beside)):
        near_leaves += expand(block.T if fresh else block, level, halves)
    tail = n - LANES
    far_out[...] = jnp.zeros_like(far_out)
    own = [a - b for a, b in zip(near_leaves, far_leaves)]
    for group, blocks in enumerate((own, far_leaves)):
        for leaf, block in enumerate(blocks):
            at = (group * s.far_tiles + leaf) * LANES
            far_out[:, at : at + LANES] = block[:, :LANES]
            at = (group * s.far_tiles + s.nz + leaf // 2) * LANES + leaf % 2 * RIM
            far_out[:, at : at + tail] = block[:, LANES:]


def half_kernel(s, *refs):
    *messages, _, out = refs
    acc = messages[0][s.half :, :]
    for message in messages[1:]:
        acc = acc + message[s.half :, :]
    out[...] = acc


def layer_kernel(s, message, *refs):
    *sums, out = refs
    acc = sums[0][...]
    for part in sums[1:]:
        acc = acc + part[...]
    out[0] = message[s.half :, :]
    out[1] = acc


def far_potential(s, charges, far_op):
    rows = []
    for group in range(2):
        tiles = [layer[group] for layer in charges]
        rows += tiles
        for leaf in range(0, s.nz, 2):
            pair = tiles[leaf]
            if leaf + 1 < s.nz:
                lane = lax.broadcasted_iota(jnp.int32, (8, LANES), 1)
                pair = jnp.where(lane < RIM, pair, pltpu.roll(tiles[leaf + 1], RIM, 1))
            rows.append(pltpu.roll(pair, 4, 0))
    columns = [[], [], []]
    for r in range(0, s.skel, 64):
        acc = [None] * 3
        for index, row in enumerate(rows):
            block = far_op[r : r + 64, index * LANES : (index + 1) * LANES]
            for c in range(3):
                term = block * row[c : c + 1]
                acc[c] = term if acc[c] is None else acc[c] + term
        for c in range(3):
            columns[c].append(jnp.sum(acc[c], axis=1, keepdims=True))
    return columns


def far_values(s, charges, far_op, cells):
    columns = far_potential(s, charges, far_op)
    out = []
    for c in range(3):
        acc = jnp.zeros((1, s.bodies), f32)
        for index, r in enumerate(range(0, s.skel, 64)):
            row = lax.broadcasted_iota(jnp.int32, (64, s.bodies), 0) + r
            acc = acc + jnp.sum(jnp.where(cells == row, columns[c][index], 0.0), axis=0, keepdims=True)
        out.append(acc)
    return out


def near_kernel(s, loc, gat, nh, nl, gh, gl, *refs):
    *messages, out = refs
    rims = [message[: s.half, :] for message in messages]
    gathered = gat[...] + product(mm, split(unpack_rims(rims, s)), (gh[...], gl[...]))
    out[...] = loc[...] + product(mm, (nh[...], nl[...]), split(gathered))


def with_far(s, part, layers, far_op, cells, col):
    values = far_values(s, layers, far_op, cells[0])
    return part[...] + stacked([col * value for value in values], s)


def first_kernel(s, part, far_op, cells, col, *refs):
    *layers, u_out, message_out = refs
    weight_col = col[:, :1]
    u = with_far(s, part, layers, far_op, cells, weight_col)
    u_out[...] = u
    message_out[...] = pack_message(u, weight_col, cells[0], s)


def safe_inverse(x):
    return jnp.where(x > 0.0, 1.0 / jnp.where(x > 0.0, x, 1.0), 0.0)


def middle_kernel(s, u_in, f_in, rot, sh, sl, oh, ol, loc_out, gat_out, ortho_out, stat_out):
    u, f = u_in[...], f_in[...]
    loc, gat = local_part(u, s, rot[...], (sh[...], sl[...]), (oh[...], ol[...]))
    loc_out[...] = loc
    gat_out[...] = gat
    ff = total(f * f)
    fu = total(f * u) * safe_inverse(ff)
    ortho = u - fu * f
    ortho_out[...] = ortho
    oo = total(ortho * ortho)
    stat_out[...] = jnp.broadcast_to(
        jnp.concatenate([ff, fu, oo, jnp.zeros((5, 1), f32)], axis=0), (8, LANES)
    )


def second_kernel(s, part, far_op, cells, col, f_in, ortho_in, stat, *refs):
    *layers, stat_out = refs
    t = with_far(s, part, layers, far_op, cells, col[:, :1])
    f, ortho = f_in[...], ortho_in[...]
    ff, fu, oo = (stat[i : i + 1, :1] for i in range(3))
    ft = total(f * t) * safe_inverse(ff)
    ot = total(ortho * t) * safe_inverse(oo)
    rest_t = t - ft * f - ot * ortho
    tt = total(rest_t * rest_t)
    rf, ro = jnp.sqrt(ff), jnp.sqrt(oo)
    stats = jnp.concatenate(
        [rf, rf * fu, ro, rf * ft, ro * ot, jnp.sqrt(tt), jnp.zeros((2, 1), f32)], axis=0
    )
    stat_out[...] = jnp.broadcast_to(jnp.broadcast_to(stats, (8, LANES))[None], stat_out.shape)


def finish_kernel(s, f_in, u_in, stats, x_out, lsq_out, raw, sem):
    groups = []
    for g in range(s.groups):
        lane = lax.broadcasted_iota(jnp.int32, (8, LANES), 1) + g * LANES
        acc = jnp.zeros((8, LANES), f32)
        for d in range(g * LANES, min(s.devices, (g + 1) * LANES)):
            acc = acc + jnp.where(lane == d, stats[d], 0.0)
        groups.append(acc)
    rows = jnp.concatenate(groups, axis=1) if len(groups) > 1 else groups[0]
    f1, u1, u2, t1, t2, t3 = (rows[i : i + 1] for i in range(6))

    def along(x):
        return jnp.sum(x, axis=1, keepdims=True)

    beta = jnp.sqrt(along(f1 * f1) + epsilon)
    v = f1 / beta
    w1, w2 = u1 / beta, u2 / beta
    h11 = along(w1 * v)
    r1 = w1 - h11 * v
    h21 = jnp.sqrt(along(r1 * r1 + w2 * w2) + epsilon)
    b1, b2 = r1 / h21, w2 / h21
    z1, z2, z3 = ((t1 / beta - h11 * w1) / h21, (t2 / beta - h11 * w2) / h21, t3 / beta / h21)
    h12 = along(z1 * v)
    h22 = along(z1 * b1 + z2 * b2)
    d1, d2 = z1 - h12 * v - h22 * b1, z2 - h22 * b2
    h32 = jnp.sqrt(along(d1 * d1 + d2 * d2 + z3 * z3) + epsilon)
    first_norm = jnp.sqrt(h11 * h11 + h21 * h21)
    c1, s1 = h11 / first_norm, h21 / first_norm
    t12, t22 = c1 * h12 + s1 * h22, c1 * h22 - s1 * h12
    second_norm = jnp.sqrt(t22 * t22 + h32 * h32)
    c2, s2 = t22 / second_norm, h32 / second_norm
    g2 = -s1 * beta
    y2 = c2 * g2 / second_norm
    y1 = (c1 * beta - t12 * y2) / first_norm
    lsq_out[...] = jnp.abs(s2 * g2)
    on_u = y2 / h21 / beta
    on_f = y1 / beta - on_u * h11
    for c in range(3):
        part = slice(c * s.step, c * s.step + s.blobs)
        raw[c * s.blobs : (c + 1) * s.blobs, 0, :] = on_f * f_in[part, :] + on_u * u_in[part, :]
    move = pltpu.make_async_copy(raw, x_out, sem)
    move.start()
    move.wait()


def call(kernel, outs, args, scalars=0, far_args=0, far_outs=0, scratch=(), flops=0):
    vmem = pl.BlockSpec(memory_space=pltpu.VMEM)
    smem = pl.BlockSpec(memory_space=pltpu.SMEM)
    hbm = pl.BlockSpec(memory_space=pltpu.HBM)
    near_args = len(args) - far_args
    args = args[:near_args] + [pltpu.with_memory_space_constraint(x, pltpu.HBM) for x in args[near_args:]]
    return pl.pallas_call(
        kernel,
        out_shape=[jax.ShapeDtypeStruct(shape, kind) for shape, kind in outs],
        in_specs=[smem] * scalars + [vmem] * (near_args - scalars) + [hbm] * far_args,
        out_specs=[hbm] * far_outs + [vmem] * (len(outs) - far_outs),
        scratch_shapes=list(scratch),
        compiler_params=pltpu.CompilerParams(vmem_limit_bytes=16 * 2**20),
        cost_estimate=pl.CostEstimate(flops=flops, bytes_accessed=2**20, transcendentals=0),
    )(*args)


def body(
    mesh_shape, rhs, angles, self_mob, near_mat, near_weight, neighbours, cells, blob_weight,
    skel_perm, interp, sibling_ops, root_op,
):
    s = Sizes(mesh_shape, rhs, skel_perm)
    full = (s.rows, s.bodies)
    square = (s.rows, s.rows)
    tile = (8, LANES)
    far_shape = (s.skel, 2 * s.far_tiles * LANES)
    column = lax.axis_index("gx") * s.ny + lax.axis_index("gy")
    ids = jnp.stack([column, lax.axis_index("gz")]).astype(jnp.int32)

    def fetch(x, kind, dy):
        pairs = []
        for gx in range(s.nx):
            for gy in range(s.ny):
                pairs.append((s.beside(kind, gx) * s.ny + (gy + dy) % s.ny, gx * s.ny + gy))
        return lax.ppermute(x, ("gx", "gy"), pairs)

    def fetch_layers(x):
        return [x] + [
            lax.ppermute(x, "gz", [(z ^ k, z) for z in range(s.nz)]) for k in range(1, s.nz)
        ]

    def fetch_messages(message):
        got = {}
        for dy in s.shifts:
            got["same", dy] = fetch(message, "same", dy)
        for dy in s.shifts:
            got["other", dy] = fetch(message, "other", dy)
        got["other", 0] = fetch(message, "other", 0)
        got["partner", 0] = fetch(message, "partner", 0)
        for dy in s.shifts:
            got["partner", dy] = fetch(got["same", dy], "partner", 0)
        return got

    def share_charges(message, got, after):
        if s.direct:
            quarter = [message] + [got[key] for key in s.sources if key[0] != "partner"]
            (half,) = call(functools.partial(half_kernel, s), [(tile, f32)], quarter + [after])
            sums = [half, fetch(half, "partner", 0)]
        else:
            sums = [lax.psum(message[s.half :], ("gx", "gy"))]
        (pair,) = call(functools.partial(layer_kernel, s), [((2,) + tile, f32)], [message] + sums)
        return fetch_layers(pair)

    def near_part(loc, gat, got):
        return call(
            functools.partial(near_kernel, s),
            [(full, f32)],
            [loc, gat, nh, nl, gh, gl] + [got[key] for key in s.sources],
            flops=10**9,
        )[0]

    flat = (3 * s.blobs, 1, s.bodies)
    small = (1, s.blobs)
    message, col, cells, f = call(
        functools.partial(start_kernel, s),
        [((s.message, LANES), f32), ((s.step, LANES), f32), (cells.shape, jnp.int32), (full, f32)],
        [rhs.reshape(flat), cells, blob_weight.reshape(small)],
        far_args=3,
        scratch=[pltpu.VMEM(flat, f32), pltpu.VMEM(small, f32), pltpu.SemaphoreType.DMA((3,))],
        flops=10**7,
    )
    got = fetch_messages(message)
    operators = [
        angles.reshape(3, 1, s.bodies), near_weight, neighbours, self_mob, near_mat, skel_perm, interp,
        sibling_ops, root_op,
    ]
    loc, gat, rot, sh, sl, nh, nl, oh, ol, gh, gl, far_op = call(
        functools.partial(setup_kernel, s),
        [(full, f32), (full, f32), ((16, s.bodies), f32)]
        + [(square, bf16)] * 4
        + [((s.bodies, s.bodies), bf16)] * 2
        + [((s.ghosts, s.bodies), bf16)] * 2
        + [(far_shape, f32)],
        [ids, f] + operators,
        scalars=1,
        far_args=len(operators),
        scratch=[pltpu.VMEM(square, f32), pltpu.VMEM((s.levels, 2 * s.skel, s.skel), f32)]
        + [pltpu.VMEM(x.shape, x.dtype) for x in operators]
        + [pltpu.SemaphoreType.DMA((len(operators),))],
        flops=5 * 10**9,
    )
    part = near_part(loc, gat, got)
    layers = share_charges(message, got, rot)
    u, message = call(
        functools.partial(first_kernel, s),
        [(full, f32), ((s.message, LANES), f32)],
        [part, far_op, cells, col, *layers],
        flops=10**8,
    )
    got = fetch_messages(message)
    loc, gat, ortho, stat = call(
        functools.partial(middle_kernel, s),
        [(full, f32), (full, f32), (full, f32), (tile, f32)],
        [u, f, rot, sh, sl, oh, ol],
        flops=10**9,
    )
    part = near_part(loc, gat, got)
    layers = share_charges(message, got, stat)
    (stats,) = call(
        functools.partial(second_kernel, s),
        [((s.devices,) + tile, f32)],
        [part, far_op, cells, col, f, ortho, stat, *layers],
        flops=10**8,
    )
    stats = lax.all_to_all(stats, ("gx", "gy", "gz"), 0, 0)
    result, lsq = call(
        functools.partial(finish_kernel, s),
        [(flat, f32), ((1, 1), f32)],
        [f, u, stats],
        far_outs=1,
        scratch=[pltpu.VMEM(flat, f32), pltpu.SemaphoreType.DMA],
        flops=10**7,
    )
    return result.reshape(rhs.shape), lsq.reshape(())


def solution(mesh):
    in_specs = (
        P("gx", "gy", None, None, "gz"),
        P("gx", "gy", None, "gz"),
        P(),
        P(),
        P("gx", "gy", None, "gz"),
        P("gx", "gy", None, "gz"),
        P("gx", "gy", "gz"),
        P(),
        P(),
        P(),
        P(),
        P(),
    )
    out_specs = (P("gx", "gy", None, None, "gz"), P())
    inner = functools.partial(body, dict(mesh.shape))
    return jax.shard_map(inner, mesh=mesh, in_specs=in_specs, out_specs=out_specs, check_vma=False)
```

```python
import functools

import jax
import jax.numpy as jnp
from jax import lax
from jax.experimental import pallas as pl
from jax.experimental.pallas import tpu as pltpu
from jax.sharding import PartitionSpec as P

epsilon = 1e-06
f32 = jnp.float32
bf16 = jnp.bfloat16
RIM = 64
LANES = 128


def round_up(value, unit):
    return -(-value // unit) * unit


def split(x):
    hi = x.astype(bf16)
    lo = (x - hi.astype(f32)).astype(bf16)
    return hi, lo


def mm(a, b):
    return lax.dot_general(a, b, (((1,), (0,)), ((), ())), preferred_element_type=f32)


def mt(a, b):
    return lax.dot_general(a, b, (((1,), (1,)), ((), ())), preferred_element_type=f32)


def product(dot, a, b):
    return dot(a[0], b[0]) + (dot(a[0], b[1]) + dot(a[1], b[0]))


def total(x):
    return jnp.sum(jnp.sum(x, axis=0, keepdims=True), axis=1, keepdims=True)


class Sizes:
    def __init__(self, mesh_shape, rhs, skel_perm):
        self.nx, self.ny, self.nz = (mesh_shape[a] for a in ("gx", "gy", "gz"))
        self.devices = self.nx * self.ny * self.nz
        self.blobs, self.bodies = rhs.shape[-2:]
        self.step = round_up(self.blobs, 8)
        self.rows = round_up(3 * self.step, 16)
        self.half = self.rows // 2
        self.message = self.half + 8
        self.direct = (self.nx, self.ny) == (4, 2)
        self.levels = skel_perm.shape[0]
        self.skel = skel_perm.shape[1] // 2
        shifts = sorted({(dy % self.ny) for dy in (-1, 1)} - {0})
        self.shifts = shifts
        self.sources = [("same", dy) for dy in shifts]
        for kind in ("other", "partner"):
            self.sources += [(kind, dy) for dy in [0] + shifts]
        self.ghosts = round_up(len(self.sources) * RIM, LANES)
        self.far_tiles = self.nz + -(-self.nz // 2)

    def slot_start(self, slot, parity):
        dx, dy = slot // 3 - 1, (slot % 3 - 1) % self.ny
        kind = "same" if dx == 0 else "partner" if dx == 1 - 2 * parity else "other"
        if (kind, dy) == ("same", 0):
            return 0
        return self.bodies + RIM * self.sources.index((kind, dy))

    def beside(self, kind, x):
        if kind == "same":
            return x
        if kind == "partner":
            return x ^ 1
        return (x + 2 * (x % 2) - 1) % self.nx


def pieces(x, s):
    return [x[c * s.step : c * s.step + s.step] for c in range(3)]


def turn(parts, rot, inverse):
    out = []
    for target in range(3):
        acc = None
        for source in range(3):
            row = 3 * source + target if inverse else 3 * target + source
            term = rot[row : row + 1] * parts[source]
            acc = term if acc is None else acc + term
        out.append(acc)
    return out


def stacked(parts, s):
    rest = s.rows - 3 * s.step
    if rest:
        parts = list(parts) + [jnp.zeros((rest, s.bodies), f32)]
    return jnp.concatenate(parts, axis=0)


def occupancy(cells, s):
    row = lax.broadcasted_iota(jnp.int32, (s.skel, s.bodies), 0)
    return jnp.where(cells == row, 1.0, 0.0).astype(bf16)


def pack_charges(parts, weight_col, occ, s):
    moments = [jnp.sum(part * weight_col, axis=0, keepdims=True) for part in parts]
    moments = jnp.concatenate(moments + [jnp.zeros((5, s.bodies), f32)], axis=0)
    high, rest = split(moments)
    mid, low = split(moments - high.astype(f32))
    stack = jnp.concatenate([high.astype(f32), mid.astype(f32), low.astype(f32)], axis=0).astype(bf16)
    sums = mt(stack, occ)
    charges = sums[0:8] + (sums[8:16] + sums[16:24])
    tail = jnp.concatenate([charges[:, LANES:], jnp.zeros((8, 2 * LANES - s.skel), f32)], axis=1)
    row = lax.broadcasted_iota(jnp.int32, (8, LANES), 0)
    return jnp.where(row < 4, charges[:, :LANES], pltpu.roll(tail, 4, 0))


def pack_rim(x, s):
    lane = lax.broadcasted_iota(jnp.int32, (s.half, LANES), 1)
    top, bottom = x[: s.half, :LANES], x[s.half :, :LANES]
    return jnp.where(lane < RIM, top, pltpu.roll(bottom, RIM, 1))


def unpack_rims(rims, s):
    lane = lax.broadcasted_iota(jnp.int32, (s.half, LANES), 1)
    tops, bottoms = [], []
    for i in range(0, s.ghosts // RIM, 2):
        a = rims[i]
        b = rims[i + 1] if i + 1 < len(rims) else jnp.zeros_like(a)
        tops.append(jnp.where(lane < RIM, a, pltpu.roll(b, RIM, 1)))
        bottoms.append(jnp.where(lane < RIM, pltpu.roll(a, RIM, 1), b))
    return jnp.concatenate(
        [jnp.concatenate(tops, axis=1), jnp.concatenate(bottoms, axis=1)], axis=0
    )


def pack_message(x, weight_col, cells, s):
    charges = pack_charges(pieces(x, s), weight_col, occupancy(cells, s), s)
    return jnp.concatenate([pack_rim(x, s), charges], axis=0)


def begin(sources, targets, sems):
    moves = [pltpu.make_async_copy(a, b, sems.at[i]) for i, (a, b) in enumerate(zip(sources, targets))]
    for move in moves:
        move.start()
    return moves


def start_kernel(s, rhs, cells, weight, message_out, col_out, cells_out, f_out, raw, wide, sems):
    moves = begin((weight, cells, rhs), (wide, cells_out, raw), sems)
    f_out[...] = jnp.zeros_like(f_out)
    moves[0].wait()
    row = jnp.concatenate([wide[...], jnp.zeros((1, 2 * LANES - s.blobs), f32)], axis=1)
    col = jnp.broadcast_to(row, (LANES, 2 * LANES)).T[: s.step]
    col_out[...] = col
    for move in moves[1:]:
        move.wait()
    for c in range(3):
        f_out[c * s.step : c * s.step + s.blobs, :] = raw[c * s.blobs : (c + 1) * s.blobs, 0, :]
    message_out[...] = pack_message(f_out[...], col[:, :1], cells_out[0], s)


def frame_rows(angles):
    cos, sin = jnp.cos(angles), jnp.sin(angles)
    cy, cp, cr = cos[0:1], cos[1:2], cos[2:3]
    sy, sp, sr = sin[0:1], sin[1:2], sin[2:3]
    return [
        cy * cp,
        cy * sp * sr - sy * cr,
        cy * sp * cr + sy * sr,
        sy * cp,
        sy * sp * sr + cy * cr,
        sy * sp * cr - cy * sr,
        -sp,
        cp * sr,
        cp * cr,
    ]


def local_part(f, s, rot, mob, own):
    parts = pieces(f, s)
    turned = stacked(turn(parts, rot, False), s)
    mixed = product(mm, mob, split(turned))
    back = turn(pieces(mixed, s), rot, True)
    return f + stacked(back, s), product(mm, split(f), own)


def product_many(dot, blocks, b):
    rows = blocks[0].shape[0]
    out = product(dot, split(jnp.concatenate(blocks, axis=0)), split(b))
    return [out[i * rows : (i + 1) * rows] for i in range(len(blocks))]


def expand_once(groups, halves):
    flat = [block for group in groups for block in group]
    sides = [product_many(mt, flat, half) for half in halves]
    out, at = [], 0
    for group in groups:
        spread = []
        for i in range(at, at + len(group)):
            spread += [sides[0][i], sides[1][i]]
        at += len(group)
        out.append(spread)
    return out


def setup_kernel(
    s, ids, f_in, *refs
):
    count = 9
    sources, refs = refs[:count], refs[count:]
    copies, refs = refs[-1 - count :], refs[: -1 - count]
    copies, sems = copies[:-1], copies[-1]
    setup(s, ids, f_in, begin(sources, copies, sems), *copies, *refs)


def setup(
    s, ids, f_in, moves, angles, near_weight, neighbours, self_mob, near_mat, perm, interp, sibling, root,
    loc_out, gat_out, rot_out, sh_out, sl_out, nh_out, nl_out, oh_out, ol_out, gh_out, gl_out,
    far_out, padded, ups_ref,
):
    f = f_in[...]
    for move in moves[:3]:
        move.wait()
    rot = jnp.concatenate(frame_rows(angles[:, 0, :]) + [jnp.zeros((7, s.bodies), f32)], axis=0)
    rot_out[...] = rot

    links = neighbours[0, 0]
    slot = links // s.bodies
    base = jnp.zeros_like(links)
    odd = (ids[0] // s.ny) % 2
    for index in range(9):
        start = jnp.where(odd == 1, s.slot_start(index, 1), s.slot_start(index, 0))
        base = jnp.where(slot == index, start, base)
    column = base + links % s.bodies
    coef = near_weight[0, 0]
    for first, count, hi_out, lo_out in (
        (0, s.bodies, oh_out, ol_out),
        (s.bodies, s.ghosts, gh_out, gl_out),
    ):
        for r in range(0, count, 64):
            row = lax.broadcasted_iota(jnp.int32, (64, s.bodies), 0) + (first + r)
            acc = jnp.zeros((64, s.bodies), f32)
            for k in range(coef.shape[0]):
                acc = acc + jnp.where(column[k : k + 1] == row, coef[k : k + 1], 0.0)
            hi, lo = split(acc)
            hi_out[r : r + 64, :] = hi
            lo_out[r : r + 64, :] = lo

    for move in moves[3:]:
        move.wait()
    padded[...] = jnp.zeros_like(padded)
    for matrix, hi_out, lo_out in ((self_mob, sh_out, sl_out), (near_mat, nh_out, nl_out)):
        for c in range(3):
            for d in range(3):
                padded[c * s.step : c * s.step + s.blobs, d * s.step : d * s.step + s.blobs] = matrix[
                    c * s.blobs : (c + 1) * s.blobs, d * s.blobs : (d + 1) * s.blobs
                ]
        hi, lo = split(padded[...])
        hi_out[...] = hi
        lo_out[...] = lo

    loc, gat = local_part(f, s, rot, (sh_out[...], sl_out[...]), (oh_out[...], ol_out[...]))
    loc_out[...] = loc
    gat_out[...] = gat

    n = s.skel
    z = ids[1]
    halves = []
    spot = lax.broadcasted_iota(jnp.int32, (2 * n, n), 0)
    for level in range(s.levels):
        kept = jnp.where(perm[level : level + 1, :n] == spot, 1.0, 0.0)
        moved = jnp.where(perm[level : level + 1, n:] == spot, 1.0, 0.0).astype(bf16)
        hi, lo = split(interp[level])
        ups_ref[level] = kept + (mm(moved, hi) + mm(moved, lo))
        bit = (z >> level) & 1
        halves.append(
            [ups_ref[level, pl.ds(pl.multiple_of(side * n, 8), n), :] for side in (bit, 1 - bit)]
        )

    def down(block, level, dot):
        return product(dot, split(halves[level][0]), split(block))

    spread = root[...]
    beside = []
    for level in reversed(range(s.levels)):
        spread = down(spread, level, mt if level == s.levels - 1 else mm)
        beside = [(down(block, level, mt if fresh else mm), False) for block, fresh in beside]
        beside.append((sibling[level], True))
    beside = [block.T if fresh else block for block, fresh in reversed(beside)]
    leaves = [[spread]]
    for level in reversed(range(s.levels)):
        leaves = expand_once(leaves, halves[level])
        leaves.append([beside[level]])
    far_leaves, *sub = leaves
    near_leaves = [jnp.zeros((n, n), f32)]
    for blocks in reversed(sub):
        near_leaves += blocks
    tail = n - LANES
    far_out[...] = jnp.zeros_like(far_out)
    own = [a - b for a, b in zip(near_leaves, far_leaves)]
    for group, blocks in enumerate((own, far_leaves)):
        for leaf, block in enumerate(blocks):
            at = (group * s.far_tiles + leaf) * LANES
            far_out[:, at : at + LANES] = block[:, :LANES]
            at = (group * s.far_tiles + s.nz + leaf // 2) * LANES + leaf % 2 * RIM
            far_out[:, at : at + tail] = block[:, LANES:]


def half_kernel(s, *refs):
    *messages, _, out = refs
    acc = messages[0][s.half :, :]
    for message in messages[1:]:
        acc = acc + message[s.half :, :]
    out[...] = acc


def layer_kernel(s, message, *refs):
    *sums, _, out = refs
    acc = sums[0][...]
    for part in sums[1:]:
        acc = acc + part[...]
    out[0] = message[s.half :, :]
    out[1] = acc


def far_potential(s, charges, far_op):
    rows = []
    for group in range(2):
        tiles = [layer[group] for layer in charges]
        rows += tiles
        for leaf in range(0, s.nz, 2):
            pair = tiles[leaf]
            if leaf + 1 < s.nz:
                lane = lax.broadcasted_iota(jnp.int32, (8, LANES), 1)
                pair = jnp.where(lane < RIM, pair, pltpu.roll(tiles[leaf + 1], RIM, 1))
            rows.append(pltpu.roll(pair, 4, 0))
    columns = [[], [], []]
    for r in range(0, s.skel, 64):
        acc = [None] * 3
        for index, row in enumerate(rows):
            block = far_op[r : r + 64, index * LANES : (index + 1) * LANES]
            for c in range(3):
                term = block * row[c : c + 1]
                acc[c] = term if acc[c] is None else acc[c] + term
        for c in range(3):
            columns[c].append(jnp.sum(acc[c], axis=1, keepdims=True))
    return columns


def far_values(s, charges, far_op, cells):
    columns = far_potential(s, charges, far_op)
    out = []
    for c in range(3):
        acc = jnp.zeros((1, s.bodies), f32)
        for index, r in enumerate(range(0, s.skel, 64)):
            row = lax.broadcasted_iota(jnp.int32, (64, s.bodies), 0) + r
            acc = acc + jnp.sum(jnp.where(cells == row, columns[c][index], 0.0), axis=0, keepdims=True)
        out.append(acc)
    return out


def gather_kernel(s, gat, gh, gl, *refs):
    *messages, _, hi_out, lo_out = refs
    rims = [message[: s.half, :] for message in messages]
    gathered = gat[...] + product(mm, split(unpack_rims(rims, s)), (gh[...], gl[...]))
    hi_out[...], lo_out[...] = split(gathered)


def near_kernel(s, loc, nh, nl, hi, lo, out):
    out[...] = loc[...] + product(mm, (nh[...], nl[...]), (hi[...], lo[...]))


def with_far(s, part, layers, far_op, cells, col):
    values = far_values(s, layers, far_op, cells[0])
    return part[...] + stacked([col * value for value in values], s)


def first_kernel(s, part, far_op, cells, col, *refs):
    *layers, u_out, message_out = refs
    weight_col = col[:, :1]
    u = with_far(s, part, layers, far_op, cells, weight_col)
    u_out[...] = u
    message_out[...] = pack_message(u, weight_col, cells[0], s)


def safe_inverse(x):
    return jnp.where(x > 0.0, 1.0 / jnp.where(x > 0.0, x, 1.0), 0.0)


def middle_kernel(s, u_in, f_in, rot, sh, sl, oh, ol, loc_out, gat_out, ortho_out, stat_out):
    u, f = u_in[...], f_in[...]
    loc, gat = local_part(u, s, rot[...], (sh[...], sl[...]), (oh[...], ol[...]))
    loc_out[...] = loc
    gat_out[...] = gat
    ff = total(f * f)
    fu = total(f * u) * safe_inverse(ff)
    ortho = u - fu * f
    ortho_out[...] = ortho
    oo = total(ortho * ortho)
    stat_out[...] = jnp.broadcast_to(
        jnp.concatenate([ff, fu, oo, jnp.zeros((5, 1), f32)], axis=0), (8, LANES)
    )


def second_kernel(s, part, far_op, cells, col, f_in, ortho_in, stat, *refs):
    *layers, stat_out = refs
    t = with_far(s, part, layers, far_op, cells, col[:, :1])
    f, ortho = f_in[...], ortho_in[...]
    ff, fu, oo = (stat[i : i + 1, :1] for i in range(3))
    ft = total(f * t) * safe_inverse(ff)
    ot = total(ortho * t) * safe_inverse(oo)
    rest_t = t - ft * f - ot * ortho
    tt = total(rest_t * rest_t)
    rf, ro = jnp.sqrt(ff), jnp.sqrt(oo)
    lane = lax.broadcasted_iota(jnp.int32, (1, LANES), 1)
    stats = jnp.zeros((1, LANES), f32)
    for index, value in enumerate((rf, rf * fu, ro, rf * ft, ro * ot, jnp.sqrt(tt))):
        stats = jnp.where(lane == index, value, stats)
    stat_out[:, 0, :] = jnp.broadcast_to(stats, (s.devices, LANES))


def finish_kernel(s, f_in, u_in, stats, x_out, lsq_out, raw, sem):
    rows = stats[:, 0, :]
    rest = round_up(s.devices, LANES) - s.devices
    if rest:
        rows = jnp.concatenate([rows, jnp.zeros((rest, LANES), f32)], axis=0)
    rows = rows.T
    f1, u1, u2, t1, t2, t3 = (rows[i : i + 1] for i in range(6))

    def along(x):
        return jnp.sum(x, axis=1, keepdims=True)

    beta = jnp.sqrt(along(f1 * f1) + epsilon)
    v = f1 / beta
    w1, w2 = u1 / beta, u2 / beta
    h11 = along(w1 * v)
    r1 = w1 - h11 * v
    h21 = jnp.sqrt(along(r1 * r1 + w2 * w2) + epsilon)
    b1, b2 = r1 / h21, w2 / h21
    z1, z2, z3 = ((t1 / beta - h11 * w1) / h21, (t2 / beta - h11 * w2) / h21, t3 / beta / h21)
    h12 = along(z1 * v)
    h22 = along(z1 * b1 + z2 * b2)
    d1, d2 = z1 - h12 * v - h22 * b1, z2 - h22 * b2
    h32 = jnp.sqrt(along(d1 * d1 + d2 * d2 + z3 * z3) + epsilon)
    first_norm = jnp.sqrt(h11 * h11 + h21 * h21)
    c1, s1 = h11 / first_norm, h21 / first_norm
    t12, t22 = c1 * h12 + s1 * h22, c1 * h22 - s1 * h12
    second_norm = jnp.sqrt(t22 * t22 + h32 * h32)
    c2, s2 = t22 / second_norm, h32 / second_norm
    g2 = -s1 * beta
    y2 = c2 * g2 / second_norm
    y1 = (c1 * beta - t12 * y2) / first_norm
    lsq_out[...] = jnp.abs(s2 * g2)
    on_u = y2 / h21 / beta
    on_f = y1 / beta - on_u * h11
    for c in range(3):
        part = slice(c * s.step, c * s.step + s.blobs)
        raw[c * s.blobs : (c + 1) * s.blobs, 0, :] = on_f * f_in[part, :] + on_u * u_in[part, :]
    move = pltpu.make_async_copy(raw, x_out, sem)
    move.start()
    move.wait()


def call(kernel, outs, args, scalars=0, far_args=0, far_outs=0, scratch=(), flops=0):
    vmem = pl.BlockSpec(memory_space=pltpu.VMEM)
    smem = pl.BlockSpec(memory_space=pltpu.SMEM)
    hbm = pl.BlockSpec(memory_space=pltpu.HBM)
    near_args = len(args) - far_args
    args = args[:near_args] + [pltpu.with_memory_space_constraint(x, pltpu.HBM) for x in args[near_args:]]
    return pl.pallas_call(
        kernel,
        out_shape=[jax.ShapeDtypeStruct(shape, kind) for shape, kind in outs],
        in_specs=[smem] * scalars + [vmem] * (near_args - scalars) + [hbm] * far_args,
        out_specs=[hbm] * far_outs + [vmem] * (len(outs) - far_outs),
        scratch_shapes=list(scratch),
        compiler_params=pltpu.CompilerParams(vmem_limit_bytes=16 * 2**20),
        cost_estimate=pl.CostEstimate(flops=flops, bytes_accessed=2**20, transcendentals=0),
    )(*args)


def body(
    mesh_shape, rhs, angles, self_mob, near_mat, near_weight, neighbours, cells, blob_weight,
    skel_perm, interp, sibling_ops, root_op,
):
    s = Sizes(mesh_shape, rhs, skel_perm)
    full = (s.rows, s.bodies)
    square = (s.rows, s.rows)
    tile = (8, LANES)
    far_shape = (s.skel, 2 * s.far_tiles * LANES)
    column = lax.axis_index("gx") * s.ny + lax.axis_index("gy")
    ids = jnp.stack([column, lax.axis_index("gz")]).astype(jnp.int32)

    def fetch(x, kind, dy):
        pairs = []
        for gx in range(s.nx):
            for gy in range(s.ny):
                pairs.append((s.beside(kind, gx) * s.ny + (gy + dy) % s.ny, gx * s.ny + gy))
        return lax.ppermute(x, ("gx", "gy"), pairs)

    def fetch_layers(x):
        return [x] + [
            lax.ppermute(x, "gz", [(z ^ k, z) for z in range(s.nz)]) for k in range(1, s.nz)
        ]

    def fetch_messages(message):
        got = {}
        for dy in s.shifts:
            got["same", dy] = fetch(message, "same", dy)
        for dy in s.shifts:
            got["other", dy] = fetch(message, "other", dy)
        got["other", 0] = fetch(message, "other", 0)
        got["partner", 0] = fetch(message, "partner", 0)
        return got

    def forward_messages(got, after):
        for dy in s.shifts:
            ready, _ = lax.optimization_barrier((got["same", dy], after))
            got["partner", dy] = fetch(ready, "partner", 0)

    def share(message, got, gat, after):
        forward_messages(got, after)
        if s.direct:
            quarter = [message] + [got[key] for key in s.sources if key[0] != "partner"]
            (half,) = call(functools.partial(half_kernel, s), [(tile, f32)], quarter + [after])
            sums = [half, fetch(half, "partner", 0)]
        else:
            half = lax.psum(message[s.half :], ("gx", "gy"))
            sums = [half]
        gathered = call(
            functools.partial(gather_kernel, s),
            [(full, bf16), (full, bf16)],
            [gat, gh, gl] + [got[key] for key in s.sources] + [half],
            flops=10**9,
        )
        (pair,) = call(
            functools.partial(layer_kernel, s), [((2,) + tile, f32)], [message] + sums + [gathered[1]]
        )
        return gathered, fetch_layers(pair)

    def near_part(loc, gathered):
        return call(
            functools.partial(near_kernel, s), [(full, f32)], [loc, nh, nl, *gathered], flops=10**9
        )[0]

    flat = (3 * s.blobs, 1, s.bodies)
    small = (1, s.blobs)
    message, col, cells, f = call(
        functools.partial(start_kernel, s),
        [((s.message, LANES), f32), ((s.step, LANES), f32), (cells.shape, jnp.int32), (full, f32)],
        [rhs.reshape(flat), cells, blob_weight.reshape(small)],
        far_args=3,
        scratch=[pltpu.VMEM(flat, f32), pltpu.VMEM(small, f32), pltpu.SemaphoreType.DMA((3,))],
        flops=10**7,
    )
    got = fetch_messages(message)
    operators = [
        angles.reshape(3, 1, s.bodies), near_weight, neighbours, self_mob, near_mat, skel_perm, interp,
        sibling_ops, root_op,
    ]
    loc, gat, rot, sh, sl, nh, nl, oh, ol, gh, gl, far_op = call(
        functools.partial(setup_kernel, s),
        [(full, f32), (full, f32), ((16, s.bodies), f32)]
        + [(square, bf16)] * 4
        + [((s.bodies, s.bodies), bf16)] * 2
        + [((s.ghosts, s.bodies), bf16)] * 2
        + [(far_shape, f32)],
        [ids, f] + operators,
        scalars=1,
        far_args=len(operators),
        scratch=[pltpu.VMEM(square, f32), pltpu.VMEM((s.levels, 2 * s.skel, s.skel), f32)]
        + [pltpu.VMEM(x.shape, x.dtype) for x in operators]
        + [pltpu.SemaphoreType.DMA((len(operators),))],
        flops=5 * 10**9,
    )
    gathered, layers = share(message, got, gat, rot)
    part = near_part(loc, gathered)
    u, message = call(
        functools.partial(first_kernel, s),
        [(full, f32), ((s.message, LANES), f32)],
        [part, far_op, cells, col, *layers],
        flops=10**8,
    )
    got = fetch_messages(message)
    loc, gat, ortho, stat = call(
        functools.partial(middle_kernel, s),
        [(full, f32), (full, f32), (full, f32), (tile, f32)],
        [u, f, rot, sh, sl, oh, ol],
        flops=10**9,
    )
    gathered, layers = share(message, got, gat, stat)
    part = near_part(loc, gathered)
    (stats,) = call(
        functools.partial(second_kernel, s),
        [((s.devices, 1, LANES), f32)],
        [part, far_op, cells, col, f, ortho, stat, *layers],
        flops=10**8,
    )
    stats = lax.all_to_all(stats, ("gx", "gy", "gz"), 0, 0)
    result, lsq = call(
        functools.partial(finish_kernel, s),
        [(flat, f32), ((1, 1), f32)],
        [f, u, stats],
        far_outs=1,
        scratch=[pltpu.VMEM(flat, f32), pltpu.SemaphoreType.DMA],
        flops=10**7,
    )
    return result.reshape(rhs.shape), lsq.reshape(())


def solution(mesh):
    in_specs = (
        P("gx", "gy", None, None, "gz"),
        P("gx", "gy", None, "gz"),
        P(),
        P(),
        P("gx", "gy", None, "gz"),
        P("gx", "gy", None, "gz"),
        P("gx", "gy", "gz"),
        P(),
        P(),
        P(),
        P(),
        P(),
    )
    out_specs = (P("gx", "gy", None, None, "gz"), P())
    inner = functools.partial(body, dict(mesh.shape))
    return jax.shard_map(inner, mesh=mesh, in_specs=in_specs, out_specs=out_specs, check_vma=False)
```

```python
import functools

import jax
import jax.numpy as jnp
from jax import lax
from jax.experimental import pallas as pl
from jax.experimental.pallas import tpu as pltpu
from jax.sharding import PartitionSpec as P

epsilon = 1e-06
f32 = jnp.float32
bf16 = jnp.bfloat16
RIM = 64
LANES = 128


def round_up(value, unit):
    return -(-value // unit) * unit


def split(x):
    hi = x.astype(bf16)
    lo = (x - hi.astype(f32)).astype(bf16)
    return hi, lo


def mm(a, b):
    return lax.dot_general(a, b, (((1,), (0,)), ((), ())), preferred_element_type=f32)


def mt(a, b):
    return lax.dot_general(a, b, (((1,), (1,)), ((), ())), preferred_element_type=f32)


def product(dot, a, b):
    return dot(a[0], b[0]) + (dot(a[0], b[1]) + dot(a[1], b[0]))


def total(x):
    return jnp.sum(jnp.sum(x, axis=0, keepdims=True), axis=1, keepdims=True)


class Sizes:
    def __init__(self, mesh_shape, rhs, skel_perm):
        self.nx, self.ny, self.nz = (mesh_shape[a] for a in ("gx", "gy", "gz"))
        self.devices = self.nx * self.ny * self.nz
        self.blobs, self.bodies = rhs.shape[-2:]
        self.step = round_up(self.blobs, 8)
        self.rows = round_up(3 * self.step, 16)
        self.half = self.rows // 2
        self.message = self.half + 8
        self.direct = (self.nx, self.ny) == (4, 2)
        self.levels = skel_perm.shape[0]
        self.skel = skel_perm.shape[1] // 2
        shifts = sorted({(dy % self.ny) for dy in (-1, 1)} - {0})
        self.shifts = shifts
        self.sources = [("same", dy) for dy in shifts]
        for kind in ("other", "partner"):
            self.sources += [(kind, dy) for dy in [0] + shifts]
        self.ghosts = round_up(len(self.sources) * RIM, LANES)
        self.far_tiles = self.nz + -(-self.nz // 2)

    def slot_start(self, slot, parity):
        dx, dy = slot // 3 - 1, (slot % 3 - 1) % self.ny
        kind = "same" if dx == 0 else "partner" if dx == 1 - 2 * parity else "other"
        if (kind, dy) == ("same", 0):
            return 0
        return self.bodies + RIM * self.sources.index((kind, dy))

    def beside(self, kind, x):
        if kind == "same":
            return x
        if kind == "partner":
            return x ^ 1
        return (x + 2 * (x % 2) - 1) % self.nx


def pieces(x, s):
    return [x[c * s.step : c * s.step + s.step] for c in range(3)]


def turn(parts, rot, inverse):
    out = []
    for target in range(3):
        acc = None
        for source in range(3):
            row = 3 * source + target if inverse else 3 * target + source
            term = rot[row : row + 1] * parts[source]
            acc = term if acc is None else acc + term
        out.append(acc)
    return out


def stacked(parts, s):
    rest = s.rows - 3 * s.step
    if rest:
        parts = list(parts) + [jnp.zeros((rest, s.bodies), f32)]
    return jnp.concatenate(parts, axis=0)


def occupancy(cells, s):
    row = lax.broadcasted_iota(jnp.int32, (s.skel, s.bodies), 0)
    return jnp.where(cells == row, 1.0, 0.0).astype(bf16)


def pack_charges(parts, weight_col, occ, s):
    moments = [jnp.sum(part * weight_col, axis=0, keepdims=True) for part in parts]
    moments = jnp.concatenate(moments + [jnp.zeros((5, s.bodies), f32)], axis=0)
    high, rest = split(moments)
    mid, low = split(moments - high.astype(f32))
    stack = jnp.concatenate([high.astype(f32), mid.astype(f32), low.astype(f32)], axis=0).astype(bf16)
    sums = mt(stack, occ)
    charges = sums[0:8] + (sums[8:16] + sums[16:24])
    tail = jnp.concatenate([charges[:, LANES:], jnp.zeros((8, 2 * LANES - s.skel), f32)], axis=1)
    row = lax.broadcasted_iota(jnp.int32, (8, LANES), 0)
    return jnp.where(row < 4, charges[:, :LANES], pltpu.roll(tail, 4, 0))


def pack_rim(x, s):
    lane = lax.broadcasted_iota(jnp.int32, (s.half, LANES), 1)
    top, bottom = x[: s.half, :LANES], x[s.half :, :LANES]
    return jnp.where(lane < RIM, top, pltpu.roll(bottom, RIM, 1))


def unpack_rims(rims, s):
    lane = lax.broadcasted_iota(jnp.int32, (s.half, LANES), 1)
    tops, bottoms = [], []
    for i in range(0, s.ghosts // RIM, 2):
        a = rims[i]
        b = rims[i + 1] if i + 1 < len(rims) else jnp.zeros_like(a)
        tops.append(jnp.where(lane < RIM, a, pltpu.roll(b, RIM, 1)))
        bottoms.append(jnp.where(lane < RIM, pltpu.roll(a, RIM, 1), b))
    return jnp.concatenate(
        [jnp.concatenate(tops, axis=1), jnp.concatenate(bottoms, axis=1)], axis=0
    )


def pack_message(x, weight_col, cells, s):
    charges = pack_charges(pieces(x, s), weight_col, occupancy(cells, s), s)
    return jnp.concatenate([pack_rim(x, s), charges], axis=0)


def begin(sources, targets, sems):
    moves = [pltpu.make_async_copy(a, b, sems.at[i]) for i, (a, b) in enumerate(zip(sources, targets))]
    for move in moves:
        move.start()
    return moves


def start_kernel(s, rhs, cells, weight, message_out, col_out, cells_out, f_out, raw, wide, sems):
    moves = begin((weight, cells, rhs), (wide, cells_out, raw), sems)
    f_out[...] = jnp.zeros_like(f_out)
    moves[0].wait()
    row = jnp.concatenate([wide[...], jnp.zeros((1, 2 * LANES - s.blobs), f32)], axis=1)
    col = jnp.broadcast_to(row, (LANES, 2 * LANES)).T[: s.step]
    col_out[...] = col
    for move in moves[1:]:
        move.wait()
    for c in range(3):
        f_out[c * s.step : c * s.step + s.blobs, :] = raw[c * s.blobs : (c + 1) * s.blobs, 0, :]
    message_out[...] = pack_message(f_out[...], col[:, :1], cells_out[0], s)


def frame_rows(angles):
    cos, sin = jnp.cos(angles), jnp.sin(angles)
    cy, cp, cr = cos[0:1], cos[1:2], cos[2:3]
    sy, sp, sr = sin[0:1], sin[1:2], sin[2:3]
    return [
        cy * cp,
        cy * sp * sr - sy * cr,
        cy * sp * cr + sy * sr,
        sy * cp,
        sy * sp * sr + cy * cr,
        sy * sp * cr - cy * sr,
        -sp,
        cp * sr,
        cp * cr,
    ]


def local_part(f, s, rot, mob, own):
    parts = pieces(f, s)
    turned = stacked(turn(parts, rot, False), s)
    mixed = product(mm, mob, split(turned))
    back = turn(pieces(mixed, s), rot, True)
    return f + stacked(back, s), product(mm, split(f), own)


def product_many(dot, blocks, b):
    rows = blocks[0].shape[0]
    out = product(dot, split(jnp.concatenate(blocks, axis=0)), split(b))
    return [out[i * rows : (i + 1) * rows] for i in range(len(blocks))]


def expand_once(groups, halves):
    flat = [block for group in groups for block in group]
    sides = [product_many(mt, flat, half) for half in halves]
    out, at = [], 0
    for group in groups:
        spread = []
        for i in range(at, at + len(group)):
            spread += [sides[0][i], sides[1][i]]
        at += len(group)
        out.append(spread)
    return out


def setup_kernel(s, ids, f_in, *refs):
    sources, tree, outs, (padded, *copies, sems) = refs[:9], refs[9:13], refs[13:24], refs[24:]
    moves = begin(sources, (*copies, *tree), sems)
    setup(s, ids, f_in, moves[:5], *copies, *outs, padded)
    for move in moves[5:]:
        move.wait()


def setup(
    s, ids, f_in, moves, angles, near_weight, neighbours, self_mob, near_mat,
    loc_out, gat_out, rot_out, sh_out, sl_out, nh_out, nl_out, oh_out, ol_out, gh_out, gl_out, padded,
):
    f = f_in[...]
    for move in moves[:3]:
        move.wait()
    rot = jnp.concatenate(frame_rows(angles[:, 0, :]) + [jnp.zeros((7, s.bodies), f32)], axis=0)
    rot_out[...] = rot

    links = neighbours[0, 0]
    slot = links // s.bodies
    base = jnp.zeros_like(links)
    odd = (ids[0] // s.ny) % 2
    for index in range(9):
        start = jnp.where(odd == 1, s.slot_start(index, 1), s.slot_start(index, 0))
        base = jnp.where(slot == index, start, base)
    column = base + links % s.bodies
    coef = near_weight[0, 0]
    for first, count, hi_out, lo_out in (
        (0, s.bodies, oh_out, ol_out),
        (s.bodies, s.ghosts, gh_out, gl_out),
    ):
        for r in range(0, count, 64):
            row = lax.broadcasted_iota(jnp.int32, (64, s.bodies), 0) + (first + r)
            acc = jnp.zeros((64, s.bodies), f32)
            for k in range(coef.shape[0]):
                acc = acc + jnp.where(column[k : k + 1] == row, coef[k : k + 1], 0.0)
            hi, lo = split(acc)
            hi_out[r : r + 64, :] = hi
            lo_out[r : r + 64, :] = lo

    for move in moves[3:]:
        move.wait()
    padded[...] = jnp.zeros_like(padded)
    for matrix, hi_out, lo_out in ((self_mob, sh_out, sl_out), (near_mat, nh_out, nl_out)):
        for c in range(3):
            for d in range(3):
                padded[c * s.step : c * s.step + s.blobs, d * s.step : d * s.step + s.blobs] = matrix[
                    c * s.blobs : (c + 1) * s.blobs, d * s.blobs : (d + 1) * s.blobs
                ]
        hi, lo = split(padded[...])
        hi_out[...] = hi
        lo_out[...] = lo

    loc, gat = local_part(f, s, rot, (sh_out[...], sl_out[...]), (oh_out[...], ol_out[...]))
    loc_out[...] = loc
    gat_out[...] = gat


def far_kernel(s, ids, perm, interp, sibling, root, _, far_out, ups_ref):
    n = s.skel
    z = ids[1]
    halves = []
    spot = lax.broadcasted_iota(jnp.int32, (2 * n, n), 0)
    for level in range(s.levels):
        kept = jnp.where(perm[level : level + 1, :n] == spot, 1.0, 0.0)
        moved = jnp.where(perm[level : level + 1, n:] == spot, 1.0, 0.0).astype(bf16)
        hi, lo = split(interp[level])
        ups_ref[level] = kept + (mm(moved, hi) + mm(moved, lo))
        bit = (z >> level) & 1
        halves.append(
            [ups_ref[level, pl.ds(pl.multiple_of(side * n, 8), n), :] for side in (bit, 1 - bit)]
        )

    def down(block, level, dot):
        return product(dot, split(halves[level][0]), split(block))

    spread = root[...]
    beside = []
    for level in reversed(range(s.levels)):
        spread = down(spread, level, mt if level == s.levels - 1 else mm)
        beside = [(down(block, level, mt if fresh else mm), False) for block, fresh in beside]
        beside.append((sibling[level], True))
    beside = [block.T if fresh else block for block, fresh in reversed(beside)]
    leaves = [[spread]]
    for level in reversed(range(s.levels)):
        leaves = expand_once(leaves, halves[level])
        leaves.append([beside[level]])
    far_leaves, *sub = leaves
    near_leaves = [jnp.zeros((n, n), f32)]
    for blocks in reversed(sub):
        near_leaves += blocks
    tail = n - LANES
    far_out[...] = jnp.zeros_like(far_out)
    own = [a - b for a, b in zip(near_leaves, far_leaves)]
    for group, blocks in enumerate((own, far_leaves)):
        for leaf, block in enumerate(blocks):
            at = (group * s.far_tiles + leaf) * LANES
            far_out[:, at : at + LANES] = block[:, :LANES]
            at = (group * s.far_tiles + s.nz + leaf // 2) * LANES + leaf % 2 * RIM
            far_out[:, at : at + tail] = block[:, LANES:]


def half_kernel(s, *refs):
    *messages, _, out = refs
    acc = messages[0][-8:, :]
    for message in messages[1:]:
        acc = acc + message[-8:, :]
    out[...] = acc


def layer_kernel(s, message, *refs):
    *sums, _, out = refs
    acc = sums[0][...]
    for part in sums[1:]:
        acc = acc + part[...]
    out[0] = message[-8:, :]
    out[1] = acc


def far_potential(s, charges, far_op):
    rows = []
    for group in range(2):
        tiles = [layer[group] for layer in charges]
        rows += tiles
        for leaf in range(0, s.nz, 2):
            pair = tiles[leaf]
            if leaf + 1 < s.nz:
                lane = lax.broadcasted_iota(jnp.int32, (8, LANES), 1)
                pair = jnp.where(lane < RIM, pair, pltpu.roll(tiles[leaf + 1], RIM, 1))
            rows.append(pltpu.roll(pair, 4, 0))
    columns = [[], [], []]
    for r in range(0, s.skel, 64):
        acc = [None] * 3
        for index, row in enumerate(rows):
            block = far_op[r : r + 64, index * LANES : (index + 1) * LANES]
            for c in range(3):
                term = block * row[c : c + 1]
                acc[c] = term if acc[c] is None else acc[c] + term
        for c in range(3):
            columns[c].append(jnp.sum(acc[c], axis=1, keepdims=True))
    return columns


def far_values(s, charges, far_op, cells):
    columns = far_potential(s, charges, far_op)
    out = []
    for c in range(3):
        acc = jnp.zeros((1, s.bodies), f32)
        for index, r in enumerate(range(0, s.skel, 64)):
            row = lax.broadcasted_iota(jnp.int32, (64, s.bodies), 0) + r
            acc = acc + jnp.sum(jnp.where(cells == row, columns[c][index], 0.0), axis=0, keepdims=True)
        out.append(acc)
    return out


def gather_kernel(s, gat, gh, gl, *refs):
    *messages, _, hi_out, lo_out = refs
    rims = [message[: s.half, :] for message in messages]
    gathered = gat[...] + product(mm, split(unpack_rims(rims, s)), (gh[...], gl[...]))
    hi_out[...], lo_out[...] = split(gathered)


def near_kernel(s, loc, nh, nl, hi, lo, out):
    out[...] = loc[...] + product(mm, (nh[...], nl[...]), (hi[...], lo[...]))


def with_far(s, part, layers, far_op, cells, col):
    values = far_values(s, layers, far_op, cells[0])
    return part[...] + stacked([col * value for value in values], s)


def first_kernel(s, part, far_op, cells, col, *refs):
    *layers, u_out, rim_out, charges_out = refs
    weight_col = col[:, :1]
    u = with_far(s, part, layers, far_op, cells, weight_col)
    u_out[...] = u
    rim_out[...] = pack_rim(u, s)
    charges_out[...] = pack_charges(pieces(u, s), weight_col, occupancy(cells[0], s), s)


def safe_inverse(x):
    return jnp.where(x > 0.0, 1.0 / jnp.where(x > 0.0, x, 1.0), 0.0)


def middle_kernel(s, u_in, f_in, rot, sh, sl, oh, ol, loc_out, gat_out, ortho_out, stat_out):
    u, f = u_in[...], f_in[...]
    loc, gat = local_part(u, s, rot[...], (sh[...], sl[...]), (oh[...], ol[...]))
    loc_out[...] = loc
    gat_out[...] = gat
    ff = total(f * f)
    fu = total(f * u) * safe_inverse(ff)
    ortho = u - fu * f
    ortho_out[...] = ortho
    oo = total(ortho * ortho)
    stat_out[...] = jnp.broadcast_to(
        jnp.concatenate([ff, fu, oo, jnp.zeros((5, 1), f32)], axis=0), (8, LANES)
    )


def second_kernel(s, part, far_op, cells, col, f_in, ortho_in, stat, *refs):
    *layers, stat_out = refs
    t = with_far(s, part, layers, far_op, cells, col[:, :1])
    f, ortho = f_in[...], ortho_in[...]
    ff, fu, oo = (stat[i : i + 1, :1] for i in range(3))
    ft = total(f * t) * safe_inverse(ff)
    ot = total(ortho * t) * safe_inverse(oo)
    rest_t = t - ft * f - ot * ortho
    tt = total(rest_t * rest_t)
    rf, ro = jnp.sqrt(ff), jnp.sqrt(oo)
    lane = lax.broadcasted_iota(jnp.int32, (1, LANES), 1)
    stats = jnp.zeros((1, LANES), f32)
    for index, value in enumerate((rf, rf * fu, ro, rf * ft, ro * ot, jnp.sqrt(tt))):
        stats = jnp.where(lane == index, value, stats)
    stat_out[:, 0, :] = jnp.broadcast_to(stats, (s.devices, LANES))


def finish_kernel(s, f_in, u_in, stats, x_out, lsq_out, raw, sem):
    rows = stats[:, 0, :]
    rest = round_up(s.devices, LANES) - s.devices
    if rest:
        rows = jnp.concatenate([rows, jnp.zeros((rest, LANES), f32)], axis=0)
    rows = rows.T
    f1, u1, u2, t1, t2, t3 = (rows[i : i + 1] for i in range(6))

    def along(x):
        return jnp.sum(x, axis=1, keepdims=True)

    beta = jnp.sqrt(along(f1 * f1) + epsilon)
    v = f1 / beta
    w1, w2 = u1 / beta, u2 / beta
    h11 = along(w1 * v)
    r1 = w1 - h11 * v
    h21 = jnp.sqrt(along(r1 * r1 + w2 * w2) + epsilon)
    b1, b2 = r1 / h21, w2 / h21
    z1, z2, z3 = ((t1 / beta - h11 * w1) / h21, (t2 / beta - h11 * w2) / h21, t3 / beta / h21)
    h12 = along(z1 * v)
    h22 = along(z1 * b1 + z2 * b2)
    d1, d2 = z1 - h12 * v - h22 * b1, z2 - h22 * b2
    h32 = jnp.sqrt(along(d1 * d1 + d2 * d2 + z3 * z3) + epsilon)
    first_norm = jnp.sqrt(h11 * h11 + h21 * h21)
    c1, s1 = h11 / first_norm, h21 / first_norm
    t12, t22 = c1 * h12 + s1 * h22, c1 * h22 - s1 * h12
    second_norm = jnp.sqrt(t22 * t22 + h32 * h32)
    c2, s2 = t22 / second_norm, h32 / second_norm
    g2 = -s1 * beta
    y2 = c2 * g2 / second_norm
    y1 = (c1 * beta - t12 * y2) / first_norm
    lsq_out[...] = jnp.abs(s2 * g2)
    on_u = y2 / h21 / beta
    on_f = y1 / beta - on_u * h11
    for c in range(3):
        part = slice(c * s.step, c * s.step + s.blobs)
        raw[c * s.blobs : (c + 1) * s.blobs, 0, :] = on_f * f_in[part, :] + on_u * u_in[part, :]
    move = pltpu.make_async_copy(raw, x_out, sem)
    move.start()
    move.wait()


def call(kernel, outs, args, scalars=0, far_args=0, far_outs=0, scratch=(), flops=0):
    vmem = pl.BlockSpec(memory_space=pltpu.VMEM)
    smem = pl.BlockSpec(memory_space=pltpu.SMEM)
    hbm = pl.BlockSpec(memory_space=pltpu.HBM)
    near_args = len(args) - far_args
    args = args[:near_args] + [pltpu.with_memory_space_constraint(x, pltpu.HBM) for x in args[near_args:]]
    return pl.pallas_call(
        kernel,
        out_shape=[jax.ShapeDtypeStruct(shape, kind) for shape, kind in outs],
        in_specs=[smem] * scalars + [vmem] * (near_args - scalars) + [hbm] * far_args,
        out_specs=[hbm] * far_outs + [vmem] * (len(outs) - far_outs),
        scratch_shapes=list(scratch),
        compiler_params=pltpu.CompilerParams(vmem_limit_bytes=16 * 2**20),
        cost_estimate=pl.CostEstimate(flops=flops, bytes_accessed=2**20, transcendentals=0),
    )(*args)


def body(
    mesh_shape, rhs, angles, self_mob, near_mat, near_weight, neighbours, cells, blob_weight,
    skel_perm, interp, sibling_ops, root_op,
):
    s = Sizes(mesh_shape, rhs, skel_perm)
    full = (s.rows, s.bodies)
    square = (s.rows, s.rows)
    tile = (8, LANES)
    far_shape = (s.skel, 2 * s.far_tiles * LANES)
    column = lax.axis_index("gx") * s.ny + lax.axis_index("gy")
    ids = jnp.stack([column, lax.axis_index("gz")]).astype(jnp.int32)

    def fetch(x, kind, dy):
        pairs = []
        for gx in range(s.nx):
            for gy in range(s.ny):
                pairs.append((s.beside(kind, gx) * s.ny + (gy + dy) % s.ny, gx * s.ny + gy))
        return lax.ppermute(x, ("gx", "gy"), pairs)

    def fetch_layers(x):
        return [x] + [
            lax.ppermute(x, "gz", [(z ^ k, z) for z in range(s.nz)]) for k in range(1, s.nz)
        ]

    def fetch_rims(rim):
        got = {}
        for dy in s.shifts:
            got["same", dy] = fetch(rim, "same", dy)
        for dy in s.shifts:
            got["other", dy] = fetch(rim, "other", dy)
        got["other", 0] = fetch(rim, "other", 0)
        got["partner", 0] = fetch(rim, "partner", 0)
        return got

    def forward_rims(got, after):
        for dy in s.shifts:
            ready, _ = lax.optimization_barrier((got["same", dy], after))
            got["partner", dy] = fetch(ready, "partner", 0)

    def half_sum(own, got, after):
        if not s.direct:
            return [lax.psum(own[-8:], ("gx", "gy"))]
        parts = [own] + [got[key] for key in s.sources if key[0] != "partner" and key in got]
        (half,) = call(functools.partial(half_kernel, s), [(tile, f32)], parts + [after])
        return [half, fetch(half, "partner", 0)]

    def gather(gat, got, after):
        return call(
            functools.partial(gather_kernel, s),
            [(full, bf16), (full, bf16)],
            [gat, gh, gl] + [got[key] for key in s.sources] + [after],
            flops=10**9,
        )

    def layer_pair(own, sums, after):
        return call(
            functools.partial(layer_kernel, s), [((2,) + tile, f32)], [own] + sums + [after]
        )[0]

    def near_part(loc, gathered):
        return call(
            functools.partial(near_kernel, s), [(full, f32)], [loc, nh, nl, *gathered], flops=10**9
        )[0]

    flat = (3 * s.blobs, 1, s.bodies)
    small = (1, s.blobs)
    message, col, cells, f = call(
        functools.partial(start_kernel, s),
        [((s.message, LANES), f32), ((s.step, LANES), f32), (cells.shape, jnp.int32), (full, f32)],
        [rhs.reshape(flat), cells, blob_weight.reshape(small)],
        far_args=3,
        scratch=[pltpu.VMEM(flat, f32), pltpu.VMEM(small, f32), pltpu.SemaphoreType.DMA((3,))],
        flops=10**7,
    )
    got = fetch_rims(message)
    tree = [skel_perm, interp, sibling_ops, root_op]
    operators = [angles.reshape(3, 1, s.bodies), near_weight, neighbours, self_mob, near_mat]
    *tree, loc, gat, rot, sh, sl, nh, nl, oh, ol, gh, gl = call(
        functools.partial(setup_kernel, s),
        [(x.shape, x.dtype) for x in tree]
        + [(full, f32), (full, f32), ((16, s.bodies), f32)]
        + [(square, bf16)] * 4
        + [((s.bodies, s.bodies), bf16)] * 2
        + [((s.ghosts, s.bodies), bf16)] * 2,
        [ids, f] + operators + tree,
        scalars=1,
        far_args=9,
        scratch=[pltpu.VMEM(square, f32)]
        + [pltpu.VMEM(x.shape, x.dtype) for x in operators]
        + [pltpu.SemaphoreType.DMA((9,))],
        flops=4 * 10**9,
    )
    sums = half_sum(message, got, rot)
    forward_rims(got, rot)
    gathered = gather(gat, got, sums[0])
    pair = layer_pair(message, sums, gathered[1])
    layers = fetch_layers(pair)
    part = near_part(loc, gathered)
    (far_op,) = call(
        functools.partial(far_kernel, s),
        [(far_shape, f32)],
        [ids, *tree, pair],
        scalars=1,
        scratch=[pltpu.VMEM((s.levels, 2 * s.skel, s.skel), f32)],
        flops=2 * 10**9,
    )
    u, rim, charges = call(
        functools.partial(first_kernel, s),
        [(full, f32), ((s.half, LANES), f32), (tile, f32)],
        [part, far_op, cells, col, *layers],
        flops=10**8,
    )
    got = {}
    if s.direct:
        for key in s.sources:
            if key[0] != "partner":
                got[key] = fetch(charges, *key)
    loc, gat, ortho, stat = call(
        functools.partial(middle_kernel, s),
        [(full, f32), (full, f32), (full, f32), (tile, f32)],
        [u, f, rot, sh, sl, oh, ol],
        flops=10**9,
    )
    sums = half_sum(charges, got, stat)
    rim, _ = lax.optimization_barrier((rim, sums[0]))
    got = fetch_rims(rim)
    pair = layer_pair(charges, sums, stat)
    layers = fetch_layers(pair)
    forward_rims(got, pair)
    gathered = gather(gat, got, pair)
    part = near_part(loc, gathered)
    (stats,) = call(
        functools.partial(second_kernel, s),
        [((s.devices, 1, LANES), f32)],
        [part, far_op, cells, col, f, ortho, stat, *layers],
        flops=10**8,
    )
    stats = lax.all_to_all(stats, ("gx", "gy", "gz"), 0, 0)
    result, lsq = call(
        functools.partial(finish_kernel, s),
        [(flat, f32), ((1, 1), f32)],
        [f, u, stats],
        far_outs=1,
        scratch=[pltpu.VMEM(flat, f32), pltpu.SemaphoreType.DMA],
        flops=10**7,
    )
    return result.reshape(rhs.shape), lsq.reshape(())


def solution(mesh):
    in_specs = (
        P("gx", "gy", None, None, "gz"),
        P("gx", "gy", None, "gz"),
        P(),
        P(),
        P("gx", "gy", None, "gz"),
        P("gx", "gy", None, "gz"),
        P("gx", "gy", "gz"),
        P(),
        P(),
        P(),
        P(),
        P(),
    )
    out_specs = (P("gx", "gy", None, None, "gz"), P())
    inner = functools.partial(body, dict(mesh.shape))
    return jax.shard_map(inner, mesh=mesh, in_specs=in_specs, out_specs=out_specs, check_vma=False)
```

```python
import functools

import jax
import jax.numpy as jnp
from jax import lax
from jax.experimental import pallas as pl
from jax.experimental.pallas import tpu as pltpu
from jax.sharding import PartitionSpec as P

epsilon = 1e-06
f32 = jnp.float32
bf16 = jnp.bfloat16
RIM = 64
LANES = 128


def round_up(value, unit):
    return -(-value // unit) * unit


def split(x):
    hi = x.astype(bf16)
    lo = (x - hi.astype(f32)).astype(bf16)
    return hi, lo


def mm(a, b):
    return lax.dot_general(a, b, (((1,), (0,)), ((), ())), preferred_element_type=f32)


def mt(a, b):
    return lax.dot_general(a, b, (((1,), (1,)), ((), ())), preferred_element_type=f32)


def product(dot, a, b):
    return dot(a[0], b[0]) + (dot(a[0], b[1]) + dot(a[1], b[0]))


def total(x):
    return jnp.sum(jnp.sum(x, axis=0, keepdims=True), axis=1, keepdims=True)


class Sizes:
    def __init__(self, mesh_shape, rhs, skel_perm):
        self.nx, self.ny, self.nz = (mesh_shape[a] for a in ("gx", "gy", "gz"))
        self.devices = self.nx * self.ny * self.nz
        self.blobs, self.bodies = rhs.shape[-2:]
        self.step = round_up(self.blobs, 8)
        self.rows = round_up(3 * self.step, 16)
        self.half = self.rows // 2
        self.message = self.half + 8
        self.direct = (self.nx, self.ny) == (4, 2)
        self.levels = skel_perm.shape[0]
        self.skel = skel_perm.shape[1] // 2
        shifts = sorted({(dy % self.ny) for dy in (-1, 1)} - {0})
        self.shifts = shifts
        self.sources = [("same", dy) for dy in shifts]
        for kind in ("other", "partner"):
            self.sources += [(kind, dy) for dy in [0] + shifts]
        self.ghosts = round_up(len(self.sources) * RIM, LANES)
        self.far_tiles = self.nz + -(-self.nz // 2)

    def slot_start(self, slot, parity):
        dx, dy = slot // 3 - 1, (slot % 3 - 1) % self.ny
        kind = "same" if dx == 0 else "partner" if dx == 1 - 2 * parity else "other"
        if (kind, dy) == ("same", 0):
            return 0
        return self.bodies + RIM * self.sources.index((kind, dy))

    def beside(self, kind, x):
        if kind == "same":
            return x
        if kind == "partner":
            return x ^ 1
        return (x + 2 * (x % 2) - 1) % self.nx


def pieces(x, s):
    return [x[c * s.step : c * s.step + s.step] for c in range(3)]


def turn(parts, rot, inverse):
    out = []
    for target in range(3):
        acc = None
        for source in range(3):
            row = 3 * source + target if inverse else 3 * target + source
            term = rot[row : row + 1] * parts[source]
            acc = term if acc is None else acc + term
        out.append(acc)
    return out


def stacked(parts, s):
    rest = s.rows - 3 * s.step
    if rest:
        parts = list(parts) + [jnp.zeros((rest, s.bodies), f32)]
    return jnp.concatenate(parts, axis=0)


def occupancy(cells, s):
    row = lax.broadcasted_iota(jnp.int32, (s.skel, s.bodies), 0)
    return jnp.where(cells == row, 1.0, 0.0).astype(bf16)


def pack_charges(parts, weight_col, occ, s, count=False):
    moments = [jnp.sum(part * weight_col, axis=0, keepdims=True) for part in parts]
    moments.append(jnp.full((1, s.bodies), 1.0 if count else 0.0, f32))
    moments = jnp.concatenate(moments + [jnp.zeros((4, s.bodies), f32)], axis=0)
    high, rest = split(moments)
    mid, low = split(moments - high.astype(f32))
    stack = jnp.concatenate([high.astype(f32), mid.astype(f32), low.astype(f32)], axis=0).astype(bf16)
    sums = mt(stack, occ)
    charges = sums[0:8] + (sums[8:16] + sums[16:24])
    tail = jnp.concatenate([charges[:, LANES:], jnp.zeros((8, 2 * LANES - s.skel), f32)], axis=1)
    row = lax.broadcasted_iota(jnp.int32, (8, LANES), 0)
    return jnp.where(row < 4, charges[:, :LANES], pltpu.roll(tail, 4, 0))


def pack_rim(x, s):
    lane = lax.broadcasted_iota(jnp.int32, (s.half, LANES), 1)
    top, bottom = x[: s.half, :LANES], x[s.half :, :LANES]
    return jnp.where(lane < RIM, top, pltpu.roll(bottom, RIM, 1))


def unpack_rims(rims, s):
    lane = lax.broadcasted_iota(jnp.int32, (s.half, LANES), 1)
    tops, bottoms = [], []
    for i in range(0, s.ghosts // RIM, 2):
        a = rims[i]
        b = rims[i + 1] if i + 1 < len(rims) else jnp.zeros_like(a)
        tops.append(jnp.where(lane < RIM, a, pltpu.roll(b, RIM, 1)))
        bottoms.append(jnp.where(lane < RIM, pltpu.roll(a, RIM, 1), b))
    return jnp.concatenate(
        [jnp.concatenate(tops, axis=1), jnp.concatenate(bottoms, axis=1)], axis=0
    )


def pack_message(x, weight_col, cells, s):
    charges = pack_charges(pieces(x, s), weight_col, occupancy(cells, s), s)
    return jnp.concatenate([pack_rim(x, s), charges], axis=0)


def begin(sources, targets, sems):
    moves = [pltpu.make_async_copy(a, b, sems.at[i]) for i, (a, b) in enumerate(zip(sources, targets))]
    for move in moves:
        move.start()
    return moves


def start_kernel(s, rhs, cells, weight, message_out, col_out, cells_out, f_out, raw, wide, sems):
    moves = begin((weight, cells, rhs), (wide, cells_out, raw), sems)
    f_out[...] = jnp.zeros_like(f_out)
    moves[0].wait()
    row = jnp.concatenate([wide[...], jnp.zeros((1, 2 * LANES - s.blobs), f32)], axis=1)
    col = jnp.broadcast_to(row, (LANES, 2 * LANES)).T[: s.step]
    col_out[...] = col
    for move in moves[1:]:
        move.wait()
    for c in range(3):
        f_out[c * s.step : c * s.step + s.blobs, :] = raw[c * s.blobs : (c + 1) * s.blobs, 0, :]
    message_out[...] = pack_message(f_out[...], col[:, :1], cells_out[0], s)


def frame_rows(angles):
    cos, sin = jnp.cos(angles), jnp.sin(angles)
    cy, cp, cr = cos[0:1], cos[1:2], cos[2:3]
    sy, sp, sr = sin[0:1], sin[1:2], sin[2:3]
    return [
        cy * cp,
        cy * sp * sr - sy * cr,
        cy * sp * cr + sy * sr,
        sy * cp,
        sy * sp * sr + cy * cr,
        sy * sp * cr - cy * sr,
        -sp,
        cp * sr,
        cp * cr,
    ]


def local_part(f, s, rot, mob, own):
    parts = pieces(f, s)
    turned = stacked(turn(parts, rot, False), s)
    mixed = product(mm, mob, split(turned))
    back = turn(pieces(mixed, s), rot, True)
    return f + stacked(back, s), product(mm, split(f), own)


def product_many(dot, blocks, b):
    rows = blocks[0].shape[0]
    out = product(dot, split(jnp.concatenate(blocks, axis=0)), split(b))
    return [out[i * rows : (i + 1) * rows] for i in range(len(blocks))]


def expand_once(groups, halves):
    flat = [block for group in groups for block in group]
    sides = [product_many(mt, flat, half) for half in halves]
    out, at = [], 0
    for group in groups:
        spread = []
        for i in range(at, at + len(group)):
            spread += [sides[0][i], sides[1][i]]
        at += len(group)
        out.append(spread)
    return out


def setup_kernel(
    s, ids, f_in, *refs
):
    count = 9
    sources, refs = refs[:count], refs[count:]
    copies, refs = refs[-1 - count :], refs[: -1 - count]
    copies, sems = copies[:-1], copies[-1]
    setup(s, ids, f_in, begin(sources, copies, sems), *copies, *refs)


def setup(
    s, ids, f_in, moves, angles, near_weight, neighbours, self_mob, near_mat, perm, interp, sibling, root,
    loc_out, gat_out, rot_out, sh_out, sl_out, nh_out, nl_out, oh_out, ol_out, gh_out, gl_out,
    far_out, uh_out, ul_out, bh_out, bl_out, rh_out, rl_out, padded, ups_ref,
):
    f = f_in[...]
    for move in moves[:3]:
        move.wait()
    rot = jnp.concatenate(frame_rows(angles[:, 0, :]) + [jnp.zeros((7, s.bodies), f32)], axis=0)
    rot_out[...] = rot

    links = neighbours[0, 0]
    slot = links // s.bodies
    base = jnp.zeros_like(links)
    odd = (ids[0] // s.ny) % 2
    for index in range(9):
        start = jnp.where(odd == 1, s.slot_start(index, 1), s.slot_start(index, 0))
        base = jnp.where(slot == index, start, base)
    column = base + links % s.bodies
    coef = near_weight[0, 0]
    for first, count, hi_out, lo_out in (
        (0, s.bodies, oh_out, ol_out),
        (s.bodies, s.ghosts, gh_out, gl_out),
    ):
        for r in range(0, count, 64):
            row = lax.broadcasted_iota(jnp.int32, (64, s.bodies), 0) + (first + r)
            acc = jnp.zeros((64, s.bodies), f32)
            for k in range(coef.shape[0]):
                acc = acc + jnp.where(column[k : k + 1] == row, coef[k : k + 1], 0.0)
            hi, lo = split(acc)
            hi_out[r : r + 64, :] = hi
            lo_out[r : r + 64, :] = lo

    for move in moves[3:]:
        move.wait()
    padded[...] = jnp.zeros_like(padded)
    for matrix, hi_out, lo_out in ((self_mob, sh_out, sl_out), (near_mat, nh_out, nl_out)):
        for c in range(3):
            for d in range(3):
                padded[c * s.step : c * s.step + s.blobs, d * s.step : d * s.step + s.blobs] = matrix[
                    c * s.blobs : (c + 1) * s.blobs, d * s.blobs : (d + 1) * s.blobs
                ]
        hi, lo = split(padded[...])
        hi_out[...] = hi
        lo_out[...] = lo

    loc, gat = local_part(f, s, rot, (sh_out[...], sl_out[...]), (oh_out[...], ol_out[...]))
    loc_out[...] = loc
    gat_out[...] = gat

    n = s.skel
    z = ids[1]
    halves = []
    spot = lax.broadcasted_iota(jnp.int32, (2 * n, n), 0)
    for level in range(s.levels):
        kept = jnp.where(perm[level : level + 1, :n] == spot, 1.0, 0.0)
        moved = jnp.where(perm[level : level + 1, n:] == spot, 1.0, 0.0).astype(bf16)
        hi, lo = split(interp[level])
        up = kept + (mm(moved, hi) + mm(moved, lo))
        ups_ref[level] = up
        uh_out[level], ul_out[level] = split(up)
        bh_out[level], bl_out[level] = split(sibling[level])
        bit = (z >> level) & 1
        halves.append(
            [ups_ref[level, pl.ds(pl.multiple_of(side * n, 8), n), :] for side in (bit, 1 - bit)]
        )

    def down(block, level, dot):
        return product(dot, split(halves[level][0]), split(block))

    spread = root[...]
    rh_out[...], rl_out[...] = split(spread)
    beside = []
    for level in reversed(range(s.levels)):
        spread = down(spread, level, mt if level == s.levels - 1 else mm)
        beside = [(down(block, level, mt if fresh else mm), False) for block, fresh in beside]
        beside.append((sibling[level], True))
    beside = [block.T if fresh else block for block, fresh in reversed(beside)]
    leaves = [[spread]]
    for level in reversed(range(s.levels)):
        leaves = expand_once(leaves, halves[level])
        leaves.append([beside[level]])
    far_leaves, *sub = leaves
    near_leaves = [jnp.zeros((n, n), f32)]
    for blocks in reversed(sub):
        near_leaves += blocks
    tail = n - LANES
    far_out[...] = jnp.zeros_like(far_out)
    own = [a - b for a, b in zip(near_leaves, far_leaves)]
    for group, blocks in enumerate((own, far_leaves)):
        for leaf, block in enumerate(blocks):
            at = (group * s.far_tiles + leaf) * LANES
            far_out[:, at : at + LANES] = block[:, :LANES]
            at = (group * s.far_tiles + s.nz + leaf // 2) * LANES + leaf % 2 * RIM
            far_out[:, at : at + tail] = block[:, LANES:]


def half_kernel(s, *refs):
    *messages, _, out = refs
    acc = messages[0][s.half :, :]
    for message in messages[1:]:
        acc = acc + message[s.half :, :]
    out[...] = acc


def layer_kernel(s, message, *refs):
    *sums, _, out = refs
    acc = sums[0][...]
    for part in sums[1:]:
        acc = acc + part[...]
    out[0] = message[s.half :, :]
    out[1] = acc


def far_potential(s, charges, far_op):
    rows = []
    for group in range(2):
        tiles = [layer[group] for layer in charges]
        rows += tiles
        for leaf in range(0, s.nz, 2):
            pair = tiles[leaf]
            if leaf + 1 < s.nz:
                lane = lax.broadcasted_iota(jnp.int32, (8, LANES), 1)
                pair = jnp.where(lane < RIM, pair, pltpu.roll(tiles[leaf + 1], RIM, 1))
            rows.append(pltpu.roll(pair, 4, 0))
    columns = [[], [], []]
    for r in range(0, s.skel, 64):
        acc = [None] * 3
        for index, row in enumerate(rows):
            block = far_op[r : r + 64, index * LANES : (index + 1) * LANES]
            for c in range(3):
                term = block * row[c : c + 1]
                acc[c] = term if acc[c] is None else acc[c] + term
        for c in range(3):
            columns[c].append(jnp.sum(acc[c], axis=1, keepdims=True))
    return columns


def far_values(s, charges, far_op, cells):
    columns = far_potential(s, charges, far_op)
    out = []
    for c in range(3):
        acc = jnp.zeros((1, s.bodies), f32)
        for index, r in enumerate(range(0, s.skel, 64)):
            row = lax.broadcasted_iota(jnp.int32, (64, s.bodies), 0) + r
            acc = acc + jnp.sum(jnp.where(cells == row, columns[c][index], 0.0), axis=0, keepdims=True)
        out.append(acc)
    return out


def gather_kernel(s, gat, gh, gl, *refs):
    *messages, _, hi_out, lo_out = refs
    rims = [message[: s.half, :] for message in messages]
    gathered = gat[...] + product(mm, split(unpack_rims(rims, s)), (gh[...], gl[...]))
    hi_out[...], lo_out[...] = split(gathered)


def near_kernel(s, loc, nh, nl, hi, lo, out):
    out[...] = loc[...] + product(mm, (nh[...], nl[...]), (hi[...], lo[...]))


def with_far(s, part, layers, far_op, cells, col):
    values = far_values(s, layers, far_op, cells[0])
    return part[...] + stacked([col * value for value in values], s)


def first_kernel(s, part, far_op, cells, col, *refs):
    *layers, u_out, rim_out, charges_out = refs
    weight_col = col[:, :1]
    u = with_far(s, part, layers, far_op, cells, weight_col)
    u_out[...] = u
    rim_out[...] = pack_rim(u, s)
    charges_out[...] = pack_charges(pieces(u, s), weight_col, occupancy(cells[0], s), s)


def safe_inverse(x):
    return jnp.where(x > 0.0, 1.0 / jnp.where(x > 0.0, x, 1.0), 0.0)


def middle_kernel(s, u_in, f_in, rot, sh, sl, oh, ol, loc_out, gat_out, ortho_out, stat_out):
    u, f = u_in[...], f_in[...]
    loc, gat = local_part(u, s, rot[...], (sh[...], sl[...]), (oh[...], ol[...]))
    loc_out[...] = loc
    gat_out[...] = gat
    ff = total(f * f)
    fu = total(f * u) * safe_inverse(ff)
    ortho = u - fu * f
    ortho_out[...] = ortho
    oo = total(ortho * ortho)
    stat_out[...] = jnp.broadcast_to(
        jnp.concatenate([ff, fu, oo, jnp.zeros((5, 1), f32)], axis=0), (8, LANES)
    )


def second_kernel(
    s, loc, nh, nl, hi, lo, cells, col, f_in, ortho_in, stat, charges_f, charges_u, packed_out
):
    part = loc[...] + product(mm, (nh[...], nl[...]), (hi[...], lo[...]))
    f, ortho = f_in[...], ortho_in[...]
    ff, fu, oo = (stat[i : i + 1, :1] for i in range(3))
    fa = total(f * part) * safe_inverse(ff)
    oa = total(ortho * part) * safe_inverse(oo)
    rest = part - fa * f - oa * ortho
    aa = total(rest * rest)
    rf, ro = jnp.sqrt(ff), jnp.sqrt(oo)
    of_f = charges_f[-8:, :]
    of_u = charges_u[...]
    of_a = pack_charges(pieces(rest, s), col[:, :1], occupancy(cells[0], s), s, count=True)
    row = lax.broadcasted_iota(jnp.int32, (8, LANES), 0)
    lane = lax.broadcasted_iota(jnp.int32, (8, LANES), 1)
    left = lane < RIM
    first = jnp.where(left, of_u, pltpu.roll(of_a, RIM, 1))
    first = jnp.where(row < 4, of_u, first)
    first = jnp.where((row == 7) & left, pltpu.roll(of_f, 1, 0), first)
    for index, value in enumerate((rf, rf * fu, ro, rf * fa, ro * oa, aa)):
        first = jnp.where((row == 3) & (lane == index), value, first)
    tails = jnp.where(left, pltpu.roll(of_f, 3, 0), pltpu.roll(pltpu.roll(of_f, 2, 0), RIM, 1))
    second = jnp.where(row < 3, of_f, of_a)
    second = jnp.where(row < 4, second, pltpu.roll(of_a, 4, 0))
    second = jnp.where(row == 7, tails, second)
    packed = jnp.concatenate([first, second], axis=0)
    packed_out[...] = jnp.broadcast_to(packed[None], packed_out.shape)


def tree(s, leaves, ups, siblings, root):
    def apply(dot, blocks, factor):
        rows = blocks[0].shape[0]
        out = product(dot, split(jnp.concatenate(blocks, axis=0)), factor)
        return [out[i * rows : (i + 1) * rows] for i in range(len(blocks))]

    n = s.skel
    halves = [[(hi[level, j * n : (j + 1) * n, :], lo[level, j * n : (j + 1) * n, :]) for j in range(2)]
              for level, (hi, lo) in ((k, ups) for k in range(s.levels))]
    charges = [leaves]
    for level in range(s.levels):
        low, high = (apply(mm, charges[-1][j::2], halves[level][j]) for j in range(2))
        charges.append([a + b for a, b in zip(low, high)])
    own = charges[-1][0]
    whole = own[:8]
    for column in range(1, s.nx * s.ny):
        whole = whole + own[8 * column : 8 * column + 8]
    others = jnp.concatenate([whole] * (s.nx * s.ny), axis=0) - own
    potential = apply(mm, [others], root)
    for level in reversed(range(s.levels)):
        beside = apply(mm, charges[level], (siblings[0][level], siblings[1][level]))
        down = [apply(mt, potential, halves[level][j]) for j in range(2)]
        potential = [
            down[z % 2][z // 2] + beside[z ^ 1] for z in range(len(charges[level]))
        ]
    return potential


def box_numbers(s, boxes, ups, siblings, root):
    columns = s.nx * s.ny
    row = lax.broadcasted_iota(jnp.int32, (8, LANES), 0)
    lane = lax.broadcasted_iota(jnp.int32, (8, LANES), 1)
    left, valid = lane < RIM, row < 3
    leaves = []
    for z in range(s.nz):
        wide = []
        for column in range(columns):
            tile = boxes[column * s.nz + z, :8, :]
            wide.append(jnp.concatenate([tile, pltpu.roll(tile, 4, 0)], axis=1)[:, : s.skel])
        leaves.append(jnp.concatenate(wide, axis=0))
    potential = tree(s, leaves, ups, siblings, root)
    out = []
    for start in range(0, s.devices, 8):
        sums = [jnp.zeros((8, LANES), f32) for _ in range(5)]
        for box in range(start, min(s.devices, start + 8)):
            column, z = box // s.nz, box % s.nz
            phi = potential[z][8 * column : 8 * column + 8]
            main, tail = phi[:, :LANES], phi[:, LANES:]
            tail = jnp.concatenate([tail, tail], axis=1)
            first, second = boxes[box, :8, :], boxes[box, 8:, :]
            both = pltpu.roll(first, 4, 0) * tail
            of_f = jnp.where(row == 0, pltpu.roll(second, 1, 0), jnp.where(row == 1, pltpu.roll(second, 2, 0), pltpu.roll(first, 3, 0)))
            of_f = jnp.where(left == (row != 1), of_f * tail, 0.0)
            count = jnp.broadcast_to(second[3:4], (8, LANES))
            count_tail = jnp.where(left, 0.0, jnp.broadcast_to(first[7:8], (8, LANES)))
            terms = (
                second * main + of_f,
                first * main + jnp.where(left, both, 0.0),
                pltpu.roll(second, 4, 0) * main + jnp.where(left, 0.0, both),
                count * (main * main) + count_tail * (tail * tail),
            )
            here = row == box - start
            for index, term in enumerate(terms):
                value = jnp.sum(jnp.where(valid, term, 0.0), axis=0, keepdims=True)
                sums[index] = jnp.where(here, value, sums[index])
            sums[4] = jnp.where(here, first[3:4], sums[4])
        numbers = sums[4]
        for index in range(4):
            numbers = jnp.where(lane == 6 + index, jnp.sum(sums[index], axis=1, keepdims=True), numbers)
        out.append(numbers)
    rest = round_up(s.devices, LANES) - 8 * len(out)
    if rest:
        out.append(jnp.zeros((rest, LANES), f32))
    return jnp.concatenate(out, axis=0)


def finish_kernel(s, f_in, u_in, boxes, col, uh, ul, bh, bl, rh, rl, x_out, lsq_out, raw, sem):
    rows = box_numbers(s, boxes, (uh, ul), (bh, bl), (rh[...], rl[...])).T
    f1, u1, u2, t1, t2, aa, far_f, far_u, far_a, far_far = (rows[i : i + 1] for i in range(10))
    by_f = safe_inverse(f1)
    by_o = jnp.where(u2 * u2 > 1e-10 * (u1 * u1), safe_inverse(u2), 0.0)
    on_one = far_f * by_f
    on_two = (far_u - u1 * by_f * far_f) * by_o
    weight = jnp.sum(col[:, :1] * col[:, :1], axis=0, keepdims=True)
    t3 = aa + 2.0 * far_a + weight * far_far - on_one * on_one - on_two * on_two
    t1, t2, t3 = t1 + on_one, t2 + on_two, jnp.sqrt(jnp.maximum(t3, 0.0))

    def along(x):
        return jnp.sum(x, axis=1, keepdims=True)

    beta = jnp.sqrt(along(f1 * f1) + epsilon)
    v = f1 / beta
    w1, w2 = u1 / beta, u2 / beta
    h11 = along(w1 * v)
    r1 = w1 - h11 * v
    h21 = jnp.sqrt(along(r1 * r1 + w2 * w2) + epsilon)
    b1, b2 = r1 / h21, w2 / h21
    z1, z2, z3 = ((t1 / beta - h11 * w1) / h21, (t2 / beta - h11 * w2) / h21, t3 / beta / h21)
    h12 = along(z1 * v)
    h22 = along(z1 * b1 + z2 * b2)
    d1, d2 = z1 - h12 * v - h22 * b1, z2 - h22 * b2
    h32 = jnp.sqrt(along(d1 * d1 + d2 * d2 + z3 * z3) + epsilon)
    first_norm = jnp.sqrt(h11 * h11 + h21 * h21)
    c1, s1 = h11 / first_norm, h21 / first_norm
    t12, t22 = c1 * h12 + s1 * h22, c1 * h22 - s1 * h12
    second_norm = jnp.sqrt(t22 * t22 + h32 * h32)
    c2, s2 = t22 / second_norm, h32 / second_norm
    g2 = -s1 * beta
    y2 = c2 * g2 / second_norm
    y1 = (c1 * beta - t12 * y2) / first_norm
    lsq_out[...] = jnp.abs(s2 * g2)
    on_u = y2 / h21 / beta
    on_f = y1 / beta - on_u * h11
    for c in range(3):
        part = slice(c * s.step, c * s.step + s.blobs)
        raw[c * s.blobs : (c + 1) * s.blobs, 0, :] = on_f * f_in[part, :] + on_u * u_in[part, :]
    move = pltpu.make_async_copy(raw, x_out, sem)
    move.start()
    move.wait()


def call(kernel, outs, args, scalars=0, far_args=0, far_outs=0, scratch=(), flops=0):
    vmem = pl.BlockSpec(memory_space=pltpu.VMEM)
    smem = pl.BlockSpec(memory_space=pltpu.SMEM)
    hbm = pl.BlockSpec(memory_space=pltpu.HBM)
    near_args = len(args) - far_args
    args = args[:near_args] + [pltpu.with_memory_space_constraint(x, pltpu.HBM) for x in args[near_args:]]
    return pl.pallas_call(
        kernel,
        out_shape=[jax.ShapeDtypeStruct(shape, kind) for shape, kind in outs],
        in_specs=[smem] * scalars + [vmem] * (near_args - scalars) + [hbm] * far_args,
        out_specs=[hbm] * far_outs + [vmem] * (len(outs) - far_outs),
        scratch_shapes=list(scratch),
        compiler_params=pltpu.CompilerParams(vmem_limit_bytes=16 * 2**20),
        cost_estimate=pl.CostEstimate(flops=flops, bytes_accessed=2**20, transcendentals=0),
    )(*args)


def body(
    mesh_shape, rhs, angles, self_mob, near_mat, near_weight, neighbours, cells, blob_weight,
    skel_perm, interp, sibling_ops, root_op,
):
    s = Sizes(mesh_shape, rhs, skel_perm)
    full = (s.rows, s.bodies)
    square = (s.rows, s.rows)
    tile = (8, LANES)
    far_shape = (s.skel, 2 * s.far_tiles * LANES)
    column = lax.axis_index("gx") * s.ny + lax.axis_index("gy")
    ids = jnp.stack([column, lax.axis_index("gz")]).astype(jnp.int32)

    def fetch(x, kind, dy):
        pairs = []
        for gx in range(s.nx):
            for gy in range(s.ny):
                pairs.append((s.beside(kind, gx) * s.ny + (gy + dy) % s.ny, gx * s.ny + gy))
        return lax.ppermute(x, ("gx", "gy"), pairs)

    def fetch_layers(x):
        return [x] + [
            lax.ppermute(x, "gz", [(z ^ k, z) for z in range(s.nz)]) for k in range(1, s.nz)
        ]

    def fetch_rims(rim):
        got = {}
        for dy in s.shifts:
            got["same", dy] = fetch(rim, "same", dy)
        for dy in s.shifts:
            got["other", dy] = fetch(rim, "other", dy)
        got["other", 0] = fetch(rim, "other", 0)
        got["partner", 0] = fetch(rim, "partner", 0)
        return got

    def forward_rims(got, after):
        for dy in s.shifts:
            ready, _ = lax.optimization_barrier((got["same", dy], after))
            got["partner", dy] = fetch(ready, "partner", 0)

    def gather(gat, got, after):
        return call(
            functools.partial(gather_kernel, s),
            [(full, bf16), (full, bf16)],
            [gat, gh, gl] + [got[key] for key in s.sources] + [after],
            flops=10**9,
        )

    def share(message, got, gat, after):
        forward_rims(got, after)
        if s.direct:
            quarter = [message] + [got[key] for key in s.sources if key[0] != "partner"]
            (half,) = call(functools.partial(half_kernel, s), [(tile, f32)], quarter + [after])
            sums = [half, fetch(half, "partner", 0)]
        else:
            half = lax.psum(message[s.half :], ("gx", "gy"))
            sums = [half]
        gathered = gather(gat, got, half)
        (pair,) = call(
            functools.partial(layer_kernel, s), [((2,) + tile, f32)], [message] + sums + [gathered[1]]
        )
        return gathered, fetch_layers(pair)

    def near_part(loc, gathered):
        return call(
            functools.partial(near_kernel, s), [(full, f32)], [loc, nh, nl, *gathered], flops=10**9
        )[0]

    flat = (3 * s.blobs, 1, s.bodies)
    small = (1, s.blobs)
    message, col, cells, f = call(
        functools.partial(start_kernel, s),
        [((s.message, LANES), f32), ((s.step, LANES), f32), (cells.shape, jnp.int32), (full, f32)],
        [rhs.reshape(flat), cells, blob_weight.reshape(small)],
        far_args=3,
        scratch=[pltpu.VMEM(flat, f32), pltpu.VMEM(small, f32), pltpu.SemaphoreType.DMA((3,))],
        flops=10**7,
    )
    got = fetch_rims(message)
    operators = [
        angles.reshape(3, 1, s.bodies), near_weight, neighbours, self_mob, near_mat, skel_perm, interp,
        sibling_ops, root_op,
    ]
    loc, gat, rot, sh, sl, nh, nl, oh, ol, gh, gl, far_op, *operators_out = call(
        functools.partial(setup_kernel, s),
        [(full, f32), (full, f32), ((16, s.bodies), f32)]
        + [(square, bf16)] * 4
        + [((s.bodies, s.bodies), bf16)] * 2
        + [((s.ghosts, s.bodies), bf16)] * 2
        + [(far_shape, f32)]
        + [((s.levels, 2 * s.skel, s.skel), bf16)] * 2
        + [((s.levels, s.skel, s.skel), bf16)] * 2
        + [((s.skel, s.skel), bf16)] * 2,
        [ids, f] + operators,
        scalars=1,
        far_args=len(operators),
        scratch=[pltpu.VMEM(square, f32), pltpu.VMEM((s.levels, 2 * s.skel, s.skel), f32)]
        + [pltpu.VMEM(x.shape, x.dtype) for x in operators]
        + [pltpu.SemaphoreType.DMA((len(operators),))],
        flops=5 * 10**9,
    )
    gathered, layers = share(message, got, gat, rot)
    part = near_part(loc, gathered)
    u, rim, charges = call(
        functools.partial(first_kernel, s),
        [(full, f32), ((s.half, LANES), f32), (tile, f32)],
        [part, far_op, cells, col, *layers],
        flops=10**8,
    )
    got = fetch_rims(rim)
    loc, gat, ortho, stat = call(
        functools.partial(middle_kernel, s),
        [(full, f32), (full, f32), (full, f32), (tile, f32)],
        [u, f, rot, sh, sl, oh, ol],
        flops=10**9,
    )
    forward_rims(got, stat)
    gathered = gather(gat, got, stat)
    (packed,) = call(
        functools.partial(second_kernel, s),
        [((s.devices, 16, LANES), f32)],
        [loc, nh, nl, *gathered, cells, col, f, ortho, stat, message, charges],
        flops=10**9,
    )
    boxes = lax.all_to_all(packed, ("gx", "gy", "gz"), 0, 0)
    result, lsq = call(
        functools.partial(finish_kernel, s),
        [(flat, f32), ((1, 1), f32)],
        [f, u, boxes, col, *operators_out],
        far_outs=1,
        scratch=[pltpu.VMEM(flat, f32), pltpu.SemaphoreType.DMA],
        flops=10**7,
    )
    return result.reshape(rhs.shape), lsq.reshape(())


def solution(mesh):
    in_specs = (
        P("gx", "gy", None, None, "gz"),
        P("gx", "gy", None, "gz"),
        P(),
        P(),
        P("gx", "gy", None, "gz"),
        P("gx", "gy", None, "gz"),
        P("gx", "gy", "gz"),
        P(),
        P(),
        P(),
        P(),
        P(),
    )
    out_specs = (P("gx", "gy", None, None, "gz"), P())
    inner = functools.partial(body, dict(mesh.shape))
    return jax.shard_map(inner, mesh=mesh, in_specs=in_specs, out_specs=out_specs, check_vma=False)
```

```python
import functools

import jax
import jax.numpy as jnp
from jax import lax
from jax.experimental import pallas as pl
from jax.experimental.pallas import tpu as pltpu
from jax.sharding import PartitionSpec as P

epsilon = 1e-06
f32 = jnp.float32
bf16 = jnp.bfloat16
RIM = 64
LANES = 128


def round_up(value, unit):
    return -(-value // unit) * unit


def split(x):
    hi = x.astype(bf16)
    lo = (x - hi.astype(f32)).astype(bf16)
    return hi, lo


def mm(a, b):
    return lax.dot_general(a, b, (((1,), (0,)), ((), ())), preferred_element_type=f32)


def mt(a, b):
    return lax.dot_general(a, b, (((1,), (1,)), ((), ())), preferred_element_type=f32)


def product(dot, a, b):
    return dot(a[0], b[0]) + (dot(a[0], b[1]) + dot(a[1], b[0]))


def total(x):
    return jnp.sum(jnp.sum(x, axis=0, keepdims=True), axis=1, keepdims=True)


class Sizes:
    def __init__(self, mesh_shape, rhs, skel_perm):
        self.nx, self.ny, self.nz = (mesh_shape[a] for a in ("gx", "gy", "gz"))
        self.devices = self.nx * self.ny * self.nz
        self.blobs, self.bodies = rhs.shape[-2:]
        self.step = round_up(self.blobs, 8)
        self.rows = round_up(3 * self.step, 16)
        self.half = self.rows // 2
        self.message = self.half + 8
        self.direct = (self.nx, self.ny) == (4, 2)
        self.levels = skel_perm.shape[0]
        self.skel = skel_perm.shape[1] // 2
        shifts = sorted({(dy % self.ny) for dy in (-1, 1)} - {0})
        self.shifts = shifts
        self.sources = [("same", dy) for dy in shifts]
        for kind in ("other", "partner"):
            self.sources += [(kind, dy) for dy in [0] + shifts]
        self.ghosts = round_up(len(self.sources) * RIM, LANES)
        self.far_tiles = self.nz + -(-self.nz // 2)

    def slot_start(self, slot, parity):
        dx, dy = slot // 3 - 1, (slot % 3 - 1) % self.ny
        kind = "same" if dx == 0 else "partner" if dx == 1 - 2 * parity else "other"
        if (kind, dy) == ("same", 0):
            return 0
        return self.bodies + RIM * self.sources.index((kind, dy))

    def odd(self, device):
        return (device // (self.ny * self.nz)) % 2

    def beside(self, kind, x):
        if kind == "same":
            return x
        if kind == "partner":
            return x ^ 1
        return (x + 2 * (x % 2) - 1) % self.nx


def pieces(x, s):
    return [x[c * s.step : c * s.step + s.step] for c in range(3)]


def turn(parts, rot, inverse):
    out = []
    for target in range(3):
        acc = None
        for source in range(3):
            row = 3 * source + target if inverse else 3 * target + source
            term = rot[row : row + 1] * parts[source]
            acc = term if acc is None else acc + term
        out.append(acc)
    return out


def stacked(parts, s):
    rest = s.rows - 3 * s.step
    if rest:
        parts = list(parts) + [jnp.zeros((rest, s.bodies), f32)]
    return jnp.concatenate(parts, axis=0)


def occupancy(cells, s):
    row = lax.broadcasted_iota(jnp.int32, (s.skel, s.bodies), 0)
    return jnp.where(cells == row, 1.0, 0.0).astype(bf16)


def pack_charges(parts, weight_col, occ, s, count=False):
    moments = [jnp.sum(part * weight_col, axis=0, keepdims=True) for part in parts]
    moments.append(jnp.full((1, s.bodies), 1.0 if count else 0.0, f32))
    moments = jnp.concatenate(moments + [jnp.zeros((4, s.bodies), f32)], axis=0)
    high, rest = split(moments)
    mid, low = split(moments - high.astype(f32))
    stack = jnp.concatenate([high.astype(f32), mid.astype(f32), low.astype(f32)], axis=0).astype(bf16)
    sums = mt(stack, occ)
    charges = sums[0:8] + (sums[8:16] + sums[16:24])
    tail = jnp.concatenate([charges[:, LANES:], jnp.zeros((8, 2 * LANES - s.skel), f32)], axis=1)
    row = lax.broadcasted_iota(jnp.int32, (8, LANES), 0)
    return jnp.where(row < 4, charges[:, :LANES], pltpu.roll(tail, 4, 0))


def pack_rim(x, s):
    lane = lax.broadcasted_iota(jnp.int32, (s.half, LANES), 1)
    top, bottom = x[: s.half, :LANES], x[s.half :, :LANES]
    return jnp.where(lane < RIM, top, pltpu.roll(bottom, RIM, 1))


def unpack_rims(rims, s):
    lane = lax.broadcasted_iota(jnp.int32, (s.half, LANES), 1)
    tops, bottoms = [], []
    for i in range(0, s.ghosts // RIM, 2):
        a = rims[i]
        b = rims[i + 1] if i + 1 < len(rims) else jnp.zeros_like(a)
        tops.append(jnp.where(lane < RIM, a, pltpu.roll(b, RIM, 1)))
        bottoms.append(jnp.where(lane < RIM, pltpu.roll(a, RIM, 1), b))
    return jnp.concatenate(
        [jnp.concatenate(tops, axis=1), jnp.concatenate(bottoms, axis=1)], axis=0
    )


def pack_message(x, weight_col, cells, s):
    charges = pack_charges(pieces(x, s), weight_col, occupancy(cells, s), s)
    return jnp.concatenate([pack_rim(x, s), charges], axis=0)


def begin(sources, targets, sems):
    moves = [pltpu.make_async_copy(a, b, sems.at[i]) for i, (a, b) in enumerate(zip(sources, targets))]
    for move in moves:
        move.start()
    return moves


def start_kernel(s, rhs, cells, weight, message_out, col_out, cells_out, f_out, raw, wide, sems):
    moves = begin((weight, cells, rhs), (wide, cells_out, raw), sems)
    f_out[...] = jnp.zeros_like(f_out)
    moves[0].wait()
    row = jnp.concatenate([wide[...], jnp.zeros((1, 2 * LANES - s.blobs), f32)], axis=1)
    col = jnp.broadcast_to(row, (LANES, 2 * LANES)).T[: s.step]
    col_out[...] = col
    for move in moves[1:]:
        move.wait()
    for c in range(3):
        f_out[c * s.step : c * s.step + s.blobs, :] = raw[c * s.blobs : (c + 1) * s.blobs, 0, :]
    message_out[...] = pack_message(f_out[...], col[:, :1], cells_out[0], s)


def frame_rows(angles):
    cos, sin = jnp.cos(angles), jnp.sin(angles)
    cy, cp, cr = cos[0:1], cos[1:2], cos[2:3]
    sy, sp, sr = sin[0:1], sin[1:2], sin[2:3]
    return [
        cy * cp,
        cy * sp * sr - sy * cr,
        cy * sp * cr + sy * sr,
        sy * cp,
        sy * sp * sr + cy * cr,
        sy * sp * cr - cy * sr,
        -sp,
        cp * sr,
        cp * cr,
    ]


def local_part(f, s, rot, mob, own):
    parts = pieces(f, s)
    turned = stacked(turn(parts, rot, False), s)
    mixed = product(mm, mob, split(turned))
    back = turn(pieces(mixed, s), rot, True)
    return f + stacked(back, s), product(mm, split(f), own)


def product_many(dot, blocks, b):
    rows = blocks[0].shape[0]
    out = product(dot, split(jnp.concatenate(blocks, axis=0)), split(b))
    return [out[i * rows : (i + 1) * rows] for i in range(len(blocks))]


def expand_once(groups, halves):
    flat = [block for group in groups for block in group]
    sides = [product_many(mt, flat, half) for half in halves]
    out, at = [], 0
    for group in groups:
        spread = []
        for i in range(at, at + len(group)):
            spread += [sides[0][i], sides[1][i]]
        at += len(group)
        out.append(spread)
    return out


def setup_kernel(
    s, ids, f_in, *refs
):
    count = 9
    sources, refs = refs[:count], refs[count:]
    copies, refs = refs[-1 - count :], refs[: -1 - count]
    copies, sems = copies[:-1], copies[-1]
    setup(s, ids, f_in, begin(sources, copies, sems), *copies, *refs)


def setup(
    s, ids, f_in, moves, angles, near_weight, neighbours, self_mob, near_mat, perm, interp, sibling, root,
    loc_out, gat_out, rot_out, sh_out, sl_out, nh_out, nl_out, oh_out, ol_out, gh_out, gl_out,
    far_out, uh_out, ul_out, bh_out, bl_out, rh_out, rl_out, padded, ups_ref,
):
    f = f_in[...]
    for move in moves[:3]:
        move.wait()
    rot = jnp.concatenate(frame_rows(angles[:, 0, :]) + [jnp.zeros((7, s.bodies), f32)], axis=0)
    rot_out[...] = rot

    links = neighbours[0, 0]
    slot = links // s.bodies
    base = jnp.zeros_like(links)
    odd = (ids[0] // s.ny) % 2
    for index in range(9):
        start = jnp.where(odd == 1, s.slot_start(index, 1), s.slot_start(index, 0))
        base = jnp.where(slot == index, start, base)
    column = base + links % s.bodies
    coef = near_weight[0, 0]
    for first, count, hi_out, lo_out in (
        (0, s.bodies, oh_out, ol_out),
        (s.bodies, s.ghosts, gh_out, gl_out),
    ):
        for r in range(0, count, 64):
            row = lax.broadcasted_iota(jnp.int32, (64, s.bodies), 0) + (first + r)
            acc = jnp.zeros((64, s.bodies), f32)
            for k in range(coef.shape[0]):
                acc = acc + jnp.where(column[k : k + 1] == row, coef[k : k + 1], 0.0)
            hi, lo = split(acc)
            hi_out[r : r + 64, :] = hi
            lo_out[r : r + 64, :] = lo

    for move in moves[3:]:
        move.wait()
    padded[...] = jnp.zeros_like(padded)
    for matrix, hi_out, lo_out in ((self_mob, sh_out, sl_out), (near_mat, nh_out, nl_out)):
        for c in range(3):
            for d in range(3):
                padded[c * s.step : c * s.step + s.blobs, d * s.step : d * s.step + s.blobs] = matrix[
                    c * s.blobs : (c + 1) * s.blobs, d * s.blobs : (d + 1) * s.blobs
                ]
        hi, lo = split(padded[...])
        hi_out[...] = hi
        lo_out[...] = lo

    loc, gat = local_part(f, s, rot, (sh_out[...], sl_out[...]), (oh_out[...], ol_out[...]))
    loc_out[...] = loc
    gat_out[...] = gat

    n = s.skel
    z = ids[1]
    halves = []
    spot = lax.broadcasted_iota(jnp.int32, (2 * n, n), 0)
    for level in range(s.levels):
        kept = jnp.where(perm[level : level + 1, :n] == spot, 1.0, 0.0)
        moved = jnp.where(perm[level : level + 1, n:] == spot, 1.0, 0.0).astype(bf16)
        hi, lo = split(interp[level])
        up = kept + (mm(moved, hi) + mm(moved, lo))
        ups_ref[level] = up
        uh_out[level], ul_out[level] = split(up)
        bh_out[level], bl_out[level] = split(sibling[level])
        bit = (z >> level) & 1
        halves.append(
            [ups_ref[level, pl.ds(pl.multiple_of(side * n, 8), n), :] for side in (bit, 1 - bit)]
        )

    def down(block, level, dot):
        return product(dot, split(halves[level][0]), split(block))

    spread = root[...]
    rh_out[...], rl_out[...] = split(spread)
    beside = []
    for level in reversed(range(s.levels)):
        spread = down(spread, level, mt if level == s.levels - 1 else mm)
        beside = [(down(block, level, mt if fresh else mm), False) for block, fresh in beside]
        beside.append((sibling[level], True))
    beside = [block.T if fresh else block for block, fresh in reversed(beside)]
    leaves = [[spread]]
    for level in reversed(range(s.levels)):
        leaves = expand_once(leaves, halves[level])
        leaves.append([beside[level]])
    far_leaves, *sub = leaves
    near_leaves = [jnp.zeros((n, n), f32)]
    for blocks in reversed(sub):
        near_leaves += blocks
    tail = n - LANES
    far_out[...] = jnp.zeros_like(far_out)
    own = [a - b for a, b in zip(near_leaves, far_leaves)]
    for group, blocks in enumerate((own, far_leaves)):
        for leaf, block in enumerate(blocks):
            at = (group * s.far_tiles + leaf) * LANES
            far_out[:, at : at + LANES] = block[:, :LANES]
            at = (group * s.far_tiles + s.nz + leaf // 2) * LANES + leaf % 2 * RIM
            far_out[:, at : at + tail] = block[:, LANES:]


def half_kernel(s, *refs):
    *messages, _, out = refs
    acc = messages[0][s.half :, :]
    for message in messages[1:]:
        acc = acc + message[s.half :, :]
    out[...] = acc


def layer_kernel(s, message, *refs):
    *sums, _, out = refs
    acc = sums[0][...]
    for part in sums[1:]:
        acc = acc + part[...]
    out[0] = message[s.half :, :]
    out[1] = acc


def far_potential(s, charges, far_op):
    rows = []
    for group in range(2):
        tiles = [layer[group] for layer in charges]
        rows += tiles
        for leaf in range(0, s.nz, 2):
            pair = tiles[leaf]
            if leaf + 1 < s.nz:
                lane = lax.broadcasted_iota(jnp.int32, (8, LANES), 1)
                pair = jnp.where(lane < RIM, pair, pltpu.roll(tiles[leaf + 1], RIM, 1))
            rows.append(pltpu.roll(pair, 4, 0))
    columns = [[], [], []]
    for r in range(0, s.skel, 64):
        acc = [None] * 3
        for index, row in enumerate(rows):
            block = far_op[r : r + 64, index * LANES : (index + 1) * LANES]
            for c in range(3):
                term = block * row[c : c + 1]
                acc[c] = term if acc[c] is None else acc[c] + term
        for c in range(3):
            columns[c].append(jnp.sum(acc[c], axis=1, keepdims=True))
    return columns


def far_values(s, charges, far_op, cells):
    columns = far_potential(s, charges, far_op)
    out = []
    for c in range(3):
        acc = jnp.zeros((1, s.bodies), f32)
        for index, r in enumerate(range(0, s.skel, 64)):
            row = lax.broadcasted_iota(jnp.int32, (64, s.bodies), 0) + r
            acc = acc + jnp.sum(jnp.where(cells == row, columns[c][index], 0.0), axis=0, keepdims=True)
        out.append(acc)
    return out


def gather_kernel(s, gat, gh, gl, *refs):
    *messages, _, hi_out, lo_out = refs
    rims = [message[: s.half, :] for message in messages]
    gathered = gat[...] + product(mm, split(unpack_rims(rims, s)), (gh[...], gl[...]))
    hi_out[...], lo_out[...] = split(gathered)


def near_kernel(s, loc, nh, nl, hi, lo, out):
    out[...] = loc[...] + product(mm, (nh[...], nl[...]), (hi[...], lo[...]))


def with_far(s, part, layers, far_op, cells, col):
    values = far_values(s, layers, far_op, cells[0])
    return part[...] + stacked([col * value for value in values], s)


def first_kernel(s, part, far_op, cells, col, *refs):
    *layers, u_out, rim_out, charges_out = refs
    weight_col = col[:, :1]
    u = with_far(s, part, layers, far_op, cells, weight_col)
    u_out[...] = u
    rim_out[...] = pack_rim(u, s)
    charges_out[...] = pack_charges(pieces(u, s), weight_col, occupancy(cells[0], s), s)


def safe_inverse(x):
    return jnp.where(x > 0.0, 1.0 / jnp.where(x > 0.0, x, 1.0), 0.0)


def middle_kernel(s, u_in, f_in, rot, sh, sl, oh, ol, loc_out, gat_out, ortho_out, stat_out):
    u, f = u_in[...], f_in[...]
    loc, gat = local_part(u, s, rot[...], (sh[...], sl[...]), (oh[...], ol[...]))
    loc_out[...] = loc
    gat_out[...] = gat
    ff = total(f * f)
    fu = total(f * u) * safe_inverse(ff)
    ortho = u - fu * f
    ortho_out[...] = ortho
    oo = total(ortho * ortho)
    stat_out[...] = jnp.broadcast_to(
        jnp.concatenate([ff, fu, oo, jnp.zeros((5, 1), f32)], axis=0), (8, LANES)
    )


def second_kernel(
    s, loc, nh, nl, hi, lo, cells, col, f_in, ortho_in, stat, charges_f, charges_u, packed_out
):
    part = loc[...] + product(mm, (nh[...], nl[...]), (hi[...], lo[...]))
    f, ortho = f_in[...], ortho_in[...]
    ff, fu, oo = (stat[i : i + 1, :1] for i in range(3))
    fa = total(f * part) * safe_inverse(ff)
    oa = total(ortho * part) * safe_inverse(oo)
    rest = part - fa * f - oa * ortho
    aa = total(rest * rest)
    rf, ro = jnp.sqrt(ff), jnp.sqrt(oo)
    of_f = charges_f[-8:, :]
    of_u = charges_u[...]
    of_a = pack_charges(pieces(rest, s), col[:, :1], occupancy(cells[0], s), s, count=True)
    row = lax.broadcasted_iota(jnp.int32, (8, LANES), 0)
    lane = lax.broadcasted_iota(jnp.int32, (8, LANES), 1)
    left = lane < RIM
    first = jnp.where(left, of_u, pltpu.roll(of_a, RIM, 1))
    first = jnp.where(row < 4, of_u, first)
    first = jnp.where((row == 7) & left, pltpu.roll(of_f, 1, 0), first)
    for index, value in enumerate((rf, rf * fu, ro, rf * fa, ro * oa, aa)):
        first = jnp.where((row == 3) & (lane == index), value, first)
    tails = jnp.where(left, pltpu.roll(of_f, 3, 0), pltpu.roll(pltpu.roll(of_f, 2, 0), RIM, 1))
    second = jnp.where(row < 3, of_f, of_a)
    second = jnp.where(row < 4, second, pltpu.roll(of_a, 4, 0))
    second = jnp.where(row == 7, tails, second)
    for device in range(s.devices):
        packed_out[device] = second if s.odd(device) else first


def tree(s, leaves, ups, siblings, root):
    def apply(dot, blocks, factor):
        rows = blocks[0].shape[0]
        out = product(dot, split(jnp.concatenate(blocks, axis=0)), factor)
        return [out[i * rows : (i + 1) * rows] for i in range(len(blocks))]

    n = s.skel
    halves = [[(hi[level, j * n : (j + 1) * n, :], lo[level, j * n : (j + 1) * n, :]) for j in range(2)]
              for level, (hi, lo) in ((k, ups) for k in range(s.levels))]
    charges = [leaves]
    for level in range(s.levels):
        low, high = (apply(mm, charges[-1][j::2], halves[level][j]) for j in range(2))
        charges.append([a + b for a, b in zip(low, high)])
    own = charges[-1][0]
    whole = own[:8]
    for column in range(1, s.nx * s.ny):
        whole = whole + own[8 * column : 8 * column + 8]
    others = jnp.concatenate([whole] * (s.nx * s.ny), axis=0) - own
    potential = apply(mm, [others], root)
    for level in reversed(range(s.levels)):
        beside = apply(mm, charges[level], (siblings[0][level], siblings[1][level]))
        down = [apply(mt, potential, halves[level][j]) for j in range(2)]
        potential = [
            down[z % 2][z // 2] + beside[z ^ 1] for z in range(len(charges[level]))
        ]
    return potential


def box_numbers(s, firsts, seconds, ups, siblings, root):
    columns = s.nx * s.ny
    row = lax.broadcasted_iota(jnp.int32, (8, LANES), 0)
    lane = lax.broadcasted_iota(jnp.int32, (8, LANES), 1)
    left, valid = lane < RIM, row < 3
    leaves = []
    for z in range(s.nz):
        wide = []
        for column in range(columns):
            tile = firsts[column * s.nz + z]
            wide.append(jnp.concatenate([tile, pltpu.roll(tile, 4, 0)], axis=1)[:, : s.skel])
        leaves.append(jnp.concatenate(wide, axis=0))
    potential = tree(s, leaves, ups, siblings, root)
    out = []
    for start in range(0, s.devices, 8):
        sums = [jnp.zeros((8, LANES), f32) for _ in range(5)]
        for box in range(start, min(s.devices, start + 8)):
            column, z = box // s.nz, box % s.nz
            phi = potential[z][8 * column : 8 * column + 8]
            main, tail = phi[:, :LANES], phi[:, LANES:]
            tail = jnp.concatenate([tail, tail], axis=1)
            first, second = firsts[box], seconds[box]
            both = pltpu.roll(first, 4, 0) * tail
            of_f = jnp.where(row == 0, pltpu.roll(second, 1, 0), jnp.where(row == 1, pltpu.roll(second, 2, 0), pltpu.roll(first, 3, 0)))
            of_f = jnp.where(left == (row != 1), of_f * tail, 0.0)
            count = jnp.broadcast_to(second[3:4], (8, LANES))
            count_tail = jnp.where(left, 0.0, jnp.broadcast_to(first[7:8], (8, LANES)))
            terms = (
                second * main + of_f,
                first * main + jnp.where(left, both, 0.0),
                pltpu.roll(second, 4, 0) * main + jnp.where(left, 0.0, both),
                count * (main * main) + count_tail * (tail * tail),
            )
            here = row == box - start
            for index, term in enumerate(terms):
                value = jnp.sum(jnp.where(valid, term, 0.0), axis=0, keepdims=True)
                sums[index] = jnp.where(here, value, sums[index])
            sums[4] = jnp.where(here, first[3:4], sums[4])
        numbers = sums[4]
        for index in range(4):
            numbers = jnp.where(lane == 6 + index, jnp.sum(sums[index], axis=1, keepdims=True), numbers)
        out.append(numbers)
    rest = round_up(s.devices, LANES) - 8 * len(out)
    if rest:
        out.append(jnp.zeros((rest, LANES), f32))
    return jnp.concatenate(out, axis=0)


def finish_kernel(s, ids, f_in, u_in, mine, other, col, uh, ul, bh, bl, rh, rl, x_out, lsq_out, raw, sem):
    odd = (ids[0] // s.ny) % 2 == 1
    firsts = [jnp.where(odd, other[box], mine[box]) for box in range(s.devices)]
    seconds = [jnp.where(odd, mine[box], other[box]) for box in range(s.devices)]
    rows = box_numbers(s, firsts, seconds, (uh, ul), (bh, bl), (rh[...], rl[...])).T
    f1, u1, u2, t1, t2, aa, far_f, far_u, far_a, far_far = (rows[i : i + 1] for i in range(10))
    by_f = safe_inverse(f1)
    by_o = jnp.where(u2 * u2 > 1e-10 * (u1 * u1), safe_inverse(u2), 0.0)
    on_one = far_f * by_f
    on_two = (far_u - u1 * by_f * far_f) * by_o
    weight = jnp.sum(col[:, :1] * col[:, :1], axis=0, keepdims=True)
    t3 = aa + 2.0 * far_a + weight * far_far - on_one * on_one - on_two * on_two
    t1, t2, t3 = t1 + on_one, t2 + on_two, jnp.sqrt(jnp.maximum(t3, 0.0))

    def along(x):
        return jnp.sum(x, axis=1, keepdims=True)

    beta = jnp.sqrt(along(f1 * f1) + epsilon)
    v = f1 / beta
    w1, w2 = u1 / beta, u2 / beta
    h11 = along(w1 * v)
    r1 = w1 - h11 * v
    h21 = jnp.sqrt(along(r1 * r1 + w2 * w2) + epsilon)
    b1, b2 = r1 / h21, w2 / h21
    z1, z2, z3 = ((t1 / beta - h11 * w1) / h21, (t2 / beta - h11 * w2) / h21, t3 / beta / h21)
    h12 = along(z1 * v)
    h22 = along(z1 * b1 + z2 * b2)
    d1, d2 = z1 - h12 * v - h22 * b1, z2 - h22 * b2
    h32 = jnp.sqrt(along(d1 * d1 + d2 * d2 + z3 * z3) + epsilon)
    first_norm = jnp.sqrt(h11 * h11 + h21 * h21)
    c1, s1 = h11 / first_norm, h21 / first_norm
    t12, t22 = c1 * h12 + s1 * h22, c1 * h22 - s1 * h12
    second_norm = jnp.sqrt(t22 * t22 + h32 * h32)
    c2, s2 = t22 / second_norm, h32 / second_norm
    g2 = -s1 * beta
    y2 = c2 * g2 / second_norm
    y1 = (c1 * beta - t12 * y2) / first_norm
    lsq_out[...] = jnp.abs(s2 * g2)
    on_u = y2 / h21 / beta
    on_f = y1 / beta - on_u * h11
    for c in range(3):
        part = slice(c * s.step, c * s.step + s.blobs)
        raw[c * s.blobs : (c + 1) * s.blobs, 0, :] = on_f * f_in[part, :] + on_u * u_in[part, :]
    move = pltpu.make_async_copy(raw, x_out, sem)
    move.start()
    move.wait()


def call(kernel, outs, args, scalars=0, far_args=0, far_outs=0, scratch=(), flops=0):
    vmem = pl.BlockSpec(memory_space=pltpu.VMEM)
    smem = pl.BlockSpec(memory_space=pltpu.SMEM)
    hbm = pl.BlockSpec(memory_space=pltpu.HBM)
    near_args = len(args) - far_args
    args = args[:near_args] + [pltpu.with_memory_space_constraint(x, pltpu.HBM) for x in args[near_args:]]
    return pl.pallas_call(
        kernel,
        out_shape=[jax.ShapeDtypeStruct(shape, kind) for shape, kind in outs],
        in_specs=[smem] * scalars + [vmem] * (near_args - scalars) + [hbm] * far_args,
        out_specs=[hbm] * far_outs + [vmem] * (len(outs) - far_outs),
        scratch_shapes=list(scratch),
        compiler_params=pltpu.CompilerParams(vmem_limit_bytes=16 * 2**20),
        cost_estimate=pl.CostEstimate(flops=flops, bytes_accessed=2**20, transcendentals=0),
    )(*args)


def body(
    mesh_shape, rhs, angles, self_mob, near_mat, near_weight, neighbours, cells, blob_weight,
    skel_perm, interp, sibling_ops, root_op,
):
    s = Sizes(mesh_shape, rhs, skel_perm)
    full = (s.rows, s.bodies)
    square = (s.rows, s.rows)
    tile = (8, LANES)
    far_shape = (s.skel, 2 * s.far_tiles * LANES)
    column = lax.axis_index("gx") * s.ny + lax.axis_index("gy")
    ids = jnp.stack([column, lax.axis_index("gz")]).astype(jnp.int32)

    def fetch(x, kind, dy):
        pairs = []
        for gx in range(s.nx):
            for gy in range(s.ny):
                pairs.append((s.beside(kind, gx) * s.ny + (gy + dy) % s.ny, gx * s.ny + gy))
        return lax.ppermute(x, ("gx", "gy"), pairs)

    def fetch_layers(x):
        return [x] + [
            lax.ppermute(x, "gz", [(z ^ k, z) for z in range(s.nz)]) for k in range(1, s.nz)
        ]

    def fetch_rims(rim):
        got = {}
        for dy in s.shifts:
            got["other", dy] = fetch(rim, "other", dy)
        for dy in s.shifts:
            got["same", dy] = fetch(rim, "same", dy)
        got["other", 0] = fetch(rim, "other", 0)
        got["partner", 0] = fetch(rim, "partner", 0)
        return got

    def forward_rims(got, after):
        for dy in s.shifts:
            ready, _ = lax.optimization_barrier((got["same", dy], after))
            got["partner", dy] = fetch(ready, "partner", 0)

    def gather(gat, got, after):
        return call(
            functools.partial(gather_kernel, s),
            [(full, bf16), (full, bf16)],
            [gat, gh, gl] + [got[key] for key in s.sources] + [after],
            flops=10**9,
        )

    def share(message, got, gat, after):
        forward_rims(got, after)
        if s.direct:
            quarter = [message] + [got[key] for key in s.sources if key[0] != "partner"]
            (half,) = call(functools.partial(half_kernel, s), [(tile, f32)], quarter + [after])
            sums = [half, fetch(half, "partner", 0)]
        else:
            half = lax.psum(message[s.half :], ("gx", "gy"))
            sums = [half]
        gathered = gather(gat, got, half)
        (pair,) = call(
            functools.partial(layer_kernel, s), [((2,) + tile, f32)], [message] + sums + [gathered[1]]
        )
        return gathered, fetch_layers(pair)

    def near_part(loc, gathered):
        return call(
            functools.partial(near_kernel, s), [(full, f32)], [loc, nh, nl, *gathered], flops=10**9
        )[0]

    flat = (3 * s.blobs, 1, s.bodies)
    small = (1, s.blobs)
    message, col, cells, f = call(
        functools.partial(start_kernel, s),
        [((s.message, LANES), f32), ((s.step, LANES), f32), (cells.shape, jnp.int32), (full, f32)],
        [rhs.reshape(flat), cells, blob_weight.reshape(small)],
        far_args=3,
        scratch=[pltpu.VMEM(flat, f32), pltpu.VMEM(small, f32), pltpu.SemaphoreType.DMA((3,))],
        flops=10**7,
    )
    got = fetch_rims(message)
    operators = [
        angles.reshape(3, 1, s.bodies), near_weight, neighbours, self_mob, near_mat, skel_perm, interp,
        sibling_ops, root_op,
    ]
    loc, gat, rot, sh, sl, nh, nl, oh, ol, gh, gl, far_op, *operators_out = call(
        functools.partial(setup_kernel, s),
        [(full, f32), (full, f32), ((16, s.bodies), f32)]
        + [(square, bf16)] * 4
        + [((s.bodies, s.bodies), bf16)] * 2
        + [((s.ghosts, s.bodies), bf16)] * 2
        + [(far_shape, f32)]
        + [((s.levels, 2 * s.skel, s.skel), bf16)] * 2
        + [((s.levels, s.skel, s.skel), bf16)] * 2
        + [((s.skel, s.skel), bf16)] * 2,
        [ids, f] + operators,
        scalars=1,
        far_args=len(operators),
        scratch=[pltpu.VMEM(square, f32), pltpu.VMEM((s.levels, 2 * s.skel, s.skel), f32)]
        + [pltpu.VMEM(x.shape, x.dtype) for x in operators]
        + [pltpu.SemaphoreType.DMA((len(operators),))],
        flops=5 * 10**9,
    )
    gathered, layers = share(message, got, gat, rot)
    part = near_part(loc, gathered)
    u, rim, charges = call(
        functools.partial(first_kernel, s),
        [(full, f32), ((s.half, LANES), f32), (tile, f32)],
        [part, far_op, cells, col, *layers],
        flops=10**8,
    )
    got = fetch_rims(rim)
    loc, gat, ortho, stat = call(
        functools.partial(middle_kernel, s),
        [(full, f32), (full, f32), (full, f32), (tile, f32)],
        [u, f, rot, sh, sl, oh, ol],
        flops=10**9,
    )
    forward_rims(got, stat)
    gathered = gather(gat, got, stat)
    (packed,) = call(
        functools.partial(second_kernel, s),
        [((s.devices, 8, LANES), f32)],
        [loc, nh, nl, *gathered, cells, col, f, ortho, stat, message, charges],
        flops=10**9,
    )
    boxes = lax.all_to_all(packed, ("gx", "gy", "gz"), 0, 0)
    result, lsq = call(
        functools.partial(finish_kernel, s),
        [(flat, f32), ((1, 1), f32)],
        [ids, f, u, boxes, fetch(boxes, "partner", 0), col, *operators_out],
        scalars=1,
        far_outs=1,
        scratch=[pltpu.VMEM(flat, f32), pltpu.SemaphoreType.DMA],
        flops=10**7,
    )
    return result.reshape(rhs.shape), lsq.reshape(())


def solution(mesh):
    in_specs = (
        P("gx", "gy", None, None, "gz"),
        P("gx", "gy", None, "gz"),
        P(),
        P(),
        P("gx", "gy", None, "gz"),
        P("gx", "gy", None, "gz"),
        P("gx", "gy", "gz"),
        P(),
        P(),
        P(),
        P(),
        P(),
    )
    out_specs = (P("gx", "gy", None, None, "gz"), P())
    inner = functools.partial(body, dict(mesh.shape))
    return jax.shard_map(inner, mesh=mesh, in_specs=in_specs, out_specs=out_specs, check_vma=False)
```

```python
import functools

import jax
import jax.numpy as jnp
from jax import lax
from jax.experimental import pallas as pl
from jax.experimental.pallas import tpu as pltpu
from jax.sharding import PartitionSpec as P

epsilon = 1e-06
f32 = jnp.float32
bf16 = jnp.bfloat16
RIM = 64
LANES = 128


def round_up(value, unit):
    return -(-value // unit) * unit


def split(x):
    hi = x.astype(bf16)
    lo = (x - hi.astype(f32)).astype(bf16)
    return hi, lo


def mm(a, b):
    return lax.dot_general(a, b, (((1,), (0,)), ((), ())), preferred_element_type=f32)


def mt(a, b):
    return lax.dot_general(a, b, (((1,), (1,)), ((), ())), preferred_element_type=f32)


def product(dot, a, b):
    return dot(a[0], b[0]) + (dot(a[0], b[1]) + dot(a[1], b[0]))


def total(x):
    return jnp.sum(jnp.sum(x, axis=0, keepdims=True), axis=1, keepdims=True)


class Sizes:
    def __init__(self, mesh_shape, rhs, skel_perm):
        self.nx, self.ny, self.nz = (mesh_shape[a] for a in ("gx", "gy", "gz"))
        self.devices = self.nx * self.ny * self.nz
        self.blobs, self.bodies = rhs.shape[-2:]
        self.step = round_up(self.blobs, 8)
        self.rows = round_up(3 * self.step, 16)
        self.half = self.rows // 2
        self.message = self.half + 8
        self.direct = (self.nx, self.ny) == (4, 2)
        self.levels = skel_perm.shape[0]
        self.skel = skel_perm.shape[1] // 2
        shifts = sorted({(dy % self.ny) for dy in (-1, 1)} - {0})
        self.shifts = shifts
        self.sources = [("same", dy) for dy in shifts]
        for kind in ("other", "partner"):
            self.sources += [(kind, dy) for dy in [0] + shifts]
        self.ghosts = round_up(len(self.sources) * RIM, LANES)
        self.far_tiles = self.nz + -(-self.nz // 2)

    def slot_start(self, slot, parity):
        dx, dy = slot // 3 - 1, (slot % 3 - 1) % self.ny
        kind = "same" if dx == 0 else "partner" if dx == 1 - 2 * parity else "other"
        if (kind, dy) == ("same", 0):
            return 0
        return self.bodies + RIM * self.sources.index((kind, dy))

    def odd(self, device):
        return (device // (self.ny * self.nz)) % 2

    def beside(self, kind, x):
        if kind == "same":
            return x
        if kind == "partner":
            return x ^ 1
        return (x + 2 * (x % 2) - 1) % self.nx


def pieces(x, s):
    return [x[c * s.step : c * s.step + s.step] for c in range(3)]


def turn(parts, rot, inverse):
    out = []
    for target in range(3):
        acc = None
        for source in range(3):
            row = 3 * source + target if inverse else 3 * target + source
            term = rot[row : row + 1] * parts[source]
            acc = term if acc is None else acc + term
        out.append(acc)
    return out


def stacked(parts, s):
    rest = s.rows - 3 * s.step
    if rest:
        parts = list(parts) + [jnp.zeros((rest, s.bodies), f32)]
    return jnp.concatenate(parts, axis=0)


def occupancy(cells, s):
    row = lax.broadcasted_iota(jnp.int32, (s.skel, s.bodies), 0)
    return jnp.where(cells == row, 1.0, 0.0).astype(bf16)


def pack_charges(parts, weight_col, occ, s, count=False):
    moments = [jnp.sum(part * weight_col, axis=0, keepdims=True) for part in parts]
    moments.append(jnp.full((1, s.bodies), 1.0 if count else 0.0, f32))
    moments = jnp.concatenate(moments + [jnp.zeros((4, s.bodies), f32)], axis=0)
    high, rest = split(moments)
    mid, low = split(moments - high.astype(f32))
    stack = jnp.concatenate([high.astype(f32), mid.astype(f32), low.astype(f32)], axis=0).astype(bf16)
    sums = mt(stack, occ)
    charges = sums[0:8] + (sums[8:16] + sums[16:24])
    tail = jnp.concatenate([charges[:, LANES:], jnp.zeros((8, 2 * LANES - s.skel), f32)], axis=1)
    row = lax.broadcasted_iota(jnp.int32, (8, LANES), 0)
    return jnp.where(row < 4, charges[:, :LANES], pltpu.roll(tail, 4, 0))


def pack_rim(x, s):
    lane = lax.broadcasted_iota(jnp.int32, (s.half, LANES), 1)
    top, bottom = x[: s.half, :LANES], x[s.half :, :LANES]
    return jnp.where(lane < RIM, top, pltpu.roll(bottom, RIM, 1))


def unpack_rims(rims, s):
    lane = lax.broadcasted_iota(jnp.int32, (s.half, LANES), 1)
    tops, bottoms = [], []
    for i in range(0, s.ghosts // RIM, 2):
        a = rims[i]
        b = rims[i + 1] if i + 1 < len(rims) else jnp.zeros_like(a)
        tops.append(jnp.where(lane < RIM, a, pltpu.roll(b, RIM, 1)))
        bottoms.append(jnp.where(lane < RIM, pltpu.roll(a, RIM, 1), b))
    return jnp.concatenate(
        [jnp.concatenate(tops, axis=1), jnp.concatenate(bottoms, axis=1)], axis=0
    )


def pack_message(x, weight_col, cells, s):
    charges = pack_charges(pieces(x, s), weight_col, occupancy(cells, s), s)
    return jnp.concatenate([pack_rim(x, s), charges], axis=0)


def begin(sources, targets, sems):
    moves = [pltpu.make_async_copy(a, b, sems.at[i]) for i, (a, b) in enumerate(zip(sources, targets))]
    for move in moves:
        move.start()
    return moves


def start_kernel(s, rhs, cells, weight, message_out, col_out, cells_out, f_out, raw, wide, sems):
    moves = begin((weight, cells, rhs), (wide, cells_out, raw), sems)
    f_out[...] = jnp.zeros_like(f_out)
    moves[0].wait()
    row = jnp.concatenate([wide[...], jnp.zeros((1, 2 * LANES - s.blobs), f32)], axis=1)
    col = jnp.broadcast_to(row, (LANES, 2 * LANES)).T[: s.step]
    col_out[...] = col
    for move in moves[1:]:
        move.wait()
    for c in range(3):
        f_out[c * s.step : c * s.step + s.blobs, :] = raw[c * s.blobs : (c + 1) * s.blobs, 0, :]
    message_out[...] = pack_message(f_out[...], col[:, :1], cells_out[0], s)


def frame_rows(angles):
    cos, sin = jnp.cos(angles), jnp.sin(angles)
    cy, cp, cr = cos[0:1], cos[1:2], cos[2:3]
    sy, sp, sr = sin[0:1], sin[1:2], sin[2:3]
    return [
        cy * cp,
        cy * sp * sr - sy * cr,
        cy * sp * cr + sy * sr,
        sy * cp,
        sy * sp * sr + cy * cr,
        sy * sp * cr - cy * sr,
        -sp,
        cp * sr,
        cp * cr,
    ]


def local_part(f, s, rot, mob, own):
    parts = pieces(f, s)
    turned = stacked(turn(parts, rot, False), s)
    mixed = product(mm, mob, split(turned))
    back = turn(pieces(mixed, s), rot, True)
    return f + stacked(back, s), product(mm, split(f), own)


def product_many(dot, blocks, b):
    rows = blocks[0].shape[0]
    out = product(dot, split(jnp.concatenate(blocks, axis=0)), split(b))
    return [out[i * rows : (i + 1) * rows] for i in range(len(blocks))]


def expand_once(groups, halves):
    flat = [block for group in groups for block in group]
    sides = [product_many(mt, flat, half) for half in halves]
    out, at = [], 0
    for group in groups:
        spread = []
        for i in range(at, at + len(group)):
            spread += [sides[0][i], sides[1][i]]
        at += len(group)
        out.append(spread)
    return out


def setup_kernel(s, ids, f_in, *refs):
    sources, tree, outs, (padded, *copies, sems) = refs[:9], refs[9:13], refs[13:24], refs[24:]
    moves = begin(sources, (*copies, *tree), sems)
    setup(s, ids, f_in, moves[:5], *copies, *outs, padded)
    for move in moves[5:]:
        move.wait()


def setup(
    s, ids, f_in, moves, angles, near_weight, neighbours, self_mob, near_mat,
    loc_out, gat_out, rot_out, sh_out, sl_out, nh_out, nl_out, oh_out, ol_out, gh_out, gl_out, padded,
):
    f = f_in[...]
    for move in moves[:3]:
        move.wait()
    rot = jnp.concatenate(frame_rows(angles[:, 0, :]) + [jnp.zeros((7, s.bodies), f32)], axis=0)
    rot_out[...] = rot

    links = neighbours[0, 0]
    slot = links // s.bodies
    base = jnp.zeros_like(links)
    odd = (ids[0] // s.ny) % 2
    for index in range(9):
        start = jnp.where(odd == 1, s.slot_start(index, 1), s.slot_start(index, 0))
        base = jnp.where(slot == index, start, base)
    column = base + links % s.bodies
    coef = near_weight[0, 0]
    for first, count, hi_out, lo_out in (
        (0, s.bodies, oh_out, ol_out),
        (s.bodies, s.ghosts, gh_out, gl_out),
    ):
        for r in range(0, count, 64):
            row = lax.broadcasted_iota(jnp.int32, (64, s.bodies), 0) + (first + r)
            acc = jnp.zeros((64, s.bodies), f32)
            for k in range(coef.shape[0]):
                acc = acc + jnp.where(column[k : k + 1] == row, coef[k : k + 1], 0.0)
            hi, lo = split(acc)
            hi_out[r : r + 64, :] = hi
            lo_out[r : r + 64, :] = lo

    for move in moves[3:]:
        move.wait()
    padded[...] = jnp.zeros_like(padded)
    for matrix, hi_out, lo_out in ((self_mob, sh_out, sl_out), (near_mat, nh_out, nl_out)):
        for c in range(3):
            for d in range(3):
                padded[c * s.step : c * s.step + s.blobs, d * s.step : d * s.step + s.blobs] = matrix[
                    c * s.blobs : (c + 1) * s.blobs, d * s.blobs : (d + 1) * s.blobs
                ]
        hi, lo = split(padded[...])
        hi_out[...] = hi
        lo_out[...] = lo

    loc, gat = local_part(f, s, rot, (sh_out[...], sl_out[...]), (oh_out[...], ol_out[...]))
    loc_out[...] = loc
    gat_out[...] = gat


def far_kernel(
    s, ids, perm, interp, sibling, root, _, far_out, uh_out, ul_out, bh_out, bl_out, rh_out, rl_out, ups_ref
):
    n = s.skel
    z = ids[1]
    halves = []
    spot = lax.broadcasted_iota(jnp.int32, (2 * n, n), 0)
    for level in range(s.levels):
        kept = jnp.where(perm[level : level + 1, :n] == spot, 1.0, 0.0)
        moved = jnp.where(perm[level : level + 1, n:] == spot, 1.0, 0.0).astype(bf16)
        hi, lo = split(interp[level])
        up = kept + (mm(moved, hi) + mm(moved, lo))
        ups_ref[level] = up
        uh_out[level], ul_out[level] = split(up)
        bh_out[level], bl_out[level] = split(sibling[level])
        bit = (z >> level) & 1
        halves.append(
            [ups_ref[level, pl.ds(pl.multiple_of(side * n, 8), n), :] for side in (bit, 1 - bit)]
        )

    def down(block, level, dot):
        return product(dot, split(halves[level][0]), split(block))

    spread = root[...]
    rh_out[...], rl_out[...] = split(spread)
    beside = []
    for level in reversed(range(s.levels)):
        spread = down(spread, level, mt if level == s.levels - 1 else mm)
        beside = [(down(block, level, mt if fresh else mm), False) for block, fresh in beside]
        beside.append((sibling[level], True))
    beside = [block.T if fresh else block for block, fresh in reversed(beside)]
    leaves = [[spread]]
    for level in reversed(range(s.levels)):
        leaves = expand_once(leaves, halves[level])
        leaves.append([beside[level]])
    far_leaves, *sub = leaves
    near_leaves = [jnp.zeros((n, n), f32)]
    for blocks in reversed(sub):
        near_leaves += blocks
    tail = n - LANES
    far_out[...] = jnp.zeros_like(far_out)
    own = [a - b for a, b in zip(near_leaves, far_leaves)]
    for group, blocks in enumerate((own, far_leaves)):
        for leaf, block in enumerate(blocks):
            at = (group * s.far_tiles + leaf) * LANES
            far_out[:, at : at + LANES] = block[:, :LANES]
            at = (group * s.far_tiles + s.nz + leaf // 2) * LANES + leaf % 2 * RIM
            far_out[:, at : at + tail] = block[:, LANES:]


def half_kernel(s, *refs):
    *messages, _, out = refs
    acc = messages[0][s.half :, :]
    for message in messages[1:]:
        acc = acc + message[s.half :, :]
    out[...] = acc


def layer_kernel(s, message, *refs):
    *sums, out = refs
    acc = sums[0][...]
    for part in sums[1:]:
        acc = acc + part[...]
    out[0] = message[s.half :, :]
    out[1] = acc


def join_kernel(x, y, _, out):
    out[: x.shape[0]] = x[...]
    out[x.shape[0] :] = y[...]


def order_kernel(x, *refs):
    refs[-1][...] = x[...]


def far_potential(s, charges, far_op):
    rows = []
    for group in range(2):
        tiles = [layer[2 * k + group] for layer in charges for k in range(layer.shape[0] // 2)]
        rows += tiles
        for leaf in range(0, s.nz, 2):
            pair = tiles[leaf]
            if leaf + 1 < s.nz:
                lane = lax.broadcasted_iota(jnp.int32, (8, LANES), 1)
                pair = jnp.where(lane < RIM, pair, pltpu.roll(tiles[leaf + 1], RIM, 1))
            rows.append(pltpu.roll(pair, 4, 0))
    columns = [[], [], []]
    for r in range(0, s.skel, 64):
        acc = [None] * 3
        for index, row in enumerate(rows):
            block = far_op[r : r + 64, index * LANES : (index + 1) * LANES]
            for c in range(3):
                term = block * row[c : c + 1]
                acc[c] = term if acc[c] is None else acc[c] + term
        for c in range(3):
            columns[c].append(jnp.sum(acc[c], axis=1, keepdims=True))
    return columns


def far_values(s, charges, far_op, cells):
    columns = far_potential(s, charges, far_op)
    out = []
    for c in range(3):
        acc = jnp.zeros((1, s.bodies), f32)
        for index, r in enumerate(range(0, s.skel, 64)):
            row = lax.broadcasted_iota(jnp.int32, (64, s.bodies), 0) + r
            acc = acc + jnp.sum(jnp.where(cells == row, columns[c][index], 0.0), axis=0, keepdims=True)
        out.append(acc)
    return out


def gather_kernel(s, gat, gh, gl, *refs):
    *messages, _, hi_out, lo_out = refs
    rims = [message[: s.half, :] for message in messages]
    gathered = gat[...] + product(mm, split(unpack_rims(rims, s)), (gh[...], gl[...]))
    hi_out[...], lo_out[...] = split(gathered)


def near_kernel(s, loc, nh, nl, hi, lo, out):
    out[...] = loc[...] + product(mm, (nh[...], nl[...]), (hi[...], lo[...]))


def with_far(s, part, layers, far_op, cells, col):
    values = far_values(s, layers, far_op, cells[0])
    return part[...] + stacked([col * value for value in values], s)


def first_kernel(s, part, far_op, cells, col, *refs):
    *layers, u_out, rim_out, charges_out = refs
    weight_col = col[:, :1]
    u = with_far(s, part, layers, far_op, cells, weight_col)
    u_out[...] = u
    rim_out[...] = pack_rim(u, s)
    charges_out[...] = pack_charges(pieces(u, s), weight_col, occupancy(cells[0], s), s)


def safe_inverse(x):
    return jnp.where(x > 0.0, 1.0 / jnp.where(x > 0.0, x, 1.0), 0.0)


def middle_kernel(s, u_in, f_in, rot, sh, sl, oh, ol, loc_out, gat_out, ortho_out, stat_out):
    u, f = u_in[...], f_in[...]
    loc, gat = local_part(u, s, rot[...], (sh[...], sl[...]), (oh[...], ol[...]))
    loc_out[...] = loc
    gat_out[...] = gat
    ff = total(f * f)
    fu = total(f * u) * safe_inverse(ff)
    ortho = u - fu * f
    ortho_out[...] = ortho
    oo = total(ortho * ortho)
    stat_out[...] = jnp.broadcast_to(
        jnp.concatenate([ff, fu, oo, jnp.zeros((5, 1), f32)], axis=0), (8, LANES)
    )


def second_kernel(
    s, loc, nh, nl, hi, lo, cells, col, f_in, ortho_in, stat, charges_f, charges_u, packed_out
):
    part = loc[...] + product(mm, (nh[...], nl[...]), (hi[...], lo[...]))
    f, ortho = f_in[...], ortho_in[...]
    ff, fu, oo = (stat[i : i + 1, :1] for i in range(3))
    fa = total(f * part) * safe_inverse(ff)
    oa = total(ortho * part) * safe_inverse(oo)
    rest = part - fa * f - oa * ortho
    aa = total(rest * rest)
    rf, ro = jnp.sqrt(ff), jnp.sqrt(oo)
    of_f = charges_f[-8:, :]
    of_u = charges_u[...]
    of_a = pack_charges(pieces(rest, s), col[:, :1], occupancy(cells[0], s), s, count=True)
    row = lax.broadcasted_iota(jnp.int32, (8, LANES), 0)
    lane = lax.broadcasted_iota(jnp.int32, (8, LANES), 1)
    left = lane < RIM
    first = jnp.where(left, of_u, pltpu.roll(of_a, RIM, 1))
    first = jnp.where(row < 4, of_u, first)
    first = jnp.where((row == 7) & left, pltpu.roll(of_f, 1, 0), first)
    for index, value in enumerate((rf, rf * fu, ro, rf * fa, ro * oa, aa)):
        first = jnp.where((row == 3) & (lane == index), value, first)
    tails = jnp.where(left, pltpu.roll(of_f, 3, 0), pltpu.roll(pltpu.roll(of_f, 2, 0), RIM, 1))
    second = jnp.where(row < 3, of_f, of_a)
    second = jnp.where(row < 4, second, pltpu.roll(of_a, 4, 0))
    second = jnp.where(row == 7, tails, second)
    for device in range(s.devices):
        packed_out[device] = second if s.odd(device) else first


def tree(s, leaves, ups, siblings, root):
    def apply(dot, blocks, factor):
        rows = blocks[0].shape[0]
        out = product(dot, split(jnp.concatenate(blocks, axis=0)), factor)
        return [out[i * rows : (i + 1) * rows] for i in range(len(blocks))]

    n = s.skel
    halves = [[(hi[level, j * n : (j + 1) * n, :], lo[level, j * n : (j + 1) * n, :]) for j in range(2)]
              for level, (hi, lo) in ((k, ups) for k in range(s.levels))]
    charges = [leaves]
    for level in range(s.levels):
        low, high = (apply(mm, charges[-1][j::2], halves[level][j]) for j in range(2))
        charges.append([a + b for a, b in zip(low, high)])
    own = charges[-1][0]
    whole = own[:8]
    for column in range(1, s.nx * s.ny):
        whole = whole + own[8 * column : 8 * column + 8]
    others = jnp.concatenate([whole] * (s.nx * s.ny), axis=0) - own
    potential = apply(mm, [others], root)
    for level in reversed(range(s.levels)):
        beside = apply(mm, charges[level], (siblings[0][level], siblings[1][level]))
        down = [apply(mt, potential, halves[level][j]) for j in range(2)]
        potential = [
            down[z % 2][z // 2] + beside[z ^ 1] for z in range(len(charges[level]))
        ]
    return potential


def box_numbers(s, firsts, seconds, ups, siblings, root):
    columns = s.nx * s.ny
    row = lax.broadcasted_iota(jnp.int32, (8, LANES), 0)
    lane = lax.broadcasted_iota(jnp.int32, (8, LANES), 1)
    left, valid = lane < RIM, row < 3
    leaves = []
    for z in range(s.nz):
        wide = []
        for column in range(columns):
            tile = firsts[column * s.nz + z]
            wide.append(jnp.concatenate([tile, pltpu.roll(tile, 4, 0)], axis=1)[:, : s.skel])
        leaves.append(jnp.concatenate(wide, axis=0))
    potential = tree(s, leaves, ups, siblings, root)
    out = []
    for start in range(0, s.devices, 8):
        sums = [jnp.zeros((8, LANES), f32) for _ in range(5)]
        for box in range(start, min(s.devices, start + 8)):
            column, z = box // s.nz, box % s.nz
            phi = potential[z][8 * column : 8 * column + 8]
            main, tail = phi[:, :LANES], phi[:, LANES:]
            tail = jnp.concatenate([tail, tail], axis=1)
            first, second = firsts[box], seconds[box]
            both = pltpu.roll(first, 4, 0) * tail
            of_f = jnp.where(row == 0, pltpu.roll(second, 1, 0), jnp.where(row == 1, pltpu.roll(second, 2, 0), pltpu.roll(first, 3, 0)))
            of_f = jnp.where(left == (row != 1), of_f * tail, 0.0)
            count = jnp.broadcast_to(second[3:4], (8, LANES))
            count_tail = jnp.where(left, 0.0, jnp.broadcast_to(first[7:8], (8, LANES)))
            terms = (
                second * main + of_f,
                first * main + jnp.where(left, both, 0.0),
                pltpu.roll(second, 4, 0) * main + jnp.where(left, 0.0, both),
                count * (main * main) + count_tail * (tail * tail),
            )
            here = row == box - start
            for index, term in enumerate(terms):
                value = jnp.sum(jnp.where(valid, term, 0.0), axis=0, keepdims=True)
                sums[index] = jnp.where(here, value, sums[index])
            sums[4] = jnp.where(here, first[3:4], sums[4])
        numbers = sums[4]
        for index in range(4):
            numbers = jnp.where(lane == 6 + index, jnp.sum(sums[index], axis=1, keepdims=True), numbers)
        out.append(numbers)
    rest = round_up(s.devices, LANES) - 8 * len(out)
    if rest:
        out.append(jnp.zeros((rest, LANES), f32))
    return jnp.concatenate(out, axis=0)


def finish_kernel(s, ids, f_in, u_in, mine, other, col, uh, ul, bh, bl, rh, rl, x_out, lsq_out, raw, sem):
    odd = (ids[0] // s.ny) % 2 == 1
    firsts = [jnp.where(odd, other[box], mine[box]) for box in range(s.devices)]
    seconds = [jnp.where(odd, mine[box], other[box]) for box in range(s.devices)]
    rows = box_numbers(s, firsts, seconds, (uh, ul), (bh, bl), (rh[...], rl[...])).T
    f1, u1, u2, t1, t2, aa, far_f, far_u, far_a, far_far = (rows[i : i + 1] for i in range(10))
    by_f = safe_inverse(f1)
    by_o = jnp.where(u2 * u2 > 1e-10 * (u1 * u1), safe_inverse(u2), 0.0)
    on_one = far_f * by_f
    on_two = (far_u - u1 * by_f * far_f) * by_o
    weight = jnp.sum(col[:, :1] * col[:, :1], axis=0, keepdims=True)
    t3 = aa + 2.0 * far_a + weight * far_far - on_one * on_one - on_two * on_two
    t1, t2, t3 = t1 + on_one, t2 + on_two, jnp.sqrt(jnp.maximum(t3, 0.0))

    def along(x):
        return jnp.sum(x, axis=1, keepdims=True)

    beta = jnp.sqrt(along(f1 * f1) + epsilon)
    v = f1 / beta
    w1, w2 = u1 / beta, u2 / beta
    h11 = along(w1 * v)
    r1 = w1 - h11 * v
    h21 = jnp.sqrt(along(r1 * r1 + w2 * w2) + epsilon)
    b1, b2 = r1 / h21, w2 / h21
    z1, z2, z3 = ((t1 / beta - h11 * w1) / h21, (t2 / beta - h11 * w2) / h21, t3 / beta / h21)
    h12 = along(z1 * v)
    h22 = along(z1 * b1 + z2 * b2)
    d1, d2 = z1 - h12 * v - h22 * b1, z2 - h22 * b2
    h32 = jnp.sqrt(along(d1 * d1 + d2 * d2 + z3 * z3) + epsilon)
    first_norm = jnp.sqrt(h11 * h11 + h21 * h21)
    c1, s1 = h11 / first_norm, h21 / first_norm
    t12, t22 = c1 * h12 + s1 * h22, c1 * h22 - s1 * h12
    second_norm = jnp.sqrt(t22 * t22 + h32 * h32)
    c2, s2 = t22 / second_norm, h32 / second_norm
    g2 = -s1 * beta
    y2 = c2 * g2 / second_norm
    y1 = (c1 * beta - t12 * y2) / first_norm
    lsq_out[...] = jnp.abs(s2 * g2)
    on_u = y2 / h21 / beta
    on_f = y1 / beta - on_u * h11
    for c in range(3):
        part = slice(c * s.step, c * s.step + s.blobs)
        raw[c * s.blobs : (c + 1) * s.blobs, 0, :] = on_f * f_in[part, :] + on_u * u_in[part, :]
    move = pltpu.make_async_copy(raw, x_out, sem)
    move.start()
    move.wait()


def call(kernel, outs, args, scalars=0, far_args=0, far_outs=0, scratch=(), flops=0):
    vmem = pl.BlockSpec(memory_space=pltpu.VMEM)
    smem = pl.BlockSpec(memory_space=pltpu.SMEM)
    hbm = pl.BlockSpec(memory_space=pltpu.HBM)
    near_args = len(args) - far_args
    args = args[:near_args] + [pltpu.with_memory_space_constraint(x, pltpu.HBM) for x in args[near_args:]]
    return pl.pallas_call(
        kernel,
        out_shape=[jax.ShapeDtypeStruct(shape, kind) for shape, kind in outs],
        in_specs=[smem] * scalars + [vmem] * (near_args - scalars) + [hbm] * far_args,
        out_specs=[hbm] * far_outs + [vmem] * (len(outs) - far_outs),
        scratch_shapes=list(scratch),
        compiler_params=pltpu.CompilerParams(vmem_limit_bytes=16 * 2**20),
        cost_estimate=pl.CostEstimate(flops=flops, bytes_accessed=2**20, transcendentals=0),
    )(*args)


def body(
    mesh_shape, rhs, angles, self_mob, near_mat, near_weight, neighbours, cells, blob_weight,
    skel_perm, interp, sibling_ops, root_op,
):
    s = Sizes(mesh_shape, rhs, skel_perm)
    full = (s.rows, s.bodies)
    square = (s.rows, s.rows)
    tile = (8, LANES)
    far_shape = (s.skel, 2 * s.far_tiles * LANES)
    column = lax.axis_index("gx") * s.ny + lax.axis_index("gy")
    ids = jnp.stack([column, lax.axis_index("gz")]).astype(jnp.int32)

    def fetch(x, kind, dy):
        pairs = []
        for gx in range(s.nx):
            for gy in range(s.ny):
                pairs.append((s.beside(kind, gx) * s.ny + (gy + dy) % s.ny, gx * s.ny + gy))
        return lax.ppermute(x, ("gx", "gy"), pairs)

    def fetch_rims(rim):
        got = {}
        for dy in s.shifts:
            got["other", dy] = fetch(rim, "other", dy)
        for dy in s.shifts:
            got["same", dy] = fetch(rim, "same", dy)
        got["other", 0] = fetch(rim, "other", 0)
        got["partner", 0] = fetch(rim, "partner", 0)
        return got

    def forward_rims(got, after):
        for dy in s.shifts:
            held = got["same", dy]
            (held,) = call(order_kernel, [(held.shape, f32)], [held, got["other", dy], after])
            got["partner", dy] = fetch(held, "partner", 0)

    def gather(gat, got, after):
        return call(
            functools.partial(gather_kernel, s),
            [(full, bf16), (full, bf16)],
            [gat, gh, gl] + [got[key] for key in s.sources] + [after],
            flops=10**9,
        )

    def plane_pair(message, got, after):
        if s.direct:
            quarter = [message] + [got[key] for key in s.sources if key[0] != "partner"]
            (half,) = call(functools.partial(half_kernel, s), [(tile, f32)], quarter + [after])
            sums = [half, fetch(half, "partner", 0)]
        else:
            sums = [lax.psum(message[s.half :], ("gx", "gy"))]
        return call(functools.partial(layer_kernel, s), [((2,) + tile, f32)], [message] + sums)[0]

    def swap_layers(x, k):
        return lax.ppermute(x, "gz", [(z ^ k, z) for z in range(s.nz)])

    def join(x, y, after):
        shape = (2 * x.shape[0],) + tile
        return call(join_kernel, [(shape, f32)], [x, y, after])[0]

    def near_part(loc, gathered):
        return call(
            functools.partial(near_kernel, s), [(full, f32)], [loc, nh, nl, *gathered], flops=10**9
        )[0]

    flat = (3 * s.blobs, 1, s.bodies)
    small = (1, s.blobs)
    message, col, cells, f = call(
        functools.partial(start_kernel, s),
        [((s.message, LANES), f32), ((s.step, LANES), f32), (cells.shape, jnp.int32), (full, f32)],
        [rhs.reshape(flat), cells, blob_weight.reshape(small)],
        far_args=3,
        scratch=[pltpu.VMEM(flat, f32), pltpu.VMEM(small, f32), pltpu.SemaphoreType.DMA((3,))],
        flops=10**7,
    )
    got = fetch_rims(message)
    tree_in = [skel_perm, interp, sibling_ops, root_op]
    operators = [angles.reshape(3, 1, s.bodies), near_weight, neighbours, self_mob, near_mat]
    *tree_in, loc, gat, rot, sh, sl, nh, nl, oh, ol, gh, gl = call(
        functools.partial(setup_kernel, s),
        [(x.shape, x.dtype) for x in tree_in]
        + [(full, f32), (full, f32), ((16, s.bodies), f32)]
        + [(square, bf16)] * 4
        + [((s.bodies, s.bodies), bf16)] * 2
        + [((s.ghosts, s.bodies), bf16)] * 2,
        [ids, f] + operators + tree_in,
        scalars=1,
        far_args=9,
        scratch=[pltpu.VMEM(square, f32)]
        + [pltpu.VMEM(x.shape, x.dtype) for x in operators]
        + [pltpu.SemaphoreType.DMA((9,))],
        flops=4 * 10**9,
    )
    forward_rims(got, rot)
    layers = [plane_pair(message, got, rot)]
    held = layers[0]
    layers.append(swap_layers(held, 1))
    far_op, *operators_out = call(
        functools.partial(far_kernel, s),
        [(far_shape, f32)]
        + [((s.levels, 2 * s.skel, s.skel), bf16)] * 2
        + [((s.levels, s.skel, s.skel), bf16)] * 2
        + [((s.skel, s.skel), bf16)] * 2,
        [ids, *tree_in, held],
        scalars=1,
        scratch=[pltpu.VMEM((s.levels, 2 * s.skel, s.skel), f32)],
        flops=2 * 10**9,
    )
    for level in range(1, s.levels):
        held = join(held, layers[-1], far_op)
        layers.append(swap_layers(held, 1 << level))
    gathered = gather(gat, got, held)
    part = near_part(loc, gathered)
    u, rim, charges = call(
        functools.partial(first_kernel, s),
        [(full, f32), ((s.half, LANES), f32), (tile, f32)],
        [part, far_op, cells, col, *layers],
        flops=10**8,
    )
    got = fetch_rims(rim)
    loc, gat, ortho, stat = call(
        functools.partial(middle_kernel, s),
        [(full, f32), (full, f32), (full, f32), (tile, f32)],
        [u, f, rot, sh, sl, oh, ol],
        flops=10**9,
    )
    forward_rims(got, stat)
    gathered = gather(gat, got, stat)
    (packed,) = call(
        functools.partial(second_kernel, s),
        [((s.devices, 8, LANES), f32)],
        [loc, nh, nl, *gathered, cells, col, f, ortho, stat, message, charges],
        flops=10**9,
    )
    boxes = lax.all_to_all(packed, ("gx", "gy", "gz"), 0, 0)
    result, lsq = call(
        functools.partial(finish_kernel, s),
        [(flat, f32), ((1, 1), f32)],
        [ids, f, u, boxes, fetch(boxes, "partner", 0), col, *operators_out],
        scalars=1,
        far_outs=1,
        scratch=[pltpu.VMEM(flat, f32), pltpu.SemaphoreType.DMA],
        flops=10**7,
    )
    return result.reshape(rhs.shape), lsq.reshape(())


def solution(mesh):
    in_specs = (
        P("gx", "gy", None, None, "gz"),
        P("gx", "gy", None, "gz"),
        P(),
        P(),
        P("gx", "gy", None, "gz"),
        P("gx", "gy", None, "gz"),
        P("gx", "gy", "gz"),
        P(),
        P(),
        P(),
        P(),
        P(),
    )
    out_specs = (P("gx", "gy", None, None, "gz"), P())
    inner = functools.partial(body, dict(mesh.shape))
    return jax.shard_map(inner, mesh=mesh, in_specs=in_specs, out_specs=out_specs, check_vma=False)
```

```python
import functools

import jax
import jax.numpy as jnp
from jax import lax
from jax.experimental import pallas as pl
from jax.experimental.pallas import tpu as pltpu
from jax.sharding import PartitionSpec as P

epsilon = 1e-06
f32 = jnp.float32
bf16 = jnp.bfloat16
RIM = 64
LANES = 128


def round_up(value, unit):
    return -(-value // unit) * unit


def split(x):
    hi = x.astype(bf16)
    lo = (x - hi.astype(f32)).astype(bf16)
    return hi, lo


def mm(a, b):
    return lax.dot_general(a, b, (((1,), (0,)), ((), ())), preferred_element_type=f32)


def mt(a, b):
    return lax.dot_general(a, b, (((1,), (1,)), ((), ())), preferred_element_type=f32)


def product(dot, a, b):
    return dot(a[0], b[0]) + (dot(a[0], b[1]) + dot(a[1], b[0]))


def total(x):
    return jnp.sum(jnp.sum(x, axis=0, keepdims=True), axis=1, keepdims=True)


class Sizes:
    def __init__(self, mesh_shape, rhs, skel_perm):
        self.nx, self.ny, self.nz = (mesh_shape[a] for a in ("gx", "gy", "gz"))
        self.devices = self.nx * self.ny * self.nz
        self.blobs, self.bodies = rhs.shape[-2:]
        self.step = round_up(self.blobs, 8)
        self.rows = round_up(3 * self.step, 16)
        self.half = self.rows // 2
        self.message = self.half + 8
        self.direct = (self.nx, self.ny) == (4, 2)
        self.levels = skel_perm.shape[0]
        self.skel = skel_perm.shape[1] // 2
        shifts = sorted({(dy % self.ny) for dy in (-1, 1)} - {0})
        self.shifts = shifts
        self.sources = [("same", dy) for dy in shifts]
        for kind in ("other", "partner"):
            self.sources += [(kind, dy) for dy in [0] + shifts]
        self.ghosts = round_up(len(self.sources) * RIM, LANES)
        self.far_tiles = self.nz + -(-self.nz // 2)

    def slot_start(self, slot, parity):
        dx, dy = slot // 3 - 1, (slot % 3 - 1) % self.ny
        kind = "same" if dx == 0 else "partner" if dx == 1 - 2 * parity else "other"
        if (kind, dy) == ("same", 0):
            return 0
        return self.bodies + RIM * self.sources.index((kind, dy))

    def odd(self, device):
        return (device // (self.ny * self.nz)) % 2

    def beside(self, kind, x):
        if kind == "same":
            return x
        if kind == "partner":
            return x ^ 1
        return (x + 2 * (x % 2) - 1) % self.nx


def pieces(x, s):
    return [x[c * s.step : c * s.step + s.step] for c in range(3)]


def turn(parts, rot, inverse):
    out = []
    for target in range(3):
        acc = None
        for source in range(3):
            row = 3 * source + target if inverse else 3 * target + source
            term = rot[row : row + 1] * parts[source]
            acc = term if acc is None else acc + term
        out.append(acc)
    return out


def stacked(parts, s):
    rest = s.rows - 3 * s.step
    if rest:
        parts = list(parts) + [jnp.zeros((rest, parts[0].shape[1]), f32)]
    return jnp.concatenate(parts, axis=0)


def occupancy(cells, s):
    row = lax.broadcasted_iota(jnp.int32, (s.skel, s.bodies), 0)
    return jnp.where(cells == row, 1.0, 0.0).astype(bf16)


def pack_charges(parts, weight_col, occ, s, count=False):
    moments = [jnp.sum(part * weight_col, axis=0, keepdims=True) for part in parts]
    moments.append(jnp.full((1, s.bodies), 1.0 if count else 0.0, f32))
    moments = jnp.concatenate(moments + [jnp.zeros((4, s.bodies), f32)], axis=0)
    high, rest = split(moments)
    mid, low = split(moments - high.astype(f32))
    stack = jnp.concatenate([high.astype(f32), mid.astype(f32), low.astype(f32)], axis=0).astype(bf16)
    sums = mt(stack, occ)
    charges = sums[0:8] + (sums[8:16] + sums[16:24])
    tail = jnp.concatenate([charges[:, LANES:], jnp.zeros((8, 2 * LANES - s.skel), f32)], axis=1)
    row = lax.broadcasted_iota(jnp.int32, (8, LANES), 0)
    return jnp.where(row < 4, charges[:, :LANES], pltpu.roll(tail, 4, 0))


def pack_rim(x, s):
    lane = lax.broadcasted_iota(jnp.int32, (s.half, LANES), 1)
    top, bottom = x[: s.half, :LANES], x[s.half :, :LANES]
    return jnp.where(lane < RIM, top, pltpu.roll(bottom, RIM, 1))


def unpack_rims(rims, s):
    lane = lax.broadcasted_iota(jnp.int32, (s.half, LANES), 1)
    tops, bottoms = [], []
    for i in range(0, s.ghosts // RIM, 2):
        a = rims[i]
        b = rims[i + 1] if i + 1 < len(rims) else jnp.zeros_like(a)
        tops.append(jnp.where(lane < RIM, a, pltpu.roll(b, RIM, 1)))
        bottoms.append(jnp.where(lane < RIM, pltpu.roll(a, RIM, 1), b))
    return jnp.concatenate(
        [jnp.concatenate(tops, axis=1), jnp.concatenate(bottoms, axis=1)], axis=0
    )


def pack_message(x, weight_col, cells, s):
    charges = pack_charges(pieces(x, s), weight_col, occupancy(cells, s), s)
    row = lax.broadcasted_iota(jnp.int32, (8, LANES), 0)
    charges = jnp.where(row == 3, cells[:, :LANES].astype(f32), charges)
    return jnp.concatenate([pack_rim(x, s), charges], axis=0)


def begin(sources, targets, sems):
    moves = [pltpu.make_async_copy(a, b, sems.at[i]) for i, (a, b) in enumerate(zip(sources, targets))]
    for move in moves:
        move.start()
    return moves


def start_kernel(s, rhs, cells, weight, message_out, col_out, cells_out, f_out, raw, wide, sems):
    moves = begin((weight, cells, rhs), (wide, cells_out, raw), sems)
    f_out[...] = jnp.zeros_like(f_out)
    moves[0].wait()
    row = jnp.concatenate([wide[...], jnp.zeros((1, 2 * LANES - s.blobs), f32)], axis=1)
    col = jnp.broadcast_to(row, (LANES, 2 * LANES)).T[: s.step]
    col_out[...] = col
    for move in moves[1:]:
        move.wait()
    for c in range(3):
        f_out[c * s.step : c * s.step + s.blobs, :] = raw[c * s.blobs : (c + 1) * s.blobs, 0, :]
    message_out[...] = pack_message(f_out[...], col[:, :1], cells_out[0], s)


def frame_rows(angles):
    cos, sin = jnp.cos(angles), jnp.sin(angles)
    cy, cp, cr = cos[0:1], cos[1:2], cos[2:3]
    sy, sp, sr = sin[0:1], sin[1:2], sin[2:3]
    return [
        cy * cp,
        cy * sp * sr - sy * cr,
        cy * sp * cr + sy * sr,
        sy * cp,
        sy * sp * sr + cy * cr,
        sy * sp * cr - cy * sr,
        -sp,
        cp * sr,
        cp * cr,
    ]


def local_part(f, s, rot, mob, own):
    parts = pieces(f, s)
    turned = stacked(turn(parts, rot, False), s)
    mixed = product(mm, mob, split(turned))
    back = turn(pieces(mixed, s), rot, True)
    return f + stacked(back, s), product(mm, split(f), own)


def product_many(dot, blocks, b):
    rows = blocks[0].shape[0]
    out = product(dot, split(jnp.concatenate(blocks, axis=0)), split(b))
    return [out[i * rows : (i + 1) * rows] for i in range(len(blocks))]


def expand_once(groups, halves):
    flat = [block for group in groups for block in group]
    sides = [product_many(mt, flat, half) for half in halves]
    out, at = [], 0
    for group in groups:
        spread = []
        for i in range(at, at + len(group)):
            spread += [sides[0][i], sides[1][i]]
        at += len(group)
        out.append(spread)
    return out


def setup_kernel(
    s, ids, f_in, *refs
):
    count = 9
    sources, refs = refs[:count], refs[count:]
    copies, refs = refs[-1 - count :], refs[: -1 - count]
    copies, sems = copies[:-1], copies[-1]
    setup(s, ids, f_in, begin(sources, copies, sems), *copies, *refs)


def setup(
    s, ids, f_in, moves, angles, near_weight, neighbours, self_mob, near_mat, perm, interp, sibling, root,
    loc_out, gat_out, rot_out, sh_out, sl_out, nh_out, nl_out, oh_out, ol_out, gh_out, gl_out,
    fh_out, fl_out, uh_out, ul_out, bh_out, bl_out, rh_out, rl_out, padded, ups_ref, far_ref,
):
    f = f_in[...]
    for move in moves[:3]:
        move.wait()
    rot = jnp.concatenate(frame_rows(angles[:, 0, :]) + [jnp.zeros((7, s.bodies), f32)], axis=0)
    rot_out[...] = rot

    links = neighbours[0, 0]
    slot = links // s.bodies
    base = jnp.zeros_like(links)
    odd = (ids[0] // s.ny) % 2
    for index in range(9):
        start = jnp.where(odd == 1, s.slot_start(index, 1), s.slot_start(index, 0))
        base = jnp.where(slot == index, start, base)
    column = base + links % s.bodies
    coef = near_weight[0, 0]
    for first, count, hi_out, lo_out in (
        (0, s.bodies, oh_out, ol_out),
        (s.bodies, s.ghosts, gh_out, gl_out),
    ):
        for r in range(0, count, 64):
            row = lax.broadcasted_iota(jnp.int32, (64, s.bodies), 0) + (first + r)
            acc = jnp.zeros((64, s.bodies), f32)
            for k in range(coef.shape[0]):
                acc = acc + jnp.where(column[k : k + 1] == row, coef[k : k + 1], 0.0)
            hi, lo = split(acc)
            hi_out[r : r + 64, :] = hi
            lo_out[r : r + 64, :] = lo

    for move in moves[3:]:
        move.wait()
    padded[...] = jnp.zeros_like(padded)
    for matrix, hi_out, lo_out in ((self_mob, sh_out, sl_out), (near_mat, nh_out, nl_out)):
        for c in range(3):
            for d in range(3):
                padded[c * s.step : c * s.step + s.blobs, d * s.step : d * s.step + s.blobs] = matrix[
                    c * s.blobs : (c + 1) * s.blobs, d * s.blobs : (d + 1) * s.blobs
                ]
        hi, lo = split(padded[...])
        hi_out[...] = hi
        lo_out[...] = lo

    loc, gat = local_part(f, s, rot, (sh_out[...], sl_out[...]), (oh_out[...], ol_out[...]))
    loc_out[...] = loc
    gat_out[...] = gat

    n = s.skel
    z = ids[1]
    halves = []
    spot = lax.broadcasted_iota(jnp.int32, (2 * n, n), 0)
    for level in range(s.levels):
        kept = jnp.where(perm[level : level + 1, :n] == spot, 1.0, 0.0)
        moved = jnp.where(perm[level : level + 1, n:] == spot, 1.0, 0.0).astype(bf16)
        hi, lo = split(interp[level])
        up = kept + (mm(moved, hi) + mm(moved, lo))
        ups_ref[level] = up
        uh_out[level], ul_out[level] = split(up)
        bh_out[level], bl_out[level] = split(sibling[level])
        bit = (z >> level) & 1
        halves.append(
            [ups_ref[level, pl.ds(pl.multiple_of(side * n, 8), n), :] for side in (bit, 1 - bit)]
        )

    def down(block, level, dot):
        return product(dot, split(halves[level][0]), split(block))

    spread = root[...]
    rh_out[...], rl_out[...] = split(spread)
    beside = []
    for level in reversed(range(s.levels)):
        spread = down(spread, level, mt if level == s.levels - 1 else mm)
        beside = [(down(block, level, mt if fresh else mm), False) for block, fresh in beside]
        beside.append((sibling[level], True))
    beside = [block.T if fresh else block for block, fresh in reversed(beside)]
    leaves = [[spread]]
    for level in reversed(range(s.levels)):
        leaves = expand_once(leaves, halves[level])
        leaves.append([beside[level]])
    far_leaves, *sub = leaves
    near_leaves = [jnp.zeros((n, n), f32)]
    for blocks in reversed(sub):
        near_leaves += blocks
    tail = n - LANES
    far_ref[...] = jnp.zeros_like(far_ref)
    own = [a - b for a, b in zip(near_leaves, far_leaves)]
    for group, blocks in enumerate((own, far_leaves)):
        for leaf, block in enumerate(blocks):
            at = (group * s.far_tiles + leaf) * LANES
            far_ref[:, at : at + LANES] = block[:, :LANES]
            at = (group * s.far_tiles + s.nz + leaf // 2) * LANES + leaf % 2 * RIM
            far_ref[:, at : at + tail] = block[:, LANES:]
    fh_out[...], fl_out[...] = split(far_ref[...])


def half_kernel(s, *refs):
    *messages, _, out = refs
    acc = messages[0][s.half :, :]
    for message in messages[1:]:
        acc = acc + message[s.half :, :]
    out[...] = acc


def layer_kernel(s, count, message, *refs):
    sums, around, out = refs[:count], refs[count:-1], refs[-1]
    acc = sums[0][...]
    for part in sums[1:]:
        acc = acc + part[...]
    out[0] = message[s.half :, :]
    out[1] = acc
    for index, other in enumerate(around):
        out[2 + index] = other[s.half :, :]


def layer_row(s, tiles):
    row = list(tiles)
    lane = lax.broadcasted_iota(jnp.int32, (8, LANES), 1)
    for leaf in range(0, s.nz, 2):
        pair = tiles[leaf]
        if leaf + 1 < s.nz:
            pair = jnp.where(lane < RIM, pair, pltpu.roll(tiles[leaf + 1], RIM, 1))
        row.append(pltpu.roll(pair, 4, 0))
    return jnp.concatenate(row, axis=1)


def far_potentials(s, layers, far_op):
    own = [layer_row(s, [layer[k] for layer in layers]) for k in range(layers[0].shape[0])]
    wide = own[0].shape[1]
    hi, lo = far_op
    whole = product(mt, split(own.pop(1)), (hi[:, wide:], lo[:, wide:]))
    boxes = product(mt, split(jnp.concatenate(own, axis=0)), (hi[:, :wide], lo[:, :wide]))
    return [boxes[8 * k : 8 * k + 8] + whole for k in range(len(own))]


def pick(potential, onehot):
    high, _ = split(potential)
    mid, low = split(potential - high.astype(f32))
    parts = [x.astype(f32) for x in (high, mid, low)]
    picked = mm(jnp.concatenate(parts, axis=0).astype(bf16), onehot)
    n = potential.shape[0]
    return picked[:n] + (picked[n : 2 * n] + picked[2 * n :])


def rim_values(s, layers, potentials):
    lane = lax.broadcasted_iota(jnp.int32, (8, LANES), 1)
    place = lax.broadcasted_iota(jnp.int32, (s.skel, LANES), 0).astype(f32)
    count = len(potentials) - 1
    out = []
    for i in range(0, count, 2):
        last = min(i + 1, count - 1)
        cells = jnp.where(lane < RIM, layers[0][2 + i], pltpu.roll(layers[0][2 + last], RIM, 1))
        onehot = jnp.where(cells[3:4] == place, 1.0, 0.0).astype(bf16)
        both = pick(jnp.concatenate([potentials[1 + i], potentials[1 + last]], axis=0), onehot)
        out.append(jnp.where(lane < RIM, both[:8], both[8:]))
    return out


def gather_kernel(s, gat, gh, gl, *refs):
    *messages, _, hi_out, lo_out = refs
    rims = unpack_rims([message[: s.half, :] for message in messages], s)
    gathered = gat[...] + product(mm, split(rims), (gh[...], gl[...]))
    hi_out[...], lo_out[...] = split(gathered)


def gather_far_kernel(s, gat, gh, gl, col, values, *refs):
    *messages, hi_out, lo_out = refs
    rims = unpack_rims([message[...] for message in messages], s)
    far = []
    for c in range(3):
        value = jnp.concatenate([values[i, c : c + 1, :] for i in range(values.shape[0])], axis=1)
        far.append(col[:, :1] * value)
    rims = rims + stacked(far, s)
    gathered = gat[...] + product(mm, split(rims), (gh[...], gl[...]))
    hi_out[...], lo_out[...] = split(gathered)


def near_kernel(s, loc, nh, nl, hi, lo, out, rim_out):
    part = loc[...] + product(mm, (nh[...], nl[...]), (hi[...], lo[...]))
    out[...] = part
    rim_out[...] = pack_rim(part, s)


def first_kernel(s, part, fh, fl, cells, col, *refs):
    *layers, u_out, charges_out, values_out = refs
    weight_col = col[:, :1]
    occ = occupancy(cells[0], s)
    potentials = far_potentials(s, layers, (fh[...], fl[...]))
    values = pick(potentials[0], occ)
    u = part[...] + stacked([weight_col * values[c : c + 1] for c in range(3)], s)
    u_out[...] = u
    charges_out[...] = pack_charges(pieces(u, s), weight_col, occ, s)
    for index, value in enumerate(rim_values(s, layers, potentials)):
        values_out[index] = value


def order_kernel(x, _, out):
    out[...] = x[...]


def safe_inverse(x):
    return jnp.where(x > 0.0, 1.0 / jnp.where(x > 0.0, x, 1.0), 0.0)


def middle_kernel(s, u_in, f_in, rot, sh, sl, oh, ol, loc_out, gat_out, ortho_out, stat_out):
    u, f = u_in[...], f_in[...]
    loc, gat = local_part(u, s, rot[...], (sh[...], sl[...]), (oh[...], ol[...]))
    loc_out[...] = loc
    gat_out[...] = gat
    ff = total(f * f)
    fu = total(f * u) * safe_inverse(ff)
    ortho = u - fu * f
    ortho_out[...] = ortho
    oo = total(ortho * ortho)
    stat_out[...] = jnp.broadcast_to(
        jnp.concatenate([ff, fu, oo, jnp.zeros((5, 1), f32)], axis=0), (8, LANES)
    )


def second_kernel(
    s, loc, nh, nl, hi, lo, cells, col, f_in, ortho_in, stat, charges_f, charges_u, packed_out
):
    part = loc[...] + product(mm, (nh[...], nl[...]), (hi[...], lo[...]))
    f, ortho = f_in[...], ortho_in[...]
    ff, fu, oo = (stat[i : i + 1, :1] for i in range(3))
    fa = total(f * part) * safe_inverse(ff)
    oa = total(ortho * part) * safe_inverse(oo)
    rest = part - fa * f - oa * ortho
    aa = total(rest * rest)
    rf, ro = jnp.sqrt(ff), jnp.sqrt(oo)
    of_f = charges_f[-8:, :]
    of_u = charges_u[...]
    of_a = pack_charges(pieces(rest, s), col[:, :1], occupancy(cells[0], s), s, count=True)
    row = lax.broadcasted_iota(jnp.int32, (8, LANES), 0)
    lane = lax.broadcasted_iota(jnp.int32, (8, LANES), 1)
    left = lane < RIM
    first = jnp.where(left, of_u, pltpu.roll(of_a, RIM, 1))
    first = jnp.where(row < 4, of_u, first)
    first = jnp.where((row == 7) & left, pltpu.roll(of_f, 1, 0), first)
    for index, value in enumerate((rf, rf * fu, ro, rf * fa, ro * oa, aa)):
        first = jnp.where((row == 3) & (lane == index), value, first)
    tails = jnp.where(left, pltpu.roll(of_f, 3, 0), pltpu.roll(pltpu.roll(of_f, 2, 0), RIM, 1))
    second = jnp.where(row < 3, of_f, of_a)
    second = jnp.where(row < 4, second, pltpu.roll(of_a, 4, 0))
    second = jnp.where(row == 7, tails, second)
    for device in range(s.devices):
        packed_out[device] = second if s.odd(device) else first


def tree(s, leaves, ups, siblings, root):
    def apply(dot, blocks, factor):
        rows = blocks[0].shape[0]
        out = product(dot, split(jnp.concatenate(blocks, axis=0)), factor)
        return [out[i * rows : (i + 1) * rows] for i in range(len(blocks))]

    n = s.skel
    halves = [[(hi[level, j * n : (j + 1) * n, :], lo[level, j * n : (j + 1) * n, :]) for j in range(2)]
              for level, (hi, lo) in ((k, ups) for k in range(s.levels))]
    charges = [leaves]
    for level in range(s.levels):
        low, high = (apply(mm, charges[-1][j::2], halves[level][j]) for j in range(2))
        charges.append([a + b for a, b in zip(low, high)])
    own = charges[-1][0]
    whole = own[:8]
    for column in range(1, s.nx * s.ny):
        whole = whole + own[8 * column : 8 * column + 8]
    others = jnp.concatenate([whole] * (s.nx * s.ny), axis=0) - own
    potential = apply(mm, [others], root)
    for level in reversed(range(s.levels)):
        beside = apply(mm, charges[level], (siblings[0][level], siblings[1][level]))
        down = [apply(mt, potential, halves[level][j]) for j in range(2)]
        potential = [
            down[z % 2][z // 2] + beside[z ^ 1] for z in range(len(charges[level]))
        ]
    return potential


def box_numbers(s, firsts, seconds, ups, siblings, root):
    columns = s.nx * s.ny
    row = lax.broadcasted_iota(jnp.int32, (8, LANES), 0)
    lane = lax.broadcasted_iota(jnp.int32, (8, LANES), 1)
    left, valid = lane < RIM, row < 3
    leaves = []
    for z in range(s.nz):
        wide = []
        for column in range(columns):
            tile = firsts[column * s.nz + z]
            wide.append(jnp.concatenate([tile, pltpu.roll(tile, 4, 0)], axis=1)[:, : s.skel])
        leaves.append(jnp.concatenate(wide, axis=0))
    potential = tree(s, leaves, ups, siblings, root)
    out = []
    for start in range(0, s.devices, 8):
        sums = [jnp.zeros((8, LANES), f32) for _ in range(5)]
        for box in range(start, min(s.devices, start + 8)):
            column, z = box // s.nz, box % s.nz
            phi = potential[z][8 * column : 8 * column + 8]
            main, tail = phi[:, :LANES], phi[:, LANES:]
            tail = jnp.concatenate([tail, tail], axis=1)
            first, second = firsts[box], seconds[box]
            both = pltpu.roll(first, 4, 0) * tail
            of_f = jnp.where(row == 0, pltpu.roll(second, 1, 0), jnp.where(row == 1, pltpu.roll(second, 2, 0), pltpu.roll(first, 3, 0)))
            of_f = jnp.where(left == (row != 1), of_f * tail, 0.0)
            count = jnp.broadcast_to(second[3:4], (8, LANES))
            count_tail = jnp.where(left, 0.0, jnp.broadcast_to(first[7:8], (8, LANES)))
            terms = (
                second * main + of_f,
                first * main + jnp.where(left, both, 0.0),
                pltpu.roll(second, 4, 0) * main + jnp.where(left, 0.0, both),
                count * (main * main) + count_tail * (tail * tail),
            )
            here = row == box - start
            for index, term in enumerate(terms):
                value = jnp.sum(jnp.where(valid, term, 0.0), axis=0, keepdims=True)
                sums[index] = jnp.where(here, value, sums[index])
            sums[4] = jnp.where(here, first[3:4], sums[4])
        numbers = sums[4]
        for index in range(4):
            numbers = jnp.where(lane == 6 + index, jnp.sum(sums[index], axis=1, keepdims=True), numbers)
        out.append(numbers)
    rest = round_up(s.devices, LANES) - 8 * len(out)
    if rest:
        out.append(jnp.zeros((rest, LANES), f32))
    return jnp.concatenate(out, axis=0)


def finish_kernel(s, ids, f_in, u_in, mine, other, col, uh, ul, bh, bl, rh, rl, x_out, lsq_out, raw, sem):
    odd = (ids[0] // s.ny) % 2 == 1
    firsts = [jnp.where(odd, other[box], mine[box]) for box in range(s.devices)]
    seconds = [jnp.where(odd, mine[box], other[box]) for box in range(s.devices)]
    rows = box_numbers(s, firsts, seconds, (uh, ul), (bh, bl), (rh[...], rl[...])).T
    f1, u1, u2, t1, t2, aa, far_f, far_u, far_a, far_far = (rows[i : i + 1] for i in range(10))
    by_f = safe_inverse(f1)
    by_o = jnp.where(u2 * u2 > 1e-10 * (u1 * u1), safe_inverse(u2), 0.0)
    on_one = far_f * by_f
    on_two = (far_u - u1 * by_f * far_f) * by_o
    weight = jnp.sum(col[:, :1] * col[:, :1], axis=0, keepdims=True)
    t3 = aa + 2.0 * far_a + weight * far_far - on_one * on_one - on_two * on_two
    t1, t2, t3 = t1 + on_one, t2 + on_two, jnp.sqrt(jnp.maximum(t3, 0.0))

    def along(x):
        return jnp.sum(x, axis=1, keepdims=True)

    beta = jnp.sqrt(along(f1 * f1) + epsilon)
    v = f1 / beta
    w1, w2 = u1 / beta, u2 / beta
    h11 = along(w1 * v)
    r1 = w1 - h11 * v
    h21 = jnp.sqrt(along(r1 * r1 + w2 * w2) + epsilon)
    b1, b2 = r1 / h21, w2 / h21
    z1, z2, z3 = ((t1 / beta - h11 * w1) / h21, (t2 / beta - h11 * w2) / h21, t3 / beta / h21)
    h12 = along(z1 * v)
    h22 = along(z1 * b1 + z2 * b2)
    d1, d2 = z1 - h12 * v - h22 * b1, z2 - h22 * b2
    h32 = jnp.sqrt(along(d1 * d1 + d2 * d2 + z3 * z3) + epsilon)
    first_norm = jnp.sqrt(h11 * h11 + h21 * h21)
    c1, s1 = h11 / first_norm, h21 / first_norm
    t12, t22 = c1 * h12 + s1 * h22, c1 * h22 - s1 * h12
    second_norm = jnp.sqrt(t22 * t22 + h32 * h32)
    c2, s2 = t22 / second_norm, h32 / second_norm
    g2 = -s1 * beta
    y2 = c2 * g2 / second_norm
    y1 = (c1 * beta - t12 * y2) / first_norm
    lsq_out[...] = jnp.abs(s2 * g2)
    on_u = y2 / h21 / beta
    on_f = y1 / beta - on_u * h11
    for c in range(3):
        part = slice(c * s.step, c * s.step + s.blobs)
        raw[c * s.blobs : (c + 1) * s.blobs, 0, :] = on_f * f_in[part, :] + on_u * u_in[part, :]
    move = pltpu.make_async_copy(raw, x_out, sem)
    move.start()
    move.wait()


def call(kernel, outs, args, scalars=0, far_args=0, far_outs=0, scratch=(), flops=0):
    vmem = pl.BlockSpec(memory_space=pltpu.VMEM)
    smem = pl.BlockSpec(memory_space=pltpu.SMEM)
    hbm = pl.BlockSpec(memory_space=pltpu.HBM)
    near_args = len(args) - far_args
    args = args[:near_args] + [pltpu.with_memory_space_constraint(x, pltpu.HBM) for x in args[near_args:]]
    return pl.pallas_call(
        kernel,
        out_shape=[jax.ShapeDtypeStruct(shape, kind) for shape, kind in outs],
        in_specs=[smem] * scalars + [vmem] * (near_args - scalars) + [hbm] * far_args,
        out_specs=[hbm] * far_outs + [vmem] * (len(outs) - far_outs),
        scratch_shapes=list(scratch),
        compiler_params=pltpu.CompilerParams(vmem_limit_bytes=16 * 2**20),
        cost_estimate=pl.CostEstimate(flops=flops, bytes_accessed=2**20, transcendentals=0),
    )(*args)


def body(
    mesh_shape, rhs, angles, self_mob, near_mat, near_weight, neighbours, cells, blob_weight,
    skel_perm, interp, sibling_ops, root_op,
):
    s = Sizes(mesh_shape, rhs, skel_perm)
    full = (s.rows, s.bodies)
    square = (s.rows, s.rows)
    tile = (8, LANES)
    far_shape = (s.skel, 2 * s.far_tiles * LANES)
    column = lax.axis_index("gx") * s.ny + lax.axis_index("gy")
    ids = jnp.stack([column, lax.axis_index("gz")]).astype(jnp.int32)

    def fetch(x, kind, dy):
        pairs = []
        for gx in range(s.nx):
            for gy in range(s.ny):
                pairs.append((s.beside(kind, gx) * s.ny + (gy + dy) % s.ny, gx * s.ny + gy))
        return lax.ppermute(x, ("gx", "gy"), pairs)

    def fetch_layers(x):
        return [x] + [
            lax.ppermute(x, "gz", [(z ^ k, z) for z in range(s.nz)]) for k in range(1, s.nz)
        ]

    def fetch_rims(rim):
        got = {}
        for dy in s.shifts:
            got["other", dy] = fetch(rim, "other", dy)
        for dy in s.shifts:
            got["same", dy] = fetch(rim, "same", dy)
        got["other", 0] = fetch(rim, "other", 0)
        got["partner", 0] = fetch(rim, "partner", 0)
        return got

    def forward_rims(got, after):
        for dy in s.shifts:
            held = got["same", dy]
            (held,) = call(order_kernel, [(held.shape, f32)], [held, after])
            got["partner", dy] = fetch(held, "partner", 0)

    def plane_sum(message, got, after):
        if not s.direct:
            return [lax.psum(message[s.half :], ("gx", "gy"))]
        quarter = [message] + [got[key] for key in s.sources if key[0] != "partner"]
        (half,) = call(functools.partial(half_kernel, s), [(tile, f32)], quarter + [after])
        return [half, fetch(half, "partner", 0)]

    flat = (3 * s.blobs, 1, s.bodies)
    small = (1, s.blobs)
    message, col, cells, f = call(
        functools.partial(start_kernel, s),
        [((s.message, LANES), f32), ((s.step, LANES), f32), (cells.shape, jnp.int32), (full, f32)],
        [rhs.reshape(flat), cells, blob_weight.reshape(small)],
        far_args=3,
        scratch=[pltpu.VMEM(flat, f32), pltpu.VMEM(small, f32), pltpu.SemaphoreType.DMA((3,))],
        flops=10**7,
    )
    got = fetch_rims(message)
    operators = [
        angles.reshape(3, 1, s.bodies), near_weight, neighbours, self_mob, near_mat, skel_perm, interp,
        sibling_ops, root_op,
    ]
    loc, gat, rot, sh, sl, nh, nl, oh, ol, gh, gl, fh, fl, *operators_out = call(
        functools.partial(setup_kernel, s),
        [(full, f32), (full, f32), ((16, s.bodies), f32)]
        + [(square, bf16)] * 4
        + [((s.bodies, s.bodies), bf16)] * 2
        + [((s.ghosts, s.bodies), bf16)] * 2
        + [(far_shape, bf16)] * 2
        + [((s.levels, 2 * s.skel, s.skel), bf16)] * 2
        + [((s.levels, s.skel, s.skel), bf16)] * 2
        + [((s.skel, s.skel), bf16)] * 2,
        [ids, f] + operators,
        scalars=1,
        far_args=len(operators),
        scratch=[
            pltpu.VMEM(square, f32), pltpu.VMEM((s.levels, 2 * s.skel, s.skel), f32), pltpu.VMEM(far_shape, f32)
        ]
        + [pltpu.VMEM(x.shape, x.dtype) for x in operators]
        + [pltpu.SemaphoreType.DMA((len(operators),))],
        flops=5 * 10**9,
    )
    forward_rims(got, rot)
    sums = plane_sum(message, got, rot)
    around = [got[key] for key in s.sources]
    (tiles,) = call(
        functools.partial(layer_kernel, s, len(sums)),
        [((2 + len(around),) + tile, f32)],
        [message] + sums + around,
    )
    layers = fetch_layers(tiles)
    gathered = call(
        functools.partial(gather_kernel, s),
        [(full, bf16), (full, bf16)],
        [gat, gh, gl] + around + [tiles],
        flops=10**9,
    )
    part, rim = call(
        functools.partial(near_kernel, s),
        [(full, f32), ((s.half, LANES), f32)],
        [loc, nh, nl, *gathered],
        flops=10**9,
    )
    got = fetch_rims(rim)
    u, charges, values = call(
        functools.partial(first_kernel, s),
        [(full, f32), (tile, f32), ((s.ghosts // LANES,) + tile, f32)],
        [part, fh, fl, cells, col, *layers],
        flops=10**8,
    )
    loc, gat, ortho, stat = call(
        functools.partial(middle_kernel, s),
        [(full, f32), (full, f32), (full, f32), (tile, f32)],
        [u, f, rot, sh, sl, oh, ol],
        flops=10**9,
    )
    forward_rims(got, stat)
    gathered = call(
        functools.partial(gather_far_kernel, s),
        [(full, bf16), (full, bf16)],
        [gat, gh, gl, col, values] + [got[key] for key in s.sources],
        flops=10**9,
    )
    (packed,) = call(
        functools.partial(second_kernel, s),
        [((s.devices, 8, LANES), f32)],
        [loc, nh, nl, *gathered, cells, col, f, ortho, stat, message, charges],
        flops=10**9,
    )
    boxes = lax.all_to_all(packed, ("gx", "gy", "gz"), 0, 0)
    result, lsq = call(
        functools.partial(finish_kernel, s),
        [(flat, f32), ((1, 1), f32)],
        [ids, f, u, boxes, fetch(boxes, "partner", 0), col, *operators_out],
        scalars=1,
        far_outs=1,
        scratch=[pltpu.VMEM(flat, f32), pltpu.SemaphoreType.DMA],
        flops=10**7,
    )
    return result.reshape(rhs.shape), lsq.reshape(())


def solution(mesh):
    in_specs = (
        P("gx", "gy", None, None, "gz"),
        P("gx", "gy", None, "gz"),
        P(),
        P(),
        P("gx", "gy", None, "gz"),
        P("gx", "gy", None, "gz"),
        P("gx", "gy", "gz"),
        P(),
        P(),
        P(),
        P(),
        P(),
    )
    out_specs = (P("gx", "gy", None, None, "gz"), P())
    inner = functools.partial(body, dict(mesh.shape))
    return jax.shard_map(inner, mesh=mesh, in_specs=in_specs, out_specs=out_specs, check_vma=False)
```

```python
import functools

import jax
import jax.numpy as jnp
from jax import lax
from jax.experimental import pallas as pl
from jax.experimental.pallas import tpu as pltpu
from jax.sharding import PartitionSpec as P

epsilon = 1e-06
f32 = jnp.float32
bf16 = jnp.bfloat16
RIM = 64
LANES = 128


def round_up(value, unit):
    return -(-value // unit) * unit


def split(x):
    hi = x.astype(bf16)
    lo = (x - hi.astype(f32)).astype(bf16)
    return hi, lo


def mm(a, b):
    return lax.dot_general(a, b, (((1,), (0,)), ((), ())), preferred_element_type=f32)


def mt(a, b):
    return lax.dot_general(a, b, (((1,), (1,)), ((), ())), preferred_element_type=f32)


def product(dot, a, b):
    return dot(a[0], b[0]) + (dot(a[0], b[1]) + dot(a[1], b[0]))


def total(x):
    return jnp.sum(jnp.sum(x, axis=0, keepdims=True), axis=1, keepdims=True)


class Sizes:
    def __init__(self, mesh_shape, rhs, skel_perm):
        self.nx, self.ny, self.nz = (mesh_shape[a] for a in ("gx", "gy", "gz"))
        self.devices = self.nx * self.ny * self.nz
        self.blobs, self.bodies = rhs.shape[-2:]
        self.step = round_up(self.blobs, 8)
        self.rows = round_up(3 * self.step, 16)
        self.half = self.rows // 2
        self.message = self.half + 8
        self.direct = (self.nx, self.ny) == (4, 2)
        self.levels = skel_perm.shape[0]
        self.skel = skel_perm.shape[1] // 2
        shifts = sorted({(dy % self.ny) for dy in (-1, 1)} - {0})
        self.shifts = shifts
        self.sources = [("same", dy) for dy in shifts]
        for kind in ("other", "partner"):
            self.sources += [(kind, dy) for dy in [0] + shifts]
        self.ghosts = round_up(len(self.sources) * RIM, LANES)
        self.far_tiles = self.nz + -(-self.nz // 2)

    def slot_start(self, slot, parity):
        dx, dy = slot // 3 - 1, (slot % 3 - 1) % self.ny
        kind = "same" if dx == 0 else "partner" if dx == 1 - 2 * parity else "other"
        if (kind, dy) == ("same", 0):
            return 0
        return self.bodies + RIM * self.sources.index((kind, dy))

    def odd(self, device):
        return (device // (self.ny * self.nz)) % 2

    def beside(self, kind, x):
        if kind == "same":
            return x
        if kind == "partner":
            return x ^ 1
        return (x + 2 * (x % 2) - 1) % self.nx


def pieces(x, s):
    return [x[c * s.step : c * s.step + s.step] for c in range(3)]


def turn(parts, rot, inverse):
    out = []
    for target in range(3):
        acc = None
        for source in range(3):
            row = 3 * source + target if inverse else 3 * target + source
            term = rot[row : row + 1] * parts[source]
            acc = term if acc is None else acc + term
        out.append(acc)
    return out


def stacked(parts, s):
    rest = s.rows - 3 * s.step
    if rest:
        parts = list(parts) + [jnp.zeros((rest, parts[0].shape[1]), f32)]
    return jnp.concatenate(parts, axis=0)


def occupancy(cells, s):
    row = lax.broadcasted_iota(jnp.int32, (s.skel, s.bodies), 0)
    return jnp.where(cells == row, 1.0, 0.0).astype(bf16)


def pack_charges(parts, weight_col, occ, s, count=False):
    moments = [jnp.sum(part * weight_col, axis=0, keepdims=True) for part in parts]
    moments.append(jnp.full((1, s.bodies), 1.0 if count else 0.0, f32))
    moments = jnp.concatenate(moments + [jnp.zeros((4, s.bodies), f32)], axis=0)
    high, rest = split(moments)
    mid, low = split(moments - high.astype(f32))
    stack = jnp.concatenate([high.astype(f32), mid.astype(f32), low.astype(f32)], axis=0).astype(bf16)
    sums = mt(stack, occ)
    charges = sums[0:8] + (sums[8:16] + sums[16:24])
    tail = jnp.concatenate([charges[:, LANES:], jnp.zeros((8, 2 * LANES - s.skel), f32)], axis=1)
    row = lax.broadcasted_iota(jnp.int32, (8, LANES), 0)
    return jnp.where(row < 4, charges[:, :LANES], pltpu.roll(tail, 4, 0))


def pack_rim(x, s):
    lane = lax.broadcasted_iota(jnp.int32, (s.half, LANES), 1)
    top, bottom = x[: s.half, :LANES], x[s.half :, :LANES]
    return jnp.where(lane < RIM, top, pltpu.roll(bottom, RIM, 1))


def unpack_rims(rims, s):
    lane = lax.broadcasted_iota(jnp.int32, (s.half, LANES), 1)
    tops, bottoms = [], []
    for i in range(0, s.ghosts // RIM, 2):
        a = rims[i]
        b = rims[i + 1] if i + 1 < len(rims) else jnp.zeros_like(a)
        tops.append(jnp.where(lane < RIM, a, pltpu.roll(b, RIM, 1)))
        bottoms.append(jnp.where(lane < RIM, pltpu.roll(a, RIM, 1), b))
    return jnp.concatenate(
        [jnp.concatenate(tops, axis=1), jnp.concatenate(bottoms, axis=1)], axis=0
    )


def pack_message(x, weight_col, cells, s):
    charges = pack_charges(pieces(x, s), weight_col, occupancy(cells, s), s)
    row = lax.broadcasted_iota(jnp.int32, (8, LANES), 0)
    charges = jnp.where(row == 3, cells[:, :LANES].astype(f32), charges)
    return jnp.concatenate([pack_rim(x, s), charges], axis=0)


def begin(sources, targets, sems):
    moves = [pltpu.make_async_copy(a, b, sems.at[i]) for i, (a, b) in enumerate(zip(sources, targets))]
    for move in moves:
        move.start()
    return moves


def start_kernel(s, rhs, cells, weight, message_out, col_out, cells_out, f_out, raw, wide, sems):
    moves = begin((weight, cells, rhs), (wide, cells_out, raw), sems)
    f_out[...] = jnp.zeros_like(f_out)
    moves[0].wait()
    row = jnp.concatenate([wide[...], jnp.zeros((1, 2 * LANES - s.blobs), f32)], axis=1)
    col = jnp.broadcast_to(row, (LANES, 2 * LANES)).T[: s.step]
    col_out[...] = col
    for move in moves[1:]:
        move.wait()
    for c in range(3):
        f_out[c * s.step : c * s.step + s.blobs, :] = raw[c * s.blobs : (c + 1) * s.blobs, 0, :]
    message_out[...] = pack_message(f_out[...], col[:, :1], cells_out[0], s)


def frame_rows(angles):
    cos, sin = jnp.cos(angles), jnp.sin(angles)
    cy, cp, cr = cos[0:1], cos[1:2], cos[2:3]
    sy, sp, sr = sin[0:1], sin[1:2], sin[2:3]
    return [
        cy * cp,
        cy * sp * sr - sy * cr,
        cy * sp * cr + sy * sr,
        sy * cp,
        sy * sp * sr + cy * cr,
        sy * sp * cr - cy * sr,
        -sp,
        cp * sr,
        cp * cr,
    ]


def local_part(f, s, rot, mob, own):
    parts = pieces(f, s)
    turned = stacked(turn(parts, rot, False), s)
    mixed = product(mm, mob, split(turned))
    back = turn(pieces(mixed, s), rot, True)
    return f + stacked(back, s), product(mm, split(f), own)


def product_many(dot, blocks, b):
    rows = blocks[0].shape[0]
    out = product(dot, split(jnp.concatenate(blocks, axis=0)), split(b))
    return [out[i * rows : (i + 1) * rows] for i in range(len(blocks))]


def expand_once(groups, halves):
    flat = [block for group in groups for block in group]
    sides = [product_many(mt, flat, half) for half in halves]
    out, at = [], 0
    for group in groups:
        spread = []
        for i in range(at, at + len(group)):
            spread += [sides[0][i], sides[1][i]]
        at += len(group)
        out.append(spread)
    return out


def setup_kernel(
    s, ids, f_in, *refs
):
    count = 9
    sources, refs = refs[:count], refs[count:]
    copies, refs = refs[-1 - count :], refs[: -1 - count]
    copies, sems = copies[:-1], copies[-1]
    setup(s, ids, f_in, begin(sources, copies, sems), *copies, *refs)


def setup(
    s, ids, f_in, moves, angles, near_weight, neighbours, self_mob, near_mat, perm, interp, sibling, root,
    loc_out, gat_out, rot_out, sh_out, sl_out, nh_out, nl_out, oh_out, ol_out, gh_out, gl_out,
    fh_out, fl_out, uh_out, ul_out, bh_out, bl_out, rh_out, rl_out, padded, ups_ref, far_ref,
):
    f = f_in[...]
    for move in moves[:3]:
        move.wait()
    rot = jnp.concatenate(frame_rows(angles[:, 0, :]) + [jnp.zeros((7, s.bodies), f32)], axis=0)
    rot_out[...] = rot

    links = neighbours[0, 0]
    slot = links // s.bodies
    base = jnp.zeros_like(links)
    odd = (ids[0] // s.ny) % 2
    for index in range(9):
        start = jnp.where(odd == 1, s.slot_start(index, 1), s.slot_start(index, 0))
        base = jnp.where(slot == index, start, base)
    column = base + links % s.bodies
    coef = near_weight[0, 0]
    for first, count, hi_out, lo_out in (
        (0, s.bodies, oh_out, ol_out),
        (s.bodies, s.ghosts, gh_out, gl_out),
    ):
        for r in range(0, count, 64):
            row = lax.broadcasted_iota(jnp.int32, (64, s.bodies), 0) + (first + r)
            acc = jnp.zeros((64, s.bodies), f32)
            for k in range(coef.shape[0]):
                acc = acc + jnp.where(column[k : k + 1] == row, coef[k : k + 1], 0.0)
            hi, lo = split(acc)
            hi_out[r : r + 64, :] = hi
            lo_out[r : r + 64, :] = lo

    for move in moves[3:]:
        move.wait()
    padded[...] = jnp.zeros_like(padded)
    for matrix, hi_out, lo_out in ((self_mob, sh_out, sl_out), (near_mat, nh_out, nl_out)):
        for c in range(3):
            for d in range(3):
                padded[c * s.step : c * s.step + s.blobs, d * s.step : d * s.step + s.blobs] = matrix[
                    c * s.blobs : (c + 1) * s.blobs, d * s.blobs : (d + 1) * s.blobs
                ]
        hi, lo = split(padded[...])
        hi_out[...] = hi
        lo_out[...] = lo

    loc, gat = local_part(f, s, rot, (sh_out[...], sl_out[...]), (oh_out[...], ol_out[...]))
    loc_out[...] = loc
    gat_out[...] = gat

    n = s.skel
    z = ids[1]
    halves = []
    spot = lax.broadcasted_iota(jnp.int32, (2 * n, n), 0)
    for level in range(s.levels):
        kept = jnp.where(perm[level : level + 1, :n] == spot, 1.0, 0.0)
        moved = jnp.where(perm[level : level + 1, n:] == spot, 1.0, 0.0).astype(bf16)
        hi, lo = split(interp[level])
        up = kept + (mm(moved, hi) + mm(moved, lo))
        ups_ref[level] = up
        uh_out[level], ul_out[level] = split(up)
        bh_out[level], bl_out[level] = split(sibling[level])
        bit = (z >> level) & 1
        halves.append(
            [ups_ref[level, pl.ds(pl.multiple_of(side * n, 8), n), :] for side in (bit, 1 - bit)]
        )

    def down(block, level, dot):
        return product(dot, split(halves[level][0]), split(block))

    spread = root[...]
    rh_out[...], rl_out[...] = split(spread)
    beside = []
    for level in reversed(range(s.levels)):
        spread = down(spread, level, mt if level == s.levels - 1 else mm)
        beside = [(down(block, level, mt if fresh else mm), False) for block, fresh in beside]
        beside.append((sibling[level], True))
    beside = [block.T if fresh else block for block, fresh in reversed(beside)]
    leaves = [[spread]]
    for level in reversed(range(s.levels)):
        leaves = expand_once(leaves, halves[level])
        leaves.append([beside[level]])
    far_leaves, *sub = leaves
    near_leaves = [jnp.zeros((n, n), f32)]
    for blocks in reversed(sub):
        near_leaves += blocks
    tail = n - LANES
    far_ref[...] = jnp.zeros_like(far_ref)
    own = [a - b for a, b in zip(near_leaves, far_leaves)]
    for group, blocks in enumerate((own, far_leaves)):
        for leaf, block in enumerate(blocks):
            at = (group * s.far_tiles + leaf) * LANES
            far_ref[:, at : at + LANES] = block[:, :LANES]
            at = (group * s.far_tiles + s.nz + leaf // 2) * LANES + leaf % 2 * RIM
            far_ref[:, at : at + tail] = block[:, LANES:]
    fh_out[...], fl_out[...] = split(far_ref[...])


def half_kernel(s, *refs):
    *messages, _, out = refs
    acc = messages[0][s.half :, :]
    for message in messages[1:]:
        acc = acc + message[s.half :, :]
    out[...] = acc


def layer_kernel(s, count, message, *refs):
    sums, around, out = refs[:count], refs[count:-1], refs[-1]
    acc = sums[0][...]
    for part in sums[1:]:
        acc = acc + part[...]
    out[0] = message[s.half :, :]
    out[1] = acc
    for index, other in enumerate(around):
        out[2 + index] = other[s.half :, :]


def layer_row(s, tiles):
    row = list(tiles)
    lane = lax.broadcasted_iota(jnp.int32, (8, LANES), 1)
    for leaf in range(0, s.nz, 2):
        pair = tiles[leaf]
        if leaf + 1 < s.nz:
            pair = jnp.where(lane < RIM, pair, pltpu.roll(tiles[leaf + 1], RIM, 1))
        row.append(pltpu.roll(pair, 4, 0))
    return jnp.concatenate(row, axis=1)


def far_potentials(s, layers, far_op):
    own = [layer_row(s, [layer[k] for layer in layers]) for k in range(layers[0].shape[0])]
    wide = own[0].shape[1]
    hi, lo = far_op
    whole = product(mt, split(own.pop(1)), (hi[:, wide:], lo[:, wide:]))
    boxes = product(mt, split(jnp.concatenate(own, axis=0)), (hi[:, :wide], lo[:, :wide]))
    return [boxes[8 * k : 8 * k + 8] + whole for k in range(len(own))]


def pick(potential, onehot):
    high, _ = split(potential)
    mid, low = split(potential - high.astype(f32))
    parts = [x.astype(f32) for x in (high, mid, low)]
    picked = mm(jnp.concatenate(parts, axis=0).astype(bf16), onehot)
    n = potential.shape[0]
    return picked[:n] + (picked[n : 2 * n] + picked[2 * n :])


def rim_values(s, layers, potentials):
    lane = lax.broadcasted_iota(jnp.int32, (8, LANES), 1)
    place = lax.broadcasted_iota(jnp.int32, (s.skel, LANES), 0).astype(f32)
    count = len(potentials) - 1
    out = []
    for i in range(0, count, 2):
        last = min(i + 1, count - 1)
        cells = jnp.where(lane < RIM, layers[0][2 + i], pltpu.roll(layers[0][2 + last], RIM, 1))
        onehot = jnp.where(cells[3:4] == place, 1.0, 0.0).astype(bf16)
        both = pick(jnp.concatenate([potentials[1 + i], potentials[1 + last]], axis=0), onehot)
        out.append(jnp.where(lane < RIM, both[:8], both[8:]))
    return out


def gather_kernel(s, gat, gh, gl, *refs):
    *messages, _, hi_out, lo_out = refs
    rims = unpack_rims([message[: s.half, :] for message in messages], s)
    gathered = gat[...] + product(mm, split(rims), (gh[...], gl[...]))
    hi_out[...], lo_out[...] = split(gathered)


def gather_far_kernel(s, gat, gh, gl, col, values, *refs):
    *messages, hi_out, lo_out = refs
    rims = unpack_rims([message[...] for message in messages], s)
    far = []
    for c in range(3):
        value = jnp.concatenate([values[i, c : c + 1, :] for i in range(values.shape[0])], axis=1)
        far.append(col[:, :1] * value)
    rims = rims + stacked(far, s)
    gathered = gat[...] + product(mm, split(rims), (gh[...], gl[...]))
    hi_out[...], lo_out[...] = split(gathered)


def near_kernel(s, loc, nh, nl, hi, lo, out, rim_out):
    part = loc[...] + product(mm, (nh[...], nl[...]), (hi[...], lo[...]))
    out[...] = part
    rim_out[...] = pack_rim(part, s)


def first_kernel(s, part, fh, fl, cells, col, *refs):
    *layers, u_out, charges_out, values_out = refs
    layers = layers[: s.nz]
    weight_col = col[:, :1]
    occ = occupancy(cells[0], s)
    potentials = far_potentials(s, layers, (fh[...], fl[...]))
    values = pick(potentials[0], occ)
    u = part[...] + stacked([weight_col * values[c : c + 1] for c in range(3)], s)
    u_out[...] = u
    charges_out[...] = pack_charges(pieces(u, s), weight_col, occ, s)
    for index, value in enumerate(rim_values(s, layers, potentials)):
        values_out[index] = value


def order_kernel(x, _, out):
    out[...] = x[...]


def safe_inverse(x):
    return jnp.where(x > 0.0, 1.0 / jnp.where(x > 0.0, x, 1.0), 0.0)


def middle_kernel(s, u_in, f_in, rot, sh, sl, oh, ol, loc_out, gat_out, ortho_out, stat_out):
    u, f = u_in[...], f_in[...]
    loc, gat = local_part(u, s, rot[...], (sh[...], sl[...]), (oh[...], ol[...]))
    loc_out[...] = loc
    gat_out[...] = gat
    ff = total(f * f)
    fu = total(f * u) * safe_inverse(ff)
    ortho = u - fu * f
    ortho_out[...] = ortho
    oo = total(ortho * ortho)
    stat_out[...] = jnp.broadcast_to(
        jnp.concatenate([ff, fu, oo, jnp.zeros((5, 1), f32)], axis=0), (8, LANES)
    )


def second_kernel(
    s, loc, nh, nl, hi, lo, cells, col, f_in, ortho_in, stat, charges_f, charges_u, packed_out
):
    part = loc[...] + product(mm, (nh[...], nl[...]), (hi[...], lo[...]))
    f, ortho = f_in[...], ortho_in[...]
    ff, fu, oo = (stat[i : i + 1, :1] for i in range(3))
    fa = total(f * part) * safe_inverse(ff)
    oa = total(ortho * part) * safe_inverse(oo)
    rest = part - fa * f - oa * ortho
    aa = total(rest * rest)
    rf, ro = jnp.sqrt(ff), jnp.sqrt(oo)
    of_f = charges_f[-8:, :]
    of_u = charges_u[...]
    of_a = pack_charges(pieces(rest, s), col[:, :1], occupancy(cells[0], s), s, count=True)
    row = lax.broadcasted_iota(jnp.int32, (8, LANES), 0)
    lane = lax.broadcasted_iota(jnp.int32, (8, LANES), 1)
    left = lane < RIM
    first = jnp.where(left, of_u, pltpu.roll(of_a, RIM, 1))
    first = jnp.where(row < 4, of_u, first)
    first = jnp.where((row == 7) & left, pltpu.roll(of_f, 1, 0), first)
    for index, value in enumerate((rf, rf * fu, ro, rf * fa, ro * oa, aa)):
        first = jnp.where((row == 3) & (lane == index), value, first)
    tails = jnp.where(left, pltpu.roll(of_f, 3, 0), pltpu.roll(pltpu.roll(of_f, 2, 0), RIM, 1))
    second = jnp.where(row < 3, of_f, of_a)
    second = jnp.where(row < 4, second, pltpu.roll(of_a, 4, 0))
    second = jnp.where(row == 7, tails, second)
    for device in range(s.devices):
        packed_out[device] = second if s.odd(device) else first


def tree(s, leaves, ups, siblings, root):
    def apply(dot, blocks, factor):
        rows = blocks[0].shape[0]
        out = product(dot, split(jnp.concatenate(blocks, axis=0)), factor)
        return [out[i * rows : (i + 1) * rows] for i in range(len(blocks))]

    n = s.skel
    halves = [[(hi[level, j * n : (j + 1) * n, :], lo[level, j * n : (j + 1) * n, :]) for j in range(2)]
              for level, (hi, lo) in ((k, ups) for k in range(s.levels))]
    charges = [leaves]
    for level in range(s.levels):
        low, high = (apply(mm, charges[-1][j::2], halves[level][j]) for j in range(2))
        charges.append([a + b for a, b in zip(low, high)])
    own = charges[-1][0]
    whole = own[:8]
    for column in range(1, s.nx * s.ny):
        whole = whole + own[8 * column : 8 * column + 8]
    others = jnp.concatenate([whole] * (s.nx * s.ny), axis=0) - own
    potential = apply(mm, [others], root)
    for level in reversed(range(s.levels)):
        beside = apply(mm, charges[level], (siblings[0][level], siblings[1][level]))
        down = [apply(mt, potential, halves[level][j]) for j in range(2)]
        potential = [
            down[z % 2][z // 2] + beside[z ^ 1] for z in range(len(charges[level]))
        ]
    return potential


def box_numbers(s, firsts, seconds, ups, siblings, root):
    columns = s.nx * s.ny
    row = lax.broadcasted_iota(jnp.int32, (8, LANES), 0)
    lane = lax.broadcasted_iota(jnp.int32, (8, LANES), 1)
    left, valid = lane < RIM, row < 3
    leaves = []
    for z in range(s.nz):
        wide = []
        for column in range(columns):
            tile = firsts[column * s.nz + z]
            wide.append(jnp.concatenate([tile, pltpu.roll(tile, 4, 0)], axis=1)[:, : s.skel])
        leaves.append(jnp.concatenate(wide, axis=0))
    potential = tree(s, leaves, ups, siblings, root)
    out = []
    for start in range(0, s.devices, 8):
        sums = [jnp.zeros((8, LANES), f32) for _ in range(5)]
        for box in range(start, min(s.devices, start + 8)):
            column, z = box // s.nz, box % s.nz
            phi = potential[z][8 * column : 8 * column + 8]
            main, tail = phi[:, :LANES], phi[:, LANES:]
            tail = jnp.concatenate([tail, tail], axis=1)
            first, second = firsts[box], seconds[box]
            both = pltpu.roll(first, 4, 0) * tail
            of_f = jnp.where(row == 0, pltpu.roll(second, 1, 0), jnp.where(row == 1, pltpu.roll(second, 2, 0), pltpu.roll(first, 3, 0)))
            of_f = jnp.where(left == (row != 1), of_f * tail, 0.0)
            count = jnp.broadcast_to(second[3:4], (8, LANES))
            count_tail = jnp.where(left, 0.0, jnp.broadcast_to(first[7:8], (8, LANES)))
            terms = (
                second * main + of_f,
                first * main + jnp.where(left, both, 0.0),
                pltpu.roll(second, 4, 0) * main + jnp.where(left, 0.0, both),
                count * (main * main) + count_tail * (tail * tail),
            )
            here = row == box - start
            for index, term in enumerate(terms):
                value = jnp.sum(jnp.where(valid, term, 0.0), axis=0, keepdims=True)
                sums[index] = jnp.where(here, value, sums[index])
            sums[4] = jnp.where(here, first[3:4], sums[4])
        numbers = sums[4]
        for index in range(4):
            numbers = jnp.where(lane == 6 + index, jnp.sum(sums[index], axis=1, keepdims=True), numbers)
        out.append(numbers)
    rest = round_up(s.devices, LANES) - 8 * len(out)
    if rest:
        out.append(jnp.zeros((rest, LANES), f32))
    return jnp.concatenate(out, axis=0)


def finish_kernel(s, ids, f_in, u_in, mine, other, col, uh, ul, bh, bl, rh, rl, x_out, lsq_out, raw, sem):
    odd = (ids[0] // s.ny) % 2 == 1
    firsts = [jnp.where(odd, other[box], mine[box]) for box in range(s.devices)]
    seconds = [jnp.where(odd, mine[box], other[box]) for box in range(s.devices)]
    rows = box_numbers(s, firsts, seconds, (uh, ul), (bh, bl), (rh[...], rl[...])).T
    f1, u1, u2, t1, t2, aa, far_f, far_u, far_a, far_far = (rows[i : i + 1] for i in range(10))
    by_f = safe_inverse(f1)
    by_o = jnp.where(u2 * u2 > 1e-10 * (u1 * u1), safe_inverse(u2), 0.0)
    on_one = far_f * by_f
    on_two = (far_u - u1 * by_f * far_f) * by_o
    weight = jnp.sum(col[:, :1] * col[:, :1], axis=0, keepdims=True)
    t3 = aa + 2.0 * far_a + weight * far_far - on_one * on_one - on_two * on_two
    t1, t2, t3 = t1 + on_one, t2 + on_two, jnp.sqrt(jnp.maximum(t3, 0.0))

    def along(x):
        return jnp.sum(x, axis=1, keepdims=True)

    beta = jnp.sqrt(along(f1 * f1) + epsilon)
    v = f1 / beta
    w1, w2 = u1 / beta, u2 / beta
    h11 = along(w1 * v)
    r1 = w1 - h11 * v
    h21 = jnp.sqrt(along(r1 * r1 + w2 * w2) + epsilon)
    b1, b2 = r1 / h21, w2 / h21
    z1, z2, z3 = ((t1 / beta - h11 * w1) / h21, (t2 / beta - h11 * w2) / h21, t3 / beta / h21)
    h12 = along(z1 * v)
    h22 = along(z1 * b1 + z2 * b2)
    d1, d2 = z1 - h12 * v - h22 * b1, z2 - h22 * b2
    h32 = jnp.sqrt(along(d1 * d1 + d2 * d2 + z3 * z3) + epsilon)
    first_norm = jnp.sqrt(h11 * h11 + h21 * h21)
    c1, s1 = h11 / first_norm, h21 / first_norm
    t12, t22 = c1 * h12 + s1 * h22, c1 * h22 - s1 * h12
    second_norm = jnp.sqrt(t22 * t22 + h32 * h32)
    c2, s2 = t22 / second_norm, h32 / second_norm
    g2 = -s1 * beta
    y2 = c2 * g2 / second_norm
    y1 = (c1 * beta - t12 * y2) / first_norm
    lsq_out[...] = jnp.abs(s2 * g2)
    on_u = y2 / h21 / beta
    on_f = y1 / beta - on_u * h11
    for c in range(3):
        part = slice(c * s.step, c * s.step + s.blobs)
        raw[c * s.blobs : (c + 1) * s.blobs, 0, :] = on_f * f_in[part, :] + on_u * u_in[part, :]
    move = pltpu.make_async_copy(raw, x_out, sem)
    move.start()
    move.wait()


def call(kernel, outs, args, scalars=0, far_args=0, far_outs=0, scratch=(), flops=0):
    vmem = pl.BlockSpec(memory_space=pltpu.VMEM)
    smem = pl.BlockSpec(memory_space=pltpu.SMEM)
    hbm = pl.BlockSpec(memory_space=pltpu.HBM)
    near_args = len(args) - far_args
    args = args[:near_args] + [pltpu.with_memory_space_constraint(x, pltpu.HBM) for x in args[near_args:]]
    return pl.pallas_call(
        kernel,
        out_shape=[jax.ShapeDtypeStruct(shape, kind) for shape, kind in outs],
        in_specs=[smem] * scalars + [vmem] * (near_args - scalars) + [hbm] * far_args,
        out_specs=[hbm] * far_outs + [vmem] * (len(outs) - far_outs),
        scratch_shapes=list(scratch),
        compiler_params=pltpu.CompilerParams(vmem_limit_bytes=16 * 2**20),
        cost_estimate=pl.CostEstimate(flops=flops, bytes_accessed=2**20, transcendentals=0),
    )(*args)


def body(
    mesh_shape, rhs, angles, self_mob, near_mat, near_weight, neighbours, cells, blob_weight,
    skel_perm, interp, sibling_ops, root_op,
):
    s = Sizes(mesh_shape, rhs, skel_perm)
    full = (s.rows, s.bodies)
    square = (s.rows, s.rows)
    tile = (8, LANES)
    far_shape = (s.skel, 2 * s.far_tiles * LANES)
    column = lax.axis_index("gx") * s.ny + lax.axis_index("gy")
    ids = jnp.stack([column, lax.axis_index("gz")]).astype(jnp.int32)

    def fetch(x, kind, dy):
        pairs = []
        for gx in range(s.nx):
            for gy in range(s.ny):
                pairs.append((s.beside(kind, gx) * s.ny + (gy + dy) % s.ny, gx * s.ny + gy))
        return lax.ppermute(x, ("gx", "gy"), pairs)

    def fetch_layers(x):
        return [x] + [
            lax.ppermute(x, "gz", [(z ^ k, z) for z in range(s.nz)]) for k in range(1, s.nz)
        ]

    def fetch_rims(rim):
        got = {}
        for dy in s.shifts:
            got["other", dy] = fetch(rim, "other", dy)
        for dy in s.shifts:
            got["same", dy] = fetch(rim, "same", dy)
        got["other", 0] = fetch(rim, "other", 0)
        got["partner", 0] = fetch(rim, "partner", 0)
        return got

    def forward_rims(got, after):
        for dy in s.shifts:
            held = got["same", dy]
            (held,) = call(order_kernel, [(held.shape, f32)], [held, after])
            got["partner", dy] = fetch(held, "partner", 0)

    def plane_sum(message, got, after):
        if not s.direct:
            return [lax.psum(message[s.half :], ("gx", "gy"))]
        quarter = [message] + [got[key] for key in s.sources if key[0] != "partner"]
        (half,) = call(functools.partial(half_kernel, s), [(tile, f32)], quarter + [after])
        return [half, fetch(half, "partner", 0)]

    flat = (3 * s.blobs, 1, s.bodies)
    small = (1, s.blobs)
    message, col, cells, f = call(
        functools.partial(start_kernel, s),
        [((s.message, LANES), f32), ((s.step, LANES), f32), (cells.shape, jnp.int32), (full, f32)],
        [rhs.reshape(flat), cells, blob_weight.reshape(small)],
        far_args=3,
        scratch=[pltpu.VMEM(flat, f32), pltpu.VMEM(small, f32), pltpu.SemaphoreType.DMA((3,))],
        flops=10**7,
    )
    got = fetch_rims(message)
    operators = [
        angles.reshape(3, 1, s.bodies), near_weight, neighbours, self_mob, near_mat, skel_perm, interp,
        sibling_ops, root_op,
    ]
    loc, gat, rot, sh, sl, nh, nl, oh, ol, gh, gl, fh, fl, *operators_out = call(
        functools.partial(setup_kernel, s),
        [(full, f32), (full, f32), ((16, s.bodies), f32)]
        + [(square, bf16)] * 4
        + [((s.bodies, s.bodies), bf16)] * 2
        + [((s.ghosts, s.bodies), bf16)] * 2
        + [(far_shape, bf16)] * 2
        + [((s.levels, 2 * s.skel, s.skel), bf16)] * 2
        + [((s.levels, s.skel, s.skel), bf16)] * 2
        + [((s.skel, s.skel), bf16)] * 2,
        [ids, f] + operators,
        scalars=1,
        far_args=len(operators),
        scratch=[
            pltpu.VMEM(square, f32), pltpu.VMEM((s.levels, 2 * s.skel, s.skel), f32), pltpu.VMEM(far_shape, f32)
        ]
        + [pltpu.VMEM(x.shape, x.dtype) for x in operators]
        + [pltpu.SemaphoreType.DMA((len(operators),))],
        flops=5 * 10**9,
    )
    forward_rims(got, rot)
    sums = plane_sum(message, got, rot)
    around = [got[key] for key in s.sources]
    (tiles,) = call(
        functools.partial(layer_kernel, s, len(sums)),
        [((2 + len(around),) + tile, f32)],
        [message] + sums + around,
    )
    layers = fetch_layers(tiles)
    gathered = call(
        functools.partial(gather_kernel, s),
        [(full, bf16), (full, bf16)],
        [gat, gh, gl] + around + [tiles],
        flops=10**9,
    )
    part, rim = call(
        functools.partial(near_kernel, s),
        [(full, f32), ((s.half, LANES), f32)],
        [loc, nh, nl, *gathered],
        flops=10**9,
    )
    got = fetch_rims(rim)
    u, charges, values = call(
        functools.partial(first_kernel, s),
        [(full, f32), (tile, f32), ((s.ghosts // LANES,) + tile, f32)],
        [part, fh, fl, cells, col, *layers] + [got[kind, dy] for kind in ("other", "same") for dy in s.shifts],
        flops=10**8,
    )
    loc, gat, ortho, stat = call(
        functools.partial(middle_kernel, s),
        [(full, f32), (full, f32), (full, f32), (tile, f32)],
        [u, f, rot, sh, sl, oh, ol],
        flops=10**9,
    )
    forward_rims(got, charges)
    gathered = call(
        functools.partial(gather_far_kernel, s),
        [(full, bf16), (full, bf16)],
        [gat, gh, gl, col, values] + [got[key] for key in s.sources],
        flops=10**9,
    )
    (packed,) = call(
        functools.partial(second_kernel, s),
        [((s.devices, 8, LANES), f32)],
        [loc, nh, nl, *gathered, cells, col, f, ortho, stat, message, charges],
        flops=10**9,
    )
    boxes = lax.all_to_all(packed, ("gx", "gy", "gz"), 0, 0)
    result, lsq = call(
        functools.partial(finish_kernel, s),
        [(flat, f32), ((1, 1), f32)],
        [ids, f, u, boxes, fetch(boxes, "partner", 0), col, *operators_out],
        scalars=1,
        far_outs=1,
        scratch=[pltpu.VMEM(flat, f32), pltpu.SemaphoreType.DMA],
        flops=10**7,
    )
    return result.reshape(rhs.shape), lsq.reshape(())


def solution(mesh):
    in_specs = (
        P("gx", "gy", None, None, "gz"),
        P("gx", "gy", None, "gz"),
        P(),
        P(),
        P("gx", "gy", None, "gz"),
        P("gx", "gy", None, "gz"),
        P("gx", "gy", "gz"),
        P(),
        P(),
        P(),
        P(),
        P(),
    )
    out_specs = (P("gx", "gy", None, None, "gz"), P())
    inner = functools.partial(body, dict(mesh.shape))
    return jax.shard_map(inner, mesh=mesh, in_specs=in_specs, out_specs=out_specs, check_vma=False)
```

```python
import functools

import jax
import jax.numpy as jnp
from jax import lax
from jax.experimental import pallas as pl
from jax.experimental.pallas import tpu as pltpu
from jax.sharding import PartitionSpec as P

epsilon = 1e-06
f32 = jnp.float32
bf16 = jnp.bfloat16
RIM = 64
LANES = 128


def round_up(value, unit):
    return -(-value // unit) * unit


def split(x):
    hi = x.astype(bf16)
    lo = (x - hi.astype(f32)).astype(bf16)
    return hi, lo


def mm(a, b):
    return lax.dot_general(a, b, (((1,), (0,)), ((), ())), preferred_element_type=f32)


def mt(a, b):
    return lax.dot_general(a, b, (((1,), (1,)), ((), ())), preferred_element_type=f32)


def product(dot, a, b):
    return dot(a[0], b[0]) + (dot(a[0], b[1]) + dot(a[1], b[0]))


def total(x):
    return jnp.sum(jnp.sum(x, axis=0, keepdims=True), axis=1, keepdims=True)


class Sizes:
    def __init__(self, mesh_shape, rhs, skel_perm):
        self.nx, self.ny, self.nz = (mesh_shape[a] for a in ("gx", "gy", "gz"))
        self.devices = self.nx * self.ny * self.nz
        self.blobs, self.bodies = rhs.shape[-2:]
        self.step = round_up(self.blobs, 8)
        self.rows = round_up(3 * self.step, 16)
        self.half = self.rows // 2
        self.message = self.half + 8
        self.direct = (self.nx, self.ny) == (4, 2)
        self.levels = skel_perm.shape[0]
        self.skel = skel_perm.shape[1] // 2
        shifts = sorted({(dy % self.ny) for dy in (-1, 1)} - {0})
        self.shifts = shifts
        self.sources = [("same", dy) for dy in shifts]
        for kind in ("other", "partner"):
            self.sources += [(kind, dy) for dy in [0] + shifts]
        self.ghosts = round_up(len(self.sources) * RIM, LANES)
        self.far_tiles = self.nz + -(-self.nz // 2)

    def slot_start(self, slot, parity):
        dx, dy = slot // 3 - 1, (slot % 3 - 1) % self.ny
        kind = "same" if dx == 0 else "partner" if dx == 1 - 2 * parity else "other"
        if (kind, dy) == ("same", 0):
            return 0
        return self.bodies + RIM * self.sources.index((kind, dy))

    def odd(self, device):
        return (device // (self.ny * self.nz)) % 2

    def beside(self, kind, x):
        if kind == "same":
            return x
        if kind == "partner":
            return x ^ 1
        return (x + 2 * (x % 2) - 1) % self.nx


def pieces(x, s):
    return [x[c * s.step : c * s.step + s.step] for c in range(3)]


def turn(parts, rot, inverse):
    out = []
    for target in range(3):
        acc = None
        for source in range(3):
            row = 3 * source + target if inverse else 3 * target + source
            term = rot[row : row + 1] * parts[source]
            acc = term if acc is None else acc + term
        out.append(acc)
    return out


def stacked(parts, s):
    rest = s.rows - 3 * s.step
    if rest:
        parts = list(parts) + [jnp.zeros((rest, parts[0].shape[1]), f32)]
    return jnp.concatenate(parts, axis=0)


def occupancy(cells, s):
    row = lax.broadcasted_iota(jnp.int32, (s.skel, s.bodies), 0)
    return jnp.where(cells == row, 1.0, 0.0).astype(bf16)


def pack_charges(parts, weight_col, occ, s, count=False):
    moments = [jnp.sum(part * weight_col, axis=0, keepdims=True) for part in parts]
    moments.append(jnp.full((1, s.bodies), 1.0 if count else 0.0, f32))
    moments = jnp.concatenate(moments + [jnp.zeros((4, s.bodies), f32)], axis=0)
    high, rest = split(moments)
    mid, low = split(moments - high.astype(f32))
    stack = jnp.concatenate([high.astype(f32), mid.astype(f32), low.astype(f32)], axis=0).astype(bf16)
    sums = mt(stack, occ)
    charges = sums[0:8] + (sums[8:16] + sums[16:24])
    tail = jnp.concatenate([charges[:, LANES:], jnp.zeros((8, 2 * LANES - s.skel), f32)], axis=1)
    row = lax.broadcasted_iota(jnp.int32, (8, LANES), 0)
    return jnp.where(row < 4, charges[:, :LANES], pltpu.roll(tail, 4, 0))


def pack_rim(x, s):
    lane = lax.broadcasted_iota(jnp.int32, (s.half, LANES), 1)
    top, bottom = x[: s.half, :LANES], x[s.half :, :LANES]
    return jnp.where(lane < RIM, top, pltpu.roll(bottom, RIM, 1))


def unpack_rims(rims, s):
    lane = lax.broadcasted_iota(jnp.int32, (s.half, LANES), 1)
    tops, bottoms = [], []
    for i in range(0, s.ghosts // RIM, 2):
        a = rims[i]
        b = rims[i + 1] if i + 1 < len(rims) else jnp.zeros_like(a)
        tops.append(jnp.where(lane < RIM, a, pltpu.roll(b, RIM, 1)))
        bottoms.append(jnp.where(lane < RIM, pltpu.roll(a, RIM, 1), b))
    return jnp.concatenate(
        [jnp.concatenate(tops, axis=1), jnp.concatenate(bottoms, axis=1)], axis=0
    )


def pack_message(x, weight_col, cells, s):
    charges = pack_charges(pieces(x, s), weight_col, occupancy(cells, s), s)
    row = lax.broadcasted_iota(jnp.int32, (8, LANES), 0)
    charges = jnp.where(row == 3, cells[:, :LANES].astype(f32), charges)
    return jnp.concatenate([pack_rim(x, s), charges], axis=0)


def begin(sources, targets, sems):
    moves = [pltpu.make_async_copy(a, b, sems.at[i]) for i, (a, b) in enumerate(zip(sources, targets))]
    for move in moves:
        move.start()
    return moves


def start_kernel(s, rhs, cells, weight, message_out, col_out, cells_out, f_out, raw, wide, sems):
    moves = begin((weight, cells, rhs), (wide, cells_out, raw), sems)
    f_out[...] = jnp.zeros_like(f_out)
    moves[0].wait()
    row = jnp.concatenate([wide[...], jnp.zeros((1, 2 * LANES - s.blobs), f32)], axis=1)
    col = jnp.broadcast_to(row, (LANES, 2 * LANES)).T[: s.step]
    col_out[...] = col
    for move in moves[1:]:
        move.wait()
    for c in range(3):
        f_out[c * s.step : c * s.step + s.blobs, :] = raw[c * s.blobs : (c + 1) * s.blobs, 0, :]
    message_out[...] = pack_message(f_out[...], col[:, :1], cells_out[0], s)


def frame_rows(angles):
    cos, sin = jnp.cos(angles), jnp.sin(angles)
    cy, cp, cr = cos[0:1], cos[1:2], cos[2:3]
    sy, sp, sr = sin[0:1], sin[1:2], sin[2:3]
    return [
        cy * cp,
        cy * sp * sr - sy * cr,
        cy * sp * cr + sy * sr,
        sy * cp,
        sy * sp * sr + cy * cr,
        sy * sp * cr - cy * sr,
        -sp,
        cp * sr,
        cp * cr,
    ]


def local_part(f, s, rot, mob, own):
    parts = pieces(f, s)
    turned = stacked(turn(parts, rot, False), s)
    mixed = product(mm, mob, split(turned))
    back = turn(pieces(mixed, s), rot, True)
    return f + stacked(back, s), product(mm, split(f), own)


def product_many(dot, blocks, b):
    rows = blocks[0].shape[0]
    out = product(dot, split(jnp.concatenate(blocks, axis=0)), split(b))
    return [out[i * rows : (i + 1) * rows] for i in range(len(blocks))]


def expand_once(groups, halves):
    flat = [block for group in groups for block in group]
    sides = [product_many(mt, flat, half) for half in halves]
    out, at = [], 0
    for group in groups:
        spread = []
        for i in range(at, at + len(group)):
            spread += [sides[0][i], sides[1][i]]
        at += len(group)
        out.append(spread)
    return out


def setup_kernel(
    s, ids, f_in, *refs
):
    count = 9
    sources, refs = refs[:count], refs[count:]
    copies, refs = refs[-1 - count :], refs[: -1 - count]
    copies, sems = copies[:-1], copies[-1]
    setup(s, ids, f_in, begin(sources, copies, sems), *copies, *refs)


def setup(
    s, ids, f_in, moves, angles, near_weight, neighbours, self_mob, near_mat, perm, interp, sibling, root,
    loc_out, gat_out, rot_out, sh_out, sl_out, nh_out, nl_out, oh_out, ol_out, gh_out, gl_out,
    fh_out, fl_out, uh_out, ul_out, bh_out, bl_out, rh_out, rl_out, padded, ups_ref, far_ref,
):
    f = f_in[...]
    for move in moves[:3]:
        move.wait()
    rot = jnp.concatenate(frame_rows(angles[:, 0, :]) + [jnp.zeros((7, s.bodies), f32)], axis=0)
    rot_out[...] = rot

    links = neighbours[0, 0]
    slot = links // s.bodies
    base = jnp.zeros_like(links)
    odd = (ids[0] // s.ny) % 2
    for index in range(9):
        start = jnp.where(odd == 1, s.slot_start(index, 1), s.slot_start(index, 0))
        base = jnp.where(slot == index, start, base)
    column = base + links % s.bodies
    coef = near_weight[0, 0]
    for first, count, hi_out, lo_out in (
        (0, s.bodies, oh_out, ol_out),
        (s.bodies, s.ghosts, gh_out, gl_out),
    ):
        for r in range(0, count, 64):
            row = lax.broadcasted_iota(jnp.int32, (64, s.bodies), 0) + (first + r)
            acc = jnp.zeros((64, s.bodies), f32)
            for k in range(coef.shape[0]):
                acc = acc + jnp.where(column[k : k + 1] == row, coef[k : k + 1], 0.0)
            hi, lo = split(acc)
            hi_out[r : r + 64, :] = hi
            lo_out[r : r + 64, :] = lo

    for move in moves[3:]:
        move.wait()
    padded[...] = jnp.zeros_like(padded)
    for matrix, hi_out, lo_out in ((self_mob, sh_out, sl_out), (near_mat, nh_out, nl_out)):
        for c in range(3):
            for d in range(3):
                padded[c * s.step : c * s.step + s.blobs, d * s.step : d * s.step + s.blobs] = matrix[
                    c * s.blobs : (c + 1) * s.blobs, d * s.blobs : (d + 1) * s.blobs
                ]
        hi, lo = split(padded[...])
        hi_out[...] = hi
        lo_out[...] = lo

    loc, gat = local_part(f, s, rot, (sh_out[...], sl_out[...]), (oh_out[...], ol_out[...]))
    loc_out[...] = loc
    gat_out[...] = gat

    n = s.skel
    z = ids[1]
    halves = []
    spot = lax.broadcasted_iota(jnp.int32, (2 * n, n), 0)
    for level in range(s.levels):
        kept = jnp.where(perm[level : level + 1, :n] == spot, 1.0, 0.0)
        moved = jnp.where(perm[level : level + 1, n:] == spot, 1.0, 0.0).astype(bf16)
        hi, lo = split(interp[level])
        up = kept + (mm(moved, hi) + mm(moved, lo))
        ups_ref[level] = up
        uh_out[level], ul_out[level] = split(up)
        bh_out[level], bl_out[level] = split(sibling[level])
        bit = (z >> level) & 1
        halves.append(
            [ups_ref[level, pl.ds(pl.multiple_of(side * n, 8), n), :] for side in (bit, 1 - bit)]
        )

    def down(block, level, dot):
        return product(dot, split(halves[level][0]), split(block))

    spread = root[...]
    rh_out[...], rl_out[...] = split(spread)
    beside = []
    for level in reversed(range(s.levels)):
        spread = down(spread, level, mt if level == s.levels - 1 else mm)
        beside = [(down(block, level, mt if fresh else mm), False) for block, fresh in beside]
        beside.append((sibling[level], True))
    beside = [block.T if fresh else block for block, fresh in reversed(beside)]
    leaves = [[spread]]
    for level in reversed(range(s.levels)):
        leaves = expand_once(leaves, halves[level])
        leaves.append([beside[level]])
    far_leaves, *sub = leaves
    near_leaves = [jnp.zeros((n, n), f32)]
    for blocks in reversed(sub):
        near_leaves += blocks
    tail = n - LANES
    far_ref[...] = jnp.zeros_like(far_ref)
    own = [a - b for a, b in zip(near_leaves, far_leaves)]
    for group, blocks in enumerate((own, far_leaves)):
        for leaf, block in enumerate(blocks):
            at = (group * s.far_tiles + leaf) * LANES
            far_ref[:, at : at + LANES] = block[:, :LANES]
            at = (group * s.far_tiles + s.nz + leaf // 2) * LANES + leaf % 2 * RIM
            far_ref[:, at : at + tail] = block[:, LANES:]
    fh_out[...], fl_out[...] = split(far_ref[...])


def half_kernel(s, *refs):
    *messages, _, out = refs
    acc = messages[0][s.half :, :]
    for message in messages[1:]:
        acc = acc + message[s.half :, :]
    out[...] = acc


def layer_kernel(s, count, message, *refs):
    sums, around, out = refs[:count], refs[count:-1], refs[-1]
    acc = sums[0][...]
    for part in sums[1:]:
        acc = acc + part[...]
    out[0] = message[s.half :, :]
    out[1] = acc
    for index, other in enumerate(around):
        out[2 + index] = other[s.half :, :]


def layer_row(s, tiles):
    row = list(tiles)
    lane = lax.broadcasted_iota(jnp.int32, (8, LANES), 1)
    for leaf in range(0, s.nz, 2):
        pair = tiles[leaf]
        if leaf + 1 < s.nz:
            pair = jnp.where(lane < RIM, pair, pltpu.roll(tiles[leaf + 1], RIM, 1))
        row.append(pltpu.roll(pair, 4, 0))
    return jnp.concatenate(row, axis=1)


def far_potentials(s, layers, far_op):
    own = [layer_row(s, [layer[k] for layer in layers]) for k in range(layers[0].shape[0])]
    wide = own[0].shape[1]
    hi, lo = far_op
    whole = product(mt, split(own.pop(1)), (hi[:, wide:], lo[:, wide:]))
    boxes = product(mt, split(jnp.concatenate(own, axis=0)), (hi[:, :wide], lo[:, :wide]))
    return [boxes[8 * k : 8 * k + 8] + whole for k in range(len(own))]


def pick(potential, onehot):
    high, _ = split(potential)
    mid, low = split(potential - high.astype(f32))
    parts = [x.astype(f32) for x in (high, mid, low)]
    picked = mm(jnp.concatenate(parts, axis=0).astype(bf16), onehot)
    n = potential.shape[0]
    return picked[:n] + (picked[n : 2 * n] + picked[2 * n :])


def rim_values(s, layers, potentials):
    lane = lax.broadcasted_iota(jnp.int32, (8, LANES), 1)
    place = lax.broadcasted_iota(jnp.int32, (s.skel, LANES), 0).astype(f32)
    count = len(potentials) - 1
    out = []
    for i in range(0, count, 2):
        last = min(i + 1, count - 1)
        cells = jnp.where(lane < RIM, layers[0][2 + i], pltpu.roll(layers[0][2 + last], RIM, 1))
        onehot = jnp.where(cells[3:4] == place, 1.0, 0.0).astype(bf16)
        both = pick(jnp.concatenate([potentials[1 + i], potentials[1 + last]], axis=0), onehot)
        out.append(jnp.where(lane < RIM, both[:8], both[8:]))
    return out


def gather_kernel(s, gat, gh, gl, *refs):
    *messages, _, hi_out, lo_out = refs
    rims = unpack_rims([message[: s.half, :] for message in messages], s)
    gathered = gat[...] + product(mm, split(rims), (gh[...], gl[...]))
    hi_out[...], lo_out[...] = split(gathered)


def gather_far_kernel(s, gat, gh, gl, col, values, *refs):
    *messages, hi_out, lo_out = refs
    rims = unpack_rims([message[...] for message in messages], s)
    far = []
    for c in range(3):
        value = jnp.concatenate([values[i, c : c + 1, :] for i in range(values.shape[0])], axis=1)
        far.append(col[:, :1] * value)
    rims = rims + stacked(far, s)
    gathered = gat[...] + product(mm, split(rims), (gh[...], gl[...]))
    hi_out[...], lo_out[...] = split(gathered)


def near_kernel(s, loc, nh, nl, hi, lo, out, rim_out):
    part = loc[...] + product(mm, (nh[...], nl[...]), (hi[...], lo[...]))
    out[...] = part
    rim_out[...] = pack_rim(part, s)


def first_kernel(s, part, fh, fl, cells, col, *refs):
    *layers, u_out, charges_out, values_out = refs
    layers = layers[: s.nz]
    weight_col = col[:, :1]
    occ = occupancy(cells[0], s)
    potentials = far_potentials(s, layers, (fh[...], fl[...]))
    values = pick(potentials[0], occ)
    u = part[...] + stacked([weight_col * values[c : c + 1] for c in range(3)], s)
    u_out[...] = u
    charges_out[...] = pack_charges(pieces(u, s), weight_col, occ, s)
    for index, value in enumerate(rim_values(s, layers, potentials)):
        values_out[index] = value


def order_kernel(x, _, out):
    out[...] = x[...]


def safe_inverse(x):
    return jnp.where(x > 0.0, 1.0 / jnp.where(x > 0.0, x, 1.0), 0.0)


def middle_kernel(s, u_in, f_in, rot, sh, sl, oh, ol, loc_out, gat_out, ortho_out, stat_out):
    u, f = u_in[...], f_in[...]
    loc, gat = local_part(u, s, rot[...], (sh[...], sl[...]), (oh[...], ol[...]))
    loc_out[...] = loc
    gat_out[...] = gat
    ff = total(f * f)
    fu = total(f * u) * safe_inverse(ff)
    ortho = u - fu * f
    ortho_out[...] = ortho
    oo = total(ortho * ortho)
    stat_out[...] = jnp.broadcast_to(
        jnp.concatenate([ff, fu, oo, jnp.zeros((5, 1), f32)], axis=0), (8, LANES)
    )


def second_kernel(
    s, loc, nh, nl, hi, lo, cells, col, f_in, ortho_in, stat, charges_f, charges_u, packed_out
):
    part = loc[...] + product(mm, (nh[...], nl[...]), (hi[...], lo[...]))
    f, ortho = f_in[...], ortho_in[...]
    ff, fu, oo = (stat[i : i + 1, :1] for i in range(3))
    fa = total(f * part) * safe_inverse(ff)
    oa = total(ortho * part) * safe_inverse(oo)
    rest = part - fa * f - oa * ortho
    aa = total(rest * rest)
    rf, ro = jnp.sqrt(ff), jnp.sqrt(oo)
    of_f = charges_f[-8:, :]
    of_u = charges_u[...]
    of_a = pack_charges(pieces(rest, s), col[:, :1], occupancy(cells[0], s), s, count=True)
    row = lax.broadcasted_iota(jnp.int32, (8, LANES), 0)
    lane = lax.broadcasted_iota(jnp.int32, (8, LANES), 1)
    left = lane < RIM
    first = jnp.where(left, of_u, pltpu.roll(of_a, RIM, 1))
    first = jnp.where(row < 4, of_u, first)
    first = jnp.where((row == 7) & left, pltpu.roll(of_f, 1, 0), first)
    for index, value in enumerate((rf, rf * fu, ro, rf * fa, ro * oa, aa)):
        first = jnp.where((row == 3) & (lane == index), value, first)
    tails = jnp.where(left, pltpu.roll(of_f, 3, 0), pltpu.roll(pltpu.roll(of_f, 2, 0), RIM, 1))
    second = jnp.where(row < 3, of_f, of_a)
    second = jnp.where(row < 4, second, pltpu.roll(of_a, 4, 0))
    second = jnp.where(row == 7, tails, second)
    for device in range(s.devices):
        packed_out[device] = second if s.odd(device) else first


def tree(s, leaves, ups, siblings, root):
    def apply(dot, blocks, factor):
        rows = blocks[0].shape[0]
        out = product(dot, split(jnp.concatenate(blocks, axis=0)), factor)
        return [out[i * rows : (i + 1) * rows] for i in range(len(blocks))]

    n = s.skel
    halves = [[(hi[level, j * n : (j + 1) * n, :], lo[level, j * n : (j + 1) * n, :]) for j in range(2)]
              for level, (hi, lo) in ((k, ups) for k in range(s.levels))]
    charges = [leaves]
    for level in range(s.levels):
        low, high = (apply(mm, charges[-1][j::2], halves[level][j]) for j in range(2))
        charges.append([a + b for a, b in zip(low, high)])
    own = charges[-1][0]
    whole = own[:8]
    for column in range(1, s.nx * s.ny):
        whole = whole + own[8 * column : 8 * column + 8]
    others = jnp.concatenate([whole] * (s.nx * s.ny), axis=0) - own
    potential = apply(mm, [others], root)
    for level in reversed(range(s.levels)):
        beside = apply(mm, charges[level], (siblings[0][level], siblings[1][level]))
        down = [apply(mt, potential, halves[level][j]) for j in range(2)]
        potential = [
            down[z % 2][z // 2] + beside[z ^ 1] for z in range(len(charges[level]))
        ]
    return potential


def box_numbers(s, firsts, seconds, ups, siblings, root):
    columns = s.nx * s.ny
    row = lax.broadcasted_iota(jnp.int32, (8, LANES), 0)
    lane = lax.broadcasted_iota(jnp.int32, (8, LANES), 1)
    left, valid = lane < RIM, row < 3
    leaves = []
    for z in range(s.nz):
        wide = []
        for column in range(columns):
            tile = firsts[column * s.nz + z]
            wide.append(jnp.concatenate([tile, pltpu.roll(tile, 4, 0)], axis=1)[:, : s.skel])
        leaves.append(jnp.concatenate(wide, axis=0))
    potential = tree(s, leaves, ups, siblings, root)
    out = []
    for start in range(0, s.devices, 8):
        sums = [jnp.zeros((8, LANES), f32) for _ in range(5)]
        for box in range(start, min(s.devices, start + 8)):
            column, z = box // s.nz, box % s.nz
            phi = potential[z][8 * column : 8 * column + 8]
            main, tail = phi[:, :LANES], phi[:, LANES:]
            tail = jnp.concatenate([tail, tail], axis=1)
            first, second = firsts[box], seconds[box]
            both = pltpu.roll(first, 4, 0) * tail
            of_f = jnp.where(row == 0, pltpu.roll(second, 1, 0), jnp.where(row == 1, pltpu.roll(second, 2, 0), pltpu.roll(first, 3, 0)))
            of_f = jnp.where(left == (row != 1), of_f * tail, 0.0)
            count = jnp.broadcast_to(second[3:4], (8, LANES))
            count_tail = jnp.where(left, 0.0, jnp.broadcast_to(first[7:8], (8, LANES)))
            terms = (
                second * main + of_f,
                first * main + jnp.where(left, both, 0.0),
                pltpu.roll(second, 4, 0) * main + jnp.where(left, 0.0, both),
                count * (main * main) + count_tail * (tail * tail),
            )
            here = row == box - start
            for index, term in enumerate(terms):
                value = jnp.sum(jnp.where(valid, term, 0.0), axis=0, keepdims=True)
                sums[index] = jnp.where(here, value, sums[index])
            sums[4] = jnp.where(here, first[3:4], sums[4])
        numbers = sums[4]
        for index in range(4):
            numbers = jnp.where(lane == 6 + index, jnp.sum(sums[index], axis=1, keepdims=True), numbers)
        out.append(numbers)
    rest = round_up(s.devices, LANES) - 8 * len(out)
    if rest:
        out.append(jnp.zeros((rest, LANES), f32))
    return jnp.concatenate(out, axis=0)


def finish_kernel(s, ids, f_in, u_in, mine, other, col, uh, ul, bh, bl, rh, rl, x_out, lsq_out, raw, sem):
    odd = (ids[0] // s.ny) % 2 == 1
    firsts = [jnp.where(odd, other[box], mine[box]) for box in range(s.devices)]
    seconds = [jnp.where(odd, mine[box], other[box]) for box in range(s.devices)]
    rows = box_numbers(s, firsts, seconds, (uh, ul), (bh, bl), (rh[...], rl[...])).T
    f1, u1, u2, t1, t2, aa, far_f, far_u, far_a, far_far = (rows[i : i + 1] for i in range(10))
    by_f = safe_inverse(f1)
    by_o = jnp.where(u2 * u2 > 1e-10 * (u1 * u1), safe_inverse(u2), 0.0)
    on_one = far_f * by_f
    on_two = (far_u - u1 * by_f * far_f) * by_o
    weight = jnp.sum(col[:, :1] * col[:, :1], axis=0, keepdims=True)
    t3 = aa + 2.0 * far_a + weight * far_far - on_one * on_one - on_two * on_two
    t1, t2, t3 = t1 + on_one, t2 + on_two, jnp.sqrt(jnp.maximum(t3, 0.0))

    def along(x):
        return jnp.sum(x, axis=1, keepdims=True)

    beta = jnp.sqrt(along(f1 * f1) + epsilon)
    v = f1 / beta
    w1, w2 = u1 / beta, u2 / beta
    h11 = along(w1 * v)
    r1 = w1 - h11 * v
    h21 = jnp.sqrt(along(r1 * r1 + w2 * w2) + epsilon)
    b1, b2 = r1 / h21, w2 / h21
    z1, z2, z3 = ((t1 / beta - h11 * w1) / h21, (t2 / beta - h11 * w2) / h21, t3 / beta / h21)
    h12 = along(z1 * v)
    h22 = along(z1 * b1 + z2 * b2)
    d1, d2 = z1 - h12 * v - h22 * b1, z2 - h22 * b2
    h32 = jnp.sqrt(along(d1 * d1 + d2 * d2 + z3 * z3) + epsilon)
    first_norm = jnp.sqrt(h11 * h11 + h21 * h21)
    c1, s1 = h11 / first_norm, h21 / first_norm
    t12, t22 = c1 * h12 + s1 * h22, c1 * h22 - s1 * h12
    second_norm = jnp.sqrt(t22 * t22 + h32 * h32)
    c2, s2 = t22 / second_norm, h32 / second_norm
    g2 = -s1 * beta
    y2 = c2 * g2 / second_norm
    y1 = (c1 * beta - t12 * y2) / first_norm
    lsq_out[...] = jnp.abs(s2 * g2)
    on_u = y2 / h21 / beta
    on_f = y1 / beta - on_u * h11
    for c in range(3):
        part = slice(c * s.step, c * s.step + s.blobs)
        raw[c * s.blobs : (c + 1) * s.blobs, 0, :] = on_f * f_in[part, :] + on_u * u_in[part, :]
    move = pltpu.make_async_copy(raw, x_out, sem)
    move.start()
    move.wait()


def call(kernel, outs, args, scalars=0, far_args=0, far_outs=0, scratch=(), flops=0):
    vmem = pl.BlockSpec(memory_space=pltpu.VMEM)
    smem = pl.BlockSpec(memory_space=pltpu.SMEM)
    hbm = pl.BlockSpec(memory_space=pltpu.HBM)
    near_args = len(args) - far_args
    args = args[:near_args] + [pltpu.with_memory_space_constraint(x, pltpu.HBM) for x in args[near_args:]]
    return pl.pallas_call(
        kernel,
        out_shape=[jax.ShapeDtypeStruct(shape, kind) for shape, kind in outs],
        in_specs=[smem] * scalars + [vmem] * (near_args - scalars) + [hbm] * far_args,
        out_specs=[hbm] * far_outs + [vmem] * (len(outs) - far_outs),
        scratch_shapes=list(scratch),
        compiler_params=pltpu.CompilerParams(vmem_limit_bytes=16 * 2**20),
        cost_estimate=pl.CostEstimate(flops=flops, bytes_accessed=2**20, transcendentals=0),
    )(*args)


def body(
    mesh_shape, rhs, angles, self_mob, near_mat, near_weight, neighbours, cells, blob_weight,
    skel_perm, interp, sibling_ops, root_op,
):
    s = Sizes(mesh_shape, rhs, skel_perm)
    full = (s.rows, s.bodies)
    square = (s.rows, s.rows)
    tile = (8, LANES)
    far_shape = (s.skel, 2 * s.far_tiles * LANES)
    column = lax.axis_index("gx") * s.ny + lax.axis_index("gy")
    ids = jnp.stack([column, lax.axis_index("gz")]).astype(jnp.int32)

    def fetch(x, kind, dy):
        pairs = []
        for gx in range(s.nx):
            for gy in range(s.ny):
                pairs.append((s.beside(kind, gx) * s.ny + (gy + dy) % s.ny, gx * s.ny + gy))
        return lax.ppermute(x, ("gx", "gy"), pairs)

    def fetch_layers(x):
        return [x] + [
            lax.ppermute(x, "gz", [(z ^ k, z) for z in range(s.nz)]) for k in range(1, s.nz)
        ]

    def fetch_rims(rim):
        got = {}
        for dy in s.shifts:
            got["other", dy] = fetch(rim, "other", dy)
        for dy in s.shifts:
            got["same", dy] = fetch(rim, "same", dy)
        got["other", 0] = fetch(rim, "other", 0)
        got["partner", 0] = fetch(rim, "partner", 0)
        return got

    def forward_rims(got, after):
        for dy in s.shifts:
            held = got["same", dy]
            (held,) = call(order_kernel, [(held.shape, f32)], [held, after])
            got["partner", dy] = fetch(held, "partner", 0)

    def plane_sum(message, got, after):
        if not s.direct:
            return [lax.psum(message[s.half :], ("gx", "gy"))]
        quarter = [message] + [got[key] for key in s.sources if key[0] != "partner"]
        (half,) = call(functools.partial(half_kernel, s), [(tile, f32)], quarter + [after])
        return [half, fetch(half, "partner", 0)]

    flat = (3 * s.blobs, 1, s.bodies)
    small = (1, s.blobs)
    message, col, cells, f = call(
        functools.partial(start_kernel, s),
        [((s.message, LANES), f32), ((s.step, LANES), f32), (cells.shape, jnp.int32), (full, f32)],
        [rhs.reshape(flat), cells, blob_weight.reshape(small)],
        far_args=3,
        scratch=[pltpu.VMEM(flat, f32), pltpu.VMEM(small, f32), pltpu.SemaphoreType.DMA((3,))],
        flops=10**7,
    )
    got = fetch_rims(message)
    operators = [
        angles.reshape(3, 1, s.bodies), near_weight, neighbours, self_mob, near_mat, skel_perm, interp,
        sibling_ops, root_op,
    ]
    loc, gat, rot, sh, sl, nh, nl, oh, ol, gh, gl, fh, fl, *operators_out = call(
        functools.partial(setup_kernel, s),
        [(full, f32), (full, f32), ((16, s.bodies), f32)]
        + [(square, bf16)] * 4
        + [((s.bodies, s.bodies), bf16)] * 2
        + [((s.ghosts, s.bodies), bf16)] * 2
        + [(far_shape, bf16)] * 2
        + [((s.levels, 2 * s.skel, s.skel), bf16)] * 2
        + [((s.levels, s.skel, s.skel), bf16)] * 2
        + [((s.skel, s.skel), bf16)] * 2,
        [ids, f] + operators,
        scalars=1,
        far_args=len(operators),
        scratch=[
            pltpu.VMEM(square, f32), pltpu.VMEM((s.levels, 2 * s.skel, s.skel), f32), pltpu.VMEM(far_shape, f32)
        ]
        + [pltpu.VMEM(x.shape, x.dtype) for x in operators]
        + [pltpu.SemaphoreType.DMA((len(operators),))],
        flops=5 * 10**9,
    )
    forward_rims(got, rot)
    sums = plane_sum(message, got, rot)
    around = [got[key] for key in s.sources]
    (tiles,) = call(
        functools.partial(layer_kernel, s, len(sums)),
        [((2 + len(around),) + tile, f32)],
        [message] + sums + around,
    )
    layers = fetch_layers(tiles)
    gathered = call(
        functools.partial(gather_kernel, s),
        [(full, bf16), (full, bf16)],
        [gat, gh, gl] + around + [tiles],
        flops=10**9,
    )
    part, rim = call(
        functools.partial(near_kernel, s),
        [(full, f32), ((s.half, LANES), f32)],
        [loc, nh, nl, *gathered],
        flops=10**9,
    )
    got = fetch_rims(rim)
    ahead = [got["other", 0]] + [got[kind, dy] for kind in ("other", "same") for dy in s.shifts]
    u, charges, values = call(
        functools.partial(first_kernel, s),
        [(full, f32), (tile, f32), ((s.ghosts // LANES,) + tile, f32)],
        [part, fh, fl, cells, col, *layers] + ahead,
        flops=10**8,
    )
    loc, gat, ortho, stat = call(
        functools.partial(middle_kernel, s),
        [(full, f32), (full, f32), (full, f32), (tile, f32)],
        [u, f, rot, sh, sl, oh, ol],
        flops=10**9,
    )
    forward_rims(got, charges)
    gathered = call(
        functools.partial(gather_far_kernel, s),
        [(full, bf16), (full, bf16)],
        [gat, gh, gl, col, values] + [got[key] for key in s.sources],
        flops=10**9,
    )
    (packed,) = call(
        functools.partial(second_kernel, s),
        [((s.devices, 8, LANES), f32)],
        [loc, nh, nl, *gathered, cells, col, f, ortho, stat, message, charges],
        flops=10**9,
    )
    boxes = lax.all_to_all(packed, ("gx", "gy", "gz"), 0, 0)
    result, lsq = call(
        functools.partial(finish_kernel, s),
        [(flat, f32), ((1, 1), f32)],
        [ids, f, u, boxes, fetch(boxes, "partner", 0), col, *operators_out],
        scalars=1,
        far_outs=1,
        scratch=[pltpu.VMEM(flat, f32), pltpu.SemaphoreType.DMA],
        flops=10**7,
    )
    return result.reshape(rhs.shape), lsq.reshape(())


def solution(mesh):
    in_specs = (
        P("gx", "gy", None, None, "gz"),
        P("gx", "gy", None, "gz"),
        P(),
        P(),
        P("gx", "gy", None, "gz"),
        P("gx", "gy", None, "gz"),
        P("gx", "gy", "gz"),
        P(),
        P(),
        P(),
        P(),
        P(),
    )
    out_specs = (P("gx", "gy", None, None, "gz"), P())
    inner = functools.partial(body, dict(mesh.shape))
    return jax.shard_map(inner, mesh=mesh, in_specs=in_specs, out_specs=out_specs, check_vma=False)
```

```python
import functools

import jax
import jax.numpy as jnp
from jax import lax
from jax.experimental import pallas as pl
from jax.experimental.pallas import tpu as pltpu
from jax.sharding import PartitionSpec as P

epsilon = 1e-06
f32 = jnp.float32
bf16 = jnp.bfloat16
RIM = 64
LANES = 128


def round_up(value, unit):
    return -(-value // unit) * unit


def split(x):
    hi = x.astype(bf16)
    lo = (x - hi.astype(f32)).astype(bf16)
    return hi, lo


def mm(a, b):
    return lax.dot_general(a, b, (((1,), (0,)), ((), ())), preferred_element_type=f32)


def mt(a, b):
    return lax.dot_general(a, b, (((1,), (1,)), ((), ())), preferred_element_type=f32)


def product(dot, a, b):
    return dot(a[0], b[0]) + (dot(a[0], b[1]) + dot(a[1], b[0]))


def total(x):
    return jnp.sum(jnp.sum(x, axis=0, keepdims=True), axis=1, keepdims=True)


class Sizes:
    def __init__(self, mesh_shape, rhs, skel_perm):
        self.nx, self.ny, self.nz = (mesh_shape[a] for a in ("gx", "gy", "gz"))
        self.devices = self.nx * self.ny * self.nz
        self.blobs, self.bodies = rhs.shape[-2:]
        self.step = round_up(self.blobs, 8)
        self.rows = round_up(3 * self.step, 16)
        self.half = self.rows // 2
        self.message = self.half + 8
        self.direct = (self.nx, self.ny) == (4, 2)
        self.levels = skel_perm.shape[0]
        self.skel = skel_perm.shape[1] // 2
        shifts = sorted({(dy % self.ny) for dy in (-1, 1)} - {0})
        self.shifts = shifts
        self.sources = [("same", dy) for dy in shifts]
        for kind in ("other", "partner"):
            self.sources += [(kind, dy) for dy in [0] + shifts]
        self.ghosts = round_up(len(self.sources) * RIM, LANES)
        self.far_tiles = self.nz + -(-self.nz // 2)

    def slot_start(self, slot, parity):
        dx, dy = slot // 3 - 1, (slot % 3 - 1) % self.ny
        kind = "same" if dx == 0 else "partner" if dx == 1 - 2 * parity else "other"
        if (kind, dy) == ("same", 0):
            return 0
        return self.bodies + RIM * self.sources.index((kind, dy))

    def odd(self, device):
        return (device // (self.ny * self.nz)) % 2

    def beside(self, kind, x):
        if kind == "same":
            return x
        if kind == "partner":
            return x ^ 1
        return (x + 2 * (x % 2) - 1) % self.nx


def pieces(x, s):
    return [x[c * s.step : c * s.step + s.step] for c in range(3)]


def turn(parts, rot, inverse):
    out = []
    for target in range(3):
        acc = None
        for source in range(3):
            row = 3 * source + target if inverse else 3 * target + source
            term = rot[row : row + 1] * parts[source]
            acc = term if acc is None else acc + term
        out.append(acc)
    return out


def stacked(parts, s):
    rest = s.rows - 3 * s.step
    if rest:
        parts = list(parts) + [jnp.zeros((rest, parts[0].shape[1]), f32)]
    return jnp.concatenate(parts, axis=0)


def occupancy(cells, s):
    row = lax.broadcasted_iota(jnp.int32, (s.skel, s.bodies), 0)
    return jnp.where(cells == row, 1.0, 0.0).astype(bf16)


def pack_charges(parts, weight_col, occ, s, count=False):
    moments = [jnp.sum(part * weight_col, axis=0, keepdims=True) for part in parts]
    moments.append(jnp.full((1, s.bodies), 1.0 if count else 0.0, f32))
    moments = jnp.concatenate(moments + [jnp.zeros((4, s.bodies), f32)], axis=0)
    high, rest = split(moments)
    mid, low = split(moments - high.astype(f32))
    stack = jnp.concatenate([high.astype(f32), mid.astype(f32), low.astype(f32)], axis=0).astype(bf16)
    sums = mt(stack, occ)
    charges = sums[0:8] + (sums[8:16] + sums[16:24])
    tail = jnp.concatenate([charges[:, LANES:], jnp.zeros((8, 2 * LANES - s.skel), f32)], axis=1)
    row = lax.broadcasted_iota(jnp.int32, (8, LANES), 0)
    return jnp.where(row < 4, charges[:, :LANES], pltpu.roll(tail, 4, 0))


def pack_rim(x, s):
    lane = lax.broadcasted_iota(jnp.int32, (s.half, LANES), 1)
    top, bottom = x[: s.half, :LANES], x[s.half :, :LANES]
    return jnp.where(lane < RIM, top, pltpu.roll(bottom, RIM, 1))


def unpack_rims(rims, s):
    lane = lax.broadcasted_iota(jnp.int32, (s.half, LANES), 1)
    tops, bottoms = [], []
    for i in range(0, s.ghosts // RIM, 2):
        a = rims[i]
        b = rims[i + 1] if i + 1 < len(rims) else jnp.zeros_like(a)
        tops.append(jnp.where(lane < RIM, a, pltpu.roll(b, RIM, 1)))
        bottoms.append(jnp.where(lane < RIM, pltpu.roll(a, RIM, 1), b))
    return jnp.concatenate(
        [jnp.concatenate(tops, axis=1), jnp.concatenate(bottoms, axis=1)], axis=0
    )


def pack_message(x, weight_col, cells, s):
    charges = pack_charges(pieces(x, s), weight_col, occupancy(cells, s), s)
    row = lax.broadcasted_iota(jnp.int32, (8, LANES), 0)
    charges = jnp.where(row == 3, cells[:, :LANES].astype(f32), charges)
    return jnp.concatenate([pack_rim(x, s), charges], axis=0)


def begin(sources, targets, sems):
    moves = [pltpu.make_async_copy(a, b, sems.at[i]) for i, (a, b) in enumerate(zip(sources, targets))]
    for move in moves:
        move.start()
    return moves


def start_kernel(s, rhs, cells, weight, message_out, col_out, cells_out, f_out, raw, wide, sems):
    moves = begin((weight, cells, rhs), (wide, cells_out, raw), sems)
    f_out[...] = jnp.zeros_like(f_out)
    moves[0].wait()
    row = jnp.concatenate([wide[...], jnp.zeros((1, 2 * LANES - s.blobs), f32)], axis=1)
    col = jnp.broadcast_to(row, (LANES, 2 * LANES)).T[: s.step]
    col_out[...] = col
    for move in moves[1:]:
        move.wait()
    for c in range(3):
        f_out[c * s.step : c * s.step + s.blobs, :] = raw[c * s.blobs : (c + 1) * s.blobs, 0, :]
    message_out[...] = pack_message(f_out[...], col[:, :1], cells_out[0], s)


def frame_rows(angles):
    cos, sin = jnp.cos(angles), jnp.sin(angles)
    cy, cp, cr = cos[0:1], cos[1:2], cos[2:3]
    sy, sp, sr = sin[0:1], sin[1:2], sin[2:3]
    return [
        cy * cp,
        cy * sp * sr - sy * cr,
        cy * sp * cr + sy * sr,
        sy * cp,
        sy * sp * sr + cy * cr,
        sy * sp * cr - cy * sr,
        -sp,
        cp * sr,
        cp * cr,
    ]


def local_part(f, s, rot, mob, own):
    parts = pieces(f, s)
    turned = stacked(turn(parts, rot, False), s)
    mixed = product(mm, mob, split(turned))
    back = turn(pieces(mixed, s), rot, True)
    return f + stacked(back, s), product(mm, split(f), own)


def product_many(dot, blocks, b):
    rows = blocks[0].shape[0]
    out = product(dot, split(jnp.concatenate(blocks, axis=0)), split(b))
    return [out[i * rows : (i + 1) * rows] for i in range(len(blocks))]


def expand_once(groups, halves):
    flat = [block for group in groups for block in group]
    sides = [product_many(mt, flat, half) for half in halves]
    out, at = [], 0
    for group in groups:
        spread = []
        for i in range(at, at + len(group)):
            spread += [sides[0][i], sides[1][i]]
        at += len(group)
        out.append(spread)
    return out


def setup_kernel(
    s, ids, f_in, *refs
):
    count = 9
    sources, refs = refs[:count], refs[count:]
    copies, refs = refs[-1 - count :], refs[: -1 - count]
    copies, sems = copies[:-1], copies[-1]
    setup(s, ids, f_in, begin(sources, copies, sems), *copies, *refs)


def setup(
    s, ids, f_in, moves, angles, near_weight, neighbours, self_mob, near_mat, perm, interp, sibling, root,
    loc_out, gat_out, rot_out, sh_out, sl_out, nh_out, nl_out, oh_out, ol_out, gh_out, gl_out,
    fh_out, fl_out, uh_out, ul_out, bh_out, bl_out, rh_out, rl_out, padded, ups_ref, far_ref,
):
    f = f_in[...]
    for move in moves[:3]:
        move.wait()
    rot = jnp.concatenate(frame_rows(angles[:, 0, :]) + [jnp.zeros((7, s.bodies), f32)], axis=0)
    rot_out[...] = rot

    links = neighbours[0, 0]
    slot = links // s.bodies
    base = jnp.zeros_like(links)
    odd = (ids[0] // s.ny) % 2
    for index in range(9):
        start = jnp.where(odd == 1, s.slot_start(index, 1), s.slot_start(index, 0))
        base = jnp.where(slot == index, start, base)
    column = base + links % s.bodies
    coef = near_weight[0, 0]
    for first, count, hi_out, lo_out in (
        (0, s.bodies, oh_out, ol_out),
        (s.bodies, s.ghosts, gh_out, gl_out),
    ):
        for r in range(0, count, 64):
            row = lax.broadcasted_iota(jnp.int32, (64, s.bodies), 0) + (first + r)
            acc = jnp.zeros((64, s.bodies), f32)
            for k in range(coef.shape[0]):
                acc = acc + jnp.where(column[k : k + 1] == row, coef[k : k + 1], 0.0)
            hi, lo = split(acc)
            hi_out[r : r + 64, :] = hi
            lo_out[r : r + 64, :] = lo

    for move in moves[3:]:
        move.wait()
    padded[...] = jnp.zeros_like(padded)
    for matrix, hi_out, lo_out in ((self_mob, sh_out, sl_out), (near_mat, nh_out, nl_out)):
        for c in range(3):
            for d in range(3):
                padded[c * s.step : c * s.step + s.blobs, d * s.step : d * s.step + s.blobs] = matrix[
                    c * s.blobs : (c + 1) * s.blobs, d * s.blobs : (d + 1) * s.blobs
                ]
        hi, lo = split(padded[...])
        hi_out[...] = hi
        lo_out[...] = lo

    loc, gat = local_part(f, s, rot, (sh_out[...], sl_out[...]), (oh_out[...], ol_out[...]))
    loc_out[...] = loc
    gat_out[...] = gat

    n = s.skel
    z = ids[1]
    halves = []
    spot = lax.broadcasted_iota(jnp.int32, (2 * n, n), 0)
    for level in range(s.levels):
        kept = jnp.where(perm[level : level + 1, :n] == spot, 1.0, 0.0)
        moved = jnp.where(perm[level : level + 1, n:] == spot, 1.0, 0.0).astype(bf16)
        hi, lo = split(interp[level])
        up = kept + (mm(moved, hi) + mm(moved, lo))
        ups_ref[level] = up
        uh_out[level], ul_out[level] = split(up)
        bh_out[level], bl_out[level] = split(sibling[level])
        bit = (z >> level) & 1
        halves.append(
            [ups_ref[level, pl.ds(pl.multiple_of(side * n, 8), n), :] for side in (bit, 1 - bit)]
        )

    def down(block, level, dot):
        return product(dot, split(halves[level][0]), split(block))

    spread = root[...]
    rh_out[...], rl_out[...] = split(spread)
    beside = []
    for level in reversed(range(s.levels)):
        spread = down(spread, level, mt if level == s.levels - 1 else mm)
        beside = [(down(block, level, mt if fresh else mm), False) for block, fresh in beside]
        beside.append((sibling[level], True))
    beside = [block.T if fresh else block for block, fresh in reversed(beside)]
    leaves = [[spread]]
    for level in reversed(range(s.levels)):
        leaves = expand_once(leaves, halves[level])
        leaves.append([beside[level]])
    far_leaves, *sub = leaves
    near_leaves = [jnp.zeros((n, n), f32)]
    for blocks in reversed(sub):
        near_leaves += blocks
    tail = n - LANES
    far_ref[...] = jnp.zeros_like(far_ref)
    own = [a - b for a, b in zip(near_leaves, far_leaves)]
    for group, blocks in enumerate((own, far_leaves)):
        for leaf, block in enumerate(blocks):
            at = (group * s.far_tiles + leaf) * LANES
            far_ref[:, at : at + LANES] = block[:, :LANES]
            at = (group * s.far_tiles + s.nz + leaf // 2) * LANES + leaf % 2 * RIM
            far_ref[:, at : at + tail] = block[:, LANES:]
    fh_out[...], fl_out[...] = split(far_ref[...])


def half_kernel(s, *refs):
    *messages, _, out = refs
    acc = messages[0][s.half :, :]
    for message in messages[1:]:
        acc = acc + message[s.half :, :]
    out[...] = acc


def layer_kernel(s, count, message, *refs):
    sums, around, out = refs[:count], refs[count:-2], refs[-1]
    acc = sums[0][...]
    for part in sums[1:]:
        acc = acc + part[...]
    out[0] = message[s.half :, :]
    out[1] = acc
    for index, other in enumerate(around):
        out[2 + index] = other[s.half :, :]


def join_kernel(x, y, out):
    out[: x.shape[0]] = x[...]
    out[x.shape[0] :] = y[...]


def layer_row(s, tiles):
    row = list(tiles)
    lane = lax.broadcasted_iota(jnp.int32, (8, LANES), 1)
    for leaf in range(0, s.nz, 2):
        pair = tiles[leaf]
        if leaf + 1 < s.nz:
            pair = jnp.where(lane < RIM, pair, pltpu.roll(tiles[leaf + 1], RIM, 1))
        row.append(pltpu.roll(pair, 4, 0))
    return jnp.concatenate(row, axis=1)


def far_potentials(s, layers, far_op):
    own = [layer_row(s, [layer[k] for layer in layers]) for k in range(len(layers[0]))]
    wide = own[0].shape[1]
    hi, lo = far_op
    whole = product(mt, split(own.pop(1)), (hi[:, wide:], lo[:, wide:]))
    boxes = product(mt, split(jnp.concatenate(own, axis=0)), (hi[:, :wide], lo[:, :wide]))
    return [boxes[8 * k : 8 * k + 8] + whole for k in range(len(own))]


def pick(potential, onehot):
    high, _ = split(potential)
    mid, low = split(potential - high.astype(f32))
    parts = [x.astype(f32) for x in (high, mid, low)]
    picked = mm(jnp.concatenate(parts, axis=0).astype(bf16), onehot)
    n = potential.shape[0]
    return picked[:n] + (picked[n : 2 * n] + picked[2 * n :])


def place_kernel(s, cells, tiles, own_out, rims_out):
    own_out[...] = occupancy(cells[0], s)
    lane = lax.broadcasted_iota(jnp.int32, (8, LANES), 1)
    place = lax.broadcasted_iota(jnp.int32, (s.skel, LANES), 0).astype(f32)
    count = len(s.sources)
    for i in range(0, count, 2):
        last = min(i + 1, count - 1)
        pair = jnp.where(lane < RIM, tiles[2 + i], pltpu.roll(tiles[2 + last], RIM, 1))
        rims_out[i // 2] = jnp.where(pair[3:4] == place, 1.0, 0.0).astype(bf16)


def rim_values(s, potentials, onehots):
    lane = lax.broadcasted_iota(jnp.int32, (8, LANES), 1)
    count = len(potentials) - 1
    out = []
    for i in range(0, count, 2):
        last = min(i + 1, count - 1)
        both = pick(jnp.concatenate([potentials[1 + i], potentials[1 + last]], axis=0), onehots[i // 2])
        out.append(jnp.where(lane < RIM, both[:8], both[8:]))
    return out


def gather_kernel(s, gat, gh, gl, *refs):
    *messages, _, hi_out, lo_out = refs
    rims = unpack_rims([message[: s.half, :] for message in messages], s)
    gathered = gat[...] + product(mm, split(rims), (gh[...], gl[...]))
    hi_out[...], lo_out[...] = split(gathered)


def gather_far_kernel(s, gat, gh, gl, col, values, *refs):
    *messages, hi_out, lo_out = refs
    rims = unpack_rims([message[...] for message in messages], s)
    far = []
    for c in range(3):
        value = jnp.concatenate([values[i, c : c + 1, :] for i in range(values.shape[0])], axis=1)
        far.append(col[:, :1] * value)
    rims = rims + stacked(far, s)
    gathered = gat[...] + product(mm, split(rims), (gh[...], gl[...]))
    hi_out[...], lo_out[...] = split(gathered)


def near_kernel(s, loc, nh, nl, hi, lo, out, rim_out):
    part = loc[...] + product(mm, (nh[...], nl[...]), (hi[...], lo[...]))
    out[...] = part
    rim_out[...] = pack_rim(part, s)


def first_kernel(s, part, fh, fl, own, rims, col, *refs):
    *layers, u_out, charges_out, values_out = refs
    count = 2 + len(s.sources)
    parts = layers[: s.levels + 1]
    layers = [[part[at + k] for k in range(count)] for part in parts for at in range(0, part.shape[0], count)]
    weight_col = col[:, :1]
    occ = own[...]
    potentials = far_potentials(s, layers, (fh[...], fl[...]))
    values = pick(potentials[0], occ)
    u = part[...] + stacked([weight_col * values[c : c + 1] for c in range(3)], s)
    u_out[...] = u
    charges_out[...] = pack_charges(pieces(u, s), weight_col, occ, s)
    for index, value in enumerate(rim_values(s, potentials, rims)):
        values_out[index] = value


def order_kernel(x, _, out):
    out[...] = x[...]


def safe_inverse(x):
    return jnp.where(x > 0.0, 1.0 / jnp.where(x > 0.0, x, 1.0), 0.0)


def middle_kernel(s, u_in, f_in, rot, sh, sl, oh, ol, loc_out, gat_out, ortho_out, stat_out):
    u, f = u_in[...], f_in[...]
    loc, gat = local_part(u, s, rot[...], (sh[...], sl[...]), (oh[...], ol[...]))
    loc_out[...] = loc
    gat_out[...] = gat
    ff = total(f * f)
    fu = total(f * u) * safe_inverse(ff)
    ortho = u - fu * f
    ortho_out[...] = ortho
    oo = total(ortho * ortho)
    stat_out[...] = jnp.broadcast_to(
        jnp.concatenate([ff, fu, oo, jnp.zeros((5, 1), f32)], axis=0), (8, LANES)
    )


def second_kernel(
    s, loc, nh, nl, hi, lo, cells, col, f_in, ortho_in, stat, charges_f, charges_u, packed_out
):
    part = loc[...] + product(mm, (nh[...], nl[...]), (hi[...], lo[...]))
    f, ortho = f_in[...], ortho_in[...]
    ff, fu, oo = (stat[i : i + 1, :1] for i in range(3))
    fa = total(f * part) * safe_inverse(ff)
    oa = total(ortho * part) * safe_inverse(oo)
    rest = part - fa * f - oa * ortho
    aa = total(rest * rest)
    rf, ro = jnp.sqrt(ff), jnp.sqrt(oo)
    of_f = charges_f[-8:, :]
    of_u = charges_u[...]
    of_a = pack_charges(pieces(rest, s), col[:, :1], occupancy(cells[0], s), s, count=True)
    row = lax.broadcasted_iota(jnp.int32, (8, LANES), 0)
    lane = lax.broadcasted_iota(jnp.int32, (8, LANES), 1)
    left = lane < RIM
    first = jnp.where(left, of_u, pltpu.roll(of_a, RIM, 1))
    first = jnp.where(row < 4, of_u, first)
    first = jnp.where((row == 7) & left, pltpu.roll(of_f, 1, 0), first)
    for index, value in enumerate((rf, rf * fu, ro, rf * fa, ro * oa, aa)):
        first = jnp.where((row == 3) & (lane == index), value, first)
    tails = jnp.where(left, pltpu.roll(of_f, 3, 0), pltpu.roll(pltpu.roll(of_f, 2, 0), RIM, 1))
    second = jnp.where(row < 3, of_f, of_a)
    second = jnp.where(row < 4, second, pltpu.roll(of_a, 4, 0))
    second = jnp.where(row == 7, tails, second)
    for device in range(s.devices):
        packed_out[device] = second if s.odd(device) else first


def tree(s, leaves, ups, siblings, root):
    def apply(dot, blocks, factor):
        rows = blocks[0].shape[0]
        out = product(dot, split(jnp.concatenate(blocks, axis=0)), factor)
        return [out[i * rows : (i + 1) * rows] for i in range(len(blocks))]

    n = s.skel
    halves = [[(hi[level, j * n : (j + 1) * n, :], lo[level, j * n : (j + 1) * n, :]) for j in range(2)]
              for level, (hi, lo) in ((k, ups) for k in range(s.levels))]
    charges = [leaves]
    for level in range(s.levels):
        low, high = (apply(mm, charges[-1][j::2], halves[level][j]) for j in range(2))
        charges.append([a + b for a, b in zip(low, high)])
    own = charges[-1][0]
    whole = own[:8]
    for column in range(1, s.nx * s.ny):
        whole = whole + own[8 * column : 8 * column + 8]
    others = jnp.concatenate([whole] * (s.nx * s.ny), axis=0) - own
    potential = apply(mm, [others], root)
    for level in reversed(range(s.levels)):
        beside = apply(mm, charges[level], (siblings[0][level], siblings[1][level]))
        down = [apply(mt, potential, halves[level][j]) for j in range(2)]
        potential = [
            down[z % 2][z // 2] + beside[z ^ 1] for z in range(len(charges[level]))
        ]
    return potential


def box_numbers(s, firsts, seconds, ups, siblings, root):
    columns = s.nx * s.ny
    row = lax.broadcasted_iota(jnp.int32, (8, LANES), 0)
    lane = lax.broadcasted_iota(jnp.int32, (8, LANES), 1)
    left, valid = lane < RIM, row < 3
    leaves = []
    for z in range(s.nz):
        wide = []
        for column in range(columns):
            tile = firsts[column * s.nz + z]
            wide.append(jnp.concatenate([tile, pltpu.roll(tile, 4, 0)], axis=1)[:, : s.skel])
        leaves.append(jnp.concatenate(wide, axis=0))
    potential = tree(s, leaves, ups, siblings, root)
    out = []
    for start in range(0, s.devices, 8):
        sums = [jnp.zeros((8, LANES), f32) for _ in range(5)]
        for box in range(start, min(s.devices, start + 8)):
            column, z = box // s.nz, box % s.nz
            phi = potential[z][8 * column : 8 * column + 8]
            main, tail = phi[:, :LANES], phi[:, LANES:]
            tail = jnp.concatenate([tail, tail], axis=1)
            first, second = firsts[box], seconds[box]
            both = pltpu.roll(first, 4, 0) * tail
            of_f = jnp.where(row == 0, pltpu.roll(second, 1, 0), jnp.where(row == 1, pltpu.roll(second, 2, 0), pltpu.roll(first, 3, 0)))
            of_f = jnp.where(left == (row != 1), of_f * tail, 0.0)
            count = jnp.broadcast_to(second[3:4], (8, LANES))
            count_tail = jnp.where(left, 0.0, jnp.broadcast_to(first[7:8], (8, LANES)))
            terms = (
                second * main + of_f,
                first * main + jnp.where(left, both, 0.0),
                pltpu.roll(second, 4, 0) * main + jnp.where(left, 0.0, both),
                count * (main * main) + count_tail * (tail * tail),
            )
            here = row == box - start
            for index, term in enumerate(terms):
                value = jnp.sum(jnp.where(valid, term, 0.0), axis=0, keepdims=True)
                sums[index] = jnp.where(here, value, sums[index])
            sums[4] = jnp.where(here, first[3:4], sums[4])
        numbers = sums[4]
        for index in range(4):
            numbers = jnp.where(lane == 6 + index, jnp.sum(sums[index], axis=1, keepdims=True), numbers)
        out.append(numbers)
    rest = round_up(s.devices, LANES) - 8 * len(out)
    if rest:
        out.append(jnp.zeros((rest, LANES), f32))
    return jnp.concatenate(out, axis=0)


def finish_kernel(s, ids, f_in, u_in, mine, other, col, uh, ul, bh, bl, rh, rl, x_out, lsq_out, raw, sem):
    odd = (ids[0] // s.ny) % 2 == 1
    firsts = [jnp.where(odd, other[box], mine[box]) for box in range(s.devices)]
    seconds = [jnp.where(odd, mine[box], other[box]) for box in range(s.devices)]
    rows = box_numbers(s, firsts, seconds, (uh, ul), (bh, bl), (rh[...], rl[...])).T
    f1, u1, u2, t1, t2, aa, far_f, far_u, far_a, far_far = (rows[i : i + 1] for i in range(10))
    by_f = safe_inverse(f1)
    by_o = jnp.where(u2 * u2 > 1e-10 * (u1 * u1), safe_inverse(u2), 0.0)
    on_one = far_f * by_f
    on_two = (far_u - u1 * by_f * far_f) * by_o
    weight = jnp.sum(col[:, :1] * col[:, :1], axis=0, keepdims=True)
    t3 = aa + 2.0 * far_a + weight * far_far - on_one * on_one - on_two * on_two
    t1, t2, t3 = t1 + on_one, t2 + on_two, jnp.sqrt(jnp.maximum(t3, 0.0))

    def along(x):
        return jnp.sum(x, axis=1, keepdims=True)

    beta = jnp.sqrt(along(f1 * f1) + epsilon)
    v = f1 / beta
    w1, w2 = u1 / beta, u2 / beta
    h11 = along(w1 * v)
    r1 = w1 - h11 * v
    h21 = jnp.sqrt(along(r1 * r1 + w2 * w2) + epsilon)
    b1, b2 = r1 / h21, w2 / h21
    z1, z2, z3 = ((t1 / beta - h11 * w1) / h21, (t2 / beta - h11 * w2) / h21, t3 / beta / h21)
    h12 = along(z1 * v)
    h22 = along(z1 * b1 + z2 * b2)
    d1, d2 = z1 - h12 * v - h22 * b1, z2 - h22 * b2
    h32 = jnp.sqrt(along(d1 * d1 + d2 * d2 + z3 * z3) + epsilon)
    first_norm = jnp.sqrt(h11 * h11 + h21 * h21)
    c1, s1 = h11 / first_norm, h21 / first_norm
    t12, t22 = c1 * h12 + s1 * h22, c1 * h22 - s1 * h12
    second_norm = jnp.sqrt(t22 * t22 + h32 * h32)
    c2, s2 = t22 / second_norm, h32 / second_norm
    g2 = -s1 * beta
    y2 = c2 * g2 / second_norm
    y1 = (c1 * beta - t12 * y2) / first_norm
    lsq_out[...] = jnp.abs(s2 * g2)
    on_u = y2 / h21 / beta
    on_f = y1 / beta - on_u * h11
    for c in range(3):
        part = slice(c * s.step, c * s.step + s.blobs)
        raw[c * s.blobs : (c + 1) * s.blobs, 0, :] = on_f * f_in[part, :] + on_u * u_in[part, :]
    move = pltpu.make_async_copy(raw, x_out, sem)
    move.start()
    move.wait()


def call(kernel, outs, args, scalars=0, far_args=0, far_outs=0, scratch=(), flops=0):
    vmem = pl.BlockSpec(memory_space=pltpu.VMEM)
    smem = pl.BlockSpec(memory_space=pltpu.SMEM)
    hbm = pl.BlockSpec(memory_space=pltpu.HBM)
    near_args = len(args) - far_args
    args = args[:near_args] + [pltpu.with_memory_space_constraint(x, pltpu.HBM) for x in args[near_args:]]
    return pl.pallas_call(
        kernel,
        out_shape=[jax.ShapeDtypeStruct(shape, kind) for shape, kind in outs],
        in_specs=[smem] * scalars + [vmem] * (near_args - scalars) + [hbm] * far_args,
        out_specs=[hbm] * far_outs + [vmem] * (len(outs) - far_outs),
        scratch_shapes=list(scratch),
        compiler_params=pltpu.CompilerParams(vmem_limit_bytes=16 * 2**20),
        cost_estimate=pl.CostEstimate(flops=flops, bytes_accessed=2**20, transcendentals=0),
    )(*args)


def body(
    mesh_shape, rhs, angles, self_mob, near_mat, near_weight, neighbours, cells, blob_weight,
    skel_perm, interp, sibling_ops, root_op,
):
    s = Sizes(mesh_shape, rhs, skel_perm)
    full = (s.rows, s.bodies)
    square = (s.rows, s.rows)
    tile = (8, LANES)
    far_shape = (s.skel, 2 * s.far_tiles * LANES)
    column = lax.axis_index("gx") * s.ny + lax.axis_index("gy")
    ids = jnp.stack([column, lax.axis_index("gz")]).astype(jnp.int32)

    def fetch(x, kind, dy):
        pairs = []
        for gx in range(s.nx):
            for gy in range(s.ny):
                pairs.append((s.beside(kind, gx) * s.ny + (gy + dy) % s.ny, gx * s.ny + gy))
        return lax.ppermute(x, ("gx", "gy"), pairs)

    def fetch_layers(x):
        parts = [x]
        for level in range(s.levels):
            pairs = [(z ^ (1 << level), z) for z in range(s.nz)]
            parts.append(lax.ppermute(x, "gz", pairs))
            if level + 1 < s.levels:
                (x,) = call(join_kernel, [((2 * x.shape[0],) + tile, f32)], [x, parts[-1]])
        return parts

    def fetch_rims(rim):
        got = {}
        for dy in s.shifts:
            got["other", dy] = fetch(rim, "other", dy)
        for dy in s.shifts:
            got["same", dy] = fetch(rim, "same", dy)
        got["other", 0] = fetch(rim, "other", 0)
        got["partner", 0] = fetch(rim, "partner", 0)
        return got

    def forward_rims(got, after):
        for dy in s.shifts:
            held = got["same", dy]
            (held,) = call(order_kernel, [(held.shape, f32)], [held, after])
            got["partner", dy] = fetch(held, "partner", 0)

    def plane_sum(message, got, after):
        if not s.direct:
            return [lax.psum(message[s.half :], ("gx", "gy"))]
        quarter = [message] + [got[key] for key in s.sources if key[0] != "partner"]
        (half,) = call(functools.partial(half_kernel, s), [(tile, f32)], quarter + [after])
        return [half, fetch(half, "partner", 0)]

    flat = (3 * s.blobs, 1, s.bodies)
    small = (1, s.blobs)
    message, col, cells, f = call(
        functools.partial(start_kernel, s),
        [((s.message, LANES), f32), ((s.step, LANES), f32), (cells.shape, jnp.int32), (full, f32)],
        [rhs.reshape(flat), cells, blob_weight.reshape(small)],
        far_args=3,
        scratch=[pltpu.VMEM(flat, f32), pltpu.VMEM(small, f32), pltpu.SemaphoreType.DMA((3,))],
        flops=10**7,
    )
    got = fetch_rims(message)
    operators = [
        angles.reshape(3, 1, s.bodies), near_weight, neighbours, self_mob, near_mat, skel_perm, interp,
        sibling_ops, root_op,
    ]
    loc, gat, rot, sh, sl, nh, nl, oh, ol, gh, gl, fh, fl, *operators_out = call(
        functools.partial(setup_kernel, s),
        [(full, f32), (full, f32), ((16, s.bodies), f32)]
        + [(square, bf16)] * 4
        + [((s.bodies, s.bodies), bf16)] * 2
        + [((s.ghosts, s.bodies), bf16)] * 2
        + [(far_shape, bf16)] * 2
        + [((s.levels, 2 * s.skel, s.skel), bf16)] * 2
        + [((s.levels, s.skel, s.skel), bf16)] * 2
        + [((s.skel, s.skel), bf16)] * 2,
        [ids, f] + operators,
        scalars=1,
        far_args=len(operators),
        scratch=[
            pltpu.VMEM(square, f32), pltpu.VMEM((s.levels, 2 * s.skel, s.skel), f32), pltpu.VMEM(far_shape, f32)
        ]
        + [pltpu.VMEM(x.shape, x.dtype) for x in operators]
        + [pltpu.SemaphoreType.DMA((len(operators),))],
        flops=5 * 10**9,
    )
    forward_rims(got, rot)
    sums = plane_sum(message, got, rot)
    around = [got[key] for key in s.sources]
    gathered = call(
        functools.partial(gather_kernel, s),
        [(full, bf16), (full, bf16)],
        [gat, gh, gl] + around + [sums[0]],
        flops=10**9,
    )
    part, rim = call(
        functools.partial(near_kernel, s),
        [(full, f32), ((s.half, LANES), f32)],
        [loc, nh, nl, *gathered],
        flops=10**9,
    )
    (tiles,) = call(
        functools.partial(layer_kernel, s, len(sums)),
        [((2 + len(around),) + tile, f32)],
        [message] + sums + around + [gathered[1]],
    )
    layers = fetch_layers(tiles)
    got = fetch_rims(rim)
    places = call(
        functools.partial(place_kernel, s),
        [((s.skel, s.bodies), bf16), ((s.ghosts // LANES, s.skel, LANES), bf16)],
        [cells, tiles],
        flops=2 * 10**10,
    )
    ahead = [got["other", 0]] + [got[kind, dy] for kind in ("other", "same") for dy in s.shifts]
    u, charges, values = call(
        functools.partial(first_kernel, s),
        [(full, f32), (tile, f32), ((s.ghosts // LANES,) + tile, f32)],
        [part, fh, fl, *places, col, *layers] + ahead,
        flops=10**8,
    )
    loc, gat, ortho, stat = call(
        functools.partial(middle_kernel, s),
        [(full, f32), (full, f32), (full, f32), (tile, f32)],
        [u, f, rot, sh, sl, oh, ol],
        flops=10**9,
    )
    forward_rims(got, charges)
    gathered = call(
        functools.partial(gather_far_kernel, s),
        [(full, bf16), (full, bf16)],
        [gat, gh, gl, col, values] + [got[key] for key in s.sources],
        flops=10**9,
    )
    (packed,) = call(
        functools.partial(second_kernel, s),
        [((s.devices, 8, LANES), f32)],
        [loc, nh, nl, *gathered, cells, col, f, ortho, stat, message, charges],
        flops=10**9,
    )
    boxes = lax.all_to_all(packed, ("gx", "gy", "gz"), 0, 0)
    result, lsq = call(
        functools.partial(finish_kernel, s),
        [(flat, f32), ((1, 1), f32)],
        [ids, f, u, boxes, fetch(boxes, "partner", 0), col, *operators_out],
        scalars=1,
        far_outs=1,
        scratch=[pltpu.VMEM(flat, f32), pltpu.SemaphoreType.DMA],
        flops=10**7,
    )
    return result.reshape(rhs.shape), lsq.reshape(())


def solution(mesh):
    in_specs = (
        P("gx", "gy", None, None, "gz"),
        P("gx", "gy", None, "gz"),
        P(),
        P(),
        P("gx", "gy", None, "gz"),
        P("gx", "gy", None, "gz"),
        P("gx", "gy", "gz"),
        P(),
        P(),
        P(),
        P(),
        P(),
    )
    out_specs = (P("gx", "gy", None, None, "gz"), P())
    inner = functools.partial(body, dict(mesh.shape))
    return jax.shard_map(inner, mesh=mesh, in_specs=in_specs, out_specs=out_specs, check_vma=False)
```

```python
import functools

import jax
import jax.numpy as jnp
from jax import lax
from jax.experimental import pallas as pl
from jax.experimental.pallas import tpu as pltpu
from jax.sharding import PartitionSpec as P

epsilon = 1e-06
f32 = jnp.float32
bf16 = jnp.bfloat16
RIM = 64
LANES = 128


def round_up(value, unit):
    return -(-value // unit) * unit


def split(x):
    hi = x.astype(bf16)
    lo = (x - hi.astype(f32)).astype(bf16)
    return hi, lo


def mm(a, b):
    return lax.dot_general(a, b, (((1,), (0,)), ((), ())), preferred_element_type=f32)


def mt(a, b):
    return lax.dot_general(a, b, (((1,), (1,)), ((), ())), preferred_element_type=f32)


def product(dot, a, b):
    return dot(a[0], b[0]) + (dot(a[0], b[1]) + dot(a[1], b[0]))


def total(x):
    return jnp.sum(jnp.sum(x, axis=0, keepdims=True), axis=1, keepdims=True)


class Sizes:
    def __init__(self, mesh_shape, rhs, skel_perm):
        self.nx, self.ny, self.nz = (mesh_shape[a] for a in ("gx", "gy", "gz"))
        self.devices = self.nx * self.ny * self.nz
        self.blobs, self.bodies = rhs.shape[-2:]
        self.step = round_up(self.blobs, 8)
        self.rows = round_up(3 * self.step, 16)
        self.half = self.rows // 2
        self.message = self.half + 8
        self.direct = (self.nx, self.ny) == (4, 2)
        self.levels = skel_perm.shape[0]
        self.skel = skel_perm.shape[1] // 2
        shifts = sorted({(dy % self.ny) for dy in (-1, 1)} - {0})
        self.shifts = shifts
        self.sources = [("same", dy) for dy in shifts]
        for kind in ("other", "partner"):
            self.sources += [(kind, dy) for dy in [0] + shifts]
        self.ghosts = round_up(len(self.sources) * RIM, LANES)
        self.far_tiles = self.nz + -(-self.nz // 2)

    def slot_start(self, slot, parity):
        dx, dy = slot // 3 - 1, (slot % 3 - 1) % self.ny
        kind = "same" if dx == 0 else "partner" if dx == 1 - 2 * parity else "other"
        if (kind, dy) == ("same", 0):
            return 0
        return self.bodies + RIM * self.sources.index((kind, dy))

    def odd(self, device):
        return (device // (self.ny * self.nz)) % 2

    def beside(self, kind, x):
        if kind == "same":
            return x
        if kind == "partner":
            return x ^ 1
        return (x + 2 * (x % 2) - 1) % self.nx


def pieces(x, s):
    return [x[c * s.step : c * s.step + s.step] for c in range(3)]


def turn(parts, rot, inverse):
    out = []
    for target in range(3):
        acc = None
        for source in range(3):
            row = 3 * source + target if inverse else 3 * target + source
            term = rot[row : row + 1] * parts[source]
            acc = term if acc is None else acc + term
        out.append(acc)
    return out


def stacked(parts, s):
    rest = s.rows - 3 * s.step
    if rest:
        parts = list(parts) + [jnp.zeros((rest, parts[0].shape[1]), f32)]
    return jnp.concatenate(parts, axis=0)


def occupancy(cells, s):
    row = lax.broadcasted_iota(jnp.int32, (s.skel, s.bodies), 0)
    return jnp.where(cells == row, 1.0, 0.0).astype(bf16)


def pack_charges(parts, weight_col, occ, s, count=False):
    moments = [jnp.sum(part * weight_col, axis=0, keepdims=True) for part in parts]
    moments.append(jnp.full((1, s.bodies), 1.0 if count else 0.0, f32))
    moments = jnp.concatenate(moments + [jnp.zeros((4, s.bodies), f32)], axis=0)
    high, rest = split(moments)
    mid, low = split(moments - high.astype(f32))
    stack = jnp.concatenate([high.astype(f32), mid.astype(f32), low.astype(f32)], axis=0).astype(bf16)
    sums = mt(stack, occ)
    charges = sums[0:8] + (sums[8:16] + sums[16:24])
    tail = jnp.concatenate([charges[:, LANES:], jnp.zeros((8, 2 * LANES - s.skel), f32)], axis=1)
    row = lax.broadcasted_iota(jnp.int32, (8, LANES), 0)
    return jnp.where(row < 4, charges[:, :LANES], pltpu.roll(tail, 4, 0))


def pack_rim(x, s):
    lane = lax.broadcasted_iota(jnp.int32, (s.half, LANES), 1)
    top, bottom = x[: s.half, :LANES], x[s.half :, :LANES]
    return jnp.where(lane < RIM, top, pltpu.roll(bottom, RIM, 1))


def unpack_rims(rims, s):
    lane = lax.broadcasted_iota(jnp.int32, (s.half, LANES), 1)
    tops, bottoms = [], []
    for i in range(0, s.ghosts // RIM, 2):
        a = rims[i]
        b = rims[i + 1] if i + 1 < len(rims) else jnp.zeros_like(a)
        tops.append(jnp.where(lane < RIM, a, pltpu.roll(b, RIM, 1)))
        bottoms.append(jnp.where(lane < RIM, pltpu.roll(a, RIM, 1), b))
    return jnp.concatenate(
        [jnp.concatenate(tops, axis=1), jnp.concatenate(bottoms, axis=1)], axis=0
    )


def pack_message(x, weight_col, cells, s):
    charges = pack_charges(pieces(x, s), weight_col, occupancy(cells, s), s)
    row = lax.broadcasted_iota(jnp.int32, (8, LANES), 0)
    charges = jnp.where(row == 3, cells[:, :LANES].astype(f32), charges)
    return jnp.concatenate([pack_rim(x, s), charges], axis=0)


def begin(sources, targets, sems):
    moves = [pltpu.make_async_copy(a, b, sems.at[i]) for i, (a, b) in enumerate(zip(sources, targets))]
    for move in moves:
        move.start()
    return moves


def start_kernel(s, rhs, cells, weight, message_out, col_out, cells_out, f_out, raw, wide, sems):
    moves = begin((weight, cells, rhs), (wide, cells_out, raw), sems)
    f_out[...] = jnp.zeros_like(f_out)
    moves[0].wait()
    row = jnp.concatenate([wide[...], jnp.zeros((1, 2 * LANES - s.blobs), f32)], axis=1)
    col = jnp.broadcast_to(row, (LANES, 2 * LANES)).T[: s.step]
    col_out[...] = col
    for move in moves[1:]:
        move.wait()
    for c in range(3):
        f_out[c * s.step : c * s.step + s.blobs, :] = raw[c * s.blobs : (c + 1) * s.blobs, 0, :]
    message_out[...] = pack_message(f_out[...], col[:, :1], cells_out[0], s)


def frame_rows(angles):
    cos, sin = jnp.cos(angles), jnp.sin(angles)
    cy, cp, cr = cos[0:1], cos[1:2], cos[2:3]
    sy, sp, sr = sin[0:1], sin[1:2], sin[2:3]
    return [
        cy * cp,
        cy * sp * sr - sy * cr,
        cy * sp * cr + sy * sr,
        sy * cp,
        sy * sp * sr + cy * cr,
        sy * sp * cr - cy * sr,
        -sp,
        cp * sr,
        cp * cr,
    ]


def local_part(f, s, rot, mob, own):
    parts = pieces(f, s)
    turned = stacked(turn(parts, rot, False), s)
    mixed = product(mm, mob, split(turned))
    back = turn(pieces(mixed, s), rot, True)
    return f + stacked(back, s), product(mm, split(f), own)


def product_many(dot, blocks, b):
    rows = blocks[0].shape[0]
    out = product(dot, split(jnp.concatenate(blocks, axis=0)), split(b))
    return [out[i * rows : (i + 1) * rows] for i in range(len(blocks))]


def expand_once(groups, halves):
    flat = [block for group in groups for block in group]
    sides = [product_many(mt, flat, half) for half in halves]
    out, at = [], 0
    for group in groups:
        spread = []
        for i in range(at, at + len(group)):
            spread += [sides[0][i], sides[1][i]]
        at += len(group)
        out.append(spread)
    return out


def setup_kernel(
    s, ids, f_in, *refs
):
    count = 9
    sources, refs = refs[:count], refs[count:]
    copies, refs = refs[-1 - count :], refs[: -1 - count]
    copies, sems = copies[:-1], copies[-1]
    setup(s, ids, f_in, begin(sources, copies, sems), *copies, *refs)


def setup(
    s, ids, f_in, moves, angles, near_weight, neighbours, self_mob, near_mat, perm, interp, sibling, root,
    loc_out, gat_out, rot_out, sh_out, sl_out, nh_out, nl_out, oh_out, ol_out, gh_out, gl_out,
    fh_out, fl_out, uh_out, ul_out, bh_out, bl_out, rh_out, rl_out, padded, ups_ref, far_ref,
):
    f = f_in[...]
    for move in moves[:3]:
        move.wait()
    rot = jnp.concatenate(frame_rows(angles[:, 0, :]) + [jnp.zeros((7, s.bodies), f32)], axis=0)
    rot_out[...] = rot

    links = neighbours[0, 0]
    slot = links // s.bodies
    base = jnp.zeros_like(links)
    odd = (ids[0] // s.ny) % 2
    for index in range(9):
        start = jnp.where(odd == 1, s.slot_start(index, 1), s.slot_start(index, 0))
        base = jnp.where(slot == index, start, base)
    column = base + links % s.bodies
    coef = near_weight[0, 0]
    for first, count, hi_out, lo_out in (
        (0, s.bodies, oh_out, ol_out),
        (s.bodies, s.ghosts, gh_out, gl_out),
    ):
        for r in range(0, count, 64):
            row = lax.broadcasted_iota(jnp.int32, (64, s.bodies), 0) + (first + r)
            acc = jnp.zeros((64, s.bodies), f32)
            for k in range(coef.shape[0]):
                acc = acc + jnp.where(column[k : k + 1] == row, coef[k : k + 1], 0.0)
            hi, lo = split(acc)
            hi_out[r : r + 64, :] = hi
            lo_out[r : r + 64, :] = lo

    for move in moves[3:]:
        move.wait()
    padded[...] = jnp.zeros_like(padded)
    for matrix, hi_out, lo_out in ((self_mob, sh_out, sl_out), (near_mat, nh_out, nl_out)):
        for c in range(3):
            for d in range(3):
                padded[c * s.step : c * s.step + s.blobs, d * s.step : d * s.step + s.blobs] = matrix[
                    c * s.blobs : (c + 1) * s.blobs, d * s.blobs : (d + 1) * s.blobs
                ]
        hi, lo = split(padded[...])
        hi_out[...] = hi
        lo_out[...] = lo

    loc, gat = local_part(f, s, rot, (sh_out[...], sl_out[...]), (oh_out[...], ol_out[...]))
    loc_out[...] = loc
    gat_out[...] = gat

    n = s.skel
    z = ids[1]
    halves = []
    spot = lax.broadcasted_iota(jnp.int32, (2 * n, n), 0)
    for level in range(s.levels):
        kept = jnp.where(perm[level : level + 1, :n] == spot, 1.0, 0.0)
        moved = jnp.where(perm[level : level + 1, n:] == spot, 1.0, 0.0).astype(bf16)
        hi, lo = split(interp[level])
        up = kept + (mm(moved, hi) + mm(moved, lo))
        ups_ref[level] = up
        uh_out[level], ul_out[level] = split(up)
        bh_out[level], bl_out[level] = split(sibling[level])
        bit = (z >> level) & 1
        halves.append(
            [ups_ref[level, pl.ds(pl.multiple_of(side * n, 8), n), :] for side in (bit, 1 - bit)]
        )

    def down(block, level, dot):
        return product(dot, split(halves[level][0]), split(block))

    spread = root[...]
    rh_out[...], rl_out[...] = split(spread)
    beside = []
    for level in reversed(range(s.levels)):
        spread = down(spread, level, mt if level == s.levels - 1 else mm)
        beside = [(down(block, level, mt if fresh else mm), False) for block, fresh in beside]
        beside.append((sibling[level], True))
    beside = [block.T if fresh else block for block, fresh in reversed(beside)]
    leaves = [[spread]]
    for level in reversed(range(s.levels)):
        leaves = expand_once(leaves, halves[level])
        leaves.append([beside[level]])
    far_leaves, *sub = leaves
    near_leaves = [jnp.zeros((n, n), f32)]
    for blocks in reversed(sub):
        near_leaves += blocks
    tail = n - LANES
    far_ref[...] = jnp.zeros_like(far_ref)
    own = [a - b for a, b in zip(near_leaves, far_leaves)]
    for group, blocks in enumerate((own, far_leaves)):
        for leaf, block in enumerate(blocks):
            at = (group * s.far_tiles + leaf) * LANES
            far_ref[:, at : at + LANES] = block[:, :LANES]
            at = (group * s.far_tiles + s.nz + leaf // 2) * LANES + leaf % 2 * RIM
            far_ref[:, at : at + tail] = block[:, LANES:]
    fh_out[...], fl_out[...] = split(far_ref[...])


def half_kernel(s, *refs):
    *messages, _, out = refs
    acc = messages[0][s.half :, :]
    for message in messages[1:]:
        acc = acc + message[s.half :, :]
    out[...] = acc


def layer_kernel(s, count, message, *refs):
    sums, around, out = refs[:count], refs[count:-2], refs[-1]
    acc = sums[0][...]
    for part in sums[1:]:
        acc = acc + part[...]
    out[0] = message[s.half :, :]
    out[1] = acc
    for index, other in enumerate(around):
        out[2 + index] = other[s.half :, :]


def join_kernel(x, y, out):
    out[: x.shape[0]] = x[...]
    out[x.shape[0] :] = y[...]


def layer_row(s, tiles):
    row = list(tiles)
    lane = lax.broadcasted_iota(jnp.int32, (8, LANES), 1)
    for leaf in range(0, s.nz, 2):
        pair = tiles[leaf]
        if leaf + 1 < s.nz:
            pair = jnp.where(lane < RIM, pair, pltpu.roll(tiles[leaf + 1], RIM, 1))
        row.append(pltpu.roll(pair, 4, 0))
    return jnp.concatenate(row, axis=1)


def far_potentials(s, layers, far_op):
    own = [layer_row(s, [layer[k] for layer in layers]) for k in range(len(layers[0]))]
    wide = own[0].shape[1]
    hi, lo = far_op
    whole = product(mt, split(own.pop(1)), (hi[:, wide:], lo[:, wide:]))
    boxes = product(mt, split(jnp.concatenate(own, axis=0)), (hi[:, :wide], lo[:, :wide]))
    return [boxes[8 * k : 8 * k + 8] + whole for k in range(len(own))]


def pick(potential, onehot):
    high, _ = split(potential)
    mid, low = split(potential - high.astype(f32))
    parts = [x.astype(f32) for x in (high, mid, low)]
    picked = mm(jnp.concatenate(parts, axis=0).astype(bf16), onehot)
    n = potential.shape[0]
    return picked[:n] + (picked[n : 2 * n] + picked[2 * n :])


def place_kernel(s, cells, tiles, own_out, rims_out):
    own_out[...] = occupancy(cells[0], s)
    lane = lax.broadcasted_iota(jnp.int32, (8, LANES), 1)
    place = lax.broadcasted_iota(jnp.int32, (s.skel, LANES), 0).astype(f32)
    count = len(s.sources)
    for i in range(0, count, 2):
        last = min(i + 1, count - 1)
        pair = jnp.where(lane < RIM, tiles[2 + i], pltpu.roll(tiles[2 + last], RIM, 1))
        rims_out[i // 2] = jnp.where(pair[3:4] == place, 1.0, 0.0).astype(bf16)


def rim_values(s, potentials, onehots):
    lane = lax.broadcasted_iota(jnp.int32, (8, LANES), 1)
    count = len(potentials) - 1
    out = []
    for i in range(0, count, 2):
        last = min(i + 1, count - 1)
        both = pick(jnp.concatenate([potentials[1 + i], potentials[1 + last]], axis=0), onehots[i // 2])
        out.append(jnp.where(lane < RIM, both[:8], both[8:]))
    return out


def gather_kernel(s, gat, gh, gl, *refs):
    *messages, _, hi_out, lo_out = refs
    rims = unpack_rims([message[: s.half, :] for message in messages], s)
    gathered = gat[...] + product(mm, split(rims), (gh[...], gl[...]))
    hi_out[...], lo_out[...] = split(gathered)


def gather_far_kernel(s, gat, gh, gl, col, values, *refs):
    *messages, hi_out, lo_out = refs
    rims = unpack_rims([message[...] for message in messages], s)
    far = []
    for c in range(3):
        value = jnp.concatenate([values[i, c : c + 1, :] for i in range(values.shape[0])], axis=1)
        far.append(col[:, :1] * value)
    rims = rims + stacked(far, s)
    gathered = gat[...] + product(mm, split(rims), (gh[...], gl[...]))
    hi_out[...], lo_out[...] = split(gathered)


def near_kernel(s, loc, nh, nl, hi, lo, out, rim_out):
    part = loc[...] + product(mm, (nh[...], nl[...]), (hi[...], lo[...]))
    out[...] = part
    rim_out[...] = pack_rim(part, s)


def first_kernel(s, part, fh, fl, own, rims, col, *refs):
    *layers, u_out, charges_out, values_out = refs
    count = 2 + len(s.sources)
    layers = [[part[at + k] for k in range(count)] for part in layers for at in range(0, part.shape[0], count)]
    weight_col = col[:, :1]
    occ = own[...]
    potentials = far_potentials(s, layers, (fh[...], fl[...]))
    values = pick(potentials[0], occ)
    u = part[...] + stacked([weight_col * values[c : c + 1] for c in range(3)], s)
    u_out[...] = u
    charges_out[...] = pack_charges(pieces(u, s), weight_col, occ, s)
    for index, value in enumerate(rim_values(s, potentials, rims)):
        values_out[index] = value


def order_kernel(x, _, out):
    out[...] = x[...]


def safe_inverse(x):
    return jnp.where(x > 0.0, 1.0 / jnp.where(x > 0.0, x, 1.0), 0.0)


def middle_kernel(s, u_in, f_in, rot, sh, sl, oh, ol, loc_out, gat_out, ortho_out, stat_out):
    u, f = u_in[...], f_in[...]
    loc, gat = local_part(u, s, rot[...], (sh[...], sl[...]), (oh[...], ol[...]))
    loc_out[...] = loc
    gat_out[...] = gat
    ff = total(f * f)
    fu = total(f * u) * safe_inverse(ff)
    ortho = u - fu * f
    ortho_out[...] = ortho
    oo = total(ortho * ortho)
    stat_out[...] = jnp.broadcast_to(
        jnp.concatenate([ff, fu, oo, jnp.zeros((5, 1), f32)], axis=0), (8, LANES)
    )


def second_kernel(
    s, loc, nh, nl, hi, lo, cells, col, f_in, ortho_in, stat, charges_f, charges_u, packed_out
):
    part = loc[...] + product(mm, (nh[...], nl[...]), (hi[...], lo[...]))
    f, ortho = f_in[...], ortho_in[...]
    ff, fu, oo = (stat[i : i + 1, :1] for i in range(3))
    fa = total(f * part) * safe_inverse(ff)
    oa = total(ortho * part) * safe_inverse(oo)
    rest = part - fa * f - oa * ortho
    aa = total(rest * rest)
    rf, ro = jnp.sqrt(ff), jnp.sqrt(oo)
    of_f = charges_f[-8:, :]
    of_u = charges_u[...]
    of_a = pack_charges(pieces(rest, s), col[:, :1], occupancy(cells[0], s), s, count=True)
    row = lax.broadcasted_iota(jnp.int32, (8, LANES), 0)
    lane = lax.broadcasted_iota(jnp.int32, (8, LANES), 1)
    left = lane < RIM
    first = jnp.where(left, of_u, pltpu.roll(of_a, RIM, 1))
    first = jnp.where(row < 4, of_u, first)
    first = jnp.where((row == 7) & left, pltpu.roll(of_f, 1, 0), first)
    for index, value in enumerate((rf, rf * fu, ro, rf * fa, ro * oa, aa)):
        first = jnp.where((row == 3) & (lane == index), value, first)
    tails = jnp.where(left, pltpu.roll(of_f, 3, 0), pltpu.roll(pltpu.roll(of_f, 2, 0), RIM, 1))
    second = jnp.where(row < 3, of_f, of_a)
    second = jnp.where(row < 4, second, pltpu.roll(of_a, 4, 0))
    second = jnp.where(row == 7, tails, second)
    for device in range(s.devices):
        packed_out[device] = second if s.odd(device) else first


def tree(s, leaves, ups, siblings, root):
    def apply(dot, blocks, factor):
        rows = blocks[0].shape[0]
        out = product(dot, split(jnp.concatenate(blocks, axis=0)), factor)
        return [out[i * rows : (i + 1) * rows] for i in range(len(blocks))]

    n = s.skel
    halves = [[(hi[level, j * n : (j + 1) * n, :], lo[level, j * n : (j + 1) * n, :]) for j in range(2)]
              for level, (hi, lo) in ((k, ups) for k in range(s.levels))]
    charges = [leaves]
    for level in range(s.levels):
        low, high = (apply(mm, charges[-1][j::2], halves[level][j]) for j in range(2))
        charges.append([a + b for a, b in zip(low, high)])
    own = charges[-1][0]
    whole = own[:8]
    for column in range(1, s.nx * s.ny):
        whole = whole + own[8 * column : 8 * column + 8]
    others = jnp.concatenate([whole] * (s.nx * s.ny), axis=0) - own
    potential = apply(mm, [others], root)
    for level in reversed(range(s.levels)):
        beside = apply(mm, charges[level], (siblings[0][level], siblings[1][level]))
        down = [apply(mt, potential, halves[level][j]) for j in range(2)]
        potential = [
            down[z % 2][z // 2] + beside[z ^ 1] for z in range(len(charges[level]))
        ]
    return potential


def box_numbers(s, firsts, seconds, ups, siblings, root):
    columns = s.nx * s.ny
    row = lax.broadcasted_iota(jnp.int32, (8, LANES), 0)
    lane = lax.broadcasted_iota(jnp.int32, (8, LANES), 1)
    left, valid = lane < RIM, row < 3
    leaves = []
    for z in range(s.nz):
        wide = []
        for column in range(columns):
            tile = firsts[column * s.nz + z]
            wide.append(jnp.concatenate([tile, pltpu.roll(tile, 4, 0)], axis=1)[:, : s.skel])
        leaves.append(jnp.concatenate(wide, axis=0))
    potential = tree(s, leaves, ups, siblings, root)
    out = []
    for start in range(0, s.devices, 8):
        sums = [jnp.zeros((8, LANES), f32) for _ in range(5)]
        for box in range(start, min(s.devices, start + 8)):
            column, z = box // s.nz, box % s.nz
            phi = potential[z][8 * column : 8 * column + 8]
            main, tail = phi[:, :LANES], phi[:, LANES:]
            tail = jnp.concatenate([tail, tail], axis=1)
            first, second = firsts[box], seconds[box]
            both = pltpu.roll(first, 4, 0) * tail
            of_f = jnp.where(row == 0, pltpu.roll(second, 1, 0), jnp.where(row == 1, pltpu.roll(second, 2, 0), pltpu.roll(first, 3, 0)))
            of_f = jnp.where(left == (row != 1), of_f * tail, 0.0)
            count = jnp.broadcast_to(second[3:4], (8, LANES))
            count_tail = jnp.where(left, 0.0, jnp.broadcast_to(first[7:8], (8, LANES)))
            terms = (
                second * main + of_f,
                first * main + jnp.where(left, both, 0.0),
                pltpu.roll(second, 4, 0) * main + jnp.where(left, 0.0, both),
                count * (main * main) + count_tail * (tail * tail),
            )
            here = row == box - start
            for index, term in enumerate(terms):
                value = jnp.sum(jnp.where(valid, term, 0.0), axis=0, keepdims=True)
                sums[index] = jnp.where(here, value, sums[index])
            sums[4] = jnp.where(here, first[3:4], sums[4])
        numbers = sums[4]
        for index in range(4):
            numbers = jnp.where(lane == 6 + index, jnp.sum(sums[index], axis=1, keepdims=True), numbers)
        out.append(numbers)
    rest = round_up(s.devices, LANES) - 8 * len(out)
    if rest:
        out.append(jnp.zeros((rest, LANES), f32))
    return jnp.concatenate(out, axis=0)


def finish_kernel(s, ids, f_in, u_in, mine, other, col, uh, ul, bh, bl, rh, rl, x_out, lsq_out, raw, sem):
    odd = (ids[0] // s.ny) % 2 == 1
    firsts = [jnp.where(odd, other[box], mine[box]) for box in range(s.devices)]
    seconds = [jnp.where(odd, mine[box], other[box]) for box in range(s.devices)]
    rows = box_numbers(s, firsts, seconds, (uh, ul), (bh, bl), (rh[...], rl[...])).T
    f1, u1, u2, t1, t2, aa, far_f, far_u, far_a, far_far = (rows[i : i + 1] for i in range(10))
    by_f = safe_inverse(f1)
    by_o = jnp.where(u2 * u2 > 1e-10 * (u1 * u1), safe_inverse(u2), 0.0)
    on_one = far_f * by_f
    on_two = (far_u - u1 * by_f * far_f) * by_o
    weight = jnp.sum(col[:, :1] * col[:, :1], axis=0, keepdims=True)
    t3 = aa + 2.0 * far_a + weight * far_far - on_one * on_one - on_two * on_two
    t1, t2, t3 = t1 + on_one, t2 + on_two, jnp.sqrt(jnp.maximum(t3, 0.0))

    def along(x):
        return jnp.sum(x, axis=1, keepdims=True)

    beta = jnp.sqrt(along(f1 * f1) + epsilon)
    v = f1 / beta
    w1, w2 = u1 / beta, u2 / beta
    h11 = along(w1 * v)
    r1 = w1 - h11 * v
    h21 = jnp.sqrt(along(r1 * r1 + w2 * w2) + epsilon)
    b1, b2 = r1 / h21, w2 / h21
    z1, z2, z3 = ((t1 / beta - h11 * w1) / h21, (t2 / beta - h11 * w2) / h21, t3 / beta / h21)
    h12 = along(z1 * v)
    h22 = along(z1 * b1 + z2 * b2)
    d1, d2 = z1 - h12 * v - h22 * b1, z2 - h22 * b2
    h32 = jnp.sqrt(along(d1 * d1 + d2 * d2 + z3 * z3) + epsilon)
    first_norm = jnp.sqrt(h11 * h11 + h21 * h21)
    c1, s1 = h11 / first_norm, h21 / first_norm
    t12, t22 = c1 * h12 + s1 * h22, c1 * h22 - s1 * h12
    second_norm = jnp.sqrt(t22 * t22 + h32 * h32)
    c2, s2 = t22 / second_norm, h32 / second_norm
    g2 = -s1 * beta
    y2 = c2 * g2 / second_norm
    y1 = (c1 * beta - t12 * y2) / first_norm
    lsq_out[...] = jnp.abs(s2 * g2)
    on_u = y2 / h21 / beta
    on_f = y1 / beta - on_u * h11
    for c in range(3):
        part = slice(c * s.step, c * s.step + s.blobs)
        raw[c * s.blobs : (c + 1) * s.blobs, 0, :] = on_f * f_in[part, :] + on_u * u_in[part, :]
    move = pltpu.make_async_copy(raw, x_out, sem)
    move.start()
    move.wait()


def call(kernel, outs, args, scalars=0, far_args=0, far_outs=0, scratch=(), flops=0):
    vmem = pl.BlockSpec(memory_space=pltpu.VMEM)
    smem = pl.BlockSpec(memory_space=pltpu.SMEM)
    hbm = pl.BlockSpec(memory_space=pltpu.HBM)
    near_args = len(args) - far_args
    args = args[:near_args] + [pltpu.with_memory_space_constraint(x, pltpu.HBM) for x in args[near_args:]]
    return pl.pallas_call(
        kernel,
        out_shape=[jax.ShapeDtypeStruct(shape, kind) for shape, kind in outs],
        in_specs=[smem] * scalars + [vmem] * (near_args - scalars) + [hbm] * far_args,
        out_specs=[hbm] * far_outs + [vmem] * (len(outs) - far_outs),
        scratch_shapes=list(scratch),
        compiler_params=pltpu.CompilerParams(vmem_limit_bytes=16 * 2**20),
        cost_estimate=pl.CostEstimate(flops=flops, bytes_accessed=2**20, transcendentals=0),
    )(*args)


def body(
    mesh_shape, rhs, angles, self_mob, near_mat, near_weight, neighbours, cells, blob_weight,
    skel_perm, interp, sibling_ops, root_op,
):
    s = Sizes(mesh_shape, rhs, skel_perm)
    full = (s.rows, s.bodies)
    square = (s.rows, s.rows)
    tile = (8, LANES)
    far_shape = (s.skel, 2 * s.far_tiles * LANES)
    column = lax.axis_index("gx") * s.ny + lax.axis_index("gy")
    ids = jnp.stack([column, lax.axis_index("gz")]).astype(jnp.int32)

    def fetch(x, kind, dy):
        pairs = []
        for gx in range(s.nx):
            for gy in range(s.ny):
                pairs.append((s.beside(kind, gx) * s.ny + (gy + dy) % s.ny, gx * s.ny + gy))
        return lax.ppermute(x, ("gx", "gy"), pairs)

    def fetch_layers(x):
        parts, sent = [x], [x]
        for level in range(s.levels):
            pairs = [(z ^ (1 << level), z) for z in range(s.nz)]
            parts.append(lax.ppermute(sent[-1], "gz", pairs))
            if level + 1 < s.levels:
                shape = (2 * sent[-1].shape[0],) + tile
                sent += call(join_kernel, [(shape, f32)], [sent[-1], parts[-1]])
        return parts, sent[-1]

    def fetch_rims(rim, after=None):
        got = {}
        for dy in s.shifts:
            got["other", dy] = fetch(rim, "other", dy)
        for dy in s.shifts:
            got["same", dy] = fetch(rim, "same", dy)
        if after is not None:
            (rim,) = call(order_kernel, [(rim.shape, f32)], [rim, after])
        got["other", 0] = fetch(rim, "other", 0)
        got["partner", 0] = fetch(rim, "partner", 0)
        return got

    def forward_rims(got, after):
        for dy in s.shifts:
            held = got["same", dy]
            (held,) = call(order_kernel, [(held.shape, f32)], [held, after])
            got["partner", dy] = fetch(held, "partner", 0)

    def plane_sum(message, got, after):
        if not s.direct:
            return [lax.psum(message[s.half :], ("gx", "gy"))]
        quarter = [message] + [got[key] for key in s.sources if key[0] != "partner"]
        (half,) = call(functools.partial(half_kernel, s), [(tile, f32)], quarter + [after])
        return [half, fetch(half, "partner", 0)]

    flat = (3 * s.blobs, 1, s.bodies)
    small = (1, s.blobs)
    message, col, cells, f = call(
        functools.partial(start_kernel, s),
        [((s.message, LANES), f32), ((s.step, LANES), f32), (cells.shape, jnp.int32), (full, f32)],
        [rhs.reshape(flat), cells, blob_weight.reshape(small)],
        far_args=3,
        scratch=[pltpu.VMEM(flat, f32), pltpu.VMEM(small, f32), pltpu.SemaphoreType.DMA((3,))],
        flops=10**7,
    )
    got = fetch_rims(message)
    operators = [
        angles.reshape(3, 1, s.bodies), near_weight, neighbours, self_mob, near_mat, skel_perm, interp,
        sibling_ops, root_op,
    ]
    loc, gat, rot, sh, sl, nh, nl, oh, ol, gh, gl, fh, fl, *operators_out = call(
        functools.partial(setup_kernel, s),
        [(full, f32), (full, f32), ((16, s.bodies), f32)]
        + [(square, bf16)] * 4
        + [((s.bodies, s.bodies), bf16)] * 2
        + [((s.ghosts, s.bodies), bf16)] * 2
        + [(far_shape, bf16)] * 2
        + [((s.levels, 2 * s.skel, s.skel), bf16)] * 2
        + [((s.levels, s.skel, s.skel), bf16)] * 2
        + [((s.skel, s.skel), bf16)] * 2,
        [ids, f] + operators,
        scalars=1,
        far_args=len(operators),
        scratch=[
            pltpu.VMEM(square, f32), pltpu.VMEM((s.levels, 2 * s.skel, s.skel), f32), pltpu.VMEM(far_shape, f32)
        ]
        + [pltpu.VMEM(x.shape, x.dtype) for x in operators]
        + [pltpu.SemaphoreType.DMA((len(operators),))],
        flops=5 * 10**9,
    )
    forward_rims(got, rot)
    sums = plane_sum(message, got, rot)
    around = [got[key] for key in s.sources]
    gathered = call(
        functools.partial(gather_kernel, s),
        [(full, bf16), (full, bf16)],
        [gat, gh, gl] + around + [sums[0]],
        flops=10**9,
    )
    part, rim = call(
        functools.partial(near_kernel, s),
        [(full, f32), ((s.half, LANES), f32)],
        [loc, nh, nl, *gathered],
        flops=10**9,
    )
    (tiles,) = call(
        functools.partial(layer_kernel, s, len(sums)),
        [((2 + len(around),) + tile, f32)],
        [message] + sums + around + [gathered[1]],
    )
    layers, joined = fetch_layers(tiles)
    got = fetch_rims(rim, joined)
    places = call(
        functools.partial(place_kernel, s),
        [((s.skel, s.bodies), bf16), ((s.ghosts // LANES, s.skel, LANES), bf16)],
        [cells, tiles],
        flops=2 * 10**10,
    )
    u, charges, values = call(
        functools.partial(first_kernel, s),
        [(full, f32), (tile, f32), ((s.ghosts // LANES,) + tile, f32)],
        [part, fh, fl, *places, col, *layers],
        flops=10**8,
    )
    loc, gat, ortho, stat = call(
        functools.partial(middle_kernel, s),
        [(full, f32), (full, f32), (full, f32), (tile, f32)],
        [u, f, rot, sh, sl, oh, ol],
        flops=10**9,
    )
    forward_rims(got, charges)
    gathered = call(
        functools.partial(gather_far_kernel, s),
        [(full, bf16), (full, bf16)],
        [gat, gh, gl, col, values] + [got[key] for key in s.sources],
        flops=10**9,
    )
    (packed,) = call(
        functools.partial(second_kernel, s),
        [((s.devices, 8, LANES), f32)],
        [loc, nh, nl, *gathered, cells, col, f, ortho, stat, message, charges],
        flops=10**9,
    )
    boxes = lax.all_to_all(packed, ("gx", "gy", "gz"), 0, 0)
    result, lsq = call(
        functools.partial(finish_kernel, s),
        [(flat, f32), ((1, 1), f32)],
        [ids, f, u, boxes, fetch(boxes, "partner", 0), col, *operators_out],
        scalars=1,
        far_outs=1,
        scratch=[pltpu.VMEM(flat, f32), pltpu.SemaphoreType.DMA],
        flops=10**7,
    )
    return result.reshape(rhs.shape), lsq.reshape(())


def solution(mesh):
    in_specs = (
        P("gx", "gy", None, None, "gz"),
        P("gx", "gy", None, "gz"),
        P(),
        P(),
        P("gx", "gy", None, "gz"),
        P("gx", "gy", None, "gz"),
        P("gx", "gy", "gz"),
        P(),
        P(),
        P(),
        P(),
        P(),
    )
    out_specs = (P("gx", "gy", None, None, "gz"), P())
    inner = functools.partial(body, dict(mesh.shape))
    return jax.shard_map(inner, mesh=mesh, in_specs=in_specs, out_specs=out_specs, check_vma=False)
```

```python
import functools

import jax
import jax.numpy as jnp
from jax import lax
from jax.experimental import pallas as pl
from jax.experimental.pallas import tpu as pltpu
from jax.sharding import PartitionSpec as P

epsilon = 1e-06
f32 = jnp.float32
bf16 = jnp.bfloat16
RIM = 64
LANES = 128


def round_up(value, unit):
    return -(-value // unit) * unit


def split(x):
    hi = x.astype(bf16)
    lo = (x - hi.astype(f32)).astype(bf16)
    return hi, lo


def mm(a, b):
    return lax.dot_general(a, b, (((1,), (0,)), ((), ())), preferred_element_type=f32)


def mt(a, b):
    return lax.dot_general(a, b, (((1,), (1,)), ((), ())), preferred_element_type=f32)


def product(dot, a, b):
    return dot(a[0], b[0]) + (dot(a[0], b[1]) + dot(a[1], b[0]))


def total(x):
    return jnp.sum(jnp.sum(x, axis=0, keepdims=True), axis=1, keepdims=True)


class Sizes:
    def __init__(self, mesh_shape, rhs, skel_perm):
        self.nx, self.ny, self.nz = (mesh_shape[a] for a in ("gx", "gy", "gz"))
        self.devices = self.nx * self.ny * self.nz
        self.blobs, self.bodies = rhs.shape[-2:]
        self.step = round_up(self.blobs, 8)
        self.rows = round_up(3 * self.step, 16)
        self.half = self.rows // 2
        self.message = self.half + 8
        self.direct = (self.nx, self.ny) == (4, 2)
        self.levels = skel_perm.shape[0]
        self.skel = skel_perm.shape[1] // 2
        shifts = sorted({(dy % self.ny) for dy in (-1, 1)} - {0})
        self.shifts = shifts
        self.sources = [("same", dy) for dy in shifts]
        for kind in ("other", "partner"):
            self.sources += [(kind, dy) for dy in [0] + shifts]
        self.ghosts = round_up(len(self.sources) * RIM, LANES)
        self.far_tiles = self.nz + -(-self.nz // 2)

    def slot_start(self, slot, parity):
        dx, dy = slot // 3 - 1, (slot % 3 - 1) % self.ny
        kind = "same" if dx == 0 else "partner" if dx == 1 - 2 * parity else "other"
        if (kind, dy) == ("same", 0):
            return 0
        return self.bodies + RIM * self.sources.index((kind, dy))

    def odd(self, device):
        return (device // (self.ny * self.nz)) % 2

    def beside(self, kind, x):
        if kind == "same":
            return x
        if kind == "partner":
            return x ^ 1
        return (x + 2 * (x % 2) - 1) % self.nx


def pieces(x, s):
    return [x[c * s.step : c * s.step + s.step] for c in range(3)]


def turn(parts, rot, inverse):
    out = []
    for target in range(3):
        acc = None
        for source in range(3):
            row = 3 * source + target if inverse else 3 * target + source
            term = rot[row : row + 1] * parts[source]
            acc = term if acc is None else acc + term
        out.append(acc)
    return out


def stacked(parts, s):
    rest = s.rows - 3 * s.step
    if rest:
        parts = list(parts) + [jnp.zeros((rest, parts[0].shape[1]), f32)]
    return jnp.concatenate(parts, axis=0)


def occupancy(cells, s):
    row = lax.broadcasted_iota(jnp.int32, (s.skel, s.bodies), 0)
    return jnp.where(cells == row, 1.0, 0.0).astype(bf16)


def pack_charges(parts, weight_col, occ, s, count=False):
    moments = [jnp.sum(part * weight_col, axis=0, keepdims=True) for part in parts]
    moments.append(jnp.full((1, s.bodies), 1.0 if count else 0.0, f32))
    moments = jnp.concatenate(moments + [jnp.zeros((4, s.bodies), f32)], axis=0)
    high, rest = split(moments)
    mid, low = split(moments - high.astype(f32))
    stack = jnp.concatenate([high.astype(f32), mid.astype(f32), low.astype(f32)], axis=0).astype(bf16)
    sums = mt(stack, occ)
    charges = sums[0:8] + (sums[8:16] + sums[16:24])
    tail = jnp.concatenate([charges[:, LANES:], jnp.zeros((8, 2 * LANES - s.skel), f32)], axis=1)
    row = lax.broadcasted_iota(jnp.int32, (8, LANES), 0)
    return jnp.where(row < 4, charges[:, :LANES], pltpu.roll(tail, 4, 0))


def pack_rim(x, s):
    lane = lax.broadcasted_iota(jnp.int32, (s.half, LANES), 1)
    top, bottom = x[: s.half, :LANES], x[s.half :, :LANES]
    return jnp.where(lane < RIM, top, pltpu.roll(bottom, RIM, 1))


def unpack_rims(rims, s):
    lane = lax.broadcasted_iota(jnp.int32, (s.half, LANES), 1)
    tops, bottoms = [], []
    for i in range(0, s.ghosts // RIM, 2):
        a = rims[i]
        b = rims[i + 1] if i + 1 < len(rims) else jnp.zeros_like(a)
        tops.append(jnp.where(lane < RIM, a, pltpu.roll(b, RIM, 1)))
        bottoms.append(jnp.where(lane < RIM, pltpu.roll(a, RIM, 1), b))
    return jnp.concatenate(
        [jnp.concatenate(tops, axis=1), jnp.concatenate(bottoms, axis=1)], axis=0
    )


def pack_message(x, weight_col, cells, s):
    charges = pack_charges(pieces(x, s), weight_col, occupancy(cells, s), s)
    row = lax.broadcasted_iota(jnp.int32, (8, LANES), 0)
    charges = jnp.where(row == 3, cells[:, :LANES].astype(f32), charges)
    return jnp.concatenate([pack_rim(x, s), charges], axis=0)


def begin(sources, targets, sems):
    moves = [pltpu.make_async_copy(a, b, sems.at[i]) for i, (a, b) in enumerate(zip(sources, targets))]
    for move in moves:
        move.start()
    return moves


def start_kernel(s, rhs, cells, weight, message_out, col_out, cells_out, f_out, raw, wide, sems):
    moves = begin((weight, cells, rhs), (wide, cells_out, raw), sems)
    f_out[...] = jnp.zeros_like(f_out)
    moves[0].wait()
    row = jnp.concatenate([wide[...], jnp.zeros((1, 2 * LANES - s.blobs), f32)], axis=1)
    col = jnp.broadcast_to(row, (LANES, 2 * LANES)).T[: s.step]
    col_out[...] = col
    for move in moves[1:]:
        move.wait()
    for c in range(3):
        f_out[c * s.step : c * s.step + s.blobs, :] = raw[c * s.blobs : (c + 1) * s.blobs, 0, :]
    message_out[...] = pack_message(f_out[...], col[:, :1], cells_out[0], s)


def frame_rows(angles):
    cos, sin = jnp.cos(angles), jnp.sin(angles)
    cy, cp, cr = cos[0:1], cos[1:2], cos[2:3]
    sy, sp, sr = sin[0:1], sin[1:2], sin[2:3]
    return [
        cy * cp,
        cy * sp * sr - sy * cr,
        cy * sp * cr + sy * sr,
        sy * cp,
        sy * sp * sr + cy * cr,
        sy * sp * cr - cy * sr,
        -sp,
        cp * sr,
        cp * cr,
    ]


def local_part(f, s, rot, mob, own):
    parts = pieces(f, s)
    turned = stacked(turn(parts, rot, False), s)
    mixed = product(mm, mob, split(turned))
    back = turn(pieces(mixed, s), rot, True)
    return f + stacked(back, s), product(mm, split(f), own)


def product_many(dot, blocks, b):
    rows = blocks[0].shape[0]
    out = product(dot, split(jnp.concatenate(blocks, axis=0)), split(b))
    return [out[i * rows : (i + 1) * rows] for i in range(len(blocks))]


def expand_once(groups, halves):
    flat = [block for group in groups for block in group]
    sides = [product_many(mt, flat, half) for half in halves]
    out, at = [], 0
    for group in groups:
        spread = []
        for i in range(at, at + len(group)):
            spread += [sides[0][i], sides[1][i]]
        at += len(group)
        out.append(spread)
    return out


def setup_kernel(
    s, ids, f_in, *refs
):
    count = 9
    sources, refs = refs[:count], refs[count:]
    copies, refs = refs[-1 - count :], refs[: -1 - count]
    copies, sems = copies[:-1], copies[-1]
    setup(s, ids, f_in, begin(sources, copies, sems), *copies, *refs)


def setup(
    s, ids, f_in, moves, angles, near_weight, neighbours, self_mob, near_mat, perm, interp, sibling, root,
    loc_out, gat_out, rot_out, sh_out, sl_out, nh_out, nl_out, oh_out, ol_out, gh_out, gl_out,
    fh_out, fl_out, uh_out, ul_out, bh_out, bl_out, rh_out, rl_out, padded, ups_ref, far_ref,
):
    f = f_in[...]
    for move in moves[:3]:
        move.wait()
    rot = jnp.concatenate(frame_rows(angles[:, 0, :]) + [jnp.zeros((7, s.bodies), f32)], axis=0)
    rot_out[...] = rot

    links = neighbours[0, 0]
    slot = links // s.bodies
    base = jnp.zeros_like(links)
    odd = (ids[0] // s.ny) % 2
    for index in range(9):
        start = jnp.where(odd == 1, s.slot_start(index, 1), s.slot_start(index, 0))
        base = jnp.where(slot == index, start, base)
    column = base + links % s.bodies
    coef = near_weight[0, 0]
    for first, count, hi_out, lo_out in (
        (0, s.bodies, oh_out, ol_out),
        (s.bodies, s.ghosts, gh_out, gl_out),
    ):
        for r in range(0, count, 64):
            row = lax.broadcasted_iota(jnp.int32, (64, s.bodies), 0) + (first + r)
            acc = jnp.zeros((64, s.bodies), f32)
            for k in range(coef.shape[0]):
                acc = acc + jnp.where(column[k : k + 1] == row, coef[k : k + 1], 0.0)
            hi, lo = split(acc)
            hi_out[r : r + 64, :] = hi
            lo_out[r : r + 64, :] = lo

    for move in moves[3:]:
        move.wait()
    padded[...] = jnp.zeros_like(padded)
    for matrix, hi_out, lo_out in ((self_mob, sh_out, sl_out), (near_mat, nh_out, nl_out)):
        for c in range(3):
            for d in range(3):
                padded[c * s.step : c * s.step + s.blobs, d * s.step : d * s.step + s.blobs] = matrix[
                    c * s.blobs : (c + 1) * s.blobs, d * s.blobs : (d + 1) * s.blobs
                ]
        hi, lo = split(padded[...])
        hi_out[...] = hi
        lo_out[...] = lo

    loc, gat = local_part(f, s, rot, (sh_out[...], sl_out[...]), (oh_out[...], ol_out[...]))
    loc_out[...] = loc
    gat_out[...] = gat

    n = s.skel
    z = ids[1]
    halves = []
    spot = lax.broadcasted_iota(jnp.int32, (2 * n, n), 0)
    for level in range(s.levels):
        kept = jnp.where(perm[level : level + 1, :n] == spot, 1.0, 0.0)
        moved = jnp.where(perm[level : level + 1, n:] == spot, 1.0, 0.0).astype(bf16)
        hi, lo = split(interp[level])
        up = kept + (mm(moved, hi) + mm(moved, lo))
        ups_ref[level] = up
        uh_out[level], ul_out[level] = split(up)
        bh_out[level], bl_out[level] = split(sibling[level])
        bit = (z >> level) & 1
        halves.append(
            [ups_ref[level, pl.ds(pl.multiple_of(side * n, 8), n), :] for side in (bit, 1 - bit)]
        )

    def down(block, level, dot):
        return product(dot, split(halves[level][0]), split(block))

    spread = root[...]
    rh_out[...], rl_out[...] = split(spread)
    beside = []
    for level in reversed(range(s.levels)):
        spread = down(spread, level, mt if level == s.levels - 1 else mm)
        beside = [(down(block, level, mt if fresh else mm), False) for block, fresh in beside]
        beside.append((sibling[level], True))
    beside = [block.T if fresh else block for block, fresh in reversed(beside)]
    leaves = [[spread]]
    for level in reversed(range(s.levels)):
        leaves = expand_once(leaves, halves[level])
        leaves.append([beside[level]])
    far_leaves, *sub = leaves
    near_leaves = [jnp.zeros((n, n), f32)]
    for blocks in reversed(sub):
        near_leaves += blocks
    tail = n - LANES
    far_ref[...] = jnp.zeros_like(far_ref)
    own = [a - b for a, b in zip(near_leaves, far_leaves)]
    for group, blocks in enumerate((own, far_leaves)):
        for leaf, block in enumerate(blocks):
            at = (group * s.far_tiles + leaf) * LANES
            far_ref[:, at : at + LANES] = block[:, :LANES]
            at = (group * s.far_tiles + s.nz + leaf // 2) * LANES + leaf % 2 * RIM
            far_ref[:, at : at + tail] = block[:, LANES:]
    fh_out[...], fl_out[...] = split(far_ref[...])


def half_kernel(s, *refs):
    *messages, _, out = refs
    acc = messages[0][s.half :, :]
    for message in messages[1:]:
        acc = acc + message[s.half :, :]
    out[...] = acc


def layer_kernel(s, count, message, *refs):
    sums, around, out = refs[:count], refs[count:-2], refs[-1]
    acc = sums[0][...]
    for part in sums[1:]:
        acc = acc + part[...]
    out[0] = message[s.half :, :]
    out[1] = acc
    for index, other in enumerate(around):
        out[2 + index] = other[s.half :, :]


def join_kernel(x, y, out):
    out[: x.shape[0]] = x[...]
    out[x.shape[0] :] = y[...]


def layer_row(s, tiles):
    row = list(tiles)
    lane = lax.broadcasted_iota(jnp.int32, (8, LANES), 1)
    for leaf in range(0, s.nz, 2):
        pair = tiles[leaf]
        if leaf + 1 < s.nz:
            pair = jnp.where(lane < RIM, pair, pltpu.roll(tiles[leaf + 1], RIM, 1))
        row.append(pltpu.roll(pair, 4, 0))
    return jnp.concatenate(row, axis=1)


def far_potentials(s, layers, far_op):
    own = [layer_row(s, [layer[k] for layer in layers]) for k in range(len(layers[0]))]
    wide = own[0].shape[1]
    hi, lo = far_op
    whole = product(mt, split(own.pop(1)), (hi[:, wide:], lo[:, wide:]))
    boxes = product(mt, split(jnp.concatenate(own, axis=0)), (hi[:, :wide], lo[:, :wide]))
    return [boxes[8 * k : 8 * k + 8] + whole for k in range(len(own))]


def pick(potential, onehot):
    high, _ = split(potential)
    mid, low = split(potential - high.astype(f32))
    parts = [x.astype(f32) for x in (high, mid, low)]
    picked = mm(jnp.concatenate(parts, axis=0).astype(bf16), onehot)
    n = potential.shape[0]
    return picked[:n] + (picked[n : 2 * n] + picked[2 * n :])


def place_kernel(s, cells, tiles, own_out, rims_out):
    own_out[...] = occupancy(cells[0], s)
    lane = lax.broadcasted_iota(jnp.int32, (8, LANES), 1)
    place = lax.broadcasted_iota(jnp.int32, (s.skel, LANES), 0).astype(f32)
    count = len(s.sources)
    for i in range(0, count, 2):
        last = min(i + 1, count - 1)
        pair = jnp.where(lane < RIM, tiles[2 + i], pltpu.roll(tiles[2 + last], RIM, 1))
        rims_out[i // 2] = jnp.where(pair[3:4] == place, 1.0, 0.0).astype(bf16)


def rim_values(s, potentials, onehots):
    lane = lax.broadcasted_iota(jnp.int32, (8, LANES), 1)
    count = len(potentials) - 1
    out = []
    for i in range(0, count, 2):
        last = min(i + 1, count - 1)
        both = pick(jnp.concatenate([potentials[1 + i], potentials[1 + last]], axis=0), onehots[i // 2])
        out.append(jnp.where(lane < RIM, both[:8], both[8:]))
    return out


def gather_kernel(s, gat, gh, gl, *refs):
    *messages, _, hi_out, lo_out = refs
    rims = unpack_rims([message[: s.half, :] for message in messages], s)
    gathered = gat[...] + product(mm, split(rims), (gh[...], gl[...]))
    hi_out[...], lo_out[...] = split(gathered)


def gather_far_kernel(s, gat, gh, gl, col, values, *refs):
    *messages, hi_out, lo_out = refs
    rims = unpack_rims([message[...] for message in messages], s)
    far = []
    for c in range(3):
        value = jnp.concatenate([values[i, c : c + 1, :] for i in range(values.shape[0])], axis=1)
        far.append(col[:, :1] * value)
    rims = rims + stacked(far, s)
    gathered = gat[...] + product(mm, split(rims), (gh[...], gl[...]))
    hi_out[...], lo_out[...] = split(gathered)


def near_kernel(s, loc, nh, nl, hi, lo, out, rim_out):
    part = loc[...] + product(mm, (nh[...], nl[...]), (hi[...], lo[...]))
    out[...] = part
    rim_out[...] = pack_rim(part, s)


def first_kernel(s, part, fh, fl, own, rims, col, *refs):
    *layers, u_out, charges_out, values_out = refs
    count = 2 + len(s.sources)
    layers = [[part[at + k] for k in range(count)] for part in layers for at in range(0, part.shape[0], count)]
    weight_col = col[:, :1]
    occ = own[...]
    potentials = far_potentials(s, layers, (fh[...], fl[...]))
    values = pick(potentials[0], occ)
    u = part[...] + stacked([weight_col * values[c : c + 1] for c in range(3)], s)
    u_out[...] = u
    charges_out[...] = pack_charges(pieces(u, s), weight_col, occ, s)
    for index, value in enumerate(rim_values(s, potentials, rims)):
        values_out[index] = value


def order_kernel(x, _, out):
    out[...] = x[...]


def safe_inverse(x):
    return jnp.where(x > 0.0, 1.0 / jnp.where(x > 0.0, x, 1.0), 0.0)


def middle_kernel(s, u_in, f_in, rot, sh, sl, oh, ol, loc_out, gat_out, ortho_out, stat_out):
    u, f = u_in[...], f_in[...]
    loc, gat = local_part(u, s, rot[...], (sh[...], sl[...]), (oh[...], ol[...]))
    loc_out[...] = loc
    gat_out[...] = gat
    ff = total(f * f)
    fu = total(f * u) * safe_inverse(ff)
    ortho = u - fu * f
    ortho_out[...] = ortho
    oo = total(ortho * ortho)
    stat_out[...] = jnp.broadcast_to(
        jnp.concatenate([ff, fu, oo, jnp.zeros((5, 1), f32)], axis=0), (8, LANES)
    )


def second_kernel(
    s, loc, nh, nl, hi, lo, cells, col, f_in, ortho_in, stat, charges_f, charges_u, packed_out
):
    part = loc[...] + product(mm, (nh[...], nl[...]), (hi[...], lo[...]))
    f, ortho = f_in[...], ortho_in[...]
    ff, fu, oo = (stat[i : i + 1, :1] for i in range(3))
    fa = total(f * part) * safe_inverse(ff)
    oa = total(ortho * part) * safe_inverse(oo)
    rest = part - fa * f - oa * ortho
    aa = total(rest * rest)
    rf, ro = jnp.sqrt(ff), jnp.sqrt(oo)
    of_f = charges_f[-8:, :]
    of_u = charges_u[...]
    of_a = pack_charges(pieces(rest, s), col[:, :1], occupancy(cells[0], s), s, count=True)
    row = lax.broadcasted_iota(jnp.int32, (8, LANES), 0)
    lane = lax.broadcasted_iota(jnp.int32, (8, LANES), 1)
    left = lane < RIM
    first = jnp.where(left, of_u, pltpu.roll(of_a, RIM, 1))
    first = jnp.where(row < 4, of_u, first)
    first = jnp.where((row == 7) & left, pltpu.roll(of_f, 1, 0), first)
    for index, value in enumerate((rf, rf * fu, ro, rf * fa, ro * oa, aa)):
        first = jnp.where((row == 3) & (lane == index), value, first)
    tails = jnp.where(left, pltpu.roll(of_f, 3, 0), pltpu.roll(pltpu.roll(of_f, 2, 0), RIM, 1))
    second = jnp.where(row < 3, of_f, of_a)
    second = jnp.where(row < 4, second, pltpu.roll(of_a, 4, 0))
    second = jnp.where(row == 7, tails, second)
    for device in range(s.devices):
        packed_out[device] = second if s.odd(device) else first


def tree(s, leaves, ups, siblings, root):
    def apply(dot, blocks, factor):
        rows = blocks[0].shape[0]
        out = product(dot, split(jnp.concatenate(blocks, axis=0)), factor)
        return [out[i * rows : (i + 1) * rows] for i in range(len(blocks))]

    n = s.skel
    halves = [[(hi[level, j * n : (j + 1) * n, :], lo[level, j * n : (j + 1) * n, :]) for j in range(2)]
              for level, (hi, lo) in ((k, ups) for k in range(s.levels))]
    charges = [leaves]
    for level in range(s.levels):
        low, high = (apply(mm, charges[-1][j::2], halves[level][j]) for j in range(2))
        charges.append([a + b for a, b in zip(low, high)])
    own = charges[-1][0]
    whole = own[:8]
    for column in range(1, s.nx * s.ny):
        whole = whole + own[8 * column : 8 * column + 8]
    others = jnp.concatenate([whole] * (s.nx * s.ny), axis=0) - own
    potential = apply(mm, [others], root)
    for level in reversed(range(s.levels)):
        beside = apply(mm, charges[level], (siblings[0][level], siblings[1][level]))
        down = [apply(mt, potential, halves[level][j]) for j in range(2)]
        potential = [
            down[z % 2][z // 2] + beside[z ^ 1] for z in range(len(charges[level]))
        ]
    return potential


def box_numbers(s, firsts, seconds, ups, siblings, root):
    columns = s.nx * s.ny
    row = lax.broadcasted_iota(jnp.int32, (8, LANES), 0)
    lane = lax.broadcasted_iota(jnp.int32, (8, LANES), 1)
    left, valid = lane < RIM, row < 3
    leaves = []
    for z in range(s.nz):
        wide = []
        for column in range(columns):
            tile = firsts[column * s.nz + z]
            wide.append(jnp.concatenate([tile, pltpu.roll(tile, 4, 0)], axis=1)[:, : s.skel])
        leaves.append(jnp.concatenate(wide, axis=0))
    potential = tree(s, leaves, ups, siblings, root)
    out = []
    for start in range(0, s.devices, 8):
        sums = [jnp.zeros((8, LANES), f32) for _ in range(5)]
        for box in range(start, min(s.devices, start + 8)):
            column, z = box // s.nz, box % s.nz
            phi = potential[z][8 * column : 8 * column + 8]
            main, tail = phi[:, :LANES], phi[:, LANES:]
            tail = jnp.concatenate([tail, tail], axis=1)
            first, second = firsts[box], seconds[box]
            both = pltpu.roll(first, 4, 0) * tail
            of_f = jnp.where(row == 0, pltpu.roll(second, 1, 0), jnp.where(row == 1, pltpu.roll(second, 2, 0), pltpu.roll(first, 3, 0)))
            of_f = jnp.where(left == (row != 1), of_f * tail, 0.0)
            count = jnp.broadcast_to(second[3:4], (8, LANES))
            count_tail = jnp.where(left, 0.0, jnp.broadcast_to(first[7:8], (8, LANES)))
            terms = (
                second * main + of_f,
                first * main + jnp.where(left, both, 0.0),
                pltpu.roll(second, 4, 0) * main + jnp.where(left, 0.0, both),
                count * (main * main) + count_tail * (tail * tail),
            )
            here = row == box - start
            for index, term in enumerate(terms):
                value = jnp.sum(jnp.where(valid, term, 0.0), axis=0, keepdims=True)
                sums[index] = jnp.where(here, value, sums[index])
            sums[4] = jnp.where(here, first[3:4], sums[4])
        numbers = sums[4]
        for index in range(4):
            numbers = jnp.where(lane == 6 + index, jnp.sum(sums[index], axis=1, keepdims=True), numbers)
        out.append(numbers)
    rest = round_up(s.devices, LANES) - 8 * len(out)
    if rest:
        out.append(jnp.zeros((rest, LANES), f32))
    return jnp.concatenate(out, axis=0)


def finish_kernel(s, ids, f_in, u_in, mine, other, col, uh, ul, bh, bl, rh, rl, x_out, lsq_out, raw, sem):
    odd = (ids[0] // s.ny) % 2 == 1
    firsts = [jnp.where(odd, other[box], mine[box]) for box in range(s.devices)]
    seconds = [jnp.where(odd, mine[box], other[box]) for box in range(s.devices)]
    rows = box_numbers(s, firsts, seconds, (uh, ul), (bh, bl), (rh[...], rl[...])).T
    f1, u1, u2, t1, t2, aa, far_f, far_u, far_a, far_far = (rows[i : i + 1] for i in range(10))
    by_f = safe_inverse(f1)
    by_o = jnp.where(u2 * u2 > 1e-10 * (u1 * u1), safe_inverse(u2), 0.0)
    on_one = far_f * by_f
    on_two = (far_u - u1 * by_f * far_f) * by_o
    weight = jnp.sum(col[:, :1] * col[:, :1], axis=0, keepdims=True)
    t3 = aa + 2.0 * far_a + weight * far_far - on_one * on_one - on_two * on_two
    t1, t2, t3 = t1 + on_one, t2 + on_two, jnp.sqrt(jnp.maximum(t3, 0.0))

    def along(x):
        return jnp.sum(x, axis=1, keepdims=True)

    beta = jnp.sqrt(along(f1 * f1) + epsilon)
    v = f1 / beta
    w1, w2 = u1 / beta, u2 / beta
    h11 = along(w1 * v)
    r1 = w1 - h11 * v
    h21 = jnp.sqrt(along(r1 * r1 + w2 * w2) + epsilon)
    b1, b2 = r1 / h21, w2 / h21
    z1, z2, z3 = ((t1 / beta - h11 * w1) / h21, (t2 / beta - h11 * w2) / h21, t3 / beta / h21)
    h12 = along(z1 * v)
    h22 = along(z1 * b1 + z2 * b2)
    d1, d2 = z1 - h12 * v - h22 * b1, z2 - h22 * b2
    h32 = jnp.sqrt(along(d1 * d1 + d2 * d2 + z3 * z3) + epsilon)
    first_norm = jnp.sqrt(h11 * h11 + h21 * h21)
    c1, s1 = h11 / first_norm, h21 / first_norm
    t12, t22 = c1 * h12 + s1 * h22, c1 * h22 - s1 * h12
    second_norm = jnp.sqrt(t22 * t22 + h32 * h32)
    c2, s2 = t22 / second_norm, h32 / second_norm
    g2 = -s1 * beta
    y2 = c2 * g2 / second_norm
    y1 = (c1 * beta - t12 * y2) / first_norm
    lsq_out[...] = jnp.abs(s2 * g2)
    on_u = y2 / h21 / beta
    on_f = y1 / beta - on_u * h11
    for c in range(3):
        part = slice(c * s.step, c * s.step + s.blobs)
        raw[c * s.blobs : (c + 1) * s.blobs, 0, :] = on_f * f_in[part, :] + on_u * u_in[part, :]
    move = pltpu.make_async_copy(raw, x_out, sem)
    move.start()
    move.wait()


def call(kernel, outs, args, scalars=0, far_args=0, far_outs=0, scratch=(), flops=0):
    vmem = pl.BlockSpec(memory_space=pltpu.VMEM)
    smem = pl.BlockSpec(memory_space=pltpu.SMEM)
    hbm = pl.BlockSpec(memory_space=pltpu.HBM)
    near_args = len(args) - far_args
    args = args[:near_args] + [pltpu.with_memory_space_constraint(x, pltpu.HBM) for x in args[near_args:]]
    return pl.pallas_call(
        kernel,
        out_shape=[jax.ShapeDtypeStruct(shape, kind) for shape, kind in outs],
        in_specs=[smem] * scalars + [vmem] * (near_args - scalars) + [hbm] * far_args,
        out_specs=[hbm] * far_outs + [vmem] * (len(outs) - far_outs),
        scratch_shapes=list(scratch),
        compiler_params=pltpu.CompilerParams(vmem_limit_bytes=16 * 2**20),
        cost_estimate=pl.CostEstimate(flops=flops, bytes_accessed=2**20, transcendentals=0),
    )(*args)


def body(
    mesh_shape, rhs, angles, self_mob, near_mat, near_weight, neighbours, cells, blob_weight,
    skel_perm, interp, sibling_ops, root_op,
):
    s = Sizes(mesh_shape, rhs, skel_perm)
    full = (s.rows, s.bodies)
    square = (s.rows, s.rows)
    tile = (8, LANES)
    far_shape = (s.skel, 2 * s.far_tiles * LANES)
    column = lax.axis_index("gx") * s.ny + lax.axis_index("gy")
    ids = jnp.stack([column, lax.axis_index("gz")]).astype(jnp.int32)

    def fetch(x, kind, dy):
        pairs = []
        for gx in range(s.nx):
            for gy in range(s.ny):
                pairs.append((s.beside(kind, gx) * s.ny + (gy + dy) % s.ny, gx * s.ny + gy))
        return lax.ppermute(x, ("gx", "gy"), pairs)

    def fetch_layers(x):
        parts, sent = [x], [x]
        for level in range(s.levels):
            pairs = [(z ^ (1 << level), z) for z in range(s.nz)]
            parts.append(lax.ppermute(sent[-1], "gz", pairs))
            if level + 1 < s.levels:
                shape = (2 * sent[-1].shape[0],) + tile
                sent += call(join_kernel, [(shape, f32)], [sent[-1], parts[-1]])
        return parts, sent[-1]

    def fetch_rims(rim, after=None):
        got = {}
        for dy in [0] + s.shifts:
            got["other", dy] = fetch(rim, "other", dy)
        if after is not None:
            (rim,) = call(order_kernel, [(rim.shape, f32)], [rim, after])
        for dy in s.shifts:
            got["same", dy] = fetch(rim, "same", dy)
        got["partner", 0] = fetch(rim, "partner", 0)
        return got

    def forward_rims(got, after):
        for dy in s.shifts:
            held = got["same", dy]
            (held,) = call(order_kernel, [(held.shape, f32)], [held, after])
            got["partner", dy] = fetch(held, "partner", 0)

    def plane_sum(message, got, after):
        if not s.direct:
            return [lax.psum(message[s.half :], ("gx", "gy"))]
        quarter = [message] + [got[key] for key in s.sources if key[0] != "partner"]
        (half,) = call(functools.partial(half_kernel, s), [(tile, f32)], quarter + [after])
        return [half, fetch(half, "partner", 0)]

    flat = (3 * s.blobs, 1, s.bodies)
    small = (1, s.blobs)
    message, col, cells, f = call(
        functools.partial(start_kernel, s),
        [((s.message, LANES), f32), ((s.step, LANES), f32), (cells.shape, jnp.int32), (full, f32)],
        [rhs.reshape(flat), cells, blob_weight.reshape(small)],
        far_args=3,
        scratch=[pltpu.VMEM(flat, f32), pltpu.VMEM(small, f32), pltpu.SemaphoreType.DMA((3,))],
        flops=10**7,
    )
    got = fetch_rims(message, message)
    operators = [
        angles.reshape(3, 1, s.bodies), near_weight, neighbours, self_mob, near_mat, skel_perm, interp,
        sibling_ops, root_op,
    ]
    loc, gat, rot, sh, sl, nh, nl, oh, ol, gh, gl, fh, fl, *operators_out = call(
        functools.partial(setup_kernel, s),
        [(full, f32), (full, f32), ((16, s.bodies), f32)]
        + [(square, bf16)] * 4
        + [((s.bodies, s.bodies), bf16)] * 2
        + [((s.ghosts, s.bodies), bf16)] * 2
        + [(far_shape, bf16)] * 2
        + [((s.levels, 2 * s.skel, s.skel), bf16)] * 2
        + [((s.levels, s.skel, s.skel), bf16)] * 2
        + [((s.skel, s.skel), bf16)] * 2,
        [ids, f] + operators,
        scalars=1,
        far_args=len(operators),
        scratch=[
            pltpu.VMEM(square, f32), pltpu.VMEM((s.levels, 2 * s.skel, s.skel), f32), pltpu.VMEM(far_shape, f32)
        ]
        + [pltpu.VMEM(x.shape, x.dtype) for x in operators]
        + [pltpu.SemaphoreType.DMA((len(operators),))],
        flops=5 * 10**9,
    )
    forward_rims(got, rot)
    sums = plane_sum(message, got, rot)
    around = [got[key] for key in s.sources]
    gathered = call(
        functools.partial(gather_kernel, s),
        [(full, bf16), (full, bf16)],
        [gat, gh, gl] + around + [sums[0]],
        flops=10**9,
    )
    part, rim = call(
        functools.partial(near_kernel, s),
        [(full, f32), ((s.half, LANES), f32)],
        [loc, nh, nl, *gathered],
        flops=10**9,
    )
    (tiles,) = call(
        functools.partial(layer_kernel, s, len(sums)),
        [((2 + len(around),) + tile, f32)],
        [message] + sums + around + [gathered[1]],
    )
    layers, joined = fetch_layers(tiles)
    got = fetch_rims(rim, joined)
    places = call(
        functools.partial(place_kernel, s),
        [((s.skel, s.bodies), bf16), ((s.ghosts // LANES, s.skel, LANES), bf16)],
        [cells, tiles],
        flops=2 * 10**10,
    )
    u, charges, values = call(
        functools.partial(first_kernel, s),
        [(full, f32), (tile, f32), ((s.ghosts // LANES,) + tile, f32)],
        [part, fh, fl, *places, col, *layers],
        flops=10**8,
    )
    loc, gat, ortho, stat = call(
        functools.partial(middle_kernel, s),
        [(full, f32), (full, f32), (full, f32), (tile, f32)],
        [u, f, rot, sh, sl, oh, ol],
        flops=10**9,
    )
    forward_rims(got, charges)
    gathered = call(
        functools.partial(gather_far_kernel, s),
        [(full, bf16), (full, bf16)],
        [gat, gh, gl, col, values] + [got[key] for key in s.sources],
        flops=10**9,
    )
    (packed,) = call(
        functools.partial(second_kernel, s),
        [((s.devices, 8, LANES), f32)],
        [loc, nh, nl, *gathered, cells, col, f, ortho, stat, message, charges],
        flops=10**9,
    )
    boxes = lax.all_to_all(packed, ("gx", "gy", "gz"), 0, 0)
    result, lsq = call(
        functools.partial(finish_kernel, s),
        [(flat, f32), ((1, 1), f32)],
        [ids, f, u, boxes, fetch(boxes, "partner", 0), col, *operators_out],
        scalars=1,
        far_outs=1,
        scratch=[pltpu.VMEM(flat, f32), pltpu.SemaphoreType.DMA],
        flops=10**7,
    )
    return result.reshape(rhs.shape), lsq.reshape(())


def solution(mesh):
    in_specs = (
        P("gx", "gy", None, None, "gz"),
        P("gx", "gy", None, "gz"),
        P(),
        P(),
        P("gx", "gy", None, "gz"),
        P("gx", "gy", None, "gz"),
        P("gx", "gy", "gz"),
        P(),
        P(),
        P(),
        P(),
        P(),
    )
    out_specs = (P("gx", "gy", None, None, "gz"), P())
    inner = functools.partial(body, dict(mesh.shape))
    return jax.shard_map(inner, mesh=mesh, in_specs=in_specs, out_specs=out_specs, check_vma=False)
```

```python
import functools

import jax
import jax.numpy as jnp
from jax import lax
from jax.experimental import pallas as pl
from jax.experimental.pallas import tpu as pltpu
from jax.sharding import PartitionSpec as P

epsilon = 1e-06
f32 = jnp.float32
bf16 = jnp.bfloat16
RIM = 64
LANES = 128


def round_up(value, unit):
    return -(-value // unit) * unit


def split(x):
    hi = x.astype(bf16)
    lo = (x - hi.astype(f32)).astype(bf16)
    return hi, lo


def mm(a, b):
    return lax.dot_general(a, b, (((1,), (0,)), ((), ())), preferred_element_type=f32)


def mt(a, b):
    return lax.dot_general(a, b, (((1,), (1,)), ((), ())), preferred_element_type=f32)


def product(dot, a, b):
    return dot(a[0], b[0]) + (dot(a[0], b[1]) + dot(a[1], b[0]))


def total(x):
    return jnp.sum(jnp.sum(x, axis=0, keepdims=True), axis=1, keepdims=True)


class Sizes:
    def __init__(self, mesh_shape, rhs, skel_perm):
        self.nx, self.ny, self.nz = (mesh_shape[a] for a in ("gx", "gy", "gz"))
        self.devices = self.nx * self.ny * self.nz
        self.blobs, self.bodies = rhs.shape[-2:]
        self.step = round_up(self.blobs, 8)
        self.rows = round_up(3 * self.step, 16)
        self.half = self.rows // 2
        self.message = self.half + 8
        self.direct = (self.nx, self.ny) == (4, 2)
        self.levels = skel_perm.shape[0]
        self.skel = skel_perm.shape[1] // 2
        shifts = sorted({(dy % self.ny) for dy in (-1, 1)} - {0})
        self.shifts = shifts
        self.sources = [("same", dy) for dy in shifts]
        for kind in ("other", "partner"):
            self.sources += [(kind, dy) for dy in [0] + shifts]
        self.ghosts = round_up(len(self.sources) * RIM, LANES)
        self.far_tiles = self.nz + -(-self.nz // 2)

    def slot_start(self, slot, parity):
        dx, dy = slot // 3 - 1, (slot % 3 - 1) % self.ny
        kind = "same" if dx == 0 else "partner" if dx == 1 - 2 * parity else "other"
        if (kind, dy) == ("same", 0):
            return 0
        return self.bodies + RIM * self.sources.index((kind, dy))

    def odd(self, device):
        return (device // (self.ny * self.nz)) % 2

    def beside(self, kind, x):
        if kind == "same":
            return x
        if kind == "partner":
            return x ^ 1
        return (x + 2 * (x % 2) - 1) % self.nx


def pieces(x, s):
    return [x[c * s.step : c * s.step + s.step] for c in range(3)]


def turn(parts, rot, inverse):
    out = []
    for target in range(3):
        acc = None
        for source in range(3):
            row = 3 * source + target if inverse else 3 * target + source
            term = rot[row : row + 1] * parts[source]
            acc = term if acc is None else acc + term
        out.append(acc)
    return out


def stacked(parts, s):
    rest = s.rows - 3 * s.step
    if rest:
        parts = list(parts) + [jnp.zeros((rest, parts[0].shape[1]), f32)]
    return jnp.concatenate(parts, axis=0)


def occupancy(cells, s):
    row = lax.broadcasted_iota(jnp.int32, (s.skel, s.bodies), 0)
    return jnp.where(cells == row, 1.0, 0.0).astype(bf16)


def pack_charges(parts, weight_col, occ, s, count=False):
    moments = [jnp.sum(part * weight_col, axis=0, keepdims=True) for part in parts]
    moments.append(jnp.full((1, s.bodies), 1.0 if count else 0.0, f32))
    moments = jnp.concatenate(moments + [jnp.zeros((4, s.bodies), f32)], axis=0)
    high, rest = split(moments)
    mid, low = split(moments - high.astype(f32))
    stack = jnp.concatenate([high.astype(f32), mid.astype(f32), low.astype(f32)], axis=0).astype(bf16)
    sums = mt(stack, occ)
    charges = sums[0:8] + (sums[8:16] + sums[16:24])
    tail = jnp.concatenate([charges[:, LANES:], jnp.zeros((8, 2 * LANES - s.skel), f32)], axis=1)
    row = lax.broadcasted_iota(jnp.int32, (8, LANES), 0)
    return jnp.where(row < 4, charges[:, :LANES], pltpu.roll(tail, 4, 0))


def pack_rim(x, s):
    lane = lax.broadcasted_iota(jnp.int32, (s.half, LANES), 1)
    top, bottom = x[: s.half, :LANES], x[s.half :, :LANES]
    return jnp.where(lane < RIM, top, pltpu.roll(bottom, RIM, 1))


def unpack_rims(rims, s):
    lane = lax.broadcasted_iota(jnp.int32, (s.half, LANES), 1)
    tops, bottoms = [], []
    for i in range(0, s.ghosts // RIM, 2):
        a = rims[i]
        b = rims[i + 1] if i + 1 < len(rims) else jnp.zeros_like(a)
        tops.append(jnp.where(lane < RIM, a, pltpu.roll(b, RIM, 1)))
        bottoms.append(jnp.where(lane < RIM, pltpu.roll(a, RIM, 1), b))
    return jnp.concatenate(
        [jnp.concatenate(tops, axis=1), jnp.concatenate(bottoms, axis=1)], axis=0
    )


def pack_message(x, weight_col, cells, s):
    charges = pack_charges(pieces(x, s), weight_col, occupancy(cells, s), s)
    row = lax.broadcasted_iota(jnp.int32, (8, LANES), 0)
    charges = jnp.where(row == 3, cells[:, :LANES].astype(f32), charges)
    return jnp.concatenate([pack_rim(x, s), charges], axis=0)


def begin(sources, targets, sems):
    moves = [pltpu.make_async_copy(a, b, sems.at[i]) for i, (a, b) in enumerate(zip(sources, targets))]
    for move in moves:
        move.start()
    return moves


def start_kernel(s, rhs, cells, weight, message_out, col_out, cells_out, f_out, raw, wide, sems):
    moves = begin((weight, cells, rhs), (wide, cells_out, raw), sems)
    f_out[...] = jnp.zeros_like(f_out)
    moves[0].wait()
    row = jnp.concatenate([wide[...], jnp.zeros((1, 2 * LANES - s.blobs), f32)], axis=1)
    col = jnp.broadcast_to(row, (LANES, 2 * LANES)).T[: s.step]
    col_out[...] = col
    for move in moves[1:]:
        move.wait()
    for c in range(3):
        f_out[c * s.step : c * s.step + s.blobs, :] = raw[c * s.blobs : (c + 1) * s.blobs, 0, :]
    message_out[...] = pack_message(f_out[...], col[:, :1], cells_out[0], s)


def frame_rows(angles):
    cos, sin = jnp.cos(angles), jnp.sin(angles)
    cy, cp, cr = cos[0:1], cos[1:2], cos[2:3]
    sy, sp, sr = sin[0:1], sin[1:2], sin[2:3]
    return [
        cy * cp,
        cy * sp * sr - sy * cr,
        cy * sp * cr + sy * sr,
        sy * cp,
        sy * sp * sr + cy * cr,
        sy * sp * cr - cy * sr,
        -sp,
        cp * sr,
        cp * cr,
    ]


def local_part(f, s, rot, mob, own):
    parts = pieces(f, s)
    turned = stacked(turn(parts, rot, False), s)
    mixed = product(mm, mob, split(turned))
    back = turn(pieces(mixed, s), rot, True)
    return f + stacked(back, s), product(mm, split(f), own)


def product_many(dot, blocks, b):
    rows = blocks[0].shape[0]
    out = product(dot, split(jnp.concatenate(blocks, axis=0)), split(b))
    return [out[i * rows : (i + 1) * rows] for i in range(len(blocks))]


def expand_once(groups, halves):
    flat = [block for group in groups for block in group]
    sides = [product_many(mt, flat, half) for half in halves]
    out, at = [], 0
    for group in groups:
        spread = []
        for i in range(at, at + len(group)):
            spread += [sides[0][i], sides[1][i]]
        at += len(group)
        out.append(spread)
    return out


def setup_kernel(
    s, ids, f_in, *refs
):
    count = 9
    sources, refs = refs[:count], refs[count:]
    copies, refs = refs[-1 - count :], refs[: -1 - count]
    copies, sems = copies[:-1], copies[-1]
    setup(s, ids, f_in, begin(sources, copies, sems), *copies, *refs)


def setup(
    s, ids, f_in, moves, angles, near_weight, neighbours, self_mob, near_mat, perm, interp, sibling, root,
    loc_out, gat_out, rot_out, sh_out, sl_out, nh_out, nl_out, oh_out, ol_out, gh_out, gl_out,
    fh_out, fl_out, uh_out, ul_out, bh_out, bl_out, rh_out, rl_out, padded, ups_ref, far_ref,
):
    f = f_in[...]
    for move in moves[:3]:
        move.wait()
    rot = jnp.concatenate(frame_rows(angles[:, 0, :]) + [jnp.zeros((7, s.bodies), f32)], axis=0)
    rot_out[...] = rot

    links = neighbours[0, 0]
    slot = links // s.bodies
    base = jnp.zeros_like(links)
    odd = (ids[0] // s.ny) % 2
    for index in range(9):
        start = jnp.where(odd == 1, s.slot_start(index, 1), s.slot_start(index, 0))
        base = jnp.where(slot == index, start, base)
    column = base + links % s.bodies
    coef = near_weight[0, 0]
    for first, count, hi_out, lo_out in (
        (0, s.bodies, oh_out, ol_out),
        (s.bodies, s.ghosts, gh_out, gl_out),
    ):
        for r in range(0, count, 64):
            row = lax.broadcasted_iota(jnp.int32, (64, s.bodies), 0) + (first + r)
            acc = jnp.zeros((64, s.bodies), f32)
            for k in range(coef.shape[0]):
                acc = acc + jnp.where(column[k : k + 1] == row, coef[k : k + 1], 0.0)
            hi, lo = split(acc)
            hi_out[r : r + 64, :] = hi
            lo_out[r : r + 64, :] = lo

    for move in moves[3:]:
        move.wait()
    padded[...] = jnp.zeros_like(padded)
    for matrix, hi_out, lo_out in ((self_mob, sh_out, sl_out), (near_mat, nh_out, nl_out)):
        for c in range(3):
            for d in range(3):
                padded[c * s.step : c * s.step + s.blobs, d * s.step : d * s.step + s.blobs] = matrix[
                    c * s.blobs : (c + 1) * s.blobs, d * s.blobs : (d + 1) * s.blobs
                ]
        hi, lo = split(padded[...])
        hi_out[...] = hi
        lo_out[...] = lo

    loc, gat = local_part(f, s, rot, (sh_out[...], sl_out[...]), (oh_out[...], ol_out[...]))
    loc_out[...] = loc
    gat_out[...] = gat

    n = s.skel
    z = ids[1]
    halves = []
    spot = lax.broadcasted_iota(jnp.int32, (2 * n, n), 0)
    for level in range(s.levels):
        kept = jnp.where(perm[level : level + 1, :n] == spot, 1.0, 0.0)
        moved = jnp.where(perm[level : level + 1, n:] == spot, 1.0, 0.0).astype(bf16)
        hi, lo = split(interp[level])
        up = kept + (mm(moved, hi) + mm(moved, lo))
        ups_ref[level] = up
        uh_out[level], ul_out[level] = split(up)
        bh_out[level], bl_out[level] = split(sibling[level])
        bit = (z >> level) & 1
        halves.append(
            [ups_ref[level, pl.ds(pl.multiple_of(side * n, 8), n), :] for side in (bit, 1 - bit)]
        )

    def down(block, level, dot):
        return product(dot, split(halves[level][0]), split(block))

    spread = root[...]
    rh_out[...], rl_out[...] = split(spread)
    beside = []
    for level in reversed(range(s.levels)):
        spread = down(spread, level, mt if level == s.levels - 1 else mm)
        beside = [(down(block, level, mt if fresh else mm), False) for block, fresh in beside]
        beside.append((sibling[level], True))
    beside = [block.T if fresh else block for block, fresh in reversed(beside)]
    leaves = [[spread]]
    for level in reversed(range(s.levels)):
        leaves = expand_once(leaves, halves[level])
        leaves.append([beside[level]])
    far_leaves, *sub = leaves
    near_leaves = [jnp.zeros((n, n), f32)]
    for blocks in reversed(sub):
        near_leaves += blocks
    tail = n - LANES
    far_ref[...] = jnp.zeros_like(far_ref)
    own = [a - b for a, b in zip(near_leaves, far_leaves)]
    for group, blocks in enumerate((own, far_leaves)):
        for leaf, block in enumerate(blocks):
            at = (group * s.far_tiles + leaf) * LANES
            far_ref[:, at : at + LANES] = block[:, :LANES]
            at = (group * s.far_tiles + s.nz + leaf // 2) * LANES + leaf % 2 * RIM
            far_ref[:, at : at + tail] = block[:, LANES:]
    fh_out[...], fl_out[...] = split(far_ref[...])


def half_kernel(s, *refs):
    *messages, _, out = refs
    acc = messages[0][s.half :, :]
    for message in messages[1:]:
        acc = acc + message[s.half :, :]
    out[...] = acc


def layer_kernel(s, count, message, *refs):
    sums, around, out = refs[:count], refs[count:-2], refs[-1]
    acc = sums[0][...]
    for part in sums[1:]:
        acc = acc + part[...]
    out[0] = message[s.half :, :]
    out[1] = acc
    for index, other in enumerate(around):
        out[2 + index] = other[s.half :, :]


def join_kernel(x, y, out):
    out[: x.shape[0]] = x[...]
    out[x.shape[0] :] = y[...]


def layer_row(s, tiles):
    row = list(tiles)
    lane = lax.broadcasted_iota(jnp.int32, (8, LANES), 1)
    for leaf in range(0, s.nz, 2):
        pair = tiles[leaf]
        if leaf + 1 < s.nz:
            pair = jnp.where(lane < RIM, pair, pltpu.roll(tiles[leaf + 1], RIM, 1))
        row.append(pltpu.roll(pair, 4, 0))
    return jnp.concatenate(row, axis=1)


def far_potentials(s, layers, far_op):
    own = [layer_row(s, [layer[k] for layer in layers]) for k in range(len(layers[0]))]
    wide = own[0].shape[1]
    hi, lo = far_op
    whole = product(mt, split(own.pop(1)), (hi[:, wide:], lo[:, wide:]))
    boxes = product(mt, split(jnp.concatenate(own, axis=0)), (hi[:, :wide], lo[:, :wide]))
    return [boxes[8 * k : 8 * k + 8] + whole for k in range(len(own))]


def pick(potential, onehot):
    high, _ = split(potential)
    mid, low = split(potential - high.astype(f32))
    parts = [x.astype(f32) for x in (high, mid, low)]
    picked = mm(jnp.concatenate(parts, axis=0).astype(bf16), onehot)
    n = potential.shape[0]
    return picked[:n] + (picked[n : 2 * n] + picked[2 * n :])


def place_kernel(s, cells, tiles, own_out, rims_out):
    own_out[...] = occupancy(cells[0], s)
    lane = lax.broadcasted_iota(jnp.int32, (8, LANES), 1)
    place = lax.broadcasted_iota(jnp.int32, (s.skel, LANES), 0).astype(f32)
    count = len(s.sources)
    for i in range(0, count, 2):
        last = min(i + 1, count - 1)
        pair = jnp.where(lane < RIM, tiles[2 + i], pltpu.roll(tiles[2 + last], RIM, 1))
        rims_out[i // 2] = jnp.where(pair[3:4] == place, 1.0, 0.0).astype(bf16)


def rim_values(s, potentials, onehots):
    lane = lax.broadcasted_iota(jnp.int32, (8, LANES), 1)
    count = len(potentials) - 1
    out = []
    for i in range(0, count, 2):
        last = min(i + 1, count - 1)
        both = pick(jnp.concatenate([potentials[1 + i], potentials[1 + last]], axis=0), onehots[i // 2])
        out.append(jnp.where(lane < RIM, both[:8], both[8:]))
    return out


def gather_kernel(s, gat, gh, gl, *refs):
    *messages, _, hi_out, lo_out = refs
    rims = unpack_rims([message[: s.half, :] for message in messages], s)
    gathered = gat[...] + product(mm, split(rims), (gh[...], gl[...]))
    hi_out[...], lo_out[...] = split(gathered)


def gather_far_kernel(s, gat, gh, gl, col, values, *refs):
    *messages, hi_out, lo_out = refs
    rims = unpack_rims([message[...] for message in messages], s)
    far = []
    for c in range(3):
        value = jnp.concatenate([values[i, c : c + 1, :] for i in range(values.shape[0])], axis=1)
        far.append(col[:, :1] * value)
    rims = rims + stacked(far, s)
    gathered = gat[...] + product(mm, split(rims), (gh[...], gl[...]))
    hi_out[...], lo_out[...] = split(gathered)


def near_kernel(s, loc, nh, nl, hi, lo, out, rim_out):
    part = loc[...] + product(mm, (nh[...], nl[...]), (hi[...], lo[...]))
    out[...] = part
    rim_out[...] = pack_rim(part, s)


def first_kernel(s, part, fh, fl, own, rims, col, *refs):
    *layers, u_out, charges_out, values_out = refs
    count = 2 + len(s.sources)
    layers = [[part[at + k] for k in range(count)] for part in layers for at in range(0, part.shape[0], count)]
    weight_col = col[:, :1]
    occ = own[...]
    potentials = far_potentials(s, layers, (fh[...], fl[...]))
    values = pick(potentials[0], occ)
    u = part[...] + stacked([weight_col * values[c : c + 1] for c in range(3)], s)
    u_out[...] = u
    charges_out[...] = pack_charges(pieces(u, s), weight_col, occ, s)
    for index, value in enumerate(rim_values(s, potentials, rims)):
        values_out[index] = value


def order_kernel(x, _, out):
    out[...] = x[...]


def safe_inverse(x):
    return jnp.where(x > 0.0, 1.0 / jnp.where(x > 0.0, x, 1.0), 0.0)


def middle_kernel(s, u_in, f_in, rot, sh, sl, oh, ol, loc_out, gat_out, ortho_out, stat_out):
    u, f = u_in[...], f_in[...]
    loc, gat = local_part(u, s, rot[...], (sh[...], sl[...]), (oh[...], ol[...]))
    loc_out[...] = loc
    gat_out[...] = gat
    ff = total(f * f)
    fu = total(f * u) * safe_inverse(ff)
    ortho = u - fu * f
    ortho_out[...] = ortho
    oo = total(ortho * ortho)
    stat_out[...] = jnp.broadcast_to(
        jnp.concatenate([ff, fu, oo, jnp.zeros((5, 1), f32)], axis=0), (8, LANES)
    )


def second_kernel(
    s, loc, nh, nl, hi, lo, cells, col, f_in, ortho_in, stat, charges_f, charges_u, packed_out
):
    part = loc[...] + product(mm, (nh[...], nl[...]), (hi[...], lo[...]))
    f, ortho = f_in[...], ortho_in[...]
    ff, fu, oo = (stat[i : i + 1, :1] for i in range(3))
    fa = total(f * part) * safe_inverse(ff)
    oa = total(ortho * part) * safe_inverse(oo)
    rest = part - fa * f - oa * ortho
    aa = total(rest * rest)
    rf, ro = jnp.sqrt(ff), jnp.sqrt(oo)
    of_f = charges_f[-8:, :]
    of_u = charges_u[...]
    of_a = pack_charges(pieces(rest, s), col[:, :1], occupancy(cells[0], s), s, count=True)
    row = lax.broadcasted_iota(jnp.int32, (8, LANES), 0)
    lane = lax.broadcasted_iota(jnp.int32, (8, LANES), 1)
    left = lane < RIM
    first = jnp.where(left, of_u, pltpu.roll(of_a, RIM, 1))
    first = jnp.where(row < 4, of_u, first)
    first = jnp.where((row == 7) & left, pltpu.roll(of_f, 1, 0), first)
    for index, value in enumerate((rf, rf * fu, ro, rf * fa, ro * oa, aa)):
        first = jnp.where((row == 3) & (lane == index), value, first)
    tails = jnp.where(left, pltpu.roll(of_f, 3, 0), pltpu.roll(pltpu.roll(of_f, 2, 0), RIM, 1))
    second = jnp.where(row < 3, of_f, of_a)
    second = jnp.where(row < 4, second, pltpu.roll(of_a, 4, 0))
    second = jnp.where(row == 7, tails, second)
    for device in range(s.devices):
        packed_out[device] = second if s.odd(device) else first


def tree(s, leaves, ups, siblings, root):
    def apply(dot, blocks, factor):
        rows = blocks[0].shape[0]
        out = product(dot, split(jnp.concatenate(blocks, axis=0)), factor)
        return [out[i * rows : (i + 1) * rows] for i in range(len(blocks))]

    n = s.skel
    halves = [[(hi[level, j * n : (j + 1) * n, :], lo[level, j * n : (j + 1) * n, :]) for j in range(2)]
              for level, (hi, lo) in ((k, ups) for k in range(s.levels))]
    charges = [leaves]
    for level in range(s.levels):
        low, high = (apply(mm, charges[-1][j::2], halves[level][j]) for j in range(2))
        charges.append([a + b for a, b in zip(low, high)])
    own = charges[-1][0]
    whole = own[:8]
    for at in range(8, own.shape[0], 8):
        whole = whole + own[at : at + 8]
    whole = whole + pltpu.roll(whole, 4, 0)
    others = jnp.concatenate([whole] * (own.shape[0] // 8), axis=0) - own
    potential = apply(mm, [others], root)
    for level in reversed(range(s.levels)):
        beside = apply(mm, charges[level], (siblings[0][level], siblings[1][level]))
        down = [apply(mt, potential, halves[level][j]) for j in range(2)]
        potential = [
            down[z % 2][z // 2] + beside[z ^ 1] for z in range(len(charges[level]))
        ]
    return potential


def box_numbers(s, firsts, seconds, ups, siblings, root):
    columns = s.nx * s.ny
    row = lax.broadcasted_iota(jnp.int32, (8, LANES), 0)
    lane = lax.broadcasted_iota(jnp.int32, (8, LANES), 1)
    left, valid = lane < RIM, row < 3
    leaves = []
    for z in range(s.nz):
        wide = []
        for column in range(0, columns, 2):
            a, b = firsts[column * s.nz + z], firsts[(column + 1) * s.nz + z]
            main = jnp.where(row < 4, a, pltpu.roll(b, 4, 0))
            tail = jnp.where(row < 4, pltpu.roll(a, 4, 0), b)
            wide.append(jnp.concatenate([main, tail], axis=1)[:, : s.skel])
        leaves.append(jnp.concatenate(wide, axis=0))
    potential = tree(s, leaves, ups, siblings, root)
    out = []
    for start in range(0, s.devices, 8):
        sums = [jnp.zeros((8, LANES), f32) for _ in range(5)]
        for box in range(start, min(s.devices, start + 8)):
            column, z = box // s.nz, box % s.nz
            at = 8 * (column // 2)
            phi = potential[z][at : at + 8]
            main, tail = phi[:, :LANES], phi[:, LANES:]
            tail = jnp.concatenate([tail, tail], axis=1)
            if column % 2:
                main, tail = pltpu.roll(main, 4, 0), pltpu.roll(tail, 4, 0)
            first, second = firsts[box], seconds[box]
            both = pltpu.roll(first, 4, 0) * tail
            of_f = jnp.where(row == 0, pltpu.roll(second, 1, 0), jnp.where(row == 1, pltpu.roll(second, 2, 0), pltpu.roll(first, 3, 0)))
            of_f = jnp.where(left == (row != 1), of_f * tail, 0.0)
            count = jnp.broadcast_to(second[3:4], (8, LANES))
            count_tail = jnp.where(left, 0.0, jnp.broadcast_to(first[7:8], (8, LANES)))
            terms = (
                second * main + of_f,
                first * main + jnp.where(left, both, 0.0),
                pltpu.roll(second, 4, 0) * main + jnp.where(left, 0.0, both),
                count * (main * main) + count_tail * (tail * tail),
            )
            here = row == box - start
            for index, term in enumerate(terms):
                value = jnp.sum(jnp.where(valid, term, 0.0), axis=0, keepdims=True)
                sums[index] = jnp.where(here, value, sums[index])
            sums[4] = jnp.where(here, first[3:4], sums[4])
        numbers = sums[4]
        for index in range(4):
            numbers = jnp.where(lane == 6 + index, jnp.sum(sums[index], axis=1, keepdims=True), numbers)
        out.append(numbers)
    rest = round_up(s.devices, LANES) - 8 * len(out)
    if rest:
        out.append(jnp.zeros((rest, LANES), f32))
    return jnp.concatenate(out, axis=0)


def finish_kernel(s, ids, f_in, u_in, mine, other, col, uh, ul, bh, bl, rh, rl, x_out, lsq_out, raw, sem):
    odd = (ids[0] // s.ny) % 2 == 1
    firsts = [jnp.where(odd, other[box], mine[box]) for box in range(s.devices)]
    seconds = [jnp.where(odd, mine[box], other[box]) for box in range(s.devices)]
    rows = box_numbers(s, firsts, seconds, (uh, ul), (bh, bl), (rh[...], rl[...])).T
    f1, u1, u2, t1, t2, aa, far_f, far_u, far_a, far_far = (rows[i : i + 1] for i in range(10))
    by_f = safe_inverse(f1)
    by_o = jnp.where(u2 * u2 > 1e-10 * (u1 * u1), safe_inverse(u2), 0.0)
    on_one = far_f * by_f
    on_two = (far_u - u1 * by_f * far_f) * by_o
    weight = jnp.sum(col[:, :1] * col[:, :1], axis=0, keepdims=True)
    t3 = aa + 2.0 * far_a + weight * far_far - on_one * on_one - on_two * on_two
    t1, t2, t3 = t1 + on_one, t2 + on_two, jnp.sqrt(jnp.maximum(t3, 0.0))

    def along(x):
        return jnp.sum(x, axis=1, keepdims=True)

    beta = jnp.sqrt(along(f1 * f1) + epsilon)
    v = f1 / beta
    w1, w2 = u1 / beta, u2 / beta
    h11 = along(w1 * v)
    r1 = w1 - h11 * v
    h21 = jnp.sqrt(along(r1 * r1 + w2 * w2) + epsilon)
    b1, b2 = r1 / h21, w2 / h21
    z1, z2, z3 = ((t1 / beta - h11 * w1) / h21, (t2 / beta - h11 * w2) / h21, t3 / beta / h21)
    h12 = along(z1 * v)
    h22 = along(z1 * b1 + z2 * b2)
    d1, d2 = z1 - h12 * v - h22 * b1, z2 - h22 * b2
    h32 = jnp.sqrt(along(d1 * d1 + d2 * d2 + z3 * z3) + epsilon)
    first_norm = jnp.sqrt(h11 * h11 + h21 * h21)
    c1, s1 = h11 / first_norm, h21 / first_norm
    t12, t22 = c1 * h12 + s1 * h22, c1 * h22 - s1 * h12
    second_norm = jnp.sqrt(t22 * t22 + h32 * h32)
    c2, s2 = t22 / second_norm, h32 / second_norm
    g2 = -s1 * beta
    y2 = c2 * g2 / second_norm
    y1 = (c1 * beta - t12 * y2) / first_norm
    lsq_out[...] = jnp.abs(s2 * g2)
    on_u = y2 / h21 / beta
    on_f = y1 / beta - on_u * h11
    moves = []
    for c in range(3):
        part = slice(c * s.step, c * s.step + s.blobs)
        raw[c * s.blobs : (c + 1) * s.blobs, 0, :] = on_f * f_in[part, :] + on_u * u_in[part, :]
        rows = pl.ds(c * s.blobs, s.blobs)
        moves.append(pltpu.make_async_copy(raw.at[rows], x_out.at[rows], sem.at[c]))
        moves[-1].start()
    for move in moves:
        move.wait()


def call(kernel, outs, args, scalars=0, far_args=0, far_outs=0, scratch=(), flops=0):
    vmem = pl.BlockSpec(memory_space=pltpu.VMEM)
    smem = pl.BlockSpec(memory_space=pltpu.SMEM)
    hbm = pl.BlockSpec(memory_space=pltpu.HBM)
    near_args = len(args) - far_args
    args = args[:near_args] + [pltpu.with_memory_space_constraint(x, pltpu.HBM) for x in args[near_args:]]
    return pl.pallas_call(
        kernel,
        out_shape=[jax.ShapeDtypeStruct(shape, kind) for shape, kind in outs],
        in_specs=[smem] * scalars + [vmem] * (near_args - scalars) + [hbm] * far_args,
        out_specs=[hbm] * far_outs + [vmem] * (len(outs) - far_outs),
        scratch_shapes=list(scratch),
        compiler_params=pltpu.CompilerParams(vmem_limit_bytes=16 * 2**20),
        cost_estimate=pl.CostEstimate(flops=flops, bytes_accessed=2**20, transcendentals=0),
    )(*args)


def body(
    mesh_shape, rhs, angles, self_mob, near_mat, near_weight, neighbours, cells, blob_weight,
    skel_perm, interp, sibling_ops, root_op,
):
    s = Sizes(mesh_shape, rhs, skel_perm)
    full = (s.rows, s.bodies)
    square = (s.rows, s.rows)
    tile = (8, LANES)
    far_shape = (s.skel, 2 * s.far_tiles * LANES)
    column = lax.axis_index("gx") * s.ny + lax.axis_index("gy")
    ids = jnp.stack([column, lax.axis_index("gz")]).astype(jnp.int32)

    def fetch(x, kind, dy):
        pairs = []
        for gx in range(s.nx):
            for gy in range(s.ny):
                pairs.append((s.beside(kind, gx) * s.ny + (gy + dy) % s.ny, gx * s.ny + gy))
        return lax.ppermute(x, ("gx", "gy"), pairs)

    def fetch_layers(x):
        parts, sent = [x], [x]
        for level in range(s.levels):
            pairs = [(z ^ (1 << level), z) for z in range(s.nz)]
            parts.append(lax.ppermute(sent[-1], "gz", pairs))
            if level + 1 < s.levels:
                shape = (2 * sent[-1].shape[0],) + tile
                sent += call(join_kernel, [(shape, f32)], [sent[-1], parts[-1]])
        return parts, sent[-1]

    def fetch_rims(rim, after=None):
        got = {}
        for dy in s.shifts:
            got["other", dy] = fetch(rim, "other", dy)
        for dy in s.shifts:
            got["same", dy] = fetch(rim, "same", dy)
        if after is not None:
            (rim,) = call(order_kernel, [(rim.shape, f32)], [rim, after])
        got["other", 0] = fetch(rim, "other", 0)
        got["partner", 0] = fetch(rim, "partner", 0)
        return got

    def forward_rims(got, after):
        for dy in s.shifts:
            held = got["same", dy]
            (held,) = call(order_kernel, [(held.shape, f32)], [held, after])
            got["partner", dy] = fetch(held, "partner", 0)

    def plane_sum(message, got, after):
        if not s.direct:
            return [lax.psum(message[s.half :], ("gx", "gy"))]
        quarter = [message] + [got[key] for key in s.sources if key[0] != "partner"]
        (half,) = call(functools.partial(half_kernel, s), [(tile, f32)], quarter + [after])
        return [half, fetch(half, "partner", 0)]

    flat = (3 * s.blobs, 1, s.bodies)
    small = (1, s.blobs)
    message, col, cells, f = call(
        functools.partial(start_kernel, s),
        [((s.message, LANES), f32), ((s.step, LANES), f32), (cells.shape, jnp.int32), (full, f32)],
        [rhs.reshape(flat), cells, blob_weight.reshape(small)],
        far_args=3,
        scratch=[pltpu.VMEM(flat, f32), pltpu.VMEM(small, f32), pltpu.SemaphoreType.DMA((3,))],
        flops=10**7,
    )
    got = fetch_rims(message)
    operators = [
        angles.reshape(3, 1, s.bodies), near_weight, neighbours, self_mob, near_mat, skel_perm, interp,
        sibling_ops, root_op,
    ]
    loc, gat, rot, sh, sl, nh, nl, oh, ol, gh, gl, fh, fl, *operators_out = call(
        functools.partial(setup_kernel, s),
        [(full, f32), (full, f32), ((16, s.bodies), f32)]
        + [(square, bf16)] * 4
        + [((s.bodies, s.bodies), bf16)] * 2
        + [((s.ghosts, s.bodies), bf16)] * 2
        + [(far_shape, bf16)] * 2
        + [((s.levels, 2 * s.skel, s.skel), bf16)] * 2
        + [((s.levels, s.skel, s.skel), bf16)] * 2
        + [((s.skel, s.skel), bf16)] * 2,
        [ids, f] + operators,
        scalars=1,
        far_args=len(operators),
        scratch=[
            pltpu.VMEM(square, f32), pltpu.VMEM((s.levels, 2 * s.skel, s.skel), f32), pltpu.VMEM(far_shape, f32)
        ]
        + [pltpu.VMEM(x.shape, x.dtype) for x in operators]
        + [pltpu.SemaphoreType.DMA((len(operators),))],
        flops=5 * 10**9,
    )
    forward_rims(got, rot)
    sums = plane_sum(message, got, rot)
    around = [got[key] for key in s.sources]
    gathered = call(
        functools.partial(gather_kernel, s),
        [(full, bf16), (full, bf16)],
        [gat, gh, gl] + around + [sums[0]],
        flops=10**9,
    )
    part, rim = call(
        functools.partial(near_kernel, s),
        [(full, f32), ((s.half, LANES), f32)],
        [loc, nh, nl, *gathered],
        flops=10**9,
    )
    (tiles,) = call(
        functools.partial(layer_kernel, s, len(sums)),
        [((2 + len(around),) + tile, f32)],
        [message] + sums + around + [gathered[1]],
    )
    layers, joined = fetch_layers(tiles)
    got = fetch_rims(rim, joined)
    places = call(
        functools.partial(place_kernel, s),
        [((s.skel, s.bodies), bf16), ((s.ghosts // LANES, s.skel, LANES), bf16)],
        [cells, tiles],
        flops=2 * 10**10,
    )
    u, charges, values = call(
        functools.partial(first_kernel, s),
        [(full, f32), (tile, f32), ((s.ghosts // LANES,) + tile, f32)],
        [part, fh, fl, *places, col, *layers],
        flops=10**8,
    )
    loc, gat, ortho, stat = call(
        functools.partial(middle_kernel, s),
        [(full, f32), (full, f32), (full, f32), (tile, f32)],
        [u, f, rot, sh, sl, oh, ol],
        flops=10**9,
    )
    forward_rims(got, charges)
    gathered = call(
        functools.partial(gather_far_kernel, s),
        [(full, bf16), (full, bf16)],
        [gat, gh, gl, col, values] + [got[key] for key in s.sources],
        flops=10**9,
    )
    (packed,) = call(
        functools.partial(second_kernel, s),
        [((s.devices, 8, LANES), f32)],
        [loc, nh, nl, *gathered, cells, col, f, ortho, stat, message, charges],
        flops=10**9,
    )
    boxes = lax.all_to_all(packed, ("gx", "gy", "gz"), 0, 0)
    result, lsq = call(
        functools.partial(finish_kernel, s),
        [(flat, f32), ((1, 1), f32)],
        [ids, f, u, boxes, fetch(boxes, "partner", 0), col, *operators_out],
        scalars=1,
        far_outs=1,
        scratch=[pltpu.VMEM(flat, f32), pltpu.SemaphoreType.DMA((3,))],
        flops=10**7,
    )
    return result.reshape(rhs.shape), lsq.reshape(())


def solution(mesh):
    in_specs = (
        P("gx", "gy", None, None, "gz"),
        P("gx", "gy", None, "gz"),
        P(),
        P(),
        P("gx", "gy", None, "gz"),
        P("gx", "gy", None, "gz"),
        P("gx", "gy", "gz"),
        P(),
        P(),
        P(),
        P(),
        P(),
    )
    out_specs = (P("gx", "gy", None, None, "gz"), P())
    inner = functools.partial(body, dict(mesh.shape))
    return jax.shard_map(inner, mesh=mesh, in_specs=in_specs, out_specs=out_specs, check_vma=False)
```

```python
import functools

import jax
import jax.numpy as jnp
from jax import lax
from jax.experimental import pallas as pl
from jax.experimental.pallas import tpu as pltpu
from jax.sharding import PartitionSpec as P

epsilon = 1e-06
f32 = jnp.float32
bf16 = jnp.bfloat16
RIM = 64
LANES = 128


def round_up(value, unit):
    return -(-value // unit) * unit


def split(x):
    hi = x.astype(bf16)
    lo = (x - hi.astype(f32)).astype(bf16)
    return hi, lo


def mm(a, b):
    return lax.dot_general(a, b, (((1,), (0,)), ((), ())), preferred_element_type=f32)


def mt(a, b):
    return lax.dot_general(a, b, (((1,), (1,)), ((), ())), preferred_element_type=f32)


def product(dot, a, b):
    return dot(a[0], b[0]) + (dot(a[0], b[1]) + dot(a[1], b[0]))


def total(x):
    return jnp.sum(jnp.sum(x, axis=0, keepdims=True), axis=1, keepdims=True)


class Sizes:
    def __init__(self, mesh_shape, rhs, skel_perm):
        self.nx, self.ny, self.nz = (mesh_shape[a] for a in ("gx", "gy", "gz"))
        self.devices = self.nx * self.ny * self.nz
        self.blobs, self.bodies = rhs.shape[-2:]
        self.step = round_up(self.blobs, 8)
        self.rows = round_up(3 * self.step, 16)
        self.half = self.rows // 2
        self.message = self.half + 8
        self.direct = (self.nx, self.ny) == (4, 2)
        self.levels = skel_perm.shape[0]
        self.skel = skel_perm.shape[1] // 2
        shifts = sorted({(dy % self.ny) for dy in (-1, 1)} - {0})
        self.shifts = shifts
        self.sources = [("same", dy) for dy in shifts]
        for kind in ("other", "partner"):
            self.sources += [(kind, dy) for dy in [0] + shifts]
        self.ghosts = round_up(len(self.sources) * RIM, LANES)
        self.far_tiles = self.nz + -(-self.nz // 2)

    def slot_start(self, slot, parity):
        dx, dy = slot // 3 - 1, (slot % 3 - 1) % self.ny
        kind = "same" if dx == 0 else "partner" if dx == 1 - 2 * parity else "other"
        if (kind, dy) == ("same", 0):
            return 0
        return self.bodies + RIM * self.sources.index((kind, dy))

    def odd(self, device):
        return (device // (self.ny * self.nz)) % 2

    def beside(self, kind, x):
        if kind == "same":
            return x
        if kind == "partner":
            return x ^ 1
        return (x + 2 * (x % 2) - 1) % self.nx


def pieces(x, s):
    return [x[c * s.step : c * s.step + s.step] for c in range(3)]


def turn(parts, rot, inverse):
    out = []
    for target in range(3):
        acc = None
        for source in range(3):
            row = 3 * source + target if inverse else 3 * target + source
            term = rot[row : row + 1] * parts[source]
            acc = term if acc is None else acc + term
        out.append(acc)
    return out


def stacked(parts, s):
    rest = s.rows - 3 * s.step
    if rest:
        parts = list(parts) + [jnp.zeros((rest, parts[0].shape[1]), f32)]
    return jnp.concatenate(parts, axis=0)


def occupancy(cells, s):
    row = lax.broadcasted_iota(jnp.int32, (s.skel, s.bodies), 0)
    return jnp.where(cells == row, 1.0, 0.0).astype(bf16)


def pack_charges(parts, weight_col, occ, s, count=False):
    moments = [jnp.sum(part * weight_col, axis=0, keepdims=True) for part in parts]
    moments.append(jnp.full((1, s.bodies), 1.0 if count else 0.0, f32))
    moments = jnp.concatenate(moments + [jnp.zeros((4, s.bodies), f32)], axis=0)
    high, rest = split(moments)
    mid, low = split(moments - high.astype(f32))
    stack = jnp.concatenate([high.astype(f32), mid.astype(f32), low.astype(f32)], axis=0).astype(bf16)
    sums = mt(stack, occ)
    charges = sums[0:8] + (sums[8:16] + sums[16:24])
    tail = jnp.concatenate([charges[:, LANES:], jnp.zeros((8, 2 * LANES - s.skel), f32)], axis=1)
    row = lax.broadcasted_iota(jnp.int32, (8, LANES), 0)
    return jnp.where(row < 4, charges[:, :LANES], pltpu.roll(tail, 4, 0))


def pack_rim(x, s):
    lane = lax.broadcasted_iota(jnp.int32, (s.half, LANES), 1)
    top, bottom = x[: s.half, :LANES], x[s.half :, :LANES]
    return jnp.where(lane < RIM, top, pltpu.roll(bottom, RIM, 1))


def unpack_rims(rims, s):
    lane = lax.broadcasted_iota(jnp.int32, (s.half, LANES), 1)
    tops, bottoms = [], []
    for i in range(0, s.ghosts // RIM, 2):
        a = rims[i]
        b = rims[i + 1] if i + 1 < len(rims) else jnp.zeros_like(a)
        tops.append(jnp.where(lane < RIM, a, pltpu.roll(b, RIM, 1)))
        bottoms.append(jnp.where(lane < RIM, pltpu.roll(a, RIM, 1), b))
    return jnp.concatenate(
        [jnp.concatenate(tops, axis=1), jnp.concatenate(bottoms, axis=1)], axis=0
    )


def pack_message(x, weight_col, cells, s):
    charges = pack_charges(pieces(x, s), weight_col, occupancy(cells, s), s)
    row = lax.broadcasted_iota(jnp.int32, (8, LANES), 0)
    charges = jnp.where(row == 3, cells[:, :LANES].astype(f32), charges)
    return jnp.concatenate([pack_rim(x, s), charges], axis=0)


def begin(sources, targets, sems):
    moves = [pltpu.make_async_copy(a, b, sems.at[i]) for i, (a, b) in enumerate(zip(sources, targets))]
    for move in moves:
        move.start()
    return moves


def start_kernel(s, rhs, cells, weight, message_out, col_out, cells_out, f_out, raw, wide, sems):
    moves = begin((weight, cells, rhs), (wide, cells_out, raw), sems)
    f_out[...] = jnp.zeros_like(f_out)
    moves[0].wait()
    row = jnp.concatenate([wide[...], jnp.zeros((1, 2 * LANES - s.blobs), f32)], axis=1)
    col = jnp.broadcast_to(row, (LANES, 2 * LANES)).T[: s.step]
    col_out[...] = col
    for move in moves[1:]:
        move.wait()
    for c in range(3):
        f_out[c * s.step : c * s.step + s.blobs, :] = raw[c * s.blobs : (c + 1) * s.blobs, 0, :]
    message_out[...] = pack_message(f_out[...], col[:, :1], cells_out[0], s)


def frame_rows(angles):
    cos, sin = jnp.cos(angles), jnp.sin(angles)
    cy, cp, cr = cos[0:1], cos[1:2], cos[2:3]
    sy, sp, sr = sin[0:1], sin[1:2], sin[2:3]
    return [
        cy * cp,
        cy * sp * sr - sy * cr,
        cy * sp * cr + sy * sr,
        sy * cp,
        sy * sp * sr + cy * cr,
        sy * sp * cr - cy * sr,
        -sp,
        cp * sr,
        cp * cr,
    ]


def local_part(f, s, rot, mob, own):
    parts = pieces(f, s)
    turned = stacked(turn(parts, rot, False), s)
    mixed = product(mm, mob, split(turned))
    back = turn(pieces(mixed, s), rot, True)
    return f + stacked(back, s), product(mm, split(f), own)


def product_many(dot, blocks, b):
    rows = blocks[0].shape[0]
    out = product(dot, split(jnp.concatenate(blocks, axis=0)), split(b))
    return [out[i * rows : (i + 1) * rows] for i in range(len(blocks))]


def expand_once(groups, halves):
    flat = [block for group in groups for block in group]
    sides = [product_many(mt, flat, half) for half in halves]
    out, at = [], 0
    for group in groups:
        spread = []
        for i in range(at, at + len(group)):
            spread += [sides[0][i], sides[1][i]]
        at += len(group)
        out.append(spread)
    return out


def setup_kernel(
    s, ids, f_in, *refs
):
    count = 9
    sources, refs = refs[:count], refs[count:]
    copies, refs = refs[-1 - count :], refs[: -1 - count]
    copies, sems = copies[:-1], copies[-1]
    setup(s, ids, f_in, begin(sources, copies, sems), *copies, *refs)


def setup(
    s, ids, f_in, moves, angles, near_weight, neighbours, self_mob, near_mat, perm, interp, sibling, root,
    loc_out, gat_out, rot_out, sh_out, sl_out, nh_out, nl_out, oh_out, ol_out, gh_out, gl_out,
    fh_out, fl_out, uh_out, ul_out, bh_out, bl_out, rh_out, rl_out, padded, ups_ref, far_ref,
):
    f = f_in[...]
    for move in moves[:3]:
        move.wait()
    rot = jnp.concatenate(frame_rows(angles[:, 0, :]) + [jnp.zeros((7, s.bodies), f32)], axis=0)
    rot_out[...] = rot

    links = neighbours[0, 0]
    slot = links // s.bodies
    base = jnp.zeros_like(links)
    odd = (ids[0] // s.ny) % 2
    for index in range(9):
        start = jnp.where(odd == 1, s.slot_start(index, 1), s.slot_start(index, 0))
        base = jnp.where(slot == index, start, base)
    column = base + links % s.bodies
    coef = near_weight[0, 0]
    for first, count, hi_out, lo_out in (
        (0, s.bodies, oh_out, ol_out),
        (s.bodies, s.ghosts, gh_out, gl_out),
    ):
        for r in range(0, count, 64):
            row = lax.broadcasted_iota(jnp.int32, (64, s.bodies), 0) + (first + r)
            acc = jnp.zeros((64, s.bodies), f32)
            for k in range(coef.shape[0]):
                acc = acc + jnp.where(column[k : k + 1] == row, coef[k : k + 1], 0.0)
            hi, lo = split(acc)
            hi_out[r : r + 64, :] = hi
            lo_out[r : r + 64, :] = lo

    for move in moves[3:]:
        move.wait()
    padded[...] = jnp.zeros_like(padded)
    for matrix, hi_out, lo_out in ((self_mob, sh_out, sl_out), (near_mat, nh_out, nl_out)):
        for c in range(3):
            for d in range(3):
                padded[c * s.step : c * s.step + s.blobs, d * s.step : d * s.step + s.blobs] = matrix[
                    c * s.blobs : (c + 1) * s.blobs, d * s.blobs : (d + 1) * s.blobs
                ]
        hi, lo = split(padded[...])
        hi_out[...] = hi
        lo_out[...] = lo

    loc, gat = local_part(f, s, rot, (sh_out[...], sl_out[...]), (oh_out[...], ol_out[...]))
    loc_out[...] = loc
    gat_out[...] = gat

    n = s.skel
    z = ids[1]
    halves = []
    spot = lax.broadcasted_iota(jnp.int32, (2 * n, n), 0)
    for level in range(s.levels):
        kept = jnp.where(perm[level : level + 1, :n] == spot, 1.0, 0.0)
        moved = jnp.where(perm[level : level + 1, n:] == spot, 1.0, 0.0).astype(bf16)
        hi, lo = split(interp[level])
        up = kept + (mm(moved, hi) + mm(moved, lo))
        ups_ref[level] = up
        uh_out[level], ul_out[level] = split(up)
        bh_out[level], bl_out[level] = split(sibling[level])
        bit = (z >> level) & 1
        halves.append(
            [ups_ref[level, pl.ds(pl.multiple_of(side * n, 8), n), :] for side in (bit, 1 - bit)]
        )

    def down(block, level, dot):
        return product(dot, split(halves[level][0]), split(block))

    spread = root[...]
    rh_out[...], rl_out[...] = split(spread)
    beside = []
    for level in reversed(range(s.levels)):
        spread = down(spread, level, mt if level == s.levels - 1 else mm)
        beside = [(down(block, level, mt if fresh else mm), False) for block, fresh in beside]
        beside.append((sibling[level], True))
    beside = [block.T if fresh else block for block, fresh in reversed(beside)]
    leaves = [[spread]]
    for level in reversed(range(s.levels)):
        leaves = expand_once(leaves, halves[level])
        leaves.append([beside[level]])
    far_leaves, *sub = leaves
    near_leaves = [jnp.zeros((n, n), f32)]
    for blocks in reversed(sub):
        near_leaves += blocks
    tail = n - LANES
    far_ref[...] = jnp.zeros_like(far_ref)
    own = [a - b for a, b in zip(near_leaves, far_leaves)]
    for group, blocks in enumerate((own, far_leaves)):
        for leaf, block in enumerate(blocks):
            at = (group * s.far_tiles + leaf) * LANES
            far_ref[:, at : at + LANES] = block[:, :LANES]
            at = (group * s.far_tiles + s.nz + leaf // 2) * LANES + leaf % 2 * RIM
            far_ref[:, at : at + tail] = block[:, LANES:]
    fh_out[...], fl_out[...] = split(far_ref[...])


def half_kernel(s, *refs):
    *messages, _, out = refs
    acc = messages[0][s.half :, :]
    for message in messages[1:]:
        acc = acc + message[s.half :, :]
    out[...] = acc


def layer_kernel(s, count, message, *refs):
    sums, around, out = refs[:count], refs[count:-2], refs[-1]
    acc = sums[0][...]
    for part in sums[1:]:
        acc = acc + part[...]
    out[0] = message[s.half :, :]
    out[1] = acc
    for index, other in enumerate(around):
        out[2 + index] = other[s.half :, :]


def join_kernel(x, y, out):
    out[: x.shape[0]] = x[...]
    out[x.shape[0] :] = y[...]


def layer_row(s, tiles):
    row = list(tiles)
    lane = lax.broadcasted_iota(jnp.int32, (8, LANES), 1)
    for leaf in range(0, s.nz, 2):
        pair = tiles[leaf]
        if leaf + 1 < s.nz:
            pair = jnp.where(lane < RIM, pair, pltpu.roll(tiles[leaf + 1], RIM, 1))
        row.append(pltpu.roll(pair, 4, 0))
    return jnp.concatenate(row, axis=1)


def far_potentials(s, layers, far_op):
    own = [layer_row(s, [layer[k] for layer in layers]) for k in range(len(layers[0]))]
    wide = own[0].shape[1]
    hi, lo = far_op
    whole = product(mt, split(own.pop(1)), (hi[:, wide:], lo[:, wide:]))
    boxes = product(mt, split(jnp.concatenate(own, axis=0)), (hi[:, :wide], lo[:, :wide]))
    return [boxes[8 * k : 8 * k + 8] + whole for k in range(len(own))]


def pick(potential, onehot):
    high, _ = split(potential)
    mid, low = split(potential - high.astype(f32))
    parts = [x.astype(f32) for x in (high, mid, low)]
    picked = mm(jnp.concatenate(parts, axis=0).astype(bf16), onehot)
    n = potential.shape[0]
    return picked[:n] + (picked[n : 2 * n] + picked[2 * n :])


def place_kernel(s, cells, tiles, own_out, rims_out):
    own_out[...] = occupancy(cells[0], s)
    lane = lax.broadcasted_iota(jnp.int32, (8, LANES), 1)
    place = lax.broadcasted_iota(jnp.int32, (s.skel, LANES), 0).astype(f32)
    count = len(s.sources)
    for i in range(0, count, 2):
        last = min(i + 1, count - 1)
        pair = jnp.where(lane < RIM, tiles[2 + i], pltpu.roll(tiles[2 + last], RIM, 1))
        rims_out[i // 2] = jnp.where(pair[3:4] == place, 1.0, 0.0).astype(bf16)


def rim_values(s, potentials, onehots):
    lane = lax.broadcasted_iota(jnp.int32, (8, LANES), 1)
    count = len(potentials) - 1
    out = []
    for i in range(0, count, 2):
        last = min(i + 1, count - 1)
        both = pick(jnp.concatenate([potentials[1 + i], potentials[1 + last]], axis=0), onehots[i // 2])
        out.append(jnp.where(lane < RIM, both[:8], both[8:]))
    return out


def gather_kernel(s, gat, gh, gl, *refs):
    *messages, _, hi_out, lo_out = refs
    rims = unpack_rims([message[: s.half, :] for message in messages], s)
    gathered = gat[...] + product(mm, split(rims), (gh[...], gl[...]))
    hi_out[...], lo_out[...] = split(gathered)


def gather_far(s, gat, ghost, col, values, messages):
    rims = unpack_rims([message[...] for message in messages], s)
    far = []
    for c in range(3):
        value = jnp.concatenate([values[i, c : c + 1, :] for i in range(values.shape[0])], axis=1)
        far.append(col[:, :1] * value)
    return gat[...] + product(mm, split(rims + stacked(far, s)), ghost)


def near_kernel(s, loc, nh, nl, hi, lo, out, rim_out):
    part = loc[...] + product(mm, (nh[...], nl[...]), (hi[...], lo[...]))
    out[...] = part
    rim_out[...] = pack_rim(part, s)


def first_kernel(s, part, fh, fl, own, rims, col, f_in, rot, sh, sl, oh, ol, *refs):
    *layers, u_out, charges_out, values_out, loc_out, gat_out, ortho_out, stat_out = refs
    count = 2 + len(s.sources)
    layers = [[part[at + k] for k in range(count)] for part in layers for at in range(0, part.shape[0], count)]
    weight_col = col[:, :1]
    occ = own[...]
    potentials = far_potentials(s, layers, (fh[...], fl[...]))
    values = pick(potentials[0], occ)
    u = part[...] + stacked([weight_col * values[c : c + 1] for c in range(3)], s)
    u_out[...] = u
    charges_out[...] = pack_charges(pieces(u, s), weight_col, occ, s)
    for index, value in enumerate(rim_values(s, potentials, rims)):
        values_out[index] = value
    f = f_in[...]
    loc, gat = local_part(u, s, rot[...], (sh[...], sl[...]), (oh[...], ol[...]))
    loc_out[...] = loc
    gat_out[...] = gat
    ff = total(f * f)
    fu = total(f * u) * safe_inverse(ff)
    ortho = u - fu * f
    ortho_out[...] = ortho
    oo = total(ortho * ortho)
    stat_out[...] = jnp.broadcast_to(
        jnp.concatenate([ff, fu, oo, jnp.zeros((5, 1), f32)], axis=0), (8, LANES)
    )


def order_kernel(x, _, out):
    out[...] = x[...]


def safe_inverse(x):
    return jnp.where(x > 0.0, 1.0 / jnp.where(x > 0.0, x, 1.0), 0.0)


def second_kernel(
    s, loc, gat, nh, nl, gh, gl, cells, col, f_in, ortho_in, stat, charges_f, charges_u, values, *refs
):
    *messages, packed_out = refs
    gathered = gather_far(s, gat, (gh[...], gl[...]), col, values, messages)
    part = loc[...] + product(mm, (nh[...], nl[...]), split(gathered))
    f, ortho = f_in[...], ortho_in[...]
    ff, fu, oo = (stat[i : i + 1, :1] for i in range(3))
    fa = total(f * part) * safe_inverse(ff)
    oa = total(ortho * part) * safe_inverse(oo)
    rest = part - fa * f - oa * ortho
    aa = total(rest * rest)
    rf, ro = jnp.sqrt(ff), jnp.sqrt(oo)
    of_f = charges_f[-8:, :]
    of_u = charges_u[...]
    of_a = pack_charges(pieces(rest, s), col[:, :1], occupancy(cells[0], s), s, count=True)
    row = lax.broadcasted_iota(jnp.int32, (8, LANES), 0)
    lane = lax.broadcasted_iota(jnp.int32, (8, LANES), 1)
    left = lane < RIM
    first = jnp.where(left, of_u, pltpu.roll(of_a, RIM, 1))
    first = jnp.where(row < 4, of_u, first)
    first = jnp.where((row == 7) & left, pltpu.roll(of_f, 1, 0), first)
    for index, value in enumerate((rf, rf * fu, ro, rf * fa, ro * oa, aa)):
        first = jnp.where((row == 3) & (lane == index), value, first)
    tails = jnp.where(left, pltpu.roll(of_f, 3, 0), pltpu.roll(pltpu.roll(of_f, 2, 0), RIM, 1))
    second = jnp.where(row < 3, of_f, of_a)
    second = jnp.where(row < 4, second, pltpu.roll(of_a, 4, 0))
    second = jnp.where(row == 7, tails, second)
    for device in range(s.devices):
        packed_out[device] = second if s.odd(device) else first


def tree(s, leaves, ups, siblings, root):
    def apply(dot, blocks, factor):
        rows = blocks[0].shape[0]
        out = product(dot, split(jnp.concatenate(blocks, axis=0)), factor)
        return [out[i * rows : (i + 1) * rows] for i in range(len(blocks))]

    n = s.skel
    halves = [[(hi[level, j * n : (j + 1) * n, :], lo[level, j * n : (j + 1) * n, :]) for j in range(2)]
              for level, (hi, lo) in ((k, ups) for k in range(s.levels))]
    charges = [leaves]
    for level in range(s.levels):
        low, high = (apply(mm, charges[-1][j::2], halves[level][j]) for j in range(2))
        charges.append([a + b for a, b in zip(low, high)])
    own = charges[-1][0]
    whole = own[:8]
    for at in range(8, own.shape[0], 8):
        whole = whole + own[at : at + 8]
    whole = whole + pltpu.roll(whole, 4, 0)
    others = jnp.concatenate([whole] * (own.shape[0] // 8), axis=0) - own
    potential = apply(mm, [others], root)
    for level in reversed(range(s.levels)):
        beside = apply(mm, charges[level], (siblings[0][level], siblings[1][level]))
        down = [apply(mt, potential, halves[level][j]) for j in range(2)]
        potential = [
            down[z % 2][z // 2] + beside[z ^ 1] for z in range(len(charges[level]))
        ]
    return potential


def box_numbers(s, firsts, seconds, ups, siblings, root):
    columns = s.nx * s.ny
    row = lax.broadcasted_iota(jnp.int32, (8, LANES), 0)
    lane = lax.broadcasted_iota(jnp.int32, (8, LANES), 1)
    left, valid = lane < RIM, row < 3
    leaves = []
    for z in range(s.nz):
        wide = []
        for column in range(0, columns, 2):
            a, b = firsts[column * s.nz + z], firsts[(column + 1) * s.nz + z]
            main = jnp.where(row < 4, a, pltpu.roll(b, 4, 0))
            tail = jnp.where(row < 4, pltpu.roll(a, 4, 0), b)
            wide.append(jnp.concatenate([main, tail], axis=1)[:, : s.skel])
        leaves.append(jnp.concatenate(wide, axis=0))
    potential = tree(s, leaves, ups, siblings, root)
    out = []
    for start in range(0, s.devices, 8):
        sums = [jnp.zeros((8, LANES), f32) for _ in range(5)]
        for box in range(start, min(s.devices, start + 8)):
            column, z = box // s.nz, box % s.nz
            at = 8 * (column // 2)
            phi = potential[z][at : at + 8]
            main, tail = phi[:, :LANES], phi[:, LANES:]
            tail = jnp.concatenate([tail, tail], axis=1)
            if column % 2:
                main, tail = pltpu.roll(main, 4, 0), pltpu.roll(tail, 4, 0)
            first, second = firsts[box], seconds[box]
            both = pltpu.roll(first, 4, 0) * tail
            of_f = jnp.where(row == 0, pltpu.roll(second, 1, 0), jnp.where(row == 1, pltpu.roll(second, 2, 0), pltpu.roll(first, 3, 0)))
            of_f = jnp.where(left == (row != 1), of_f * tail, 0.0)
            count = jnp.broadcast_to(second[3:4], (8, LANES))
            count_tail = jnp.where(left, 0.0, jnp.broadcast_to(first[7:8], (8, LANES)))
            terms = (
                second * main + of_f,
                first * main + jnp.where(left, both, 0.0),
                pltpu.roll(second, 4, 0) * main + jnp.where(left, 0.0, both),
                count * (main * main) + count_tail * (tail * tail),
            )
            here = row == box - start
            for index, term in enumerate(terms):
                value = jnp.sum(jnp.where(valid, term, 0.0), axis=0, keepdims=True)
                sums[index] = jnp.where(here, value, sums[index])
            sums[4] = jnp.where(here, first[3:4], sums[4])
        numbers = sums[4]
        for index in range(4):
            numbers = jnp.where(lane == 6 + index, jnp.sum(sums[index], axis=1, keepdims=True), numbers)
        out.append(numbers)
    rest = round_up(s.devices, LANES) - 8 * len(out)
    if rest:
        out.append(jnp.zeros((rest, LANES), f32))
    return jnp.concatenate(out, axis=0)


def finish_kernel(s, ids, f_in, u_in, mine, other, col, uh, ul, bh, bl, rh, rl, x_out, lsq_out, raw, sem):
    odd = (ids[0] // s.ny) % 2 == 1
    firsts = [jnp.where(odd, other[box], mine[box]) for box in range(s.devices)]
    seconds = [jnp.where(odd, mine[box], other[box]) for box in range(s.devices)]
    rows = box_numbers(s, firsts, seconds, (uh, ul), (bh, bl), (rh[...], rl[...])).T
    f1, u1, u2, t1, t2, aa, far_f, far_u, far_a, far_far = (rows[i : i + 1] for i in range(10))
    by_f = safe_inverse(f1)
    by_o = jnp.where(u2 * u2 > 1e-10 * (u1 * u1), safe_inverse(u2), 0.0)
    on_one = far_f * by_f
    on_two = (far_u - u1 * by_f * far_f) * by_o
    weight = jnp.sum(col[:, :1] * col[:, :1], axis=0, keepdims=True)
    t3 = aa + 2.0 * far_a + weight * far_far - on_one * on_one - on_two * on_two
    t1, t2, t3 = t1 + on_one, t2 + on_two, jnp.sqrt(jnp.maximum(t3, 0.0))

    def along(x):
        return jnp.sum(x, axis=1, keepdims=True)

    beta = jnp.sqrt(along(f1 * f1) + epsilon)
    v = f1 / beta
    w1, w2 = u1 / beta, u2 / beta
    h11 = along(w1 * v)
    r1 = w1 - h11 * v
    h21 = jnp.sqrt(along(r1 * r1 + w2 * w2) + epsilon)
    b1, b2 = r1 / h21, w2 / h21
    z1, z2, z3 = ((t1 / beta - h11 * w1) / h21, (t2 / beta - h11 * w2) / h21, t3 / beta / h21)
    h12 = along(z1 * v)
    h22 = along(z1 * b1 + z2 * b2)
    d1, d2 = z1 - h12 * v - h22 * b1, z2 - h22 * b2
    h32 = jnp.sqrt(along(d1 * d1 + d2 * d2 + z3 * z3) + epsilon)
    first_norm = jnp.sqrt(h11 * h11 + h21 * h21)
    c1, s1 = h11 / first_norm, h21 / first_norm
    t12, t22 = c1 * h12 + s1 * h22, c1 * h22 - s1 * h12
    second_norm = jnp.sqrt(t22 * t22 + h32 * h32)
    c2, s2 = t22 / second_norm, h32 / second_norm
    g2 = -s1 * beta
    y2 = c2 * g2 / second_norm
    y1 = (c1 * beta - t12 * y2) / first_norm
    lsq_out[...] = jnp.abs(s2 * g2)
    on_u = y2 / h21 / beta
    on_f = y1 / beta - on_u * h11
    moves = []
    for c in range(3):
        part = slice(c * s.step, c * s.step + s.blobs)
        raw[c * s.blobs : (c + 1) * s.blobs, 0, :] = on_f * f_in[part, :] + on_u * u_in[part, :]
        rows = pl.ds(c * s.blobs, s.blobs)
        moves.append(pltpu.make_async_copy(raw.at[rows], x_out.at[rows], sem.at[c]))
        moves[-1].start()
    for move in moves:
        move.wait()


def call(kernel, outs, args, scalars=0, far_args=0, far_outs=0, scratch=(), flops=0):
    vmem = pl.BlockSpec(memory_space=pltpu.VMEM)
    smem = pl.BlockSpec(memory_space=pltpu.SMEM)
    hbm = pl.BlockSpec(memory_space=pltpu.HBM)
    near_args = len(args) - far_args
    args = args[:near_args] + [pltpu.with_memory_space_constraint(x, pltpu.HBM) for x in args[near_args:]]
    return pl.pallas_call(
        kernel,
        out_shape=[jax.ShapeDtypeStruct(shape, kind) for shape, kind in outs],
        in_specs=[smem] * scalars + [vmem] * (near_args - scalars) + [hbm] * far_args,
        out_specs=[hbm] * far_outs + [vmem] * (len(outs) - far_outs),
        scratch_shapes=list(scratch),
        compiler_params=pltpu.CompilerParams(vmem_limit_bytes=16 * 2**20),
        cost_estimate=pl.CostEstimate(flops=flops, bytes_accessed=2**20, transcendentals=0),
    )(*args)


def body(
    mesh_shape, rhs, angles, self_mob, near_mat, near_weight, neighbours, cells, blob_weight,
    skel_perm, interp, sibling_ops, root_op,
):
    s = Sizes(mesh_shape, rhs, skel_perm)
    full = (s.rows, s.bodies)
    square = (s.rows, s.rows)
    tile = (8, LANES)
    far_shape = (s.skel, 2 * s.far_tiles * LANES)
    column = lax.axis_index("gx") * s.ny + lax.axis_index("gy")
    ids = jnp.stack([column, lax.axis_index("gz")]).astype(jnp.int32)

    def fetch(x, kind, dy):
        pairs = []
        for gx in range(s.nx):
            for gy in range(s.ny):
                pairs.append((s.beside(kind, gx) * s.ny + (gy + dy) % s.ny, gx * s.ny + gy))
        return lax.ppermute(x, ("gx", "gy"), pairs)

    def fetch_layers(x):
        parts, sent = [x], [x]
        for level in range(s.levels):
            pairs = [(z ^ (1 << level), z) for z in range(s.nz)]
            parts.append(lax.ppermute(sent[-1], "gz", pairs))
            if level + 1 < s.levels:
                shape = (2 * sent[-1].shape[0],) + tile
                sent += call(join_kernel, [(shape, f32)], [sent[-1], parts[-1]])
        return parts, sent[-1]

    def fetch_rims(rim, after=None):
        got = {}
        for dy in s.shifts:
            got["other", dy] = fetch(rim, "other", dy)
        for dy in s.shifts:
            got["same", dy] = fetch(rim, "same", dy)
        if after is not None:
            (rim,) = call(order_kernel, [(rim.shape, f32)], [rim, after])
        got["other", 0] = fetch(rim, "other", 0)
        got["partner", 0] = fetch(rim, "partner", 0)
        return got

    def forward_rims(got, after):
        for dy in s.shifts:
            held = got["same", dy]
            (held,) = call(order_kernel, [(held.shape, f32)], [held, after])
            got["partner", dy] = fetch(held, "partner", 0)

    def plane_sum(message, got, after):
        if not s.direct:
            return [lax.psum(message[s.half :], ("gx", "gy"))]
        quarter = [message] + [got[key] for key in s.sources if key[0] != "partner"]
        (half,) = call(functools.partial(half_kernel, s), [(tile, f32)], quarter + [after])
        return [half, fetch(half, "partner", 0)]

    flat = (3 * s.blobs, 1, s.bodies)
    small = (1, s.blobs)
    message, col, cells, f = call(
        functools.partial(start_kernel, s),
        [((s.message, LANES), f32), ((s.step, LANES), f32), (cells.shape, jnp.int32), (full, f32)],
        [rhs.reshape(flat), cells, blob_weight.reshape(small)],
        far_args=3,
        scratch=[pltpu.VMEM(flat, f32), pltpu.VMEM(small, f32), pltpu.SemaphoreType.DMA((3,))],
        flops=10**7,
    )
    got = fetch_rims(message)
    operators = [
        angles.reshape(3, 1, s.bodies), near_weight, neighbours, self_mob, near_mat, skel_perm, interp,
        sibling_ops, root_op,
    ]
    loc, gat, rot, sh, sl, nh, nl, oh, ol, gh, gl, fh, fl, *operators_out = call(
        functools.partial(setup_kernel, s),
        [(full, f32), (full, f32), ((16, s.bodies), f32)]
        + [(square, bf16)] * 4
        + [((s.bodies, s.bodies), bf16)] * 2
        + [((s.ghosts, s.bodies), bf16)] * 2
        + [(far_shape, bf16)] * 2
        + [((s.levels, 2 * s.skel, s.skel), bf16)] * 2
        + [((s.levels, s.skel, s.skel), bf16)] * 2
        + [((s.skel, s.skel), bf16)] * 2,
        [ids, f] + operators,
        scalars=1,
        far_args=len(operators),
        scratch=[
            pltpu.VMEM(square, f32), pltpu.VMEM((s.levels, 2 * s.skel, s.skel), f32), pltpu.VMEM(far_shape, f32)
        ]
        + [pltpu.VMEM(x.shape, x.dtype) for x in operators]
        + [pltpu.SemaphoreType.DMA((len(operators),))],
        flops=5 * 10**9,
    )
    forward_rims(got, rot)
    sums = plane_sum(message, got, rot)
    around = [got[key] for key in s.sources]
    gathered = call(
        functools.partial(gather_kernel, s),
        [(full, bf16), (full, bf16)],
        [gat, gh, gl] + around + [sums[0]],
        flops=10**9,
    )
    part, rim = call(
        functools.partial(near_kernel, s),
        [(full, f32), ((s.half, LANES), f32)],
        [loc, nh, nl, *gathered],
        flops=10**9,
    )
    (tiles,) = call(
        functools.partial(layer_kernel, s, len(sums)),
        [((2 + len(around),) + tile, f32)],
        [message] + sums + around + [gathered[1]],
    )
    layers, joined = fetch_layers(tiles)
    got = fetch_rims(rim, joined)
    places = call(
        functools.partial(place_kernel, s),
        [((s.skel, s.bodies), bf16), ((s.ghosts // LANES, s.skel, LANES), bf16)],
        [cells, tiles],
        flops=2 * 10**10,
    )
    u, charges, values, loc, gat, ortho, stat = call(
        functools.partial(first_kernel, s),
        [(full, f32), (tile, f32), ((s.ghosts // LANES,) + tile, f32)] + [(full, f32)] * 3 + [(tile, f32)],
        [part, fh, fl, *places, col, f, rot, sh, sl, oh, ol, *layers],
        flops=10**9,
    )
    forward_rims(got, places[1])
    (packed,) = call(
        functools.partial(second_kernel, s),
        [((s.devices, 8, LANES), f32)],
        [loc, gat, nh, nl, gh, gl, cells, col, f, ortho, stat, message, charges, values]
        + [got[key] for key in s.sources],
        flops=10**9,
    )
    boxes = lax.all_to_all(packed, ("gx", "gy", "gz"), 0, 0)
    result, lsq = call(
        functools.partial(finish_kernel, s),
        [(flat, f32), ((1, 1), f32)],
        [ids, f, u, boxes, fetch(boxes, "partner", 0), col, *operators_out],
        scalars=1,
        far_outs=1,
        scratch=[pltpu.VMEM(flat, f32), pltpu.SemaphoreType.DMA((3,))],
        flops=10**7,
    )
    return result.reshape(rhs.shape), lsq.reshape(())


def solution(mesh):
    in_specs = (
        P("gx", "gy", None, None, "gz"),
        P("gx", "gy", None, "gz"),
        P(),
        P(),
        P("gx", "gy", None, "gz"),
        P("gx", "gy", None, "gz"),
        P("gx", "gy", "gz"),
        P(),
        P(),
        P(),
        P(),
        P(),
    )
    out_specs = (P("gx", "gy", None, None, "gz"), P())
    inner = functools.partial(body, dict(mesh.shape))
    return jax.shard_map(inner, mesh=mesh, in_specs=in_specs, out_specs=out_specs, check_vma=False)
```

```python
import functools

import jax
import jax.numpy as jnp
from jax import lax
from jax.experimental import pallas as pl
from jax.experimental.pallas import tpu as pltpu
from jax.sharding import PartitionSpec as P

epsilon = 1e-06
f32 = jnp.float32
bf16 = jnp.bfloat16
RIM = 64
LANES = 128


def round_up(value, unit):
    return -(-value // unit) * unit


def split(x):
    hi = x.astype(bf16)
    lo = (x - hi.astype(f32)).astype(bf16)
    return hi, lo


def mm(a, b):
    return lax.dot_general(a, b, (((1,), (0,)), ((), ())), preferred_element_type=f32)


def mt(a, b):
    return lax.dot_general(a, b, (((1,), (1,)), ((), ())), preferred_element_type=f32)


def product(dot, a, b):
    return dot(a[0], b[0]) + (dot(a[0], b[1]) + dot(a[1], b[0]))


def total(x):
    return jnp.sum(jnp.sum(x, axis=0, keepdims=True), axis=1, keepdims=True)


class Sizes:
    def __init__(self, mesh_shape, rhs, skel_perm):
        self.nx, self.ny, self.nz = (mesh_shape[a] for a in ("gx", "gy", "gz"))
        self.devices = self.nx * self.ny * self.nz
        self.blobs, self.bodies = rhs.shape[-2:]
        self.step = round_up(self.blobs, 8)
        self.rows = round_up(3 * self.step, 16)
        self.half = self.rows // 2
        self.message = self.half + 8
        self.direct = (self.nx, self.ny) == (4, 2)
        self.levels = skel_perm.shape[0]
        self.skel = skel_perm.shape[1] // 2
        shifts = sorted({(dy % self.ny) for dy in (-1, 1)} - {0})
        self.shifts = shifts
        self.sources = [("same", dy) for dy in shifts]
        for kind in ("other", "partner"):
            self.sources += [(kind, dy) for dy in [0] + shifts]
        self.ghosts = round_up(len(self.sources) * RIM, LANES)
        self.far_tiles = self.nz + -(-self.nz // 2)

    def slot_start(self, slot, parity):
        dx, dy = slot // 3 - 1, (slot % 3 - 1) % self.ny
        kind = "same" if dx == 0 else "partner" if dx == 1 - 2 * parity else "other"
        if (kind, dy) == ("same", 0):
            return 0
        return self.bodies + RIM * self.sources.index((kind, dy))

    def odd(self, device):
        return (device // (self.ny * self.nz)) % 2

    def beside(self, kind, x):
        if kind == "same":
            return x
        if kind == "partner":
            return x ^ 1
        return (x + 2 * (x % 2) - 1) % self.nx


def pieces(x, s):
    return [x[c * s.step : c * s.step + s.step] for c in range(3)]


def turn(parts, rot, inverse):
    out = []
    for target in range(3):
        acc = None
        for source in range(3):
            row = 3 * source + target if inverse else 3 * target + source
            term = rot[row : row + 1] * parts[source]
            acc = term if acc is None else acc + term
        out.append(acc)
    return out


def stacked(parts, s):
    rest = s.rows - 3 * s.step
    if rest:
        parts = list(parts) + [jnp.zeros((rest, parts[0].shape[1]), f32)]
    return jnp.concatenate(parts, axis=0)


def occupancy(cells, s):
    row = lax.broadcasted_iota(jnp.int32, (s.skel, s.bodies), 0)
    return jnp.where(cells == row, 1.0, 0.0).astype(bf16)


def pack_charges(parts, weight_col, occ, s, count=False):
    moments = [jnp.sum(part * weight_col, axis=0, keepdims=True) for part in parts]
    moments.append(jnp.full((1, s.bodies), 1.0 if count else 0.0, f32))
    moments = jnp.concatenate(moments + [jnp.zeros((4, s.bodies), f32)], axis=0)
    high, rest = split(moments)
    mid, low = split(moments - high.astype(f32))
    stack = jnp.concatenate([high.astype(f32), mid.astype(f32), low.astype(f32)], axis=0).astype(bf16)
    sums = mt(stack, occ)
    charges = sums[0:8] + (sums[8:16] + sums[16:24])
    tail = jnp.concatenate([charges[:, LANES:], jnp.zeros((8, 2 * LANES - s.skel), f32)], axis=1)
    row = lax.broadcasted_iota(jnp.int32, (8, LANES), 0)
    return jnp.where(row < 4, charges[:, :LANES], pltpu.roll(tail, 4, 0))


def pack_rim(x, s):
    lane = lax.broadcasted_iota(jnp.int32, (s.half, LANES), 1)
    top, bottom = x[: s.half, :LANES], x[s.half :, :LANES]
    return jnp.where(lane < RIM, top, pltpu.roll(bottom, RIM, 1))


def unpack_rims(rims, s):
    lane = lax.broadcasted_iota(jnp.int32, (s.half, LANES), 1)
    tops, bottoms = [], []
    for i in range(0, s.ghosts // RIM, 2):
        a = rims[i]
        b = rims[i + 1] if i + 1 < len(rims) else jnp.zeros_like(a)
        tops.append(jnp.where(lane < RIM, a, pltpu.roll(b, RIM, 1)))
        bottoms.append(jnp.where(lane < RIM, pltpu.roll(a, RIM, 1), b))
    return jnp.concatenate(
        [jnp.concatenate(tops, axis=1), jnp.concatenate(bottoms, axis=1)], axis=0
    )


def pack_message(x, weight_col, cells, s):
    charges = pack_charges(pieces(x, s), weight_col, occupancy(cells, s), s)
    row = lax.broadcasted_iota(jnp.int32, (8, LANES), 0)
    charges = jnp.where(row == 3, cells[:, :LANES].astype(f32), charges)
    return jnp.concatenate([pack_rim(x, s), charges], axis=0)


def begin(sources, targets, sems):
    moves = [pltpu.make_async_copy(a, b, sems.at[i]) for i, (a, b) in enumerate(zip(sources, targets))]
    for move in moves:
        move.start()
    return moves


def start_kernel(s, rhs, cells, weight, message_out, col_out, cells_out, f_out, raw, wide, sems):
    moves = begin((weight, cells, rhs), (wide, cells_out, raw), sems)
    f_out[...] = jnp.zeros_like(f_out)
    moves[0].wait()
    row = jnp.concatenate([wide[...], jnp.zeros((1, 2 * LANES - s.blobs), f32)], axis=1)
    col = jnp.broadcast_to(row, (LANES, 2 * LANES)).T[: s.step]
    col_out[...] = col
    for move in moves[1:]:
        move.wait()
    for c in range(3):
        f_out[c * s.step : c * s.step + s.blobs, :] = raw[c * s.blobs : (c + 1) * s.blobs, 0, :]
    message_out[...] = pack_message(f_out[...], col[:, :1], cells_out[0], s)


def frame_rows(angles):
    cos, sin = jnp.cos(angles), jnp.sin(angles)
    cy, cp, cr = cos[0:1], cos[1:2], cos[2:3]
    sy, sp, sr = sin[0:1], sin[1:2], sin[2:3]
    return [
        cy * cp,
        cy * sp * sr - sy * cr,
        cy * sp * cr + sy * sr,
        sy * cp,
        sy * sp * sr + cy * cr,
        sy * sp * cr - cy * sr,
        -sp,
        cp * sr,
        cp * cr,
    ]


def local_part(f, s, rot, mob, own):
    parts = pieces(f, s)
    turned = stacked(turn(parts, rot, False), s)
    mixed = product(mm, mob, split(turned))
    back = turn(pieces(mixed, s), rot, True)
    return f + stacked(back, s), product(mm, split(f), own)


def product_many(dot, blocks, b):
    rows = blocks[0].shape[0]
    out = product(dot, split(jnp.concatenate(blocks, axis=0)), split(b))
    return [out[i * rows : (i + 1) * rows] for i in range(len(blocks))]


def expand_once(groups, halves):
    flat = [block for group in groups for block in group]
    sides = [product_many(mt, flat, half) for half in halves]
    out, at = [], 0
    for group in groups:
        spread = []
        for i in range(at, at + len(group)):
            spread += [sides[0][i], sides[1][i]]
        at += len(group)
        out.append(spread)
    return out


def setup_kernel(
    s, ids, f_in, *refs
):
    count = 9
    sources, refs = refs[:count], refs[count:]
    copies, refs = refs[-1 - count :], refs[: -1 - count]
    copies, sems = copies[:-1], copies[-1]
    setup(s, ids, f_in, begin(sources, copies, sems), *copies, *refs)


def setup(
    s, ids, f_in, moves, angles, near_weight, neighbours, self_mob, near_mat, perm, interp, sibling, root,
    loc_out, gat_out, rot_out, sh_out, sl_out, nh_out, nl_out, oh_out, ol_out, gh_out, gl_out,
    fh_out, fl_out, uh_out, ul_out, bh_out, bl_out, rh_out, rl_out, padded, ups_ref, far_ref,
):
    f = f_in[...]
    for move in moves[:3]:
        move.wait()
    rot = jnp.concatenate(frame_rows(angles[:, 0, :]) + [jnp.zeros((7, s.bodies), f32)], axis=0)
    rot_out[...] = rot

    links = neighbours[0, 0]
    slot = links // s.bodies
    base = jnp.zeros_like(links)
    odd = (ids[0] // s.ny) % 2
    for index in range(9):
        start = jnp.where(odd == 1, s.slot_start(index, 1), s.slot_start(index, 0))
        base = jnp.where(slot == index, start, base)
    column = base + links % s.bodies
    coef = near_weight[0, 0]
    for first, count, hi_out, lo_out in (
        (0, s.bodies, oh_out, ol_out),
        (s.bodies, s.ghosts, gh_out, gl_out),
    ):
        for r in range(0, count, 64):
            row = lax.broadcasted_iota(jnp.int32, (64, s.bodies), 0) + (first + r)
            acc = jnp.zeros((64, s.bodies), f32)
            for k in range(coef.shape[0]):
                acc = acc + jnp.where(column[k : k + 1] == row, coef[k : k + 1], 0.0)
            hi, lo = split(acc)
            hi_out[r : r + 64, :] = hi
            lo_out[r : r + 64, :] = lo

    for move in moves[3:]:
        move.wait()
    padded[...] = jnp.zeros_like(padded)
    for matrix, hi_out, lo_out in ((self_mob, sh_out, sl_out), (near_mat, nh_out, nl_out)):
        for c in range(3):
            for d in range(3):
                padded[c * s.step : c * s.step + s.blobs, d * s.step : d * s.step + s.blobs] = matrix[
                    c * s.blobs : (c + 1) * s.blobs, d * s.blobs : (d + 1) * s.blobs
                ]
        hi, lo = split(padded[...])
        hi_out[...] = hi
        lo_out[...] = lo

    loc, gat = local_part(f, s, rot, (sh_out[...], sl_out[...]), (oh_out[...], ol_out[...]))
    loc_out[...] = loc
    gat_out[...] = gat

    n = s.skel
    z = ids[1]
    halves = []
    spot = lax.broadcasted_iota(jnp.int32, (2 * n, n), 0)
    for level in range(s.levels):
        kept = jnp.where(perm[level : level + 1, :n] == spot, 1.0, 0.0)
        moved = jnp.where(perm[level : level + 1, n:] == spot, 1.0, 0.0).astype(bf16)
        hi, lo = split(interp[level])
        up = kept + (mm(moved, hi) + mm(moved, lo))
        ups_ref[level] = up
        uh_out[level], ul_out[level] = split(up)
        bh_out[level], bl_out[level] = split(sibling[level])
        bit = (z >> level) & 1
        halves.append(
            [ups_ref[level, pl.ds(pl.multiple_of(side * n, 8), n), :] for side in (bit, 1 - bit)]
        )

    def down(block, level, dot):
        return product(dot, split(halves[level][0]), split(block))

    spread = root[...]
    rh_out[...], rl_out[...] = split(spread)
    beside = []
    for level in reversed(range(s.levels)):
        spread = down(spread, level, mt if level == s.levels - 1 else mm)
        beside = [(down(block, level, mt if fresh else mm), False) for block, fresh in beside]
        beside.append((sibling[level], True))
    beside = [block.T if fresh else block for block, fresh in reversed(beside)]
    leaves = [[spread]]
    for level in reversed(range(s.levels)):
        leaves = expand_once(leaves, halves[level])
        leaves.append([beside[level]])
    far_leaves, *sub = leaves
    near_leaves = [jnp.zeros((n, n), f32)]
    for blocks in reversed(sub):
        near_leaves += blocks
    tail = n - LANES
    far_ref[...] = jnp.zeros_like(far_ref)
    own = [a - b for a, b in zip(near_leaves, far_leaves)]
    for group, blocks in enumerate((own, far_leaves)):
        for leaf, block in enumerate(blocks):
            at = (group * s.far_tiles + leaf) * LANES
            far_ref[:, at : at + LANES] = block[:, :LANES]
            at = (group * s.far_tiles + s.nz + leaf // 2) * LANES + leaf % 2 * RIM
            far_ref[:, at : at + tail] = block[:, LANES:]
    fh_out[...], fl_out[...] = split(far_ref[...])


def half_kernel(s, *refs):
    *messages, _, out = refs
    acc = messages[0][s.half :, :]
    for message in messages[1:]:
        acc = acc + message[s.half :, :]
    out[...] = acc


def layer_kernel(s, count, message, *refs):
    sums, around, out = refs[:count], refs[count:-2], refs[-1]
    acc = sums[0][...]
    for part in sums[1:]:
        acc = acc + part[...]
    out[0] = message[s.half :, :]
    out[1] = acc
    for index, other in enumerate(around):
        out[2 + index] = other[s.half :, :]


def join_kernel(x, y, out):
    out[: x.shape[0]] = x[...]
    out[x.shape[0] :] = y[...]


def layer_row(s, tiles):
    row = list(tiles)
    lane = lax.broadcasted_iota(jnp.int32, (8, LANES), 1)
    for leaf in range(0, s.nz, 2):
        pair = tiles[leaf]
        if leaf + 1 < s.nz:
            pair = jnp.where(lane < RIM, pair, pltpu.roll(tiles[leaf + 1], RIM, 1))
        row.append(pltpu.roll(pair, 4, 0))
    return jnp.concatenate(row, axis=1)


def far_potentials(s, layers, far_op):
    own = [layer_row(s, [layer[k] for layer in layers]) for k in range(len(layers[0]))]
    wide = own[0].shape[1]
    hi, lo = far_op
    whole = product(mt, split(own.pop(1)), (hi[:, wide:], lo[:, wide:]))
    boxes = product(mt, split(jnp.concatenate(own, axis=0)), (hi[:, :wide], lo[:, :wide]))
    return [boxes[8 * k : 8 * k + 8] + whole for k in range(len(own))]


def pick(potential, onehot):
    high, _ = split(potential)
    mid, low = split(potential - high.astype(f32))
    parts = [x.astype(f32) for x in (high, mid, low)]
    picked = mm(jnp.concatenate(parts, axis=0).astype(bf16), onehot)
    n = potential.shape[0]
    return picked[:n] + (picked[n : 2 * n] + picked[2 * n :])


def place_kernel(s, cells, tiles, own_out, rims_out):
    own_out[...] = occupancy(cells[0], s)
    lane = lax.broadcasted_iota(jnp.int32, (8, LANES), 1)
    place = lax.broadcasted_iota(jnp.int32, (s.skel, LANES), 0).astype(f32)
    count = len(s.sources)
    for i in range(0, count, 2):
        last = min(i + 1, count - 1)
        pair = jnp.where(lane < RIM, tiles[2 + i], pltpu.roll(tiles[2 + last], RIM, 1))
        rims_out[i // 2] = jnp.where(pair[3:4] == place, 1.0, 0.0).astype(bf16)


def rim_values(s, potentials, onehots):
    lane = lax.broadcasted_iota(jnp.int32, (8, LANES), 1)
    count = len(potentials) - 1
    out = []
    for i in range(0, count, 2):
        last = min(i + 1, count - 1)
        both = pick(jnp.concatenate([potentials[1 + i], potentials[1 + last]], axis=0), onehots[i // 2])
        out.append(jnp.where(lane < RIM, both[:8], both[8:]))
    return out


def gather_kernel(s, gat, gh, gl, *refs):
    *messages, _, hi_out, lo_out = refs
    rims = unpack_rims([message[: s.half, :] for message in messages], s)
    gathered = gat[...] + product(mm, split(rims), (gh[...], gl[...]))
    hi_out[...], lo_out[...] = split(gathered)


def gather_far_kernel(s, gat, gh, gl, col, values, *refs):
    *messages, hi_out, lo_out = refs
    rims = unpack_rims([message[...] for message in messages], s)
    far = []
    for c in range(3):
        value = jnp.concatenate([values[i, c : c + 1, :] for i in range(values.shape[0])], axis=1)
        far.append(col[:, :1] * value)
    gathered = gat[...] + product(mm, split(rims + stacked(far, s)), (gh[...], gl[...]))
    hi_out[...], lo_out[...] = split(gathered)


def near_kernel(s, loc, nh, nl, hi, lo, out, rim_out):
    part = loc[...] + product(mm, (nh[...], nl[...]), (hi[...], lo[...]))
    out[...] = part
    rim_out[...] = pack_rim(part, s)


def first_kernel(s, part, fh, fl, own, rims, col, f_in, rot, sh, sl, oh, ol, *refs):
    *layers, u_out, charges_out, values_out, loc_out, gat_out, ortho_out, stat_out = refs
    count = 2 + len(s.sources)
    layers = [[part[at + k] for k in range(count)] for part in layers for at in range(0, part.shape[0], count)]
    weight_col = col[:, :1]
    occ = own[...]
    potentials = far_potentials(s, layers, (fh[...], fl[...]))
    values = pick(potentials[0], occ)
    u = part[...] + stacked([weight_col * values[c : c + 1] for c in range(3)], s)
    u_out[...] = u
    charges_out[...] = pack_charges(pieces(u, s), weight_col, occ, s)
    for index, value in enumerate(rim_values(s, potentials, rims)):
        values_out[index] = value
    f = f_in[...]
    loc, gat = local_part(u, s, rot[...], (sh[...], sl[...]), (oh[...], ol[...]))
    loc_out[...] = loc
    gat_out[...] = gat
    ff = total(f * f)
    fu = total(f * u) * safe_inverse(ff)
    ortho = u - fu * f
    ortho_out[...] = ortho
    oo = total(ortho * ortho)
    stat_out[...] = jnp.broadcast_to(
        jnp.concatenate([ff, fu, oo, jnp.zeros((5, 1), f32)], axis=0), (8, LANES)
    )


def order_kernel(x, _, out):
    out[...] = x[...]


def safe_inverse(x):
    return jnp.where(x > 0.0, 1.0 / jnp.where(x > 0.0, x, 1.0), 0.0)


def second_kernel(
    s, loc, nh, nl, hi, lo, cells, col, f_in, ortho_in, stat, charges_f, charges_u, packed_out
):
    part = loc[...] + product(mm, (nh[...], nl[...]), (hi[...], lo[...]))
    f, ortho = f_in[...], ortho_in[...]
    ff, fu, oo = (stat[i : i + 1, :1] for i in range(3))
    fa = total(f * part) * safe_inverse(ff)
    oa = total(ortho * part) * safe_inverse(oo)
    rest = part - fa * f - oa * ortho
    aa = total(rest * rest)
    rf, ro = jnp.sqrt(ff), jnp.sqrt(oo)
    of_f = charges_f[-8:, :]
    of_u = charges_u[...]
    of_a = pack_charges(pieces(rest, s), col[:, :1], occupancy(cells[0], s), s, count=True)
    row = lax.broadcasted_iota(jnp.int32, (8, LANES), 0)
    lane = lax.broadcasted_iota(jnp.int32, (8, LANES), 1)
    left = lane < RIM
    first = jnp.where(left, of_u, pltpu.roll(of_a, RIM, 1))
    first = jnp.where(row < 4, of_u, first)
    first = jnp.where((row == 7) & left, pltpu.roll(of_f, 1, 0), first)
    for index, value in enumerate((rf, rf * fu, ro, rf * fa, ro * oa, aa)):
        first = jnp.where((row == 3) & (lane == index), value, first)
    tails = jnp.where(left, pltpu.roll(of_f, 3, 0), pltpu.roll(pltpu.roll(of_f, 2, 0), RIM, 1))
    second = jnp.where(row < 3, of_f, of_a)
    second = jnp.where(row < 4, second, pltpu.roll(of_a, 4, 0))
    second = jnp.where(row == 7, tails, second)
    for device in range(s.devices):
        packed_out[device] = second if s.odd(device) else first


def tree(s, leaves, ups, siblings, root):
    def apply(dot, blocks, factor):
        rows = blocks[0].shape[0]
        out = product(dot, split(jnp.concatenate(blocks, axis=0)), factor)
        return [out[i * rows : (i + 1) * rows] for i in range(len(blocks))]

    n = s.skel
    halves = [[(hi[level, j * n : (j + 1) * n, :], lo[level, j * n : (j + 1) * n, :]) for j in range(2)]
              for level, (hi, lo) in ((k, ups) for k in range(s.levels))]
    charges = [leaves]
    for level in range(s.levels):
        low, high = (apply(mm, charges[-1][j::2], halves[level][j]) for j in range(2))
        charges.append([a + b for a, b in zip(low, high)])
    own = charges[-1][0]
    whole = own[:8]
    for at in range(8, own.shape[0], 8):
        whole = whole + own[at : at + 8]
    whole = whole + pltpu.roll(whole, 4, 0)
    others = jnp.concatenate([whole] * (own.shape[0] // 8), axis=0) - own
    potential = apply(mm, [others], root)
    for level in reversed(range(s.levels)):
        beside = apply(mm, charges[level], (siblings[0][level], siblings[1][level]))
        down = [apply(mt, potential, halves[level][j]) for j in range(2)]
        potential = [
            down[z % 2][z // 2] + beside[z ^ 1] for z in range(len(charges[level]))
        ]
    return potential


def box_numbers(s, firsts, seconds, ups, siblings, root):
    columns = s.nx * s.ny
    row = lax.broadcasted_iota(jnp.int32, (8, LANES), 0)
    lane = lax.broadcasted_iota(jnp.int32, (8, LANES), 1)
    left, valid = lane < RIM, row < 3
    leaves = []
    for z in range(s.nz):
        wide = []
        for column in range(0, columns, 2):
            a, b = firsts[column * s.nz + z], firsts[(column + 1) * s.nz + z]
            main = jnp.where(row < 4, a, pltpu.roll(b, 4, 0))
            tail = jnp.where(row < 4, pltpu.roll(a, 4, 0), b)
            wide.append(jnp.concatenate([main, tail], axis=1)[:, : s.skel])
        leaves.append(jnp.concatenate(wide, axis=0))
    potential = tree(s, leaves, ups, siblings, root)
    out = []
    for start in range(0, s.devices, 8):
        sums = [jnp.zeros((8, LANES), f32) for _ in range(5)]
        for box in range(start, min(s.devices, start + 8)):
            column, z = box // s.nz, box % s.nz
            at = 8 * (column // 2)
            phi = potential[z][at : at + 8]
            main, tail = phi[:, :LANES], phi[:, LANES:]
            tail = jnp.concatenate([tail, tail], axis=1)
            if column % 2:
                main, tail = pltpu.roll(main, 4, 0), pltpu.roll(tail, 4, 0)
            first, second = firsts[box], seconds[box]
            both = pltpu.roll(first, 4, 0) * tail
            of_f = jnp.where(row == 0, pltpu.roll(second, 1, 0), jnp.where(row == 1, pltpu.roll(second, 2, 0), pltpu.roll(first, 3, 0)))
            of_f = jnp.where(left == (row != 1), of_f * tail, 0.0)
            count = jnp.broadcast_to(second[3:4], (8, LANES))
            count_tail = jnp.where(left, 0.0, jnp.broadcast_to(first[7:8], (8, LANES)))
            terms = (
                second * main + of_f,
                first * main + jnp.where(left, both, 0.0),
                pltpu.roll(second, 4, 0) * main + jnp.where(left, 0.0, both),
                count * (main * main) + count_tail * (tail * tail),
            )
            here = row == box - start
            for index, term in enumerate(terms):
                value = jnp.sum(jnp.where(valid, term, 0.0), axis=0, keepdims=True)
                sums[index] = jnp.where(here, value, sums[index])
            sums[4] = jnp.where(here, first[3:4], sums[4])
        numbers = sums[4]
        for index in range(4):
            numbers = jnp.where(lane == 6 + index, jnp.sum(sums[index], axis=1, keepdims=True), numbers)
        out.append(numbers)
    rest = round_up(s.devices, LANES) - 8 * len(out)
    if rest:
        out.append(jnp.zeros((rest, LANES), f32))
    return jnp.concatenate(out, axis=0)


def finish_kernel(s, ids, f_in, u_in, mine, other, col, uh, ul, bh, bl, rh, rl, x_out, lsq_out, raw, sem):
    odd = (ids[0] // s.ny) % 2 == 1
    firsts = [jnp.where(odd, other[box], mine[box]) for box in range(s.devices)]
    seconds = [jnp.where(odd, mine[box], other[box]) for box in range(s.devices)]
    rows = box_numbers(s, firsts, seconds, (uh, ul), (bh, bl), (rh[...], rl[...])).T
    f1, u1, u2, t1, t2, aa, far_f, far_u, far_a, far_far = (rows[i : i + 1] for i in range(10))
    by_f = safe_inverse(f1)
    by_o = jnp.where(u2 * u2 > 1e-10 * (u1 * u1), safe_inverse(u2), 0.0)
    on_one = far_f * by_f
    on_two = (far_u - u1 * by_f * far_f) * by_o
    weight = jnp.sum(col[:, :1] * col[:, :1], axis=0, keepdims=True)
    t3 = aa + 2.0 * far_a + weight * far_far - on_one * on_one - on_two * on_two
    t1, t2, t3 = t1 + on_one, t2 + on_two, jnp.sqrt(jnp.maximum(t3, 0.0))

    def along(x):
        return jnp.sum(x, axis=1, keepdims=True)

    beta = jnp.sqrt(along(f1 * f1) + epsilon)
    v = f1 / beta
    w1, w2 = u1 / beta, u2 / beta
    h11 = along(w1 * v)
    r1 = w1 - h11 * v
    h21 = jnp.sqrt(along(r1 * r1 + w2 * w2) + epsilon)
    b1, b2 = r1 / h21, w2 / h21
    z1, z2, z3 = ((t1 / beta - h11 * w1) / h21, (t2 / beta - h11 * w2) / h21, t3 / beta / h21)
    h12 = along(z1 * v)
    h22 = along(z1 * b1 + z2 * b2)
    d1, d2 = z1 - h12 * v - h22 * b1, z2 - h22 * b2
    h32 = jnp.sqrt(along(d1 * d1 + d2 * d2 + z3 * z3) + epsilon)
    first_norm = jnp.sqrt(h11 * h11 + h21 * h21)
    c1, s1 = h11 / first_norm, h21 / first_norm
    t12, t22 = c1 * h12 + s1 * h22, c1 * h22 - s1 * h12
    second_norm = jnp.sqrt(t22 * t22 + h32 * h32)
    c2, s2 = t22 / second_norm, h32 / second_norm
    g2 = -s1 * beta
    y2 = c2 * g2 / second_norm
    y1 = (c1 * beta - t12 * y2) / first_norm
    lsq_out[...] = jnp.abs(s2 * g2)
    on_u = y2 / h21 / beta
    on_f = y1 / beta - on_u * h11
    moves = []
    for c in range(3):
        part = slice(c * s.step, c * s.step + s.blobs)
        raw[c * s.blobs : (c + 1) * s.blobs, 0, :] = on_f * f_in[part, :] + on_u * u_in[part, :]
        rows = pl.ds(c * s.blobs, s.blobs)
        moves.append(pltpu.make_async_copy(raw.at[rows], x_out.at[rows], sem.at[c]))
        moves[-1].start()
    for move in moves:
        move.wait()


def call(kernel, outs, args, scalars=0, far_args=0, far_outs=0, scratch=(), flops=0):
    vmem = pl.BlockSpec(memory_space=pltpu.VMEM)
    smem = pl.BlockSpec(memory_space=pltpu.SMEM)
    hbm = pl.BlockSpec(memory_space=pltpu.HBM)
    near_args = len(args) - far_args
    args = args[:near_args] + [pltpu.with_memory_space_constraint(x, pltpu.HBM) for x in args[near_args:]]
    return pl.pallas_call(
        kernel,
        out_shape=[jax.ShapeDtypeStruct(shape, kind) for shape, kind in outs],
        in_specs=[smem] * scalars + [vmem] * (near_args - scalars) + [hbm] * far_args,
        out_specs=[hbm] * far_outs + [vmem] * (len(outs) - far_outs),
        scratch_shapes=list(scratch),
        compiler_params=pltpu.CompilerParams(vmem_limit_bytes=16 * 2**20),
        cost_estimate=pl.CostEstimate(flops=flops, bytes_accessed=2**20, transcendentals=0),
    )(*args)


def body(
    mesh_shape, rhs, angles, self_mob, near_mat, near_weight, neighbours, cells, blob_weight,
    skel_perm, interp, sibling_ops, root_op,
):
    s = Sizes(mesh_shape, rhs, skel_perm)
    full = (s.rows, s.bodies)
    square = (s.rows, s.rows)
    tile = (8, LANES)
    far_shape = (s.skel, 2 * s.far_tiles * LANES)
    column = lax.axis_index("gx") * s.ny + lax.axis_index("gy")
    ids = jnp.stack([column, lax.axis_index("gz")]).astype(jnp.int32)

    def fetch(x, kind, dy):
        pairs = []
        for gx in range(s.nx):
            for gy in range(s.ny):
                pairs.append((s.beside(kind, gx) * s.ny + (gy + dy) % s.ny, gx * s.ny + gy))
        return lax.ppermute(x, ("gx", "gy"), pairs)

    def fetch_layers(x):
        parts, sent = [x], [x]
        for level in range(s.levels):
            pairs = [(z ^ (1 << level), z) for z in range(s.nz)]
            parts.append(lax.ppermute(sent[-1], "gz", pairs))
            if level + 1 < s.levels:
                shape = (2 * sent[-1].shape[0],) + tile
                sent += call(join_kernel, [(shape, f32)], [sent[-1], parts[-1]])
        return parts, sent[-1]

    def fetch_rims(rim, after=None):
        got = {}
        for dy in s.shifts:
            got["other", dy] = fetch(rim, "other", dy)
        for dy in s.shifts:
            got["same", dy] = fetch(rim, "same", dy)
        if after is not None:
            (rim,) = call(order_kernel, [(rim.shape, f32)], [rim, after])
        got["other", 0] = fetch(rim, "other", 0)
        got["partner", 0] = fetch(rim, "partner", 0)
        return got

    def forward_rims(got, after):
        for dy in s.shifts:
            held = got["same", dy]
            (held,) = call(order_kernel, [(held.shape, f32)], [held, after])
            got["partner", dy] = fetch(held, "partner", 0)

    def plane_sum(message, got, after):
        if not s.direct:
            return [lax.psum(message[s.half :], ("gx", "gy"))]
        quarter = [message] + [got[key] for key in s.sources if key[0] != "partner"]
        (half,) = call(functools.partial(half_kernel, s), [(tile, f32)], quarter + [after])
        return [half, fetch(half, "partner", 0)]

    flat = (3 * s.blobs, 1, s.bodies)
    small = (1, s.blobs)
    message, col, cells, f = call(
        functools.partial(start_kernel, s),
        [((s.message, LANES), f32), ((s.step, LANES), f32), (cells.shape, jnp.int32), (full, f32)],
        [rhs.reshape(flat), cells, blob_weight.reshape(small)],
        far_args=3,
        scratch=[pltpu.VMEM(flat, f32), pltpu.VMEM(small, f32), pltpu.SemaphoreType.DMA((3,))],
        flops=10**7,
    )
    got = fetch_rims(message)
    operators = [
        angles.reshape(3, 1, s.bodies), near_weight, neighbours, self_mob, near_mat, skel_perm, interp,
        sibling_ops, root_op,
    ]
    loc, gat, rot, sh, sl, nh, nl, oh, ol, gh, gl, fh, fl, *operators_out = call(
        functools.partial(setup_kernel, s),
        [(full, f32), (full, f32), ((16, s.bodies), f32)]
        + [(square, bf16)] * 4
        + [((s.bodies, s.bodies), bf16)] * 2
        + [((s.ghosts, s.bodies), bf16)] * 2
        + [(far_shape, bf16)] * 2
        + [((s.levels, 2 * s.skel, s.skel), bf16)] * 2
        + [((s.levels, s.skel, s.skel), bf16)] * 2
        + [((s.skel, s.skel), bf16)] * 2,
        [ids, f] + operators,
        scalars=1,
        far_args=len(operators),
        scratch=[
            pltpu.VMEM(square, f32), pltpu.VMEM((s.levels, 2 * s.skel, s.skel), f32), pltpu.VMEM(far_shape, f32)
        ]
        + [pltpu.VMEM(x.shape, x.dtype) for x in operators]
        + [pltpu.SemaphoreType.DMA((len(operators),))],
        flops=5 * 10**9,
    )
    forward_rims(got, rot)
    sums = plane_sum(message, got, rot)
    around = [got[key] for key in s.sources]
    gathered = call(
        functools.partial(gather_kernel, s),
        [(full, bf16), (full, bf16)],
        [gat, gh, gl] + around + [sums[0]],
        flops=10**9,
    )
    part, rim = call(
        functools.partial(near_kernel, s),
        [(full, f32), ((s.half, LANES), f32)],
        [loc, nh, nl, *gathered],
        flops=10**9,
    )
    (tiles,) = call(
        functools.partial(layer_kernel, s, len(sums)),
        [((2 + len(around),) + tile, f32)],
        [message] + sums + around + [gathered[1]],
    )
    layers, joined = fetch_layers(tiles)
    got = fetch_rims(rim, joined)
    places = call(
        functools.partial(place_kernel, s),
        [((s.skel, s.bodies), bf16), ((s.ghosts // LANES, s.skel, LANES), bf16)],
        [cells, tiles],
        flops=2 * 10**10,
    )
    u, charges, values, loc, gat, ortho, stat = call(
        functools.partial(first_kernel, s),
        [(full, f32), (tile, f32), ((s.ghosts // LANES,) + tile, f32)] + [(full, f32)] * 3 + [(tile, f32)],
        [part, fh, fl, *places, col, f, rot, sh, sl, oh, ol, *layers],
        flops=10**9,
    )
    forward_rims(got, places[1])
    gathered = call(
        functools.partial(gather_far_kernel, s),
        [(full, bf16), (full, bf16)],
        [gat, gh, gl, col, values] + [got[key] for key in s.sources],
        flops=10**9,
    )
    (packed,) = call(
        functools.partial(second_kernel, s),
        [((s.devices, 8, LANES), f32)],
        [loc, nh, nl, *gathered, cells, col, f, ortho, stat, message, charges],
        flops=10**9,
    )
    boxes = lax.all_to_all(packed, ("gx", "gy", "gz"), 0, 0)
    result, lsq = call(
        functools.partial(finish_kernel, s),
        [(flat, f32), ((1, 1), f32)],
        [ids, f, u, boxes, fetch(boxes, "partner", 0), col, *operators_out],
        scalars=1,
        far_outs=1,
        scratch=[pltpu.VMEM(flat, f32), pltpu.SemaphoreType.DMA((3,))],
        flops=10**7,
    )
    return result.reshape(rhs.shape), lsq.reshape(())


def solution(mesh):
    in_specs = (
        P("gx", "gy", None, None, "gz"),
        P("gx", "gy", None, "gz"),
        P(),
        P(),
        P("gx", "gy", None, "gz"),
        P("gx", "gy", None, "gz"),
        P("gx", "gy", "gz"),
        P(),
        P(),
        P(),
        P(),
        P(),
    )
    out_specs = (P("gx", "gy", None, None, "gz"), P())
    inner = functools.partial(body, dict(mesh.shape))
    return jax.shard_map(inner, mesh=mesh, in_specs=in_specs, out_specs=out_specs, check_vma=False)
```

```python
import functools

import jax
import jax.numpy as jnp
from jax import lax
from jax.experimental import pallas as pl
from jax.experimental.pallas import tpu as pltpu
from jax.sharding import PartitionSpec as P

epsilon = 1e-06
f32 = jnp.float32
bf16 = jnp.bfloat16
RIM = 64
LANES = 128


def round_up(value, unit):
    return -(-value // unit) * unit


def split(x):
    hi = x.astype(bf16)
    lo = (x - hi.astype(f32)).astype(bf16)
    return hi, lo


def mm(a, b):
    return lax.dot_general(a, b, (((1,), (0,)), ((), ())), preferred_element_type=f32)


def mt(a, b):
    return lax.dot_general(a, b, (((1,), (1,)), ((), ())), preferred_element_type=f32)


def product(dot, a, b):
    return dot(a[0], b[0]) + (dot(a[0], b[1]) + dot(a[1], b[0]))


def total(x):
    return jnp.sum(jnp.sum(x, axis=0, keepdims=True), axis=1, keepdims=True)


class Sizes:
    def __init__(self, mesh_shape, rhs, skel_perm):
        self.nx, self.ny, self.nz = (mesh_shape[a] for a in ("gx", "gy", "gz"))
        self.devices = self.nx * self.ny * self.nz
        self.blobs, self.bodies = rhs.shape[-2:]
        self.step = round_up(self.blobs, 8)
        self.rows = round_up(3 * self.step, 16)
        self.half = self.rows // 2
        self.message = self.half + 8
        self.direct = (self.nx, self.ny) == (4, 2)
        self.levels = skel_perm.shape[0]
        self.skel = skel_perm.shape[1] // 2
        shifts = sorted({(dy % self.ny) for dy in (-1, 1)} - {0})
        self.shifts = shifts
        self.sources = [("same", dy) for dy in shifts]
        for kind in ("other", "partner"):
            self.sources += [(kind, dy) for dy in [0] + shifts]
        self.ghosts = round_up(len(self.sources) * RIM, LANES)
        self.far_tiles = self.nz + -(-self.nz // 2)

    def slot_start(self, slot, parity):
        dx, dy = slot // 3 - 1, (slot % 3 - 1) % self.ny
        kind = "same" if dx == 0 else "partner" if dx == 1 - 2 * parity else "other"
        if (kind, dy) == ("same", 0):
            return 0
        return self.bodies + RIM * self.sources.index((kind, dy))

    def odd(self, device):
        return (device // (self.ny * self.nz)) % 2

    def beside(self, kind, x):
        if kind == "same":
            return x
        if kind == "partner":
            return x ^ 1
        return (x + 2 * (x % 2) - 1) % self.nx


def pieces(x, s):
    return [x[c * s.step : c * s.step + s.step] for c in range(3)]


def turn(parts, rot, inverse):
    out = []
    for target in range(3):
        acc = None
        for source in range(3):
            row = 3 * source + target if inverse else 3 * target + source
            term = rot[row : row + 1] * parts[source]
            acc = term if acc is None else acc + term
        out.append(acc)
    return out


def stacked(parts, s):
    rest = s.rows - 3 * s.step
    if rest:
        parts = list(parts) + [jnp.zeros((rest, parts[0].shape[1]), f32)]
    return jnp.concatenate(parts, axis=0)


def occupancy(cells, s):
    row = lax.broadcasted_iota(jnp.int32, (s.skel, s.bodies), 0)
    return jnp.where(cells == row, 1.0, 0.0).astype(bf16)


def pack_charges(parts, weight_col, occ, s, count=False):
    moments = [jnp.sum(part * weight_col, axis=0, keepdims=True) for part in parts]
    moments.append(jnp.full((1, s.bodies), 1.0 if count else 0.0, f32))
    moments = jnp.concatenate(moments + [jnp.zeros((4, s.bodies), f32)], axis=0)
    high, rest = split(moments)
    mid, low = split(moments - high.astype(f32))
    stack = jnp.concatenate([high.astype(f32), mid.astype(f32), low.astype(f32)], axis=0).astype(bf16)
    sums = mt(stack, occ)
    charges = sums[0:8] + (sums[8:16] + sums[16:24])
    tail = jnp.concatenate([charges[:, LANES:], jnp.zeros((8, 2 * LANES - s.skel), f32)], axis=1)
    row = lax.broadcasted_iota(jnp.int32, (8, LANES), 0)
    return jnp.where(row < 4, charges[:, :LANES], pltpu.roll(tail, 4, 0))


def pack_rim(x, s):
    lane = lax.broadcasted_iota(jnp.int32, (s.half, LANES), 1)
    top, bottom = x[: s.half, :LANES], x[s.half :, :LANES]
    return jnp.where(lane < RIM, top, pltpu.roll(bottom, RIM, 1))


def unpack_rims(rims, s):
    lane = lax.broadcasted_iota(jnp.int32, (s.half, LANES), 1)
    tops, bottoms = [], []
    for i in range(0, s.ghosts // RIM, 2):
        a = rims[i]
        b = rims[i + 1] if i + 1 < len(rims) else jnp.zeros_like(a)
        tops.append(jnp.where(lane < RIM, a, pltpu.roll(b, RIM, 1)))
        bottoms.append(jnp.where(lane < RIM, pltpu.roll(a, RIM, 1), b))
    return jnp.concatenate(
        [jnp.concatenate(tops, axis=1), jnp.concatenate(bottoms, axis=1)], axis=0
    )


def pack_message(x, weight_col, cells, s):
    charges = pack_charges(pieces(x, s), weight_col, occupancy(cells, s), s)
    row = lax.broadcasted_iota(jnp.int32, (8, LANES), 0)
    charges = jnp.where(row == 3, cells[:, :LANES].astype(f32), charges)
    return jnp.concatenate([pack_rim(x, s), charges], axis=0)


def begin(sources, targets, sems):
    moves = [pltpu.make_async_copy(a, b, sems.at[i]) for i, (a, b) in enumerate(zip(sources, targets))]
    for move in moves:
        move.start()
    return moves


def start_kernel(s, rhs, cells, weight, message_out, col_out, cells_out, f_out, raw, wide, sems):
    moves = begin((weight, cells, rhs), (wide, cells_out, raw), sems)
    f_out[...] = jnp.zeros_like(f_out)
    moves[0].wait()
    row = jnp.concatenate([wide[...], jnp.zeros((1, 2 * LANES - s.blobs), f32)], axis=1)
    col = jnp.broadcast_to(row, (LANES, 2 * LANES)).T[: s.step]
    col_out[...] = col
    for move in moves[1:]:
        move.wait()
    for c in range(3):
        f_out[c * s.step : c * s.step + s.blobs, :] = raw[c * s.blobs : (c + 1) * s.blobs, 0, :]
    message_out[...] = pack_message(f_out[...], col[:, :1], cells_out[0], s)


def frame_rows(angles):
    cos, sin = jnp.cos(angles), jnp.sin(angles)
    cy, cp, cr = cos[0:1], cos[1:2], cos[2:3]
    sy, sp, sr = sin[0:1], sin[1:2], sin[2:3]
    return [
        cy * cp,
        cy * sp * sr - sy * cr,
        cy * sp * cr + sy * sr,
        sy * cp,
        sy * sp * sr + cy * cr,
        sy * sp * cr - cy * sr,
        -sp,
        cp * sr,
        cp * cr,
    ]


def local_part(f, s, rot, mob, own):
    parts = pieces(f, s)
    turned = stacked(turn(parts, rot, False), s)
    mixed = product(mm, mob, split(turned))
    back = turn(pieces(mixed, s), rot, True)
    return f + stacked(back, s), product(mm, split(f), own)


def product_many(dot, blocks, b):
    rows = blocks[0].shape[0]
    out = product(dot, split(jnp.concatenate(blocks, axis=0)), split(b))
    return [out[i * rows : (i + 1) * rows] for i in range(len(blocks))]


def expand_once(groups, halves):
    flat = [block for group in groups for block in group]
    sides = [product_many(mt, flat, half) for half in halves]
    out, at = [], 0
    for group in groups:
        spread = []
        for i in range(at, at + len(group)):
            spread += [sides[0][i], sides[1][i]]
        at += len(group)
        out.append(spread)
    return out


def setup_kernel(
    s, ids, f_in, *refs
):
    count = 9
    sources, refs = refs[:count], refs[count:]
    copies, refs = refs[-1 - count :], refs[: -1 - count]
    copies, sems = copies[:-1], copies[-1]
    setup(s, ids, f_in, begin(sources, copies, sems), *copies, *refs)


def setup(
    s, ids, f_in, moves, angles, near_weight, neighbours, self_mob, near_mat, perm, interp, sibling, root,
    loc_out, gat_out, rot_out, sh_out, sl_out, nh_out, nl_out, oh_out, ol_out, gh_out, gl_out,
    fh_out, fl_out, uh_out, ul_out, bh_out, bl_out, rh_out, rl_out, padded, ups_ref, far_ref,
):
    f = f_in[...]
    for move in moves[:3]:
        move.wait()
    rot = jnp.concatenate(frame_rows(angles[:, 0, :]) + [jnp.zeros((7, s.bodies), f32)], axis=0)
    rot_out[...] = rot

    links = neighbours[0, 0]
    slot = links // s.bodies
    base = jnp.zeros_like(links)
    odd = (ids[0] // s.ny) % 2
    for index in range(9):
        start = jnp.where(odd == 1, s.slot_start(index, 1), s.slot_start(index, 0))
        base = jnp.where(slot == index, start, base)
    column = base + links % s.bodies
    coef = near_weight[0, 0]
    for first, count, hi_out, lo_out in (
        (0, s.bodies, oh_out, ol_out),
        (s.bodies, s.ghosts, gh_out, gl_out),
    ):
        for r in range(0, count, 64):
            row = lax.broadcasted_iota(jnp.int32, (64, s.bodies), 0) + (first + r)
            acc = jnp.zeros((64, s.bodies), f32)
            for k in range(coef.shape[0]):
                acc = acc + jnp.where(column[k : k + 1] == row, coef[k : k + 1], 0.0)
            hi, lo = split(acc)
            hi_out[r : r + 64, :] = hi
            lo_out[r : r + 64, :] = lo

    for move in moves[3:]:
        move.wait()
    padded[...] = jnp.zeros_like(padded)
    for matrix, hi_out, lo_out in ((self_mob, sh_out, sl_out), (near_mat, nh_out, nl_out)):
        for c in range(3):
            for d in range(3):
                padded[c * s.step : c * s.step + s.blobs, d * s.step : d * s.step + s.blobs] = matrix[
                    c * s.blobs : (c + 1) * s.blobs, d * s.blobs : (d + 1) * s.blobs
                ]
        hi, lo = split(padded[...])
        hi_out[...] = hi
        lo_out[...] = lo

    loc, gat = local_part(f, s, rot, (sh_out[...], sl_out[...]), (oh_out[...], ol_out[...]))
    loc_out[...] = loc
    gat_out[...] = gat

    n = s.skel
    z = ids[1]
    halves = []
    spot = lax.broadcasted_iota(jnp.int32, (2 * n, n), 0)
    for level in range(s.levels):
        kept = jnp.where(perm[level : level + 1, :n] == spot, 1.0, 0.0)
        moved = jnp.where(perm[level : level + 1, n:] == spot, 1.0, 0.0).astype(bf16)
        hi, lo = split(interp[level])
        up = kept + (mm(moved, hi) + mm(moved, lo))
        ups_ref[level] = up
        uh_out[level], ul_out[level] = split(up)
        bh_out[level], bl_out[level] = split(sibling[level])
        bit = (z >> level) & 1
        halves.append(
            [ups_ref[level, pl.ds(pl.multiple_of(side * n, 8), n), :] for side in (bit, 1 - bit)]
        )

    def down(block, level, dot):
        return product(dot, split(halves[level][0]), split(block))

    spread = root[...]
    rh_out[...], rl_out[...] = split(spread)
    beside = []
    for level in reversed(range(s.levels)):
        spread = down(spread, level, mt if level == s.levels - 1 else mm)
        beside = [(down(block, level, mt if fresh else mm), False) for block, fresh in beside]
        beside.append((sibling[level], True))
    beside = [block.T if fresh else block for block, fresh in reversed(beside)]
    leaves = [[spread]]
    for level in reversed(range(s.levels)):
        leaves = expand_once(leaves, halves[level])
        leaves.append([beside[level]])
    far_leaves, *sub = leaves
    near_leaves = [jnp.zeros((n, n), f32)]
    for blocks in reversed(sub):
        near_leaves += blocks
    tail = n - LANES
    far_ref[...] = jnp.zeros_like(far_ref)
    own = [a - b for a, b in zip(near_leaves, far_leaves)]
    for group, blocks in enumerate((own, far_leaves)):
        for leaf, block in enumerate(blocks):
            at = (group * s.far_tiles + leaf) * LANES
            far_ref[:, at : at + LANES] = block[:, :LANES]
            at = (group * s.far_tiles + s.nz + leaf // 2) * LANES + leaf % 2 * RIM
            far_ref[:, at : at + tail] = block[:, LANES:]
    fh_out[...], fl_out[...] = split(far_ref[...])


def half_kernel(s, *refs):
    *messages, _, out = refs
    acc = messages[0][s.half :, :]
    for message in messages[1:]:
        acc = acc + message[s.half :, :]
    out[...] = acc


def layer_kernel(s, count, message, *refs):
    sums, around, out = refs[:count], refs[count:-2], refs[-1]
    acc = sums[0][...]
    for part in sums[1:]:
        acc = acc + part[...]
    out[0] = message[s.half :, :]
    out[1] = acc
    for index, other in enumerate(around):
        out[2 + index] = other[s.half :, :]


def join_kernel(x, y, out):
    out[: x.shape[0]] = x[...]
    out[x.shape[0] :] = y[...]


def layer_row(s, tiles):
    row = list(tiles)
    lane = lax.broadcasted_iota(jnp.int32, (8, LANES), 1)
    for leaf in range(0, s.nz, 2):
        pair = tiles[leaf]
        if leaf + 1 < s.nz:
            pair = jnp.where(lane < RIM, pair, pltpu.roll(tiles[leaf + 1], RIM, 1))
        row.append(pltpu.roll(pair, 4, 0))
    return jnp.concatenate(row, axis=1)


def far_potentials(s, layers, far_op):
    own = [layer_row(s, [layer[k] for layer in layers]) for k in range(len(layers[0]))]
    wide = own[0].shape[1]
    hi, lo = far_op
    whole = product(mt, split(own.pop(1)), (hi[:, wide:], lo[:, wide:]))
    boxes = product(mt, split(jnp.concatenate(own, axis=0)), (hi[:, :wide], lo[:, :wide]))
    return [boxes[8 * k : 8 * k + 8] + whole for k in range(len(own))]


def pick(potential, onehot):
    high, _ = split(potential)
    mid, low = split(potential - high.astype(f32))
    parts = [x.astype(f32) for x in (high, mid, low)]
    picked = mm(jnp.concatenate(parts, axis=0).astype(bf16), onehot)
    n = potential.shape[0]
    return picked[:n] + (picked[n : 2 * n] + picked[2 * n :])


def place_kernel(s, cells, tiles, own_out, rims_out):
    own_out[...] = occupancy(cells[0], s)
    lane = lax.broadcasted_iota(jnp.int32, (8, LANES), 1)
    place = lax.broadcasted_iota(jnp.int32, (s.skel, LANES), 0).astype(f32)
    count = len(s.sources)
    for i in range(0, count, 2):
        last = min(i + 1, count - 1)
        pair = jnp.where(lane < RIM, tiles[2 + i], pltpu.roll(tiles[2 + last], RIM, 1))
        rims_out[i // 2] = jnp.where(pair[3:4] == place, 1.0, 0.0).astype(bf16)


def rim_values(s, potentials, onehots):
    lane = lax.broadcasted_iota(jnp.int32, (8, LANES), 1)
    count = len(potentials) - 1
    out = []
    for i in range(0, count, 2):
        last = min(i + 1, count - 1)
        both = pick(jnp.concatenate([potentials[1 + i], potentials[1 + last]], axis=0), onehots[i // 2])
        out.append(jnp.where(lane < RIM, both[:8], both[8:]))
    return out


def gather_kernel(s, gat, gh, gl, *refs):
    *messages, _, hi_out, lo_out = refs
    rims = unpack_rims([message[: s.half, :] for message in messages], s)
    gathered = gat[...] + product(mm, split(rims), (gh[...], gl[...]))
    hi_out[...], lo_out[...] = split(gathered)


def gather_far_kernel(s, gat, gh, gl, col, values, *refs):
    *messages, hi_out, lo_out = refs
    rims = unpack_rims([message[...] for message in messages], s)
    far = []
    for c in range(3):
        value = jnp.concatenate([values[i, c : c + 1, :] for i in range(values.shape[0])], axis=1)
        far.append(col[:, :1] * value)
    gathered = gat[...] + product(mm, split(rims + stacked(far, s)), (gh[...], gl[...]))
    hi_out[...], lo_out[...] = split(gathered)


def near_kernel(s, loc, nh, nl, hi, lo, out, rim_out):
    part = loc[...] + product(mm, (nh[...], nl[...]), (hi[...], lo[...]))
    out[...] = part
    rim_out[...] = pack_rim(part, s)


def first_kernel(s, part, fh, fl, own, rims, col, f_in, rot, sh, sl, oh, ol, *refs):
    *layers, u_out, charges_out, values_out, loc_out, gat_out, ortho_out, stat_out = refs
    count = 2 + len(s.sources)
    layers = [[part[at + k] for k in range(count)] for part in layers for at in range(0, part.shape[0], count)]
    weight_col = col[:, :1]
    occ = own[...]
    potentials = far_potentials(s, layers, (fh[...], fl[...]))
    values = pick(potentials[0], occ)
    u = part[...] + stacked([weight_col * values[c : c + 1] for c in range(3)], s)
    u_out[...] = u
    charges_out[...] = pack_charges(pieces(u, s), weight_col, occ, s)
    for index, value in enumerate(rim_values(s, potentials, rims)):
        values_out[index] = value
    f = f_in[...]
    loc, gat = local_part(u, s, rot[...], (sh[...], sl[...]), (oh[...], ol[...]))
    loc_out[...] = loc
    gat_out[...] = gat
    ff = total(f * f)
    fu = total(f * u) * safe_inverse(ff)
    ortho = u - fu * f
    ortho_out[...] = ortho
    oo = total(ortho * ortho)
    stat_out[...] = jnp.broadcast_to(
        jnp.concatenate([ff, fu, oo, jnp.zeros((5, 1), f32)], axis=0), (8, LANES)
    )


def order_kernel(x, _, out):
    out[...] = x[...]


def safe_inverse(x):
    return jnp.where(x > 0.0, 1.0 / jnp.where(x > 0.0, x, 1.0), 0.0)


def second_kernel(
    s, loc, nh, nl, hi, lo, cells, col, f_in, ortho_in, stat, charges_f, charges_u, packed_out
):
    part = loc[...] + product(mm, (nh[...], nl[...]), (hi[...], lo[...]))
    f, ortho = f_in[...], ortho_in[...]
    ff, fu, oo = (stat[i : i + 1, :1] for i in range(3))
    fa = total(f * part) * safe_inverse(ff)
    oa = total(ortho * part) * safe_inverse(oo)
    rest = part - fa * f - oa * ortho
    aa = total(rest * rest)
    rf, ro = jnp.sqrt(ff), jnp.sqrt(oo)
    of_f = charges_f[-8:, :]
    of_u = charges_u[...]
    of_a = pack_charges(pieces(rest, s), col[:, :1], occupancy(cells[0], s), s, count=True)
    row = lax.broadcasted_iota(jnp.int32, (8, LANES), 0)
    lane = lax.broadcasted_iota(jnp.int32, (8, LANES), 1)
    left = lane < RIM
    first = jnp.where(left, of_u, pltpu.roll(of_a, RIM, 1))
    first = jnp.where(row < 4, of_u, first)
    first = jnp.where((row == 7) & left, pltpu.roll(of_f, 1, 0), first)
    for index, value in enumerate((rf, rf * fu, ro, rf * fa, ro * oa, aa)):
        first = jnp.where((row == 3) & (lane == index), value, first)
    tails = jnp.where(left, pltpu.roll(of_f, 3, 0), pltpu.roll(pltpu.roll(of_f, 2, 0), RIM, 1))
    second = jnp.where(row < 3, of_f, of_a)
    second = jnp.where(row < 4, second, pltpu.roll(of_a, 4, 0))
    second = jnp.where(row == 7, tails, second)
    for device in range(s.devices):
        packed_out[device] = second if s.odd(device) else first


def tree(s, leaves, ups, siblings, root):
    def apply(dot, blocks, factor):
        rows = blocks[0].shape[0]
        out = product(dot, split(jnp.concatenate(blocks, axis=0)), factor)
        return [out[i * rows : (i + 1) * rows] for i in range(len(blocks))]

    n = s.skel
    halves = [[(hi[level, j * n : (j + 1) * n, :], lo[level, j * n : (j + 1) * n, :]) for j in range(2)]
              for level, (hi, lo) in ((k, ups) for k in range(s.levels))]
    charges = [leaves]
    for level in range(s.levels):
        low, high = (apply(mm, charges[-1][j::2], halves[level][j]) for j in range(2))
        charges.append([a + b for a, b in zip(low, high)])
    own = charges[-1][0]
    whole = own[:8]
    for at in range(8, own.shape[0], 8):
        whole = whole + own[at : at + 8]
    whole = whole + pltpu.roll(whole, 4, 0)
    others = jnp.concatenate([whole] * (own.shape[0] // 8), axis=0) - own
    potential = apply(mm, [others], root)
    for level in reversed(range(s.levels)):
        beside = apply(mm, charges[level], (siblings[0][level], siblings[1][level]))
        down = [apply(mt, potential, halves[level][j]) for j in range(2)]
        potential = [
            down[z % 2][z // 2] + beside[z ^ 1] for z in range(len(charges[level]))
        ]
    return potential


def box_numbers(s, firsts, seconds, ups, siblings, root):
    columns = s.nx * s.ny
    row = lax.broadcasted_iota(jnp.int32, (8, LANES), 0)
    lane = lax.broadcasted_iota(jnp.int32, (8, LANES), 1)
    left, valid = lane < RIM, row < 3
    leaves = []
    for z in range(s.nz):
        wide = []
        for column in range(0, columns, 2):
            a, b = firsts[column * s.nz + z], firsts[(column + 1) * s.nz + z]
            main = jnp.where(row < 4, a, pltpu.roll(b, 4, 0))
            tail = jnp.where(row < 4, pltpu.roll(a, 4, 0), b)
            wide.append(jnp.concatenate([main, tail], axis=1)[:, : s.skel])
        leaves.append(jnp.concatenate(wide, axis=0))
    potential = tree(s, leaves, ups, siblings, root)
    out = []
    for start in range(0, s.devices, 8):
        sums = [jnp.zeros((8, LANES), f32) for _ in range(5)]
        for box in range(start, min(s.devices, start + 8)):
            column, z = box // s.nz, box % s.nz
            at = 8 * (column // 2)
            phi = potential[z][at : at + 8]
            main, tail = phi[:, :LANES], phi[:, LANES:]
            tail = jnp.concatenate([tail, tail], axis=1)
            if column % 2:
                main, tail = pltpu.roll(main, 4, 0), pltpu.roll(tail, 4, 0)
            first, second = firsts[box], seconds[box]
            both = pltpu.roll(first, 4, 0) * tail
            of_f = jnp.where(row == 0, pltpu.roll(second, 1, 0), jnp.where(row == 1, pltpu.roll(second, 2, 0), pltpu.roll(first, 3, 0)))
            of_f = jnp.where(left == (row != 1), of_f * tail, 0.0)
            count = jnp.broadcast_to(second[3:4], (8, LANES))
            count_tail = jnp.where(left, 0.0, jnp.broadcast_to(first[7:8], (8, LANES)))
            terms = (
                second * main + of_f,
                first * main + jnp.where(left, both, 0.0),
                pltpu.roll(second, 4, 0) * main + jnp.where(left, 0.0, both),
                count * (main * main) + count_tail * (tail * tail),
            )
            here = row == box - start
            for index, term in enumerate(terms):
                value = jnp.sum(jnp.where(valid, term, 0.0), axis=0, keepdims=True)
                sums[index] = jnp.where(here, value, sums[index])
            sums[4] = jnp.where(here, first[3:4], sums[4])
        numbers = sums[4]
        for index in range(4):
            numbers = jnp.where(lane == 6 + index, jnp.sum(sums[index], axis=1, keepdims=True), numbers)
        out.append(numbers)
    rest = round_up(s.devices, LANES) - 8 * len(out)
    if rest:
        out.append(jnp.zeros((rest, LANES), f32))
    return jnp.concatenate(out, axis=0)


def finish_kernel(s, ids, f_in, u_in, mine, other, col, uh, ul, bh, bl, rh, rl, x_out, lsq_out, raw, sem):
    odd = (ids[0] // s.ny) % 2 == 1
    firsts = [jnp.where(odd, other[box], mine[box]) for box in range(s.devices)]
    seconds = [jnp.where(odd, mine[box], other[box]) for box in range(s.devices)]
    rows = box_numbers(s, firsts, seconds, (uh, ul), (bh, bl), (rh[...], rl[...])).T
    f1, u1, u2, t1, t2, aa, far_f, far_u, far_a, far_far = (rows[i : i + 1] for i in range(10))
    by_f = safe_inverse(f1)
    by_o = jnp.where(u2 * u2 > 1e-10 * (u1 * u1), safe_inverse(u2), 0.0)
    on_one = far_f * by_f
    on_two = (far_u - u1 * by_f * far_f) * by_o
    weight = jnp.sum(col[:, :1] * col[:, :1], axis=0, keepdims=True)
    t3 = aa + 2.0 * far_a + weight * far_far - on_one * on_one - on_two * on_two
    t1, t2, t3 = t1 + on_one, t2 + on_two, jnp.sqrt(jnp.maximum(t3, 0.0))

    def along(x):
        return jnp.sum(x, axis=1, keepdims=True)

    beta = jnp.sqrt(along(f1 * f1) + epsilon)
    v = f1 / beta
    w1, w2 = u1 / beta, u2 / beta
    h11 = along(w1 * v)
    r1 = w1 - h11 * v
    h21 = jnp.sqrt(along(r1 * r1 + w2 * w2) + epsilon)
    b1, b2 = r1 / h21, w2 / h21
    z1, z2, z3 = ((t1 / beta - h11 * w1) / h21, (t2 / beta - h11 * w2) / h21, t3 / beta / h21)
    h12 = along(z1 * v)
    h22 = along(z1 * b1 + z2 * b2)
    d1, d2 = z1 - h12 * v - h22 * b1, z2 - h22 * b2
    h32 = jnp.sqrt(along(d1 * d1 + d2 * d2 + z3 * z3) + epsilon)
    first_norm = jnp.sqrt(h11 * h11 + h21 * h21)
    c1, s1 = h11 / first_norm, h21 / first_norm
    t12, t22 = c1 * h12 + s1 * h22, c1 * h22 - s1 * h12
    second_norm = jnp.sqrt(t22 * t22 + h32 * h32)
    c2, s2 = t22 / second_norm, h32 / second_norm
    g2 = -s1 * beta
    y2 = c2 * g2 / second_norm
    y1 = (c1 * beta - t12 * y2) / first_norm
    lsq_out[...] = jnp.abs(s2 * g2)
    on_u = y2 / h21 / beta
    on_f = y1 / beta - on_u * h11
    moves = []
    for c in range(3):
        part = slice(c * s.step, c * s.step + s.blobs)
        raw[c * s.blobs : (c + 1) * s.blobs, 0, :] = on_f * f_in[part, :] + on_u * u_in[part, :]
        rows = pl.ds(c * s.blobs, s.blobs)
        moves.append(pltpu.make_async_copy(raw.at[rows], x_out.at[rows], sem.at[c]))
        moves[-1].start()
    for move in moves:
        move.wait()


def call(kernel, outs, args, scalars=0, far_args=0, far_outs=0, scratch=(), flops=0):
    vmem = pl.BlockSpec(memory_space=pltpu.VMEM)
    smem = pl.BlockSpec(memory_space=pltpu.SMEM)
    hbm = pl.BlockSpec(memory_space=pltpu.HBM)
    near_args = len(args) - far_args
    args = args[:near_args] + [pltpu.with_memory_space_constraint(x, pltpu.HBM) for x in args[near_args:]]
    return pl.pallas_call(
        kernel,
        out_shape=[jax.ShapeDtypeStruct(shape, kind) for shape, kind in outs],
        in_specs=[smem] * scalars + [vmem] * (near_args - scalars) + [hbm] * far_args,
        out_specs=[hbm] * far_outs + [vmem] * (len(outs) - far_outs),
        scratch_shapes=list(scratch),
        compiler_params=pltpu.CompilerParams(vmem_limit_bytes=16 * 2**20),
        cost_estimate=pl.CostEstimate(flops=flops, bytes_accessed=2**20, transcendentals=0),
    )(*args)


def body(
    mesh_shape, rhs, angles, self_mob, near_mat, near_weight, neighbours, cells, blob_weight,
    skel_perm, interp, sibling_ops, root_op,
):
    s = Sizes(mesh_shape, rhs, skel_perm)
    full = (s.rows, s.bodies)
    square = (s.rows, s.rows)
    tile = (8, LANES)
    far_shape = (s.skel, 2 * s.far_tiles * LANES)
    column = lax.axis_index("gx") * s.ny + lax.axis_index("gy")
    ids = jnp.stack([column, lax.axis_index("gz")]).astype(jnp.int32)

    def fetch(x, kind, dy):
        pairs = []
        for gx in range(s.nx):
            for gy in range(s.ny):
                pairs.append((s.beside(kind, gx) * s.ny + (gy + dy) % s.ny, gx * s.ny + gy))
        return lax.ppermute(x, ("gx", "gy"), pairs)

    def fetch_layers(x):
        parts, sent = [x], [x]
        for level in range(s.levels):
            pairs = [(z ^ (1 << level), z) for z in range(s.nz)]
            parts.append(lax.ppermute(sent[-1], "gz", pairs))
            if level + 1 < s.levels:
                shape = (2 * sent[-1].shape[0],) + tile
                sent += call(join_kernel, [(shape, f32)], [sent[-1], parts[-1]])
        return parts, sent[-1]

    def fetch_rims(rim, after=None):
        got = {}
        for dy in s.shifts:
            got["same", dy] = fetch(rim, "same", dy)
        got["other", 0] = fetch(rim, "other", 0)
        if after is not None:
            (rim,) = call(order_kernel, [(rim.shape, f32)], [rim, after])
        for dy in s.shifts:
            got["other", dy] = fetch(rim, "other", dy)
        got["partner", 0] = fetch(rim, "partner", 0)
        return got

    def forward_rims(got, after):
        for dy in s.shifts:
            held = got["same", dy]
            (held,) = call(order_kernel, [(held.shape, f32)], [held, after])
            got["partner", dy] = fetch(held, "partner", 0)

    def plane_sum(message, got, after):
        if not s.direct:
            return [lax.psum(message[s.half :], ("gx", "gy"))]
        quarter = [message] + [got[key] for key in s.sources if key[0] != "partner"]
        (half,) = call(functools.partial(half_kernel, s), [(tile, f32)], quarter + [after])
        return [half, fetch(half, "partner", 0)]

    flat = (3 * s.blobs, 1, s.bodies)
    small = (1, s.blobs)
    message, col, cells, f = call(
        functools.partial(start_kernel, s),
        [((s.message, LANES), f32), ((s.step, LANES), f32), (cells.shape, jnp.int32), (full, f32)],
        [rhs.reshape(flat), cells, blob_weight.reshape(small)],
        far_args=3,
        scratch=[pltpu.VMEM(flat, f32), pltpu.VMEM(small, f32), pltpu.SemaphoreType.DMA((3,))],
        flops=10**7,
    )
    got = fetch_rims(message)
    operators = [
        angles.reshape(3, 1, s.bodies), near_weight, neighbours, self_mob, near_mat, skel_perm, interp,
        sibling_ops, root_op,
    ]
    loc, gat, rot, sh, sl, nh, nl, oh, ol, gh, gl, fh, fl, *operators_out = call(
        functools.partial(setup_kernel, s),
        [(full, f32), (full, f32), ((16, s.bodies), f32)]
        + [(square, bf16)] * 4
        + [((s.bodies, s.bodies), bf16)] * 2
        + [((s.ghosts, s.bodies), bf16)] * 2
        + [(far_shape, bf16)] * 2
        + [((s.levels, 2 * s.skel, s.skel), bf16)] * 2
        + [((s.levels, s.skel, s.skel), bf16)] * 2
        + [((s.skel, s.skel), bf16)] * 2,
        [ids, f] + operators,
        scalars=1,
        far_args=len(operators),
        scratch=[
            pltpu.VMEM(square, f32), pltpu.VMEM((s.levels, 2 * s.skel, s.skel), f32), pltpu.VMEM(far_shape, f32)
        ]
        + [pltpu.VMEM(x.shape, x.dtype) for x in operators]
        + [pltpu.SemaphoreType.DMA((len(operators),))],
        flops=5 * 10**9,
    )
    forward_rims(got, rot)
    sums = plane_sum(message, got, rot)
    around = [got[key] for key in s.sources]
    gathered = call(
        functools.partial(gather_kernel, s),
        [(full, bf16), (full, bf16)],
        [gat, gh, gl] + around + [sums[0]],
        flops=10**9,
    )
    part, rim = call(
        functools.partial(near_kernel, s),
        [(full, f32), ((s.half, LANES), f32)],
        [loc, nh, nl, *gathered],
        flops=10**9,
    )
    (tiles,) = call(
        functools.partial(layer_kernel, s, len(sums)),
        [((2 + len(around),) + tile, f32)],
        [message] + sums + around + [gathered[1]],
    )
    layers, joined = fetch_layers(tiles)
    got = fetch_rims(rim, joined)
    places = call(
        functools.partial(place_kernel, s),
        [((s.skel, s.bodies), bf16), ((s.ghosts // LANES, s.skel, LANES), bf16)],
        [cells, tiles],
        flops=2 * 10**10,
    )
    u, charges, values, loc, gat, ortho, stat = call(
        functools.partial(first_kernel, s),
        [(full, f32), (tile, f32), ((s.ghosts // LANES,) + tile, f32)] + [(full, f32)] * 3 + [(tile, f32)],
        [part, fh, fl, *places, col, f, rot, sh, sl, oh, ol, *layers],
        flops=10**9,
    )
    forward_rims(got, places[1])
    gathered = call(
        functools.partial(gather_far_kernel, s),
        [(full, bf16), (full, bf16)],
        [gat, gh, gl, col, values] + [got[key] for key in s.sources],
        flops=10**9,
    )
    (packed,) = call(
        functools.partial(second_kernel, s),
        [((s.devices, 8, LANES), f32)],
        [loc, nh, nl, *gathered, cells, col, f, ortho, stat, message, charges],
        flops=10**9,
    )
    boxes = lax.all_to_all(packed, ("gx", "gy", "gz"), 0, 0)
    result, lsq = call(
        functools.partial(finish_kernel, s),
        [(flat, f32), ((1, 1), f32)],
        [ids, f, u, boxes, fetch(boxes, "partner", 0), col, *operators_out],
        scalars=1,
        far_outs=1,
        scratch=[pltpu.VMEM(flat, f32), pltpu.SemaphoreType.DMA((3,))],
        flops=10**7,
    )
    return result.reshape(rhs.shape), lsq.reshape(())


def solution(mesh):
    in_specs = (
        P("gx", "gy", None, None, "gz"),
        P("gx", "gy", None, "gz"),
        P(),
        P(),
        P("gx", "gy", None, "gz"),
        P("gx", "gy", None, "gz"),
        P("gx", "gy", "gz"),
        P(),
        P(),
        P(),
        P(),
        P(),
    )
    out_specs = (P("gx", "gy", None, None, "gz"), P())
    inner = functools.partial(body, dict(mesh.shape))
    return jax.shard_map(inner, mesh=mesh, in_specs=in_specs, out_specs=out_specs, check_vma=False)
```

```python
import functools

import jax
import jax.numpy as jnp
from jax import lax
from jax.experimental import pallas as pl
from jax.experimental.pallas import tpu as pltpu
from jax.sharding import PartitionSpec as P

epsilon = 1e-06
f32 = jnp.float32
bf16 = jnp.bfloat16
RIM = 64
LANES = 128


def round_up(value, unit):
    return -(-value // unit) * unit


def split(x):
    hi = x.astype(bf16)
    lo = (x - hi.astype(f32)).astype(bf16)
    return hi, lo


def mm(a, b):
    return lax.dot_general(a, b, (((1,), (0,)), ((), ())), preferred_element_type=f32)


def mt(a, b):
    return lax.dot_general(a, b, (((1,), (1,)), ((), ())), preferred_element_type=f32)


def product(dot, a, b):
    return dot(a[0], b[0]) + (dot(a[0], b[1]) + dot(a[1], b[0]))


def total(x):
    return jnp.sum(jnp.sum(x, axis=0, keepdims=True), axis=1, keepdims=True)


class Sizes:
    def __init__(self, mesh_shape, rhs, skel_perm):
        self.nx, self.ny, self.nz = (mesh_shape[a] for a in ("gx", "gy", "gz"))
        self.devices = self.nx * self.ny * self.nz
        self.blobs, self.bodies = rhs.shape[-2:]
        self.step = round_up(self.blobs, 8)
        self.rows = round_up(3 * self.step, 16)
        self.half = self.rows // 2
        self.message = self.half + 8
        self.direct = (self.nx, self.ny) == (4, 2)
        self.levels = skel_perm.shape[0]
        self.skel = skel_perm.shape[1] // 2
        shifts = sorted({(dy % self.ny) for dy in (-1, 1)} - {0})
        self.shifts = shifts
        self.sources = [("same", dy) for dy in shifts]
        for kind in ("other", "partner"):
            self.sources += [(kind, dy) for dy in [0] + shifts]
        self.ghosts = round_up(len(self.sources) * RIM, LANES)
        self.far_tiles = self.nz + -(-self.nz // 2)

    def slot_start(self, slot, parity):
        dx, dy = slot // 3 - 1, (slot % 3 - 1) % self.ny
        kind = "same" if dx == 0 else "partner" if dx == 1 - 2 * parity else "other"
        if (kind, dy) == ("same", 0):
            return 0
        return self.bodies + RIM * self.sources.index((kind, dy))

    def odd(self, device):
        return (device // (self.ny * self.nz)) % 2

    def beside(self, kind, x):
        if kind == "same":
            return x
        if kind == "partner":
            return x ^ 1
        return (x + 2 * (x % 2) - 1) % self.nx


def pieces(x, s):
    return [x[c * s.step : c * s.step + s.step] for c in range(3)]


def turn(parts, rot, inverse):
    out = []
    for target in range(3):
        acc = None
        for source in range(3):
            row = 3 * source + target if inverse else 3 * target + source
            term = rot[row : row + 1] * parts[source]
            acc = term if acc is None else acc + term
        out.append(acc)
    return out


def stacked(parts, s):
    rest = s.rows - 3 * s.step
    if rest:
        parts = list(parts) + [jnp.zeros((rest, parts[0].shape[1]), f32)]
    return jnp.concatenate(parts, axis=0)


def occupancy(cells, s):
    row = lax.broadcasted_iota(jnp.int32, (s.skel, s.bodies), 0)
    return jnp.where(cells == row, 1.0, 0.0).astype(bf16)


def pack_charges(parts, weight_col, occ, s, count=False):
    moments = [jnp.sum(part * weight_col, axis=0, keepdims=True) for part in parts]
    moments.append(jnp.full((1, s.bodies), 1.0 if count else 0.0, f32))
    moments = jnp.concatenate(moments + [jnp.zeros((4, s.bodies), f32)], axis=0)
    high, rest = split(moments)
    mid, low = split(moments - high.astype(f32))
    stack = jnp.concatenate([high.astype(f32), mid.astype(f32), low.astype(f32)], axis=0).astype(bf16)
    sums = mt(stack, occ)
    charges = sums[0:8] + (sums[8:16] + sums[16:24])
    tail = jnp.concatenate([charges[:, LANES:], jnp.zeros((8, 2 * LANES - s.skel), f32)], axis=1)
    row = lax.broadcasted_iota(jnp.int32, (8, LANES), 0)
    return jnp.where(row < 4, charges[:, :LANES], pltpu.roll(tail, 4, 0))


def pack_rim(x, s):
    lane = lax.broadcasted_iota(jnp.int32, (s.half, LANES), 1)
    top, bottom = x[: s.half, :LANES], x[s.half :, :LANES]
    return jnp.where(lane < RIM, top, pltpu.roll(bottom, RIM, 1))


def unpack_rims(rims, s):
    lane = lax.broadcasted_iota(jnp.int32, (s.half, LANES), 1)
    tops, bottoms = [], []
    for i in range(0, s.ghosts // RIM, 2):
        a = rims[i]
        b = rims[i + 1] if i + 1 < len(rims) else jnp.zeros_like(a)
        tops.append(jnp.where(lane < RIM, a, pltpu.roll(b, RIM, 1)))
        bottoms.append(jnp.where(lane < RIM, pltpu.roll(a, RIM, 1), b))
    return jnp.concatenate(
        [jnp.concatenate(tops, axis=1), jnp.concatenate(bottoms, axis=1)], axis=0
    )


def pack_message(x, weight_col, cells, s):
    charges = pack_charges(pieces(x, s), weight_col, occupancy(cells, s), s)
    row = lax.broadcasted_iota(jnp.int32, (8, LANES), 0)
    charges = jnp.where(row == 3, cells[:, :LANES].astype(f32), charges)
    return jnp.concatenate([pack_rim(x, s), charges], axis=0)


def begin(sources, targets, sems):
    moves = [pltpu.make_async_copy(a, b, sems.at[i]) for i, (a, b) in enumerate(zip(sources, targets))]
    for move in moves:
        move.start()
    return moves


def start_kernel(s, rhs, cells, weight, message_out, col_out, cells_out, f_out, raw, wide, sems):
    moves = begin((weight, cells, rhs), (wide, cells_out, raw), sems)
    f_out[...] = jnp.zeros_like(f_out)
    moves[0].wait()
    row = jnp.concatenate([wide[...], jnp.zeros((1, 2 * LANES - s.blobs), f32)], axis=1)
    col = jnp.broadcast_to(row, (LANES, 2 * LANES)).T[: s.step]
    col_out[...] = col
    for move in moves[1:]:
        move.wait()
    for c in range(3):
        f_out[c * s.step : c * s.step + s.blobs, :] = raw[c * s.blobs : (c + 1) * s.blobs, 0, :]
    message_out[...] = pack_message(f_out[...], col[:, :1], cells_out[0], s)


def frame_rows(angles):
    cos, sin = jnp.cos(angles), jnp.sin(angles)
    cy, cp, cr = cos[0:1], cos[1:2], cos[2:3]
    sy, sp, sr = sin[0:1], sin[1:2], sin[2:3]
    return [
        cy * cp,
        cy * sp * sr - sy * cr,
        cy * sp * cr + sy * sr,
        sy * cp,
        sy * sp * sr + cy * cr,
        sy * sp * cr - cy * sr,
        -sp,
        cp * sr,
        cp * cr,
    ]


def local_part(f, s, rot, mob, own):
    parts = pieces(f, s)
    turned = stacked(turn(parts, rot, False), s)
    mixed = product(mm, mob, split(turned))
    back = turn(pieces(mixed, s), rot, True)
    return f + stacked(back, s), product(mm, split(f), own)


def product_many(dot, blocks, b):
    rows = blocks[0].shape[0]
    out = product(dot, split(jnp.concatenate(blocks, axis=0)), split(b))
    return [out[i * rows : (i + 1) * rows] for i in range(len(blocks))]


def expand_once(groups, halves):
    flat = [block for group in groups for block in group]
    sides = [product_many(mt, flat, half) for half in halves]
    out, at = [], 0
    for group in groups:
        spread = []
        for i in range(at, at + len(group)):
            spread += [sides[0][i], sides[1][i]]
        at += len(group)
        out.append(spread)
    return out


def setup_kernel(
    s, ids, f_in, *refs
):
    count = 9
    sources, refs = refs[:count], refs[count:]
    copies, refs = refs[-1 - count :], refs[: -1 - count]
    copies, sems = copies[:-1], copies[-1]
    setup(s, ids, f_in, begin(sources, copies, sems), *copies, *refs)


def setup(
    s, ids, f_in, moves, angles, near_weight, neighbours, self_mob, near_mat, perm, interp, sibling, root,
    loc_out, gat_out, rot_out, sh_out, sl_out, nh_out, nl_out, oh_out, ol_out, gh_out, gl_out,
    fh_out, fl_out, uh_out, ul_out, bh_out, bl_out, rh_out, rl_out, padded, ups_ref, far_ref,
):
    f = f_in[...]
    for move in moves[:3]:
        move.wait()
    rot = jnp.concatenate(frame_rows(angles[:, 0, :]) + [jnp.zeros((7, s.bodies), f32)], axis=0)
    rot_out[...] = rot

    links = neighbours[0, 0]
    slot = links // s.bodies
    base = jnp.zeros_like(links)
    odd = (ids[0] // s.ny) % 2
    for index in range(9):
        start = jnp.where(odd == 1, s.slot_start(index, 1), s.slot_start(index, 0))
        base = jnp.where(slot == index, start, base)
    column = base + links % s.bodies
    coef = near_weight[0, 0]
    for first, count, hi_out, lo_out in (
        (0, s.bodies, oh_out, ol_out),
        (s.bodies, s.ghosts, gh_out, gl_out),
    ):
        for r in range(0, count, 64):
            row = lax.broadcasted_iota(jnp.int32, (64, s.bodies), 0) + (first + r)
            acc = jnp.zeros((64, s.bodies), f32)
            for k in range(coef.shape[0]):
                acc = acc + jnp.where(column[k : k + 1] == row, coef[k : k + 1], 0.0)
            hi, lo = split(acc)
            hi_out[r : r + 64, :] = hi
            lo_out[r : r + 64, :] = lo

    for move in moves[3:]:
        move.wait()
    padded[...] = jnp.zeros_like(padded)
    for matrix, hi_out, lo_out in ((self_mob, sh_out, sl_out), (near_mat, nh_out, nl_out)):
        for c in range(3):
            for d in range(3):
                padded[c * s.step : c * s.step + s.blobs, d * s.step : d * s.step + s.blobs] = matrix[
                    c * s.blobs : (c + 1) * s.blobs, d * s.blobs : (d + 1) * s.blobs
                ]
        hi, lo = split(padded[...])
        hi_out[...] = hi
        lo_out[...] = lo

    loc, gat = local_part(f, s, rot, (sh_out[...], sl_out[...]), (oh_out[...], ol_out[...]))
    loc_out[...] = loc
    gat_out[...] = gat

    n = s.skel
    z = ids[1]
    halves = []
    spot = lax.broadcasted_iota(jnp.int32, (2 * n, n), 0)
    for level in range(s.levels):
        kept = jnp.where(perm[level : level + 1, :n] == spot, 1.0, 0.0)
        moved = jnp.where(perm[level : level + 1, n:] == spot, 1.0, 0.0).astype(bf16)
        hi, lo = split(interp[level])
        up = kept + (mm(moved, hi) + mm(moved, lo))
        ups_ref[level] = up
        uh_out[level], ul_out[level] = split(up)
        bh_out[level], bl_out[level] = split(sibling[level])
        bit = (z >> level) & 1
        halves.append(
            [ups_ref[level, pl.ds(pl.multiple_of(side * n, 8), n), :] for side in (bit, 1 - bit)]
        )

    def down(block, level, dot):
        return product(dot, split(halves[level][0]), split(block))

    spread = root[...]
    rh_out[...], rl_out[...] = split(spread)
    beside = []
    for level in reversed(range(s.levels)):
        spread = down(spread, level, mt if level == s.levels - 1 else mm)
        beside = [(down(block, level, mt if fresh else mm), False) for block, fresh in beside]
        beside.append((sibling[level], True))
    beside = [block.T if fresh else block for block, fresh in reversed(beside)]
    leaves = [[spread]]
    for level in reversed(range(s.levels)):
        leaves = expand_once(leaves, halves[level])
        leaves.append([beside[level]])
    far_leaves, *sub = leaves
    near_leaves = [jnp.zeros((n, n), f32)]
    for blocks in reversed(sub):
        near_leaves += blocks
    tail = n - LANES
    far_ref[...] = jnp.zeros_like(far_ref)
    own = [a - b for a, b in zip(near_leaves, far_leaves)]
    for group, blocks in enumerate((own, far_leaves)):
        for leaf, block in enumerate(blocks):
            at = (group * s.far_tiles + leaf) * LANES
            far_ref[:, at : at + LANES] = block[:, :LANES]
            at = (group * s.far_tiles + s.nz + leaf // 2) * LANES + leaf % 2 * RIM
            far_ref[:, at : at + tail] = block[:, LANES:]
    fh_out[...], fl_out[...] = split(far_ref[...])


def half_kernel(s, *refs):
    *messages, _, out = refs
    acc = messages[0][s.half :, :]
    for message in messages[1:]:
        acc = acc + message[s.half :, :]
    out[...] = acc


def layer_kernel(s, count, message, *refs):
    sums, around, out = refs[:count], refs[count:-2], refs[-1]
    acc = sums[0][...]
    for part in sums[1:]:
        acc = acc + part[...]
    out[0] = message[s.half :, :]
    out[1] = acc
    for index, other in enumerate(around):
        out[2 + index] = other[s.half :, :]


def join_kernel(x, y, out):
    out[: x.shape[0]] = x[...]
    out[x.shape[0] :] = y[...]


def layer_row(s, tiles):
    row = list(tiles)
    lane = lax.broadcasted_iota(jnp.int32, (8, LANES), 1)
    for leaf in range(0, s.nz, 2):
        pair = tiles[leaf]
        if leaf + 1 < s.nz:
            pair = jnp.where(lane < RIM, pair, pltpu.roll(tiles[leaf + 1], RIM, 1))
        row.append(pltpu.roll(pair, 4, 0))
    return jnp.concatenate(row, axis=1)


def far_potentials(s, layers, far_op):
    own = [layer_row(s, [layer[k] for layer in layers]) for k in range(len(layers[0]))]
    wide = own[0].shape[1]
    hi, lo = far_op
    whole = product(mt, split(own.pop(1)), (hi[:, wide:], lo[:, wide:]))
    boxes = product(mt, split(jnp.concatenate(own, axis=0)), (hi[:, :wide], lo[:, :wide]))
    return [boxes[8 * k : 8 * k + 8] + whole for k in range(len(own))]


def pick(potential, onehot):
    high, _ = split(potential)
    mid, low = split(potential - high.astype(f32))
    parts = [x.astype(f32) for x in (high, mid, low)]
    picked = mm(jnp.concatenate(parts, axis=0).astype(bf16), onehot)
    n = potential.shape[0]
    return picked[:n] + (picked[n : 2 * n] + picked[2 * n :])


def place_kernel(s, cells, tiles, own_out, rims_out):
    own_out[...] = occupancy(cells[0], s)
    lane = lax.broadcasted_iota(jnp.int32, (8, LANES), 1)
    place = lax.broadcasted_iota(jnp.int32, (s.skel, LANES), 0).astype(f32)
    count = len(s.sources)
    for i in range(0, count, 2):
        last = min(i + 1, count - 1)
        pair = jnp.where(lane < RIM, tiles[2 + i], pltpu.roll(tiles[2 + last], RIM, 1))
        rims_out[i // 2] = jnp.where(pair[3:4] == place, 1.0, 0.0).astype(bf16)


def rim_values(s, potentials, onehots):
    lane = lax.broadcasted_iota(jnp.int32, (8, LANES), 1)
    count = len(potentials) - 1
    out = []
    for i in range(0, count, 2):
        last = min(i + 1, count - 1)
        both = pick(jnp.concatenate([potentials[1 + i], potentials[1 + last]], axis=0), onehots[i // 2])
        out.append(jnp.where(lane < RIM, both[:8], both[8:]))
    return out


def gather_kernel(s, gat, gh, gl, *refs):
    *messages, _, hi_out, lo_out = refs
    rims = unpack_rims([message[: s.half, :] for message in messages], s)
    gathered = gat[...] + product(mm, split(rims), (gh[...], gl[...]))
    hi_out[...], lo_out[...] = split(gathered)


def gather_far_kernel(s, gat, gh, gl, col, values, *refs):
    *messages, hi_out, lo_out = refs
    rims = unpack_rims([message[...] for message in messages], s)
    far = []
    for c in range(3):
        value = jnp.concatenate([values[i, c : c + 1, :] for i in range(values.shape[0])], axis=1)
        far.append(col[:, :1] * value)
    gathered = gat[...] + product(mm, split(rims + stacked(far, s)), (gh[...], gl[...]))
    hi_out[...], lo_out[...] = split(gathered)


def near_kernel(s, loc, nh, nl, hi, lo, out, rim_out):
    part = loc[...] + product(mm, (nh[...], nl[...]), (hi[...], lo[...]))
    out[...] = part
    rim_out[...] = pack_rim(part, s)


def first_kernel(s, part, fh, fl, own, rims, col, f_in, rot, sh, sl, oh, ol, *refs):
    *layers, u_out, charges_out, values_out, loc_out, gat_out, ortho_out, stat_out = refs
    count = 2 + len(s.sources)
    layers = [[part[at + k] for k in range(count)] for part in layers for at in range(0, part.shape[0], count)]
    weight_col = col[:, :1]
    occ = own[...]
    potentials = far_potentials(s, layers, (fh[...], fl[...]))
    values = pick(potentials[0], occ)
    u = part[...] + stacked([weight_col * values[c : c + 1] for c in range(3)], s)
    u_out[...] = u
    charges_out[...] = pack_charges(pieces(u, s), weight_col, occ, s)
    for index, value in enumerate(rim_values(s, potentials, rims)):
        values_out[index] = value
    f = f_in[...]
    loc, gat = local_part(u, s, rot[...], (sh[...], sl[...]), (oh[...], ol[...]))
    loc_out[...] = loc
    gat_out[...] = gat
    ff = total(f * f)
    fu = total(f * u) * safe_inverse(ff)
    ortho = u - fu * f
    ortho_out[...] = ortho
    oo = total(ortho * ortho)
    stat_out[...] = jnp.broadcast_to(
        jnp.concatenate([ff, fu, oo, jnp.zeros((5, 1), f32)], axis=0), (8, LANES)
    )


def order_kernel(x, _, out):
    out[...] = x[...]


def safe_inverse(x):
    return jnp.where(x > 0.0, 1.0 / jnp.where(x > 0.0, x, 1.0), 0.0)


def second_kernel(
    s, loc, nh, nl, hi, lo, cells, col, f_in, ortho_in, stat, charges_f, charges_u, packed_out
):
    part = loc[...] + product(mm, (nh[...], nl[...]), (hi[...], lo[...]))
    f, ortho = f_in[...], ortho_in[...]
    ff, fu, oo = (stat[i : i + 1, :1] for i in range(3))
    fa = total(f * part) * safe_inverse(ff)
    oa = total(ortho * part) * safe_inverse(oo)
    rest = part - fa * f - oa * ortho
    aa = total(rest * rest)
    rf, ro = jnp.sqrt(ff), jnp.sqrt(oo)
    of_f = charges_f[-8:, :]
    of_u = charges_u[...]
    of_a = pack_charges(pieces(rest, s), col[:, :1], occupancy(cells[0], s), s, count=True)
    row = lax.broadcasted_iota(jnp.int32, (8, LANES), 0)
    lane = lax.broadcasted_iota(jnp.int32, (8, LANES), 1)
    left = lane < RIM
    first = jnp.where(left, of_u, pltpu.roll(of_a, RIM, 1))
    first = jnp.where(row < 4, of_u, first)
    first = jnp.where((row == 7) & left, pltpu.roll(of_f, 1, 0), first)
    for index, value in enumerate((rf, rf * fu, ro, rf * fa, ro * oa, aa)):
        first = jnp.where((row == 3) & (lane == index), value, first)
    tails = jnp.where(left, pltpu.roll(of_f, 3, 0), pltpu.roll(pltpu.roll(of_f, 2, 0), RIM, 1))
    second = jnp.where(row < 3, of_f, of_a)
    second = jnp.where(row < 4, second, pltpu.roll(of_a, 4, 0))
    second = jnp.where(row == 7, tails, second)
    for device in range(s.devices):
        packed_out[device] = second if s.odd(device) else first


def tree(s, leaves, ups, siblings, root):
    def apply(dot, blocks, factor):
        rows = blocks[0].shape[0]
        out = product(dot, split(jnp.concatenate(blocks, axis=0)), factor)
        return [out[i * rows : (i + 1) * rows] for i in range(len(blocks))]

    n = s.skel
    halves = [[(hi[level, j * n : (j + 1) * n, :], lo[level, j * n : (j + 1) * n, :]) for j in range(2)]
              for level, (hi, lo) in ((k, ups) for k in range(s.levels))]
    charges = [leaves]
    for level in range(s.levels):
        low, high = (apply(mm, charges[-1][j::2], halves[level][j]) for j in range(2))
        charges.append([a + b for a, b in zip(low, high)])
    own = charges[-1][0]
    whole = own[:8]
    for at in range(8, own.shape[0], 8):
        whole = whole + own[at : at + 8]
    whole = whole + pltpu.roll(whole, 4, 0)
    others = jnp.concatenate([whole] * (own.shape[0] // 8), axis=0) - own
    potential = apply(mm, [others], root)
    for level in reversed(range(s.levels)):
        beside = apply(mm, charges[level], (siblings[0][level], siblings[1][level]))
        down = [apply(mt, potential, halves[level][j]) for j in range(2)]
        potential = [
            down[z % 2][z // 2] + beside[z ^ 1] for z in range(len(charges[level]))
        ]
    return potential


def box_numbers(s, firsts, seconds, ups, siblings, root):
    columns = s.nx * s.ny
    row = lax.broadcasted_iota(jnp.int32, (8, LANES), 0)
    lane = lax.broadcasted_iota(jnp.int32, (8, LANES), 1)
    left, valid = lane < RIM, row < 3
    leaves = []
    for z in range(s.nz):
        wide = []
        for column in range(0, columns, 2):
            a, b = firsts[column * s.nz + z], firsts[(column + 1) * s.nz + z]
            main = jnp.where(row < 4, a, pltpu.roll(b, 4, 0))
            tail = jnp.where(row < 4, pltpu.roll(a, 4, 0), b)
            wide.append(jnp.concatenate([main, tail], axis=1)[:, : s.skel])
        leaves.append(jnp.concatenate(wide, axis=0))
    potential = tree(s, leaves, ups, siblings, root)
    out = []
    for start in range(0, s.devices, 8):
        sums = [jnp.zeros((8, LANES), f32) for _ in range(5)]
        for box in range(start, min(s.devices, start + 8)):
            column, z = box // s.nz, box % s.nz
            at = 8 * (column // 2)
            phi = potential[z][at : at + 8]
            main, tail = phi[:, :LANES], phi[:, LANES:]
            tail = jnp.concatenate([tail, tail], axis=1)
            if column % 2:
                main, tail = pltpu.roll(main, 4, 0), pltpu.roll(tail, 4, 0)
            first, second = firsts[box], seconds[box]
            both = pltpu.roll(first, 4, 0) * tail
            of_f = jnp.where(row == 0, pltpu.roll(second, 1, 0), jnp.where(row == 1, pltpu.roll(second, 2, 0), pltpu.roll(first, 3, 0)))
            of_f = jnp.where(left == (row != 1), of_f * tail, 0.0)
            count = jnp.broadcast_to(second[3:4], (8, LANES))
            count_tail = jnp.where(left, 0.0, jnp.broadcast_to(first[7:8], (8, LANES)))
            terms = (
                second * main + of_f,
                first * main + jnp.where(left, both, 0.0),
                pltpu.roll(second, 4, 0) * main + jnp.where(left, 0.0, both),
                count * (main * main) + count_tail * (tail * tail),
            )
            here = row == box - start
            for index, term in enumerate(terms):
                value = jnp.sum(jnp.where(valid, term, 0.0), axis=0, keepdims=True)
                sums[index] = jnp.where(here, value, sums[index])
            sums[4] = jnp.where(here, first[3:4], sums[4])
        numbers = sums[4]
        for index in range(4):
            numbers = jnp.where(lane == 6 + index, jnp.sum(sums[index], axis=1, keepdims=True), numbers)
        out.append(numbers)
    rest = round_up(s.devices, LANES) - 8 * len(out)
    if rest:
        out.append(jnp.zeros((rest, LANES), f32))
    return jnp.concatenate(out, axis=0)


def finish_kernel(s, ids, f_in, u_in, mine, other, col, uh, ul, bh, bl, rh, rl, x_out, lsq_out, raw, sem):
    odd = (ids[0] // s.ny) % 2 == 1
    firsts = [jnp.where(odd, other[box], mine[box]) for box in range(s.devices)]
    seconds = [jnp.where(odd, mine[box], other[box]) for box in range(s.devices)]
    rows = box_numbers(s, firsts, seconds, (uh, ul), (bh, bl), (rh[...], rl[...])).T
    f1, u1, u2, t1, t2, aa, far_f, far_u, far_a, far_far = (rows[i : i + 1] for i in range(10))
    by_f = safe_inverse(f1)
    by_o = jnp.where(u2 * u2 > 1e-10 * (u1 * u1), safe_inverse(u2), 0.0)
    on_one = far_f * by_f
    on_two = (far_u - u1 * by_f * far_f) * by_o
    weight = jnp.sum(col[:, :1] * col[:, :1], axis=0, keepdims=True)
    t3 = aa + 2.0 * far_a + weight * far_far - on_one * on_one - on_two * on_two
    t1, t2, t3 = t1 + on_one, t2 + on_two, jnp.sqrt(jnp.maximum(t3, 0.0))

    def along(x):
        return jnp.sum(x, axis=1, keepdims=True)

    beta = jnp.sqrt(along(f1 * f1) + epsilon)
    v = f1 / beta
    w1, w2 = u1 / beta, u2 / beta
    h11 = along(w1 * v)
    r1 = w1 - h11 * v
    h21 = jnp.sqrt(along(r1 * r1 + w2 * w2) + epsilon)
    b1, b2 = r1 / h21, w2 / h21
    z1, z2, z3 = ((t1 / beta - h11 * w1) / h21, (t2 / beta - h11 * w2) / h21, t3 / beta / h21)
    h12 = along(z1 * v)
    h22 = along(z1 * b1 + z2 * b2)
    d1, d2 = z1 - h12 * v - h22 * b1, z2 - h22 * b2
    h32 = jnp.sqrt(along(d1 * d1 + d2 * d2 + z3 * z3) + epsilon)
    first_norm = jnp.sqrt(h11 * h11 + h21 * h21)
    c1, s1 = h11 / first_norm, h21 / first_norm
    t12, t22 = c1 * h12 + s1 * h22, c1 * h22 - s1 * h12
    second_norm = jnp.sqrt(t22 * t22 + h32 * h32)
    c2, s2 = t22 / second_norm, h32 / second_norm
    g2 = -s1 * beta
    y2 = c2 * g2 / second_norm
    y1 = (c1 * beta - t12 * y2) / first_norm
    lsq_out[...] = jnp.abs(s2 * g2)
    on_u = y2 / h21 / beta
    on_f = y1 / beta - on_u * h11
    moves = []
    for c in range(3):
        part = slice(c * s.step, c * s.step + s.blobs)
        raw[c * s.blobs : (c + 1) * s.blobs, 0, :] = on_f * f_in[part, :] + on_u * u_in[part, :]
        rows = pl.ds(c * s.blobs, s.blobs)
        moves.append(pltpu.make_async_copy(raw.at[rows], x_out.at[rows], sem.at[c]))
        moves[-1].start()
    for move in moves:
        move.wait()


def call(kernel, outs, args, scalars=0, far_args=0, far_outs=0, scratch=(), flops=0):
    vmem = pl.BlockSpec(memory_space=pltpu.VMEM)
    smem = pl.BlockSpec(memory_space=pltpu.SMEM)
    hbm = pl.BlockSpec(memory_space=pltpu.HBM)
    near_args = len(args) - far_args
    args = args[:near_args] + [pltpu.with_memory_space_constraint(x, pltpu.HBM) for x in args[near_args:]]
    return pl.pallas_call(
        kernel,
        out_shape=[jax.ShapeDtypeStruct(shape, kind) for shape, kind in outs],
        in_specs=[smem] * scalars + [vmem] * (near_args - scalars) + [hbm] * far_args,
        out_specs=[hbm] * far_outs + [vmem] * (len(outs) - far_outs),
        scratch_shapes=list(scratch),
        compiler_params=pltpu.CompilerParams(vmem_limit_bytes=16 * 2**20),
        cost_estimate=pl.CostEstimate(flops=flops, bytes_accessed=2**20, transcendentals=0),
    )(*args)


def body(
    mesh_shape, rhs, angles, self_mob, near_mat, near_weight, neighbours, cells, blob_weight,
    skel_perm, interp, sibling_ops, root_op,
):
    s = Sizes(mesh_shape, rhs, skel_perm)
    full = (s.rows, s.bodies)
    square = (s.rows, s.rows)
    tile = (8, LANES)
    far_shape = (s.skel, 2 * s.far_tiles * LANES)
    column = lax.axis_index("gx") * s.ny + lax.axis_index("gy")
    ids = jnp.stack([column, lax.axis_index("gz")]).astype(jnp.int32)

    def fetch(x, kind, dy):
        pairs = []
        for gx in range(s.nx):
            for gy in range(s.ny):
                pairs.append((s.beside(kind, gx) * s.ny + (gy + dy) % s.ny, gx * s.ny + gy))
        return lax.ppermute(x, ("gx", "gy"), pairs)

    def fetch_layers(x):
        parts, sent = [x], [x]
        for level in range(s.levels):
            pairs = [(z ^ (1 << level), z) for z in range(s.nz)]
            parts.append(lax.ppermute(sent[-1], "gz", pairs))
            if level + 1 < s.levels:
                shape = (2 * sent[-1].shape[0],) + tile
                sent += call(join_kernel, [(shape, f32)], [sent[-1], parts[-1]])
        return parts, sent[-1]

    def fetch_rims(rim, after=None):
        got = {}
        for dy in s.shifts:
            got["same", dy] = fetch(rim, "same", dy)
        if after is not None:
            (rim,) = call(order_kernel, [(rim.shape, f32)], [rim, after])
        got["other", 0] = fetch(rim, "other", 0)
        for dy in s.shifts:
            got["other", dy] = fetch(rim, "other", dy)
        got["partner", 0] = fetch(rim, "partner", 0)
        return got

    def forward_rims(got, after):
        for dy in s.shifts:
            held = got["same", dy]
            (held,) = call(order_kernel, [(held.shape, f32)], [held, after])
            got["partner", dy] = fetch(held, "partner", 0)

    def plane_sum(message, got, after):
        if not s.direct:
            return [lax.psum(message[s.half :], ("gx", "gy"))]
        quarter = [message] + [got[key] for key in s.sources if key[0] != "partner"]
        (half,) = call(functools.partial(half_kernel, s), [(tile, f32)], quarter + [after])
        return [half, fetch(half, "partner", 0)]

    flat = (3 * s.blobs, 1, s.bodies)
    small = (1, s.blobs)
    message, col, cells, f = call(
        functools.partial(start_kernel, s),
        [((s.message, LANES), f32), ((s.step, LANES), f32), (cells.shape, jnp.int32), (full, f32)],
        [rhs.reshape(flat), cells, blob_weight.reshape(small)],
        far_args=3,
        scratch=[pltpu.VMEM(flat, f32), pltpu.VMEM(small, f32), pltpu.SemaphoreType.DMA((3,))],
        flops=10**7,
    )
    got = fetch_rims(message)
    operators = [
        angles.reshape(3, 1, s.bodies), near_weight, neighbours, self_mob, near_mat, skel_perm, interp,
        sibling_ops, root_op,
    ]
    loc, gat, rot, sh, sl, nh, nl, oh, ol, gh, gl, fh, fl, *operators_out = call(
        functools.partial(setup_kernel, s),
        [(full, f32), (full, f32), ((16, s.bodies), f32)]
        + [(square, bf16)] * 4
        + [((s.bodies, s.bodies), bf16)] * 2
        + [((s.ghosts, s.bodies), bf16)] * 2
        + [(far_shape, bf16)] * 2
        + [((s.levels, 2 * s.skel, s.skel), bf16)] * 2
        + [((s.levels, s.skel, s.skel), bf16)] * 2
        + [((s.skel, s.skel), bf16)] * 2,
        [ids, f] + operators,
        scalars=1,
        far_args=len(operators),
        scratch=[
            pltpu.VMEM(square, f32), pltpu.VMEM((s.levels, 2 * s.skel, s.skel), f32), pltpu.VMEM(far_shape, f32)
        ]
        + [pltpu.VMEM(x.shape, x.dtype) for x in operators]
        + [pltpu.SemaphoreType.DMA((len(operators),))],
        flops=5 * 10**9,
    )
    forward_rims(got, rot)
    sums = plane_sum(message, got, rot)
    around = [got[key] for key in s.sources]
    gathered = call(
        functools.partial(gather_kernel, s),
        [(full, bf16), (full, bf16)],
        [gat, gh, gl] + around + [sums[0]],
        flops=10**9,
    )
    part, rim = call(
        functools.partial(near_kernel, s),
        [(full, f32), ((s.half, LANES), f32)],
        [loc, nh, nl, *gathered],
        flops=10**9,
    )
    (tiles,) = call(
        functools.partial(layer_kernel, s, len(sums)),
        [((2 + len(around),) + tile, f32)],
        [message] + sums + around + [gathered[1]],
    )
    layers, joined = fetch_layers(tiles)
    got = fetch_rims(rim, joined)
    places = call(
        functools.partial(place_kernel, s),
        [((s.skel, s.bodies), bf16), ((s.ghosts // LANES, s.skel, LANES), bf16)],
        [cells, tiles],
        flops=2 * 10**10,
    )
    u, charges, values, loc, gat, ortho, stat = call(
        functools.partial(first_kernel, s),
        [(full, f32), (tile, f32), ((s.ghosts // LANES,) + tile, f32)] + [(full, f32)] * 3 + [(tile, f32)],
        [part, fh, fl, *places, col, f, rot, sh, sl, oh, ol, *layers],
        flops=10**9,
    )
    forward_rims(got, places[1])
    gathered = call(
        functools.partial(gather_far_kernel, s),
        [(full, bf16), (full, bf16)],
        [gat, gh, gl, col, values] + [got[key] for key in s.sources],
        flops=10**9,
    )
    (packed,) = call(
        functools.partial(second_kernel, s),
        [((s.devices, 8, LANES), f32)],
        [loc, nh, nl, *gathered, cells, col, f, ortho, stat, message, charges],
        flops=10**9,
    )
    boxes = lax.all_to_all(packed, ("gx", "gy", "gz"), 0, 0)
    result, lsq = call(
        functools.partial(finish_kernel, s),
        [(flat, f32), ((1, 1), f32)],
        [ids, f, u, boxes, fetch(boxes, "partner", 0), col, *operators_out],
        scalars=1,
        far_outs=1,
        scratch=[pltpu.VMEM(flat, f32), pltpu.SemaphoreType.DMA((3,))],
        flops=10**7,
    )
    return result.reshape(rhs.shape), lsq.reshape(())


def solution(mesh):
    in_specs = (
        P("gx", "gy", None, None, "gz"),
        P("gx", "gy", None, "gz"),
        P(),
        P(),
        P("gx", "gy", None, "gz"),
        P("gx", "gy", None, "gz"),
        P("gx", "gy", "gz"),
        P(),
        P(),
        P(),
        P(),
        P(),
    )
    out_specs = (P("gx", "gy", None, None, "gz"), P())
    inner = functools.partial(body, dict(mesh.shape))
    return jax.shard_map(inner, mesh=mesh, in_specs=in_specs, out_specs=out_specs, check_vma=False)
```
